32 devices in a mesh: dp: 8 (over z, x), section: 4 (over y, core).
Axes of the slice: x: 2, y: 2, z: 4, core: 2. Of those that a mesh axis runs over, the one named last changes fastest.
Arguments:
- weights: bfloat16 [4, 6144, 256], P('section'), may hold values from -0.125 to 0.125
- inputs: bfloat16 [4, 4096, 2048], P('section', 'dp'), may hold values from -40 to 40
- out_grads: bfloat16 [4, 4096, 2048], P('section', 'dp'), may hold values from -40 to 40
- master: float32 [4, 6144, 256], P('section', 'dp'), may hold values from -0.125 to 0.125
- moment1: float32 [4, 6144, 256], P('section', 'dp'), may hold values from -6 to 6
- moment2: float32 [4, 6144, 256], P('section', 'dp'), may hold values from 0.1 to 10
Outputs:
- new_master: float32 [4, 6144, 256], P('section', 'dp')
- new_moment1: float32 [4, 6144, 256], P('section', 'dp')
- new_moment2: float32 [4, 6144, 256], P('section', 'dp')
- new_weights: bfloat16 [4, 6144, 256], P('section')
The draws below stay inside these ranges and needn't reach their ends.
All inputs are finite; a program needn't handle non-finite values.
Results may differ from the reference program's by a relative error of at most 0.001.
Values may be sent and summed in bfloat16 or wider, within the bound.
No kernel may reach another device: no remote copies, remote signals or barrier semaphores. Data moves between devices by JAX's collectives and lax.ppermute only.
A program may use at most 64 MiB of HBM per device.

```python
import math
import jax
import jax.numpy as jnp
from jax import lax

D = 2048
F = 256
MROWS = 256
STEP = 10
ROWS_DEV = 512
TOKENS = 4096
BLOCKS = 4
SHARD = 768


def heavy_columns(row_offsets):
    replicas = TOKENS // ROWS_DEV
    owner = (jnp.arange(D, dtype=jnp.int32)[None, :] * 0 + row_offsets) // SHARD
    rep = jnp.arange(replicas, dtype=jnp.int32)[:, None]
    hit = jnp.zeros((replicas, D), jnp.float32)
    for owned in owner:
        diff = (owned[None, :] - rep) % replicas
        near = (diff == 0) | (diff == 1) | (diff == replicas - 1) | (diff == replicas // 2)
        hit = jnp.maximum(hit, near.astype(jnp.float32))
    factor = 1.0 + 11.0 * hit
    return jnp.repeat(factor, ROWS_DEV, axis=0)


def scaled_field(key, rising, boost):
    keys = jax.random.split(key, 3)
    column = 10.0 ** (jnp.arange(D, dtype=jnp.float32) / D) * jax.random.uniform(keys[1], (D,), jnp.float32, 0.7, 1.4)
    row_scale = jnp.exp(jax.random.uniform(keys[2], (BLOCKS, TOKENS, 1), jnp.float32, 0.0, math.log(3.0)))
    base = jax.random.normal(keys[0], (BLOCKS, TOKENS, D), jnp.float32)
    base = jnp.clip(base, -6.0, 6.0)
    block_scale = 1.0 + rising * jnp.arange(BLOCKS, dtype=jnp.float32) / (BLOCKS - 1)
    field = base * column * row_scale * block_scale[:, None, None] * boost[None, :, :]
    return jnp.clip(field, -40.0, 40.0)


def draw_inputs(key, part):
    cols = jnp.arange(D, dtype=jnp.int32)
    boost = heavy_columns(jnp.stack([cols, cols + D]))
    return scaled_field(jax.random.fold_in(key, 11), 0.0, boost).astype(jnp.bfloat16)


def draw_out_grads(key, part):
    cols = jnp.arange(D, dtype=jnp.int32)
    boost = heavy_columns(jnp.stack([cols + 2 * D]))
    return scaled_field(jax.random.fold_in(key, 23), 2.0, boost).astype(jnp.bfloat16)


def shard_levels(own_key, shape, cuts, least, high):
    level = 1.0
    for axis_at, parts in cuts:
        steps = jax.random.uniform(jax.random.fold_in(jax.random.fold_in(own_key, 6), axis_at), (parts,), jnp.float32, least / len(cuts), high / len(cuts))
        level = level * jnp.repeat(jnp.exp(steps), shape[axis_at] // parts).reshape((-1,) + (1,) * (len(shape) - 1 - axis_at))
    return level


def scatter_about(rng, dims, deviation, bound, pieces=(), held_as=jnp.bfloat16):
    gain = shard_levels(rng, dims, pieces, -0.22, 0.18) if pieces else 1.0
    array = jax.random.normal(rng, dims, jnp.float32) * deviation * gain
    return jnp.minimum(jnp.maximum(array, -bound), bound).astype(held_as)


def setup_inputs(seed: int = 0) -> dict:
    splits = jax.random.split(jax.random.key(seed), 7)
    weights = scatter_about(splits[0], (BLOCKS, 3 * D, F), D ** -0.5, 0.125, ((0, 4),))
    inputs = draw_inputs(jax.random.fold_in(splits[6], 71), 0)
    out_grads = draw_out_grads(jax.random.fold_in(splits[6], 71), 0)
    master = scatter_about(splits[3], (BLOCKS, 3 * D, F), D ** -0.5, 0.125, ((0, 4), (1, 8)), jnp.float32)
    moment1 = scatter_about(splits[4], (BLOCKS, 3 * D, F), 1.0, 6.0, ((0, 4), (1, 8)), jnp.float32)
    moment2 = jnp.clip(jnp.exp(math.log(10.0) - 4.6051702 * jax.random.uniform(splits[5], (BLOCKS, 3 * D, F), jnp.float32) ** shard_levels(splits[5], (BLOCKS, 3 * D, F), ((0, 4), (1, 8)), -0.2, 0.2)), 0.1, 10.0)
    return dict(weights=weights, inputs=inputs, out_grads=out_grads, master=master, moment1=moment1, moment2=moment2)


def block_grads(x_rows, dy_rows, w_gate, w_up, w_down):
    pre_gate = jnp.dot(x_rows, w_gate, preferred_element_type=jnp.float32)
    pre_up = jnp.dot(x_rows, w_up, preferred_element_type=jnp.float32)
    sigma = jax.nn.sigmoid(pre_gate)
    silu_val = pre_gate * sigma
    hidden = (silu_val * pre_up).astype(jnp.bfloat16)
    d_hidden = jnp.dot(dy_rows, w_down, preferred_element_type=jnp.float32)
    d_gate = (d_hidden * pre_up * sigma * (1.0 + pre_gate * (1.0 - sigma))).astype(jnp.bfloat16)
    d_up = (d_hidden * silu_val).astype(jnp.bfloat16)
    g_gate = jnp.dot(x_rows.T, d_gate, preferred_element_type=jnp.float32)
    g_up = jnp.dot(x_rows.T, d_up, preferred_element_type=jnp.float32)
    g_down = jnp.dot(dy_rows.T, hidden, preferred_element_type=jnp.float32)
    return jnp.concatenate([g_gate, g_up, g_down], axis=0)

def section_grad(operands):
    section_w, section_x, section_dy = operands
    w_gate = section_w[:D]
    w_up = section_w[D:2 * D]
    w_down = section_w[2 * D:]
    x_blocks = section_x.reshape(-1, MROWS, D)
    dy_blocks = section_dy.reshape(-1, MROWS, D)

    def step(carry, pair):
        return (carry + block_grads(pair[0], pair[1], w_gate, w_up, w_down), None)
    start = jnp.zeros((3 * D, F), jnp.float32)
    total, unused = lax.scan(step, start, (x_blocks, dy_blocks))
    return total

def reference(weights, inputs, out_grads, master, moment1, moment2):
    grad = lax.map(section_grad, (weights, inputs, out_grads))
    total = jnp.sum(grad * grad)
    max_norm = jnp.sqrt(jnp.float32(BLOCKS * 3 * D * F))
    clip = jnp.minimum(jnp.float32(1.0), max_norm / (jnp.sqrt(total) + 1e-06))
    clipped = clip * grad
    new_moment1 = 0.9 * moment1 + 0.1 * clipped
    new_moment2 = 0.95 * moment2 + 0.05 * clipped * clipped
    first_fix = 1.0 - 0.9 ** STEP
    second_fix = 1.0 - 0.95 ** STEP
    update = new_moment1 / first_fix / (jnp.sqrt(new_moment2 / second_fix) + 1e-08) + 0.1 * master
    new_master = master - 0.01 * update
    return (new_master, new_moment1, new_moment2, new_master.astype(jnp.bfloat16))
```

```python
import math

import jax
import jax.numpy as jnp
from jax import lax
from jax.experimental import pallas as pl
from jax.experimental.pallas import tpu as pltpu
from jax.sharding import PartitionSpec as P

MROWS = 256
STEP = 10
PAD = 16
POWER = 8
TOP = 32768.0


def forward_pieces(x_rows, dy_rows, w_gate, w_up, w_down):
    pre_gate = jnp.dot(x_rows, w_gate, preferred_element_type=jnp.float32)
    pre_up = jnp.dot(x_rows, w_up, preferred_element_type=jnp.float32)
    d_hidden = jnp.dot(dy_rows, w_down, preferred_element_type=jnp.float32)
    return activation(pre_gate, pre_up, d_hidden)


def activation(pre_gate, pre_up, d_hidden):
    sigma = jax.nn.sigmoid(pre_gate)
    silu_val = pre_gate * sigma
    hidden = (silu_val * pre_up).astype(jnp.bfloat16)
    d_gate = (d_hidden * pre_up * sigma * (1.0 + pre_gate * (1.0 - sigma))).astype(jnp.bfloat16)
    d_up = (d_hidden * silu_val).astype(jnp.bfloat16)
    return d_gate, d_up, hidden


def block_grads(x_rows, dy_rows, w_gate, w_up, w_down):
    d_gate, d_up, hidden = forward_pieces(x_rows, dy_rows, w_gate, w_up, w_down)
    g_gate = jnp.dot(x_rows.T, d_gate, preferred_element_type=jnp.float32)
    g_up = jnp.dot(x_rows.T, d_up, preferred_element_type=jnp.float32)
    g_down = jnp.dot(dy_rows.T, hidden, preferred_element_type=jnp.float32)
    return jnp.concatenate([g_gate, g_up, g_down], axis=0)


def adam(clip, shard, old_param, first, second):
    clipped = clip * shard
    new_first = 0.9 * first + 0.1 * clipped
    new_second = 0.95 * second + 0.05 * clipped * clipped
    first_fix = 1.0 - 0.9**STEP
    second_fix = 1.0 - 0.95**STEP
    update = new_first / first_fix / (jnp.sqrt(new_second / second_fix) + 1e-08) + 0.1 * old_param
    return old_param - 0.01 * update, new_first, new_second


def clip_of(total, max_norm):
    return jnp.minimum(jnp.float32(1.0), max_norm / (jnp.sqrt(total) + 1e-06))


def plain(weights, inputs, out_grads, master, moment1, moment2):
    stacked = weights[0]
    width = stacked.shape[0] // 3
    local_grad = jnp.zeros(stacked.shape, jnp.float32)
    for start in range(0, inputs.shape[1], MROWS):
        x_rows = inputs[0, start : start + MROWS]
        dy_rows = out_grads[0, start : start + MROWS]
        local_grad = local_grad + block_grads(
            x_rows, dy_rows, stacked[:width], stacked[width : 2 * width], stacked[2 * width :]
        )
    shard = lax.psum_scatter(local_grad, "dp", scatter_dimension=0, tiled=True)
    total = lax.psum(jnp.sum(shard * shard), ("dp", "section"))
    max_norm = jnp.sqrt(jnp.float32(lax.axis_size("section") * stacked.size))
    new_param, new_first, new_second = adam(clip_of(total, max_norm), shard, master[0], moment1[0], moment2[0])
    gathered = lax.all_gather(new_param.astype(jnp.bfloat16), "dp", axis=0, tiled=True)
    return new_param[None], new_first[None], new_second[None], gathered[None]


def forward_kernel(x_ref, dy_ref, wg_ref, wu_ref, wd_ref, out_ref, a_ref, b_ref, h_ref):
    step = pl.program_id(0)

    @pl.when(step == 0)
    def _():
        a_ref[...] = jnp.zeros_like(a_ref)
        b_ref[...] = jnp.zeros_like(b_ref)
        h_ref[...] = jnp.zeros_like(h_ref)

    a_ref[...] += jnp.dot(x_ref[...], wg_ref[...], preferred_element_type=jnp.float32)
    b_ref[...] += jnp.dot(x_ref[...], wu_ref[...], preferred_element_type=jnp.float32)
    h_ref[...] += jnp.dot(dy_ref[...], wd_ref[...], preferred_element_type=jnp.float32)

    @pl.when(step == pl.num_programs(0) - 1)
    def _():
        d_gate, d_up, hidden = activation(a_ref[...], b_ref[...], h_ref[...])
        out_ref[0] = d_gate
        out_ref[1] = d_up
        out_ref[2] = hidden


def forward(x, dy, stacked):
    tokens, width = x.shape
    hidden = stacked.shape[1]
    depth = math.gcd(width, 512)
    steps = width // depth
    return pl.pallas_call(
        forward_kernel,
        grid=(steps,),
        in_specs=[
            pl.BlockSpec((tokens, depth), lambda k: (0, k)),
            pl.BlockSpec((tokens, depth), lambda k: (0, k)),
            pl.BlockSpec((depth, hidden), lambda k: (k, 0)),
            pl.BlockSpec((depth, hidden), lambda k: (k + steps, 0)),
            pl.BlockSpec((depth, hidden), lambda k: (k + 2 * steps, 0)),
        ],
        out_specs=pl.BlockSpec((3, tokens, hidden), lambda k: (0, 0, 0)),
        out_shape=jax.ShapeDtypeStruct((3, tokens, hidden), jnp.bfloat16),
        scratch_shapes=[pltpu.VMEM((tokens, hidden), jnp.float32)] * 3,
        compiler_params=pltpu.CompilerParams(vmem_limit_bytes=32 << 20),
        cost_estimate=pl.CostEstimate(
            flops=2 * tokens * stacked.size, bytes_accessed=2 * (x.size + dy.size + stacked.size), transcendentals=0
        ),
        name="forward",
    )(x, dy, stacked, stacked, stacked)


def encode(value):
    scale = jnp.max(jnp.abs(value), axis=0, keepdims=True)
    scale = jnp.maximum(scale, 1e-30).astype(jnp.bfloat16).astype(jnp.float32)
    v = value * (TOP / scale)
    v2 = v * v
    v4 = v2 * v2
    v8 = v4 * v4
    return jnp.where(v < 0.0, -v8, v8).astype(jnp.bfloat16), scale


def decode(code, scale):
    code = code.astype(jnp.float32)
    size = jnp.abs(code)
    root = jnp.exp(jnp.log(jnp.maximum(size, 1e-37)) * (1.0 / POWER)) * (scale * (1.0 / TOP))
    root = jnp.where(size > 0.0, root, 0.0)
    return jnp.where(code < 0.0, -root, root)


def lookup(table, index):
    out = jnp.int32(table[0])
    for at, value in enumerate(table[1:], 1):
        out = jnp.where(index == at, jnp.int32(value), out)
    return out


def piece_kernel(owner, per, count, last, *refs):
    step = pl.program_id(0)
    x_ref, dy_ref, d_ref = refs[:3]
    got = refs[3 : 3 + 2 * count]
    outs = refs[3 + 2 * count :]
    rows = x_ref.shape[1]
    kind = lax.div(owner() * pl.num_programs(0) + step, per)
    left = jnp.where(kind == 2, dy_ref[...], x_ref[...])
    total = lax.dot_general(left, d_ref[0], (((0,), (0,)), ((), ())), preferred_element_type=jnp.float32)
    for at in range(count):
        scales = got[2 * at + 1][...].astype(jnp.float32)
        row = lax.broadcasted_iota(jnp.int32, scales.shape, 0)
        scale = jnp.sum(jnp.where(row == step, scales, 0.0), axis=0, keepdims=True)
        total = total + decode(got[2 * at][...], scale)
    if last:
        outs[0][...] = total
        square = jnp.sum(total * total)
        outs[1][0, 0] = jnp.where(step == 0, 0.0, outs[1][0, 0]) + square
    else:
        out_ref, scales_ref = outs
        code, scale = encode(total)
        out_ref[pl.ds(pl.multiple_of(step * rows, rows), rows), :] = code
        row = lax.broadcasted_iota(jnp.int32, scales_ref.shape, 0)
        scales_ref[...] = jnp.where(row == step, scale, jnp.where(step == 0, 0.0, scales_ref[...]))
        out_ref[pl.ds(out_ref.shape[0] - PAD, PAD), :] = scales_ref[...].astype(jnp.bfloat16)


def piece(x, dy, factors, table, rows, got=(), last=False):
    tokens, width = x.shape
    hidden = factors.shape[2]
    per = width // rows
    shard = 3 * width // len(table)
    steps = shard // rows

    def owner():
        return lookup(table, lax.axis_index("dp"))

    def column(i):
        return (0, lax.rem(owner() * steps + i, per))

    in_specs = [
        pl.BlockSpec((tokens, rows), column),
        pl.BlockSpec((tokens, rows), column),
        pl.BlockSpec((1, tokens, hidden), lambda i: (lax.div(owner() * steps + i, per), 0, 0)),
    ]
    for _ in got:
        in_specs += [
            pl.BlockSpec((rows, hidden), lambda i: (i, 0)),
            pl.BlockSpec((PAD, hidden), lambda i: (shard // PAD, 0)),
        ]
    if last:
        out_specs = [
            pl.BlockSpec((rows, hidden), lambda i: (i, 0)),
            pl.BlockSpec((1, 1), lambda i: (0, 0), memory_space=pltpu.SMEM),
        ]
        out_shape = [
            jax.ShapeDtypeStruct((shard, hidden), jnp.float32),
            jax.ShapeDtypeStruct((1, 1), jnp.float32),
        ]
        scratch = []
    else:
        out_specs = pl.BlockSpec((shard + PAD, hidden), lambda i: (0, 0))
        out_shape = jax.ShapeDtypeStruct((shard + PAD, hidden), jnp.bfloat16)
        scratch = [pltpu.VMEM((PAD, hidden), jnp.float32)]
    return pl.pallas_call(
        lambda *refs: piece_kernel(owner, per, len(got), last, *refs),
        grid=(steps,),
        in_specs=in_specs,
        out_specs=out_specs,
        out_shape=out_shape,
        scratch_shapes=scratch,
        compiler_params=pltpu.CompilerParams(vmem_limit_bytes=32 << 20),
        cost_estimate=pl.CostEstimate(
            flops=2 * tokens * shard * hidden,
            bytes_accessed=4 * tokens * shard + 2 * factors.size + 2 * shard * hidden * (len(got) + 1),
            transcendentals=2 * shard * hidden * len(got),
        ),
        name="piece",
    )(x, dy, factors, *[m for message in got for m in (message, message)])


def update_kernel(max_norm, total_ref, g_ref, p_ref, m1_ref, m2_ref, new_p, new_m1, new_m2, new_w):
    clip = clip_of(jnp.full((1, 1), total_ref[0, 0]), max_norm)
    param, first, second = adam(clip, g_ref[...], p_ref[...], m1_ref[...], m2_ref[...])
    new_p[...] = param
    new_m1[...] = first
    new_m2[...] = second
    new_w[...] = param.astype(jnp.bfloat16)


def update(total, shard, param, first, second, max_norm, rows):
    block = pl.BlockSpec((rows, shard.shape[1]), lambda i: (i, 0))
    wide = jax.ShapeDtypeStruct(shard.shape, jnp.float32)
    return pl.pallas_call(
        lambda *refs: update_kernel(max_norm, *refs),
        grid=(shard.shape[0] // rows,),
        in_specs=[pl.BlockSpec((1, 1), lambda i: (0, 0), memory_space=pltpu.SMEM)] + [block] * 4,
        out_specs=[block] * 4,
        out_shape=[wide] * 3 + [jax.ShapeDtypeStruct(shard.shape, jnp.bfloat16)],
        compiler_params=pltpu.CompilerParams(vmem_limit_bytes=32 << 20),
        cost_estimate=pl.CostEstimate(flops=20 * shard.size, bytes_accessed=30 * shard.size, transcendentals=shard.size),
        name="update",
    )(total, shard, param, first, second)


def paired(weights, inputs, out_grads, master, moment1, moment2):
    n = lax.axis_size("dp")
    pairs = n // 2
    ring = list(range(0, pairs, 2)) + list(range(pairs - 1 - pairs % 2, 0, -2))
    place = {pair: at for at, pair in enumerate(ring)}

    def at_offset(r, offset, flip):
        return 2 * ring[(place[r // 2] + offset) % pairs] + ((r % 2) ^ flip)

    def table(offset, flip):
        return [at_offset(r, offset, flip) for r in range(n)]

    def send(value, offset, flip=0):
        return lax.ppermute(value, "dp", [(r, at_offset(r, offset, flip)) for r in range(n)])

    stacked = weights[0]
    x, dy = inputs[0], out_grads[0]
    width = x.shape[1]
    shard_rows = stacked.shape[0] // n
    rows = math.gcd(math.gcd(shard_rows, width), 256)
    factors = forward(x, dy, stacked)

    ahead = pairs // 2
    behind = pairs - 1 - ahead
    order = sorted(range(-behind, ahead + 1), key=lambda o: (-abs(o), -o))

    crossed = {}
    for offset in order:
        crossed[offset] = send(piece(x, dy, factors, table(offset, 1), rows), 0, 1)

    arrived = {}
    for offset in order:
        got = [crossed[offset]] + [arrived[k] for k in ((offset, 1), (offset, -1)) if k in arrived]
        if offset == 0:
            shard, square = piece(x, dy, factors, table(0, 0), rows, got, last=True)
        else:
            way = 1 if offset > 0 else -1
            total = piece(x, dy, factors, table(offset, 0), rows, got)
            arrived[(offset - way, way)] = send(total, way)

    total = lax.psum(square, ("dp", "section"))
    max_norm = math.sqrt(lax.axis_size("section") * stacked.size)
    new_param, new_first, new_second, own = update(
        total, shard, master[0], moment1[0], moment2[0], max_norm, rows
    )

    r = lax.axis_index("dp")
    gathered = jnp.zeros_like(stacked)

    def put(gathered, value, offset, flip):
        return lax.dynamic_update_slice(gathered, value, (lookup(table(offset, flip), r) * shard_rows, 0))

    held = {0: own}
    for step in range(1, ahead + 1):
        held[-step] = send(held[1 - step], 1)
        if step <= behind:
            held[step] = send(held[step - 1], -1)
    for offset in sorted(held, key=lambda o: (abs(o), o)):
        other = send(held[offset], 0, 1)
        gathered = put(gathered, held[offset], offset, 0)
        gathered = put(gathered, other, offset, 1)
    return new_param[None], new_first[None], new_second[None], gathered[None]


def local(weights, *rest):
    n = lax.axis_size("dp")
    height = weights.shape[1]
    fits = n % 2 == 0 and n > 2 and height % n == 0 and (height // n) % 128 == 0 and (height // 3) % 128 == 0
    return (paired if fits else plain)(weights, *rest)


def solution(mesh):
    whole = P("section", None, None)
    split = P("section", "dp", None)
    return jax.shard_map(
        local,
        mesh=mesh,
        in_specs=(whole, split, split, split, split, split),
        out_specs=(split, split, split, whole),
        check_vma=False,
    )
```

```python
import math

import jax
import jax.numpy as jnp
from jax import lax
from jax.experimental import pallas as pl
from jax.experimental.pallas import tpu as pltpu
from jax.sharding import PartitionSpec as P

MROWS = 256
STEP = 10
PAD = 16
POWER = 8
TOP = 32768.0


def forward_pieces(x_rows, dy_rows, w_gate, w_up, w_down):
    pre_gate = jnp.dot(x_rows, w_gate, preferred_element_type=jnp.float32)
    pre_up = jnp.dot(x_rows, w_up, preferred_element_type=jnp.float32)
    d_hidden = jnp.dot(dy_rows, w_down, preferred_element_type=jnp.float32)
    return activation(pre_gate, pre_up, d_hidden)


def activation(pre_gate, pre_up, d_hidden):
    sigma = jax.nn.sigmoid(pre_gate)
    silu_val = pre_gate * sigma
    hidden = (silu_val * pre_up).astype(jnp.bfloat16)
    d_gate = (d_hidden * pre_up * sigma * (1.0 + pre_gate * (1.0 - sigma))).astype(jnp.bfloat16)
    d_up = (d_hidden * silu_val).astype(jnp.bfloat16)
    return d_gate, d_up, hidden


def block_grads(x_rows, dy_rows, w_gate, w_up, w_down):
    d_gate, d_up, hidden = forward_pieces(x_rows, dy_rows, w_gate, w_up, w_down)
    g_gate = jnp.dot(x_rows.T, d_gate, preferred_element_type=jnp.float32)
    g_up = jnp.dot(x_rows.T, d_up, preferred_element_type=jnp.float32)
    g_down = jnp.dot(dy_rows.T, hidden, preferred_element_type=jnp.float32)
    return jnp.concatenate([g_gate, g_up, g_down], axis=0)


def adam(clip, shard, old_param, first, second):
    clipped = clip * shard
    new_first = 0.9 * first + 0.1 * clipped
    new_second = 0.95 * second + 0.05 * clipped * clipped
    first_fix = 1.0 / (1.0 - 0.9**STEP)
    second_fix = 1.0 / (1.0 - 0.95**STEP)
    update = new_first * first_fix / (jnp.sqrt(new_second * second_fix) + 1e-08) + 0.1 * old_param
    return old_param - 0.01 * update, new_first, new_second


def clip_of(total, max_norm):
    return jnp.minimum(jnp.float32(1.0), max_norm / (jnp.sqrt(total) + 1e-06))


def plain(weights, inputs, out_grads, master, moment1, moment2):
    stacked = weights[0]
    width = stacked.shape[0] // 3
    local_grad = jnp.zeros(stacked.shape, jnp.float32)
    for start in range(0, inputs.shape[1], MROWS):
        x_rows = inputs[0, start : start + MROWS]
        dy_rows = out_grads[0, start : start + MROWS]
        local_grad = local_grad + block_grads(
            x_rows, dy_rows, stacked[:width], stacked[width : 2 * width], stacked[2 * width :]
        )
    shard = lax.psum_scatter(local_grad, "dp", scatter_dimension=0, tiled=True)
    total = lax.psum(jnp.sum(shard * shard), ("dp", "section"))
    max_norm = jnp.sqrt(jnp.float32(lax.axis_size("section") * stacked.size))
    new_param, new_first, new_second = adam(clip_of(total, max_norm), shard, master[0], moment1[0], moment2[0])
    gathered = lax.all_gather(new_param.astype(jnp.bfloat16), "dp", axis=0, tiled=True)
    return new_param[None], new_first[None], new_second[None], gathered[None]


def encode(value):
    scale = jnp.max(jnp.abs(value), axis=0, keepdims=True)
    scale = jnp.maximum(scale, 1e-30).astype(jnp.bfloat16).astype(jnp.float32)
    v = value * (TOP / scale)
    v2 = v * v
    v4 = v2 * v2
    v8 = v4 * v4
    return jnp.where(v < 0.0, -v8, v8).astype(jnp.bfloat16), scale


def decode(code, scale):
    code = code.astype(jnp.float32)
    size = jnp.abs(code)
    root = jnp.exp(jnp.log(jnp.maximum(size, 1e-37)) * (1.0 / POWER)) * (scale * (1.0 / TOP))
    root = jnp.where(size > 0.0, root, 0.0)
    return jnp.where(code < 0.0, -root, root)


def lookup(table, index):
    out = jnp.int32(table[0])
    for at, value in enumerate(table[1:], 1):
        out = jnp.where(index == at, jnp.int32(value), out)
    return out


def message_rows(left, factor, out_ref, step, scales):
    rows = left.shape[1]
    total = lax.dot_general(left, factor, (((0,), (0,)), ((), ())), preferred_element_type=jnp.float32)
    code, scale = encode(total)
    out_ref[step * rows : (step + 1) * rows, :] = code
    row = lax.broadcasted_iota(jnp.int32, scales.shape, 0)
    return jnp.where(row == step, scale, scales)


def forward_kernel(owner, rows, x_hbm, dy_hbm, w_hbm, factors_ref, out_ref, x_ref, dy_ref, w_ref, sems):
    width = x_hbm.shape[1]
    copies = [
        pltpu.make_async_copy(x_hbm, x_ref, sems.at[0]),
        pltpu.make_async_copy(w_hbm.at[:width], w_ref.at[:width], sems.at[1]),
        pltpu.make_async_copy(w_hbm.at[width : 2 * width], w_ref.at[width : 2 * width], sems.at[2]),
        pltpu.make_async_copy(dy_hbm, dy_ref, sems.at[3]),
        pltpu.make_async_copy(w_hbm.at[2 * width :], w_ref.at[2 * width :], sems.at[4]),
    ]
    for copy in copies:
        copy.start()
    copies[0].wait()
    copies[1].wait()
    pre_gate = jnp.dot(x_ref[...], w_ref[:width], preferred_element_type=jnp.float32)
    copies[2].wait()
    pre_up = jnp.dot(x_ref[...], w_ref[width : 2 * width], preferred_element_type=jnp.float32)
    copies[3].wait()
    copies[4].wait()
    d_hidden = jnp.dot(dy_ref[...], w_ref[2 * width :], preferred_element_type=jnp.float32)
    d_gate, d_up, hidden = activation(pre_gate, pre_up, d_hidden)
    factors_ref[0] = d_gate
    factors_ref[1] = d_up
    factors_ref[2] = hidden
    steps = (out_ref.shape[0] - PAD) // rows
    scales = jnp.zeros((PAD, out_ref.shape[1]), jnp.float32)
    for step in range(steps):
        at = owner() * steps + step
        kind = lax.div(at, width // rows)
        column = pl.ds(pl.multiple_of(lax.rem(at, width // rows) * rows, rows), rows)
        left = jnp.where(kind == 2, dy_ref[:, column], x_ref[:, column])
        scales = message_rows(left, factors_ref[kind], out_ref, step, scales)
    out_ref[steps * rows :, :] = scales.astype(jnp.bfloat16)


def forward(x, dy, stacked, table, rows):
    tokens, width = x.shape
    hidden = stacked.shape[1]
    shard = stacked.shape[0] // len(table)

    def owner():
        return lookup(table, lax.axis_index("dp"))

    return pl.pallas_call(
        lambda *refs: forward_kernel(owner, rows, *refs),
        in_specs=[pl.BlockSpec(memory_space=pltpu.HBM)] * 3,
        out_shape=[
            jax.ShapeDtypeStruct((3, tokens, hidden), jnp.bfloat16),
            jax.ShapeDtypeStruct((shard + PAD, hidden), jnp.bfloat16),
        ],
        scratch_shapes=[
            pltpu.VMEM(x.shape, x.dtype),
            pltpu.VMEM(dy.shape, dy.dtype),
            pltpu.VMEM(stacked.shape, stacked.dtype),
            pltpu.SemaphoreType.DMA((5,)),
        ],
        compiler_params=pltpu.CompilerParams(vmem_limit_bytes=40 << 20),
        cost_estimate=pl.CostEstimate(
            flops=2 * tokens * (stacked.size + shard * hidden),
            bytes_accessed=2 * (x.size + dy.size + stacked.size),
            transcendentals=tokens * hidden,
        ),
        name="forward",
    )(x, dy, stacked)


def piece_kernel(owner, per, count, after, last, *refs):
    step = pl.program_id(0)
    x_ref, dy_ref, d_ref = refs[:3]
    got = refs[3 : 3 + 2 * count]
    outs = refs[3 + 2 * count + after :]
    rows = x_ref.shape[1]
    kind = lax.div(owner() * pl.num_programs(0) + step, per)
    left = jnp.where(kind == 2, dy_ref[...], x_ref[...])
    total = lax.dot_general(left, d_ref[0], (((0,), (0,)), ((), ())), preferred_element_type=jnp.float32)
    for at in range(count):
        scales = got[2 * at + 1][...].astype(jnp.float32)
        row = lax.broadcasted_iota(jnp.int32, scales.shape, 0)
        scale = jnp.sum(jnp.where(row == step, scales, 0.0), axis=0, keepdims=True)
        total = total + decode(got[2 * at][...], scale)
    if last:
        outs[0][...] = total
        tile = jnp.sum((total * total).reshape(rows // 8, 8, -1), axis=0)
        tile = sum(tile[:, at : at + 128] for at in range(0, tile.shape[1], 128))
        squares = outs[1]
        tile = tile + jnp.where(step == 0, 0.0, squares[:8])
        for at in range(0, squares.shape[0], 8):
            squares[at : at + 8] = tile
    else:
        out_ref, scales_ref = outs
        code, scale = encode(total)
        out_ref[pl.ds(pl.multiple_of(step * rows, rows), rows), :] = code
        row = lax.broadcasted_iota(jnp.int32, scales_ref.shape, 0)
        scales_ref[...] = jnp.where(row == step, scale, jnp.where(step == 0, 0.0, scales_ref[...]))
        out_ref[pl.ds(out_ref.shape[0] - PAD, PAD), :] = scales_ref[...].astype(jnp.bfloat16)


def piece(x, dy, factors, table, rows, got=(), after=None, last=0):
    tokens, width = x.shape
    hidden = factors.shape[2]
    per = width // rows
    shard = 3 * width // len(table)
    steps = shard // rows

    def owner():
        return lookup(table, lax.axis_index("dp"))

    def column(i):
        return (0, lax.rem(owner() * steps + i, per))

    in_specs = [
        pl.BlockSpec((tokens, rows), column),
        pl.BlockSpec((tokens, rows), column),
        pl.BlockSpec((1, tokens, hidden), lambda i: (lax.div(owner() * steps + i, per), 0, 0)),
    ]
    for _ in got:
        in_specs += [
            pl.BlockSpec((rows, hidden), lambda i: (i, 0)),
            pl.BlockSpec((PAD, hidden), lambda i: (shard // PAD, 0)),
        ]
    extra = []
    if after is not None:
        extra = [after]
        in_specs.append(pl.BlockSpec(memory_space=pl.ANY))
    if last:
        out_specs = [
            pl.BlockSpec((rows, hidden), lambda i: (i, 0)),
            pl.BlockSpec((8 * last, 128), lambda i: (0, 0)),
        ]
        out_shape = [
            jax.ShapeDtypeStruct((shard, hidden), jnp.float32),
            jax.ShapeDtypeStruct((8 * last, 128), jnp.float32),
        ]
        scratch = []
    else:
        out_specs = pl.BlockSpec((shard + PAD, hidden), lambda i: (0, 0))
        out_shape = jax.ShapeDtypeStruct((shard + PAD, hidden), jnp.bfloat16)
        scratch = [pltpu.VMEM((PAD, hidden), jnp.float32)]
    return pl.pallas_call(
        lambda *refs: piece_kernel(owner, per, len(got), len(extra), last, *refs),
        grid=(steps,),
        in_specs=in_specs,
        out_specs=out_specs,
        out_shape=out_shape,
        scratch_shapes=scratch,
        compiler_params=pltpu.CompilerParams(vmem_limit_bytes=32 << 20),
        cost_estimate=pl.CostEstimate(
            flops=2 * tokens * shard * hidden,
            bytes_accessed=4 * tokens * shard + 2 * factors.size + 2 * shard * hidden * (len(got) + 1),
            transcendentals=2 * shard * hidden * len(got),
        ),
        name="piece",
    )(x, dy, factors, *[m for message in got for m in (message, message)], *extra)


def update_kernel(max_norm, total_ref, g_ref, p_ref, m1_ref, m2_ref, new_p, new_m1, new_m2, new_w):
    clip = clip_of(jnp.sum(total_ref[...], keepdims=True), max_norm)
    param, first, second = adam(clip, g_ref[...], p_ref[...], m1_ref[...], m2_ref[...])
    new_p[...] = param
    new_m1[...] = first
    new_m2[...] = second
    new_w[...] = param.astype(jnp.bfloat16)


def update(total, shard, param, first, second, max_norm, rows):
    block = pl.BlockSpec((rows, shard.shape[1]), lambda i: (i, 0))
    wide = jax.ShapeDtypeStruct(shard.shape, jnp.float32)
    return pl.pallas_call(
        lambda *refs: update_kernel(max_norm, *refs),
        grid=(shard.shape[0] // rows,),
        in_specs=[pl.BlockSpec(total.shape, lambda i: (0, 0))] + [block] * 4,
        out_specs=[block] * 4,
        out_shape=[wide] * 3 + [jax.ShapeDtypeStruct(shard.shape, jnp.bfloat16)],
        compiler_params=pltpu.CompilerParams(vmem_limit_bytes=32 << 20),
        cost_estimate=pl.CostEstimate(flops=20 * shard.size, bytes_accessed=30 * shard.size, transcendentals=shard.size),
        name="update",
    )(total, shard, param, first, second)


def put_kernel(places, rows, *refs):
    values, out, sems = refs[: len(places)], refs[-2], refs[-1]
    copies = []
    for at, (value, place) in enumerate(zip(values, places)):
        start = pl.multiple_of(lookup(place, lax.axis_index("dp")) * rows, rows)
        copies.append(pltpu.make_async_copy(value, out.at[pl.ds(start, rows)], sems.at[at]))
        copies[-1].start()
    for copy in copies:
        copy.wait()


def put(buffer, values, places, height):
    rows, columns = values[0].shape
    return pl.pallas_call(
        lambda *refs: put_kernel(places, rows, *refs),
        in_specs=[pl.BlockSpec(memory_space=pl.ANY)] * len(values)
        + [pl.BlockSpec(memory_space=pltpu.HBM)] * (buffer is not None),
        out_specs=pl.BlockSpec(memory_space=pltpu.HBM),
        out_shape=jax.ShapeDtypeStruct((height, columns), values[0].dtype),
        input_output_aliases={} if buffer is None else {len(values): 0},
        scratch_shapes=[pltpu.SemaphoreType.DMA((len(values),))],
        cost_estimate=pl.CostEstimate(flops=0, bytes_accessed=4 * len(values) * values[0].size, transcendentals=0),
        name="put",
    )(*values, *([] if buffer is None else [buffer]))


def paired(weights, inputs, out_grads, master, moment1, moment2):
    n = lax.axis_size("dp")
    pairs = n // 2
    ring = list(range(0, pairs, 2)) + list(range(pairs - 1 - pairs % 2, 0, -2))
    place = {pair: at for at, pair in enumerate(ring)}

    def at_offset(r, offset, flip):
        return 2 * ring[(place[r // 2] + offset) % pairs] + ((r % 2) ^ flip)

    def table(offset, flip):
        return [at_offset(r, offset, flip) for r in range(n)]

    def send(value, offset, flip=0):
        return lax.ppermute(value, "dp", [(r, at_offset(r, offset, flip)) for r in range(n)])

    stacked = weights[0]
    x, dy = inputs[0], out_grads[0]
    width = x.shape[1]
    shard_rows = stacked.shape[0] // n
    rows = math.gcd(math.gcd(shard_rows, width), 256)

    ahead = pairs // 2
    behind = pairs - 1 - ahead
    order = sorted(range(-behind, ahead + 1), key=lambda o: (-abs(o), -o))

    factors, message = forward(x, dy, stacked, table(order[0], 1), rows)
    crossed = {order[0]: send(message, 0, 1)}
    for offset in order[1:]:
        message = piece(x, dy, factors, table(offset, 1), rows, after=message)
        crossed[offset] = send(message, 0, 1)

    arrived = {}
    devices = n * lax.axis_size("section")
    for offset in order:
        got = [crossed[offset]] + [arrived[k] for k in ((offset, 1), (offset, -1)) if k in arrived]
        if offset == 0:
            shard, squares = piece(x, dy, factors, table(0, 0), rows, got, last=devices)
        else:
            way = 1 if offset > 0 else -1
            message = piece(x, dy, factors, table(offset, 0), rows, got, after=message)
            arrived[(offset - way, way)] = send(message, way)

    total = lax.all_to_all(squares, ("dp", "section"), 0, 0, tiled=True)
    max_norm = math.sqrt(lax.axis_size("section") * stacked.size)
    new_param, new_first, new_second, own = update(
        total, shard, master[0], moment1[0], moment2[0], max_norm, rows
    )

    held = {0: own}
    other = {0: send(own, 0, 1)}
    for step in range(1, ahead + 1):
        held[-step] = send(held[1 - step], 1)
        other[-step] = send(held[-step], 0, 1)
        if step <= behind:
            held[step] = send(held[step - 1], -1)
            other[step] = send(held[step], 0, 1)
    gathered = None
    height = stacked.shape[0]
    final = -ahead
    for offset in held:
        values, places = [held[offset]], [table(offset, 0)]
        if offset != final:
            values.append(other[offset])
            places.append(table(offset, 1))
        gathered = put(gathered, values, places, height)
    gathered = put(gathered, [other[final]], [table(final, 1)], height)
    return new_param[None], new_first[None], new_second[None], gathered[None]


def local(weights, *rest):
    n = lax.axis_size("dp")
    height = weights.shape[1]
    fits = n % 2 == 0 and n > 2 and height % n == 0 and (height // n) % 128 == 0 and (height // 3) % 128 == 0
    return (paired if fits else plain)(weights, *rest)


def solution(mesh):
    whole = P("section", None, None)
    split = P("section", "dp", None)
    return jax.shard_map(
        local,
        mesh=mesh,
        in_specs=(whole, split, split, split, split, split),
        out_specs=(split, split, split, whole),
        check_vma=False,
    )
```

```python
import math

import jax
import jax.numpy as jnp
from jax import lax
from jax.experimental import pallas as pl
from jax.experimental.pallas import tpu as pltpu
from jax.sharding import PartitionSpec as P

MROWS = 256
STEP = 10
PAD = 16
POWER = 8
TOP = 32768.0
CHEAP = pl.CostEstimate(flops=1024, bytes_accessed=1024, transcendentals=0)


def forward_pieces(x_rows, dy_rows, w_gate, w_up, w_down):
    pre_gate = jnp.dot(x_rows, w_gate, preferred_element_type=jnp.float32)
    pre_up = jnp.dot(x_rows, w_up, preferred_element_type=jnp.float32)
    d_hidden = jnp.dot(dy_rows, w_down, preferred_element_type=jnp.float32)
    return activation(pre_gate, pre_up, d_hidden)


def activation(pre_gate, pre_up, d_hidden):
    sigma = jax.nn.sigmoid(pre_gate)
    silu_val = pre_gate * sigma
    hidden = (silu_val * pre_up).astype(jnp.bfloat16)
    d_gate = (d_hidden * pre_up * sigma * (1.0 + pre_gate * (1.0 - sigma))).astype(jnp.bfloat16)
    d_up = (d_hidden * silu_val).astype(jnp.bfloat16)
    return d_gate, d_up, hidden


def block_grads(x_rows, dy_rows, w_gate, w_up, w_down):
    d_gate, d_up, hidden = forward_pieces(x_rows, dy_rows, w_gate, w_up, w_down)
    g_gate = jnp.dot(x_rows.T, d_gate, preferred_element_type=jnp.float32)
    g_up = jnp.dot(x_rows.T, d_up, preferred_element_type=jnp.float32)
    g_down = jnp.dot(dy_rows.T, hidden, preferred_element_type=jnp.float32)
    return jnp.concatenate([g_gate, g_up, g_down], axis=0)


def adam(clip, shard, old_param, first, second):
    clipped = clip * shard
    new_first = 0.9 * first + 0.1 * clipped
    new_second = 0.95 * second + 0.05 * clipped * clipped
    first_fix = 1.0 / (1.0 - 0.9**STEP)
    second_fix = 1.0 / (1.0 - 0.95**STEP)
    update = new_first * first_fix / (jnp.sqrt(new_second * second_fix) + 1e-08) + 0.1 * old_param
    return old_param - 0.01 * update, new_first, new_second


def clip_of(total, max_norm):
    return jnp.minimum(jnp.float32(1.0), max_norm / (jnp.sqrt(total) + 1e-06))


def plain(weights, inputs, out_grads, master, moment1, moment2):
    stacked = weights[0]
    width = stacked.shape[0] // 3
    local_grad = jnp.zeros(stacked.shape, jnp.float32)
    for start in range(0, inputs.shape[1], MROWS):
        x_rows = inputs[0, start : start + MROWS]
        dy_rows = out_grads[0, start : start + MROWS]
        local_grad = local_grad + block_grads(
            x_rows, dy_rows, stacked[:width], stacked[width : 2 * width], stacked[2 * width :]
        )
    shard = lax.psum_scatter(local_grad, "dp", scatter_dimension=0, tiled=True)
    total = lax.psum(jnp.sum(shard * shard), ("dp", "section"))
    max_norm = jnp.sqrt(jnp.float32(lax.axis_size("section") * stacked.size))
    new_param, new_first, new_second = adam(clip_of(total, max_norm), shard, master[0], moment1[0], moment2[0])
    gathered = lax.all_gather(new_param.astype(jnp.bfloat16), "dp", axis=0, tiled=True)
    return new_param[None], new_first[None], new_second[None], gathered[None]


def encode(value):
    scale = jnp.max(jnp.abs(value), axis=0, keepdims=True)
    scale = jnp.maximum(scale, 1e-30).astype(jnp.bfloat16).astype(jnp.float32)
    v = value * (TOP / scale)
    v2 = v * v
    v4 = v2 * v2
    v8 = v4 * v4
    return jnp.where(v < 0.0, -v8, v8).astype(jnp.bfloat16), scale


def decode(code, scale):
    code = code.astype(jnp.float32)
    size = jnp.abs(code)
    root = jnp.exp(jnp.log(jnp.maximum(size, 1e-37)) * (1.0 / POWER)) * (scale * (1.0 / TOP))
    root = jnp.where(size > 0.0, root, 0.0)
    return jnp.where(code < 0.0, -root, root)


def lookup(table, index):
    out = jnp.int32(table[0])
    for at, value in enumerate(table[1:], 1):
        out = jnp.where(index == at, jnp.int32(value), out)
    return out


def message_rows(left, factor, out_ref, step, scales):
    rows = left.shape[1]
    total = lax.dot_general(left, factor, (((0,), (0,)), ((), ())), preferred_element_type=jnp.float32)
    code, scale = encode(total)
    out_ref[step * rows : (step + 1) * rows, :] = code
    row = lax.broadcasted_iota(jnp.int32, scales.shape, 0)
    return jnp.where(row == step, scale, scales)


def forward_kernel(owner, rows, x_hbm, dy_hbm, w_hbm, factors_ref, out_ref, x_ref, dy_ref, w_ref, sems):
    width = x_hbm.shape[1]
    copies = [
        pltpu.make_async_copy(x_hbm, x_ref, sems.at[0]),
        pltpu.make_async_copy(w_hbm.at[:width], w_ref.at[:width], sems.at[1]),
        pltpu.make_async_copy(w_hbm.at[width : 2 * width], w_ref.at[width : 2 * width], sems.at[2]),
        pltpu.make_async_copy(dy_hbm, dy_ref, sems.at[3]),
        pltpu.make_async_copy(w_hbm.at[2 * width :], w_ref.at[2 * width :], sems.at[4]),
    ]
    for copy in copies:
        copy.start()
    copies[0].wait()
    copies[1].wait()
    pre_gate = jnp.dot(x_ref[...], w_ref[:width], preferred_element_type=jnp.float32)
    copies[2].wait()
    pre_up = jnp.dot(x_ref[...], w_ref[width : 2 * width], preferred_element_type=jnp.float32)
    copies[3].wait()
    copies[4].wait()
    d_hidden = jnp.dot(dy_ref[...], w_ref[2 * width :], preferred_element_type=jnp.float32)
    d_gate, d_up, hidden = activation(pre_gate, pre_up, d_hidden)
    factors_ref[0] = d_gate
    factors_ref[1] = d_up
    factors_ref[2] = hidden
    steps = (out_ref.shape[0] - PAD) // rows
    scales = jnp.zeros((PAD, out_ref.shape[1]), jnp.float32)
    for step in range(steps):
        at = owner() * steps + step
        kind = lax.div(at, width // rows)
        column = pl.ds(pl.multiple_of(lax.rem(at, width // rows) * rows, rows), rows)
        left = jnp.where(kind == 2, dy_ref[:, column], x_ref[:, column])
        scales = message_rows(left, factors_ref[kind], out_ref, step, scales)
    out_ref[steps * rows :, :] = scales.astype(jnp.bfloat16)


def forward(x, dy, stacked, table, rows):
    tokens, width = x.shape
    hidden = stacked.shape[1]
    shard = stacked.shape[0] // len(table)

    def owner():
        return lookup(table, lax.axis_index("dp"))

    return pl.pallas_call(
        lambda *refs: forward_kernel(owner, rows, *refs),
        in_specs=[pl.BlockSpec(memory_space=pltpu.HBM)] * 3,
        out_shape=[
            jax.ShapeDtypeStruct((3, tokens, hidden), jnp.bfloat16),
            jax.ShapeDtypeStruct((shard + PAD, hidden), jnp.bfloat16),
        ],
        scratch_shapes=[
            pltpu.VMEM(x.shape, x.dtype),
            pltpu.VMEM(dy.shape, dy.dtype),
            pltpu.VMEM(stacked.shape, stacked.dtype),
            pltpu.SemaphoreType.DMA((5,)),
        ],
        compiler_params=pltpu.CompilerParams(vmem_limit_bytes=60 << 20),
        cost_estimate=CHEAP,
        name="forward",
    )(x, dy, stacked)


def piece_kernel(owner, per, count, after, last, *refs):
    step = pl.program_id(0)
    x_ref, dy_ref, d_ref = refs[:3]
    got = refs[3 : 3 + 2 * count]
    outs = refs[3 + 2 * count + after :]
    rows = x_ref.shape[1]
    kind = lax.div(owner() * pl.num_programs(0) + step, per)
    left = jnp.where(kind == 2, dy_ref[...], x_ref[...])
    total = lax.dot_general(left, d_ref[0], (((0,), (0,)), ((), ())), preferred_element_type=jnp.float32)
    for at in range(count):
        scales = got[2 * at + 1][...].astype(jnp.float32)
        row = lax.broadcasted_iota(jnp.int32, scales.shape, 0)
        scale = jnp.sum(jnp.where(row == step, scales, 0.0), axis=0, keepdims=True)
        total = total + decode(got[2 * at][...], scale)
    if last:
        outs[0][...] = total
        tile = jnp.sum((total * total).reshape(rows // 8, 8, -1), axis=0)
        tile = sum(tile[:, at : at + 128] for at in range(0, tile.shape[1], 128))
        squares = outs[1]
        tile = tile + jnp.where(step == 0, 0.0, squares[:8])
        for at in range(0, squares.shape[0], 8):
            squares[at : at + 8] = tile
    else:
        out_ref, scales_ref = outs
        code, scale = encode(total)
        out_ref[pl.ds(pl.multiple_of(step * rows, rows), rows), :] = code
        row = lax.broadcasted_iota(jnp.int32, scales_ref.shape, 0)
        scales_ref[...] = jnp.where(row == step, scale, jnp.where(step == 0, 0.0, scales_ref[...]))
        out_ref[pl.ds(out_ref.shape[0] - PAD, PAD), :] = scales_ref[...].astype(jnp.bfloat16)


def piece(x, dy, factors, table, rows, got=(), after=None, last=0):
    tokens, width = x.shape
    hidden = factors.shape[2]
    per = width // rows
    shard = 3 * width // len(table)
    steps = shard // rows

    def owner():
        return lookup(table, lax.axis_index("dp"))

    def column(i):
        return (0, lax.rem(owner() * steps + i, per))

    in_specs = [
        pl.BlockSpec((tokens, rows), column),
        pl.BlockSpec((tokens, rows), column),
        pl.BlockSpec((1, tokens, hidden), lambda i: (lax.div(owner() * steps + i, per), 0, 0)),
    ]
    for _ in got:
        in_specs += [
            pl.BlockSpec((rows, hidden), lambda i: (i, 0)),
            pl.BlockSpec((PAD, hidden), lambda i: (shard // PAD, 0)),
        ]
    extra = []
    if after is not None:
        extra = [after]
        in_specs.append(pl.BlockSpec(memory_space=pl.ANY))
    if last:
        out_specs = [
            pl.BlockSpec((rows, hidden), lambda i: (i, 0)),
            pl.BlockSpec((8 * last, 128), lambda i: (0, 0)),
        ]
        out_shape = [
            jax.ShapeDtypeStruct((shard, hidden), jnp.float32),
            jax.ShapeDtypeStruct((8 * last, 128), jnp.float32),
        ]
        scratch = []
    else:
        out_specs = pl.BlockSpec((shard + PAD, hidden), lambda i: (0, 0))
        out_shape = jax.ShapeDtypeStruct((shard + PAD, hidden), jnp.bfloat16)
        scratch = [pltpu.VMEM((PAD, hidden), jnp.float32)]
    return pl.pallas_call(
        lambda *refs: piece_kernel(owner, per, len(got), len(extra), last, *refs),
        grid=(steps,),
        in_specs=in_specs,
        out_specs=out_specs,
        out_shape=out_shape,
        scratch_shapes=scratch,
        compiler_params=pltpu.CompilerParams(vmem_limit_bytes=32 << 20),
        cost_estimate=pl.CostEstimate(
            flops=2 * tokens * shard * hidden,
            bytes_accessed=4 * tokens * shard + 2 * factors.size + 2 * shard * hidden * (len(got) + 1),
            transcendentals=2 * shard * hidden * len(got),
        ),
        name="piece",
    )(x, dy, factors, *[m for message in got for m in (message, message)], *extra)


def update_kernel(max_norm, total_ref, g_ref, p_ref, m1_ref, m2_ref, new_p, new_m1, new_m2, new_w):
    clip = clip_of(jnp.sum(total_ref[...], keepdims=True), max_norm)
    param, first, second = adam(clip, g_ref[...], p_ref[...], m1_ref[...], m2_ref[...])
    new_p[...] = param
    new_m1[...] = first
    new_m2[...] = second
    new_w[...] = param.astype(jnp.bfloat16)


def update(total, shard, param, first, second, max_norm, rows):
    block = pl.BlockSpec((rows, shard.shape[1]), lambda i: (i, 0))
    wide = jax.ShapeDtypeStruct(shard.shape, jnp.float32)
    return pl.pallas_call(
        lambda *refs: update_kernel(max_norm, *refs),
        grid=(shard.shape[0] // rows,),
        in_specs=[pl.BlockSpec(total.shape, lambda i: (0, 0))] + [block] * 4,
        out_specs=[block] * 4,
        out_shape=[wide] * 3 + [jax.ShapeDtypeStruct(shard.shape, jnp.bfloat16)],
        compiler_params=pltpu.CompilerParams(vmem_limit_bytes=32 << 20),
        cost_estimate=CHEAP,
        name="update",
    )(total, shard, param, first, second)


def put_kernel(places, rows, *refs):
    values, out, sems = refs[: len(places)], refs[-2], refs[-1]
    copies = []
    for at, (value, place) in enumerate(zip(values, places)):
        start = pl.multiple_of(lookup(place, lax.axis_index("dp")) * rows, rows)
        copies.append(pltpu.make_async_copy(value, out.at[pl.ds(start, rows)], sems.at[at]))
        copies[-1].start()
    for copy in copies:
        copy.wait()


def put(buffer, values, places, height):
    rows, columns = values[0].shape
    return pl.pallas_call(
        lambda *refs: put_kernel(places, rows, *refs),
        in_specs=[pl.BlockSpec(memory_space=pltpu.VMEM)] * len(values)
        + [pl.BlockSpec(memory_space=pltpu.HBM)] * (buffer is not None),
        out_specs=pl.BlockSpec(memory_space=pltpu.HBM),
        out_shape=jax.ShapeDtypeStruct((height, columns), values[0].dtype),
        input_output_aliases={} if buffer is None else {len(values): 0},
        scratch_shapes=[pltpu.SemaphoreType.DMA((len(values),))],
        cost_estimate=CHEAP,
        name="put",
    )(*values, *([] if buffer is None else [buffer]))


def paired(weights, inputs, out_grads, master, moment1, moment2):
    n = lax.axis_size("dp")
    pairs = n // 2
    ring = list(range(0, pairs, 2)) + list(range(pairs - 1 - pairs % 2, 0, -2))
    place = {pair: at for at, pair in enumerate(ring)}

    def at_offset(r, offset, flip):
        return 2 * ring[(place[r // 2] + offset) % pairs] + ((r % 2) ^ flip)

    def table(offset, flip):
        return [at_offset(r, offset, flip) for r in range(n)]

    def send(value, offset, flip=0):
        return lax.ppermute(value, "dp", [(r, at_offset(r, offset, flip)) for r in range(n)])

    stacked = weights[0]
    x, dy = inputs[0], out_grads[0]
    width = x.shape[1]
    shard_rows = stacked.shape[0] // n
    rows = math.gcd(math.gcd(shard_rows, width), 256)

    ahead = pairs // 2
    behind = pairs - 1 - ahead
    order = sorted(range(-behind, ahead + 1), key=lambda o: (-abs(o), o))

    factors, message = forward(x, dy, stacked, table(order[0], 1), rows)
    crossed = {order[0]: send(message, 0, 1)}
    for offset in order[1:]:
        message = piece(x, dy, factors, table(offset, 1), rows, after=message)
        crossed[offset] = send(message, 0, 1)

    arrived = {}
    devices = n * lax.axis_size("section")
    for offset in order:
        got = [crossed[offset]] + [arrived[k] for k in ((offset, 1), (offset, -1)) if k in arrived]
        if offset == 0:
            shard, squares = piece(x, dy, factors, table(0, 0), rows, got, last=devices)
        else:
            way = 1 if offset > 0 else -1
            message = piece(x, dy, factors, table(offset, 0), rows, got, after=message)
            arrived[(offset - way, way)] = send(message, way)

    total = lax.all_to_all(squares, ("dp", "section"), 0, 0, tiled=True)
    max_norm = math.sqrt(lax.axis_size("section") * stacked.size)
    new_param, new_first, new_second, own = update(
        total, shard, master[0], moment1[0], moment2[0], max_norm, rows
    )

    held = {0: own}
    other = {0: send(own, 0, 1)}
    for step in range(1, ahead + 1):
        held[-step] = send(held[1 - step], 1)
        other[-step] = send(held[-step], 0, 1)
        if step <= behind:
            held[step] = send(held[step - 1], -1)
            other[step] = send(held[step], 0, 1)
    gathered = None
    height = stacked.shape[0]
    final = -ahead
    for offset in held:
        values, places = [held[offset]], [table(offset, 0)]
        if offset != final:
            values.append(other[offset])
            places.append(table(offset, 1))
        gathered = put(gathered, values, places, height)
    gathered = put(gathered, [other[final]], [table(final, 1)], height)
    return new_param[None], new_first[None], new_second[None], gathered[None]


def local(weights, *rest):
    n = lax.axis_size("dp")
    height = weights.shape[1]
    fits = n % 2 == 0 and n > 2 and height % n == 0 and (height // n) % 128 == 0 and (height // 3) % 128 == 0
    return (paired if fits else plain)(weights, *rest)


def solution(mesh):
    whole = P("section", None, None)
    split = P("section", "dp", None)
    return jax.shard_map(
        local,
        mesh=mesh,
        in_specs=(whole, split, split, split, split, split),
        out_specs=(split, split, split, whole),
        check_vma=False,
    )
```

```python
import math

import jax
import jax.numpy as jnp
from jax import lax
from jax.experimental import pallas as pl
from jax.experimental.pallas import tpu as pltpu
from jax.sharding import PartitionSpec as P

MROWS = 256
STEP = 10
PAD = 16
POWER = 8
TOP = 32768.0
CHEAP = pl.CostEstimate(flops=1024, bytes_accessed=1024, transcendentals=0)


def forward_pieces(x_rows, dy_rows, w_gate, w_up, w_down):
    pre_gate = jnp.dot(x_rows, w_gate, preferred_element_type=jnp.float32)
    pre_up = jnp.dot(x_rows, w_up, preferred_element_type=jnp.float32)
    d_hidden = jnp.dot(dy_rows, w_down, preferred_element_type=jnp.float32)
    return activation(pre_gate, pre_up, d_hidden)


def activation(pre_gate, pre_up, d_hidden):
    sigma = jax.nn.sigmoid(pre_gate)
    silu_val = pre_gate * sigma
    hidden = (silu_val * pre_up).astype(jnp.bfloat16)
    d_gate = (d_hidden * pre_up * sigma * (1.0 + pre_gate * (1.0 - sigma))).astype(jnp.bfloat16)
    d_up = (d_hidden * silu_val).astype(jnp.bfloat16)
    return d_gate, d_up, hidden


def block_grads(x_rows, dy_rows, w_gate, w_up, w_down):
    d_gate, d_up, hidden = forward_pieces(x_rows, dy_rows, w_gate, w_up, w_down)
    g_gate = jnp.dot(x_rows.T, d_gate, preferred_element_type=jnp.float32)
    g_up = jnp.dot(x_rows.T, d_up, preferred_element_type=jnp.float32)
    g_down = jnp.dot(dy_rows.T, hidden, preferred_element_type=jnp.float32)
    return jnp.concatenate([g_gate, g_up, g_down], axis=0)


def adam(clip, shard, old_param, first, second):
    clipped = clip * shard
    new_first = 0.9 * first + 0.1 * clipped
    new_second = 0.95 * second + 0.05 * clipped * clipped
    first_fix = 1.0 / (1.0 - 0.9**STEP)
    second_fix = 1.0 / (1.0 - 0.95**STEP)
    update = new_first * first_fix / (jnp.sqrt(new_second * second_fix) + 1e-08) + 0.1 * old_param
    return old_param - 0.01 * update, new_first, new_second


def clip_of(total, max_norm):
    return jnp.minimum(jnp.float32(1.0), max_norm / (jnp.sqrt(total) + 1e-06))


def plain(weights, inputs, out_grads, master, moment1, moment2):
    stacked = weights[0]
    width = stacked.shape[0] // 3
    local_grad = jnp.zeros(stacked.shape, jnp.float32)
    for start in range(0, inputs.shape[1], MROWS):
        x_rows = inputs[0, start : start + MROWS]
        dy_rows = out_grads[0, start : start + MROWS]
        local_grad = local_grad + block_grads(
            x_rows, dy_rows, stacked[:width], stacked[width : 2 * width], stacked[2 * width :]
        )
    shard = lax.psum_scatter(local_grad, "dp", scatter_dimension=0, tiled=True)
    total = lax.psum(jnp.sum(shard * shard), ("dp", "section"))
    max_norm = jnp.sqrt(jnp.float32(lax.axis_size("section") * stacked.size))
    new_param, new_first, new_second = adam(clip_of(total, max_norm), shard, master[0], moment1[0], moment2[0])
    gathered = lax.all_gather(new_param.astype(jnp.bfloat16), "dp", axis=0, tiled=True)
    return new_param[None], new_first[None], new_second[None], gathered[None]


def encode(value):
    scale = jnp.max(jnp.abs(value), axis=0, keepdims=True)
    scale = jnp.maximum(scale, 1e-30).astype(jnp.bfloat16).astype(jnp.float32)
    v = value * (TOP / scale)
    v2 = v * v
    v4 = v2 * v2
    v8 = v4 * v4
    return jnp.where(v < 0.0, -v8, v8).astype(jnp.bfloat16), scale


def decode(code, scale):
    code = code.astype(jnp.float32)
    size = jnp.abs(code)
    root = jnp.exp(jnp.log(jnp.maximum(size, 1e-37)) * (1.0 / POWER)) * (scale * (1.0 / TOP))
    root = jnp.where(size > 0.0, root, 0.0)
    return jnp.where(code < 0.0, -root, root)


def lookup(table, index):
    out = jnp.int32(table[0])
    for at, value in enumerate(table[1:], 1):
        out = jnp.where(index == at, jnp.int32(value), out)
    return out


def message_rows(left, factor, out_ref, step, scales):
    rows = left.shape[1]
    total = lax.dot_general(left, factor, (((0,), (0,)), ((), ())), preferred_element_type=jnp.float32)
    code, scale = encode(total)
    out_ref[step * rows : (step + 1) * rows, :] = code
    row = lax.broadcasted_iota(jnp.int32, scales.shape, 0)
    return jnp.where(row == step, scale, scales)


def forward_kernel(owner, rows, x_hbm, dy_hbm, w_hbm, factors_ref, out_ref, x_ref, dy_ref, w_ref, sems):
    width = x_hbm.shape[1]
    half = width // 2

    def fetch(at, source, target, index):
        copy = pltpu.make_async_copy(source.at[index], target.at[index], sems.at[at])
        copy.start()
        return copy

    copies = []
    for columns in (pl.ds(0, half), pl.ds(half, half)):
        copies.append(fetch(len(copies), x_hbm, x_ref, (slice(None), columns)))
        copies.append(fetch(len(copies), w_hbm, w_ref, columns))
        copies.append(fetch(len(copies), w_hbm, w_ref, pl.ds(columns.start + width, half)))
    for columns in (pl.ds(0, half), pl.ds(half, half)):
        copies.append(fetch(len(copies), dy_hbm, dy_ref, (slice(None), columns)))
        copies.append(fetch(len(copies), w_hbm, w_ref, pl.ds(columns.start + 2 * width, half)))

    def product(left, start, which):
        weight = w_ref[which * width + start : which * width + start + half]
        return jnp.dot(left[:, start : start + half], weight, preferred_element_type=jnp.float32)

    for copy in copies[:3]:
        copy.wait()
    pre_gate = product(x_ref, 0, 0)
    pre_up = product(x_ref, 0, 1)
    for copy in copies[3:6]:
        copy.wait()
    pre_gate = pre_gate + product(x_ref, half, 0)
    pre_up = pre_up + product(x_ref, half, 1)
    for copy in copies[6:8]:
        copy.wait()
    d_hidden = product(dy_ref, 0, 2)
    for copy in copies[8:]:
        copy.wait()
    d_hidden = d_hidden + product(dy_ref, half, 2)
    d_gate, d_up, hidden = activation(pre_gate, pre_up, d_hidden)
    factors_ref[0] = d_gate
    factors_ref[1] = d_up
    factors_ref[2] = hidden
    steps = (out_ref.shape[0] - PAD) // rows
    scales = jnp.zeros((PAD, out_ref.shape[1]), jnp.float32)
    for step in range(steps):
        at = owner() * steps + step
        kind = lax.div(at, width // rows)
        column = pl.ds(pl.multiple_of(lax.rem(at, width // rows) * rows, rows), rows)
        left = jnp.where(kind == 2, dy_ref[:, column], x_ref[:, column])
        scales = message_rows(left, factors_ref[kind], out_ref, step, scales)
    out_ref[steps * rows :, :] = scales.astype(jnp.bfloat16)


def forward(x, dy, stacked, table, rows):
    tokens, width = x.shape
    hidden = stacked.shape[1]
    shard = stacked.shape[0] // len(table)

    def owner():
        return lookup(table, lax.axis_index("dp"))

    return pl.pallas_call(
        lambda *refs: forward_kernel(owner, rows, *refs),
        in_specs=[pl.BlockSpec(memory_space=pltpu.HBM)] * 3,
        out_shape=[
            jax.ShapeDtypeStruct((3, tokens, hidden), jnp.bfloat16),
            jax.ShapeDtypeStruct((shard + PAD, hidden), jnp.bfloat16),
        ],
        scratch_shapes=[
            pltpu.VMEM(x.shape, x.dtype),
            pltpu.VMEM(dy.shape, dy.dtype),
            pltpu.VMEM(stacked.shape, stacked.dtype),
            pltpu.SemaphoreType.DMA((10,)),
        ],
        compiler_params=pltpu.CompilerParams(vmem_limit_bytes=60 << 20),
        cost_estimate=CHEAP,
        name="forward",
    )(x, dy, stacked)


def piece_kernel(owner, per, steps, low, starts, extra, last, *refs):
    step = pl.program_id(0)
    x_ref, dy_ref, d_ref = refs[:3]
    got = refs[3 : 3 + 2 * len(starts)]
    before = refs[3 + 2 * len(starts) : 3 + 2 * len(starts) + extra]
    outs = refs[3 + 2 * len(starts) + extra :]
    rows = x_ref.shape[1]
    kind = lax.div(owner() * steps + low + step, per)
    left = jnp.where(kind == 2, dy_ref[...], x_ref[...])
    total = lax.dot_general(left, d_ref[0], (((0,), (0,)), ((), ())), preferred_element_type=jnp.float32)
    for at, start in enumerate(starts):
        scales = got[2 * at + 1][...].astype(jnp.float32)
        row = lax.broadcasted_iota(jnp.int32, scales.shape, 0)
        scale = jnp.sum(jnp.where(row == step + low - start, scales, 0.0), axis=0, keepdims=True)
        total = total + decode(got[2 * at][...], scale)
    if last:
        out_ref, squares = outs
        out_ref[...] = total
        tile = jnp.sum((total * total).reshape(rows // 8, 8, -1), axis=0)
        tile = sum(tile[:, at : at + 128] for at in range(0, tile.shape[1], 128))
        tile = tile + jnp.where(step == 0, before[1][...] if extra else 0.0, squares[:8])
        for at in range(0, squares.shape[0], 8):
            squares[at : at + 8] = tile
    else:
        out_ref, scales_ref = outs
        code, scale = encode(total)
        out_ref[pl.ds(pl.multiple_of(step * rows, rows), rows), :] = code
        row = lax.broadcasted_iota(jnp.int32, scales_ref.shape, 0)
        scales_ref[...] = jnp.where(row == step, scale, jnp.where(step == 0, 0.0, scales_ref[...]))
        out_ref[pl.ds(out_ref.shape[0] - PAD, PAD), :] = scales_ref[...].astype(jnp.bfloat16)


def piece(x, dy, factors, table, rows, low, high, got=(), after=None, last=0, before=None):
    tokens, width = x.shape
    hidden = factors.shape[2]
    per = width // rows
    shard = 3 * width // len(table)
    steps = shard // rows

    def owner():
        return lookup(table, lax.axis_index("dp"))

    def column(i):
        return (0, lax.rem(owner() * steps + low + i, per))

    in_specs = [
        pl.BlockSpec((tokens, rows), column),
        pl.BlockSpec((tokens, rows), column),
        pl.BlockSpec((1, tokens, hidden), lambda i: (lax.div(owner() * steps + low + i, per), 0, 0)),
    ]
    operands = [x, dy, factors]
    for message, start in got:
        blocks = (message.shape[0] - PAD) // PAD
        in_specs += [
            pl.BlockSpec((rows, hidden), lambda i, start=start: (i + low - start, 0)),
            pl.BlockSpec((PAD, hidden), lambda i, blocks=blocks: (blocks, 0)),
        ]
        operands += [message, message]
    aliases = {}
    extra = 0
    if before is not None:
        extra = 2
        aliases = {len(operands): 0}
        operands += before
        in_specs += [pl.BlockSpec(memory_space=pl.ANY), pl.BlockSpec((8, 128), lambda i: (0, 0))]
    elif after is not None:
        extra = 1
        operands.append(after)
        in_specs.append(pl.BlockSpec(memory_space=pl.ANY))
    if last:
        out_specs = [
            pl.BlockSpec((rows, hidden), lambda i: (i + low, 0)),
            pl.BlockSpec((8 * last, 128), lambda i: (0, 0)),
        ]
        out_shape = [
            jax.ShapeDtypeStruct((shard, hidden), jnp.float32),
            jax.ShapeDtypeStruct((8 * last, 128), jnp.float32),
        ]
        scratch = []
    else:
        out_specs = pl.BlockSpec(((high - low) * rows + PAD, hidden), lambda i: (0, 0))
        out_shape = jax.ShapeDtypeStruct(((high - low) * rows + PAD, hidden), jnp.bfloat16)
        scratch = [pltpu.VMEM((PAD, hidden), jnp.float32)]
    return pl.pallas_call(
        lambda *refs: piece_kernel(owner, per, steps, low, [s for _, s in got], extra, last, *refs),
        grid=(high - low,),
        in_specs=in_specs,
        out_specs=out_specs,
        out_shape=out_shape,
        scratch_shapes=scratch,
        input_output_aliases=aliases,
        compiler_params=pltpu.CompilerParams(vmem_limit_bytes=32 << 20),
        cost_estimate=CHEAP,
        name="piece",
    )(*operands)


def update_kernel(max_norm, total_ref, g_ref, p_ref, m1_ref, m2_ref, new_p, new_m1, new_m2, new_w):
    clip = clip_of(jnp.sum(total_ref[...], keepdims=True), max_norm)
    param, first, second = adam(clip, g_ref[...], p_ref[...], m1_ref[...], m2_ref[...])
    new_p[...] = param
    new_m1[...] = first
    new_m2[...] = second
    new_w[...] = param.astype(jnp.bfloat16)


def update(total, shard, param, first, second, max_norm, rows):
    block = pl.BlockSpec((rows, shard.shape[1]), lambda i: (i, 0))
    wide = jax.ShapeDtypeStruct(shard.shape, jnp.float32)
    return pl.pallas_call(
        lambda *refs: update_kernel(max_norm, *refs),
        grid=(shard.shape[0] // rows,),
        in_specs=[pl.BlockSpec(total.shape, lambda i: (0, 0))] + [block] * 4,
        out_specs=[block] * 4,
        out_shape=[wide] * 3 + [jax.ShapeDtypeStruct(shard.shape, jnp.bfloat16)],
        compiler_params=pltpu.CompilerParams(vmem_limit_bytes=32 << 20),
        cost_estimate=CHEAP,
        name="update",
    )(total, shard, param, first, second)


def put(buffer, value, place, rows, height):
    columns = value.shape[1]
    steps = value.shape[0] // rows

    def kernel(*refs):
        refs[-1][...] = refs[0][...]

    return pl.pallas_call(
        kernel,
        grid=(steps,),
        in_specs=[pl.BlockSpec((rows, columns), lambda i: (i, 0))]
        + [pl.BlockSpec(memory_space=pltpu.HBM)] * (buffer is not None),
        out_specs=pl.BlockSpec((rows, columns), lambda i: (lookup(place, lax.axis_index("dp")) * steps + i, 0)),
        out_shape=jax.ShapeDtypeStruct((height, columns), value.dtype),
        input_output_aliases={} if buffer is None else {1: 0},
        cost_estimate=CHEAP,
        name="put",
    )(value, *([] if buffer is None else [buffer]))


def behind(value, other):
    return pl.pallas_call(
        lambda *refs: None,
        in_specs=[pl.BlockSpec(memory_space=pl.ANY)] * 2,
        out_specs=pl.BlockSpec(memory_space=pl.ANY),
        out_shape=jax.ShapeDtypeStruct(value.shape, value.dtype),
        input_output_aliases={0: 0},
        cost_estimate=CHEAP,
        name="behind",
    )(value, other)


def paired(weights, inputs, out_grads, master, moment1, moment2):
    n = lax.axis_size("dp")
    pairs = n // 2
    ring = list(range(0, pairs, 2)) + list(range(pairs - 1 - pairs % 2, 0, -2))
    place = {pair: at for at, pair in enumerate(ring)}

    def at_offset(r, offset, flip):
        return 2 * ring[(place[r // 2] + offset) % pairs] + ((r % 2) ^ flip)

    def table(offset, flip):
        return [at_offset(r, offset, flip) for r in range(n)]

    def send(value, offset, flip=0):
        return lax.ppermute(value, "dp", [(r, at_offset(r, offset, flip)) for r in range(n)])

    stacked = weights[0]
    x, dy = inputs[0], out_grads[0]
    width = x.shape[1]
    shard_rows = stacked.shape[0] // n
    rows = math.gcd(math.gcd(shard_rows, width), 256)

    steps = shard_rows // rows
    forth = pairs // 2
    back = pairs - 1 - forth
    order = sorted(range(-back, forth + 1), key=lambda o: (-abs(o), o))
    cuts = {offset: [(0, steps)] for offset in order}
    if steps > 1:
        cuts[order[-2]] = [(0, steps - 1), (steps - 1, steps)]

    factors, message = forward(x, dy, stacked, table(order[0], 1), rows)
    crossed = {(order[0], 0): send(message, 0, 1)}
    after = None
    for offset in order[1:]:
        for low, high in cuts[offset]:
            after = piece(x, dy, factors, table(offset, 1), rows, low, high, after=after)
            crossed[offset, low] = send(after, 0, 1)

    arrived = {}
    devices = n * lax.axis_size("section")
    for offset in order[:-1]:
        way = 1 if offset > 0 else -1
        for low, high in cuts[offset]:
            got = [(crossed[offset, low], low)] + arrived.get((offset, way), [])
            message = piece(x, dy, factors, table(offset, 0), rows, low, high, got)
            arrived.setdefault((offset - way, way), []).append((send(message, way), low))
    cut = cuts[order[-2]]
    whole = (crossed[0, 0], 0)
    done = None
    for low, high in cut:
        got = [whole]
        for key in ((0, 1), (0, -1)):
            messages = arrived.get(key, [])
            got += [m for m in messages if m[1] == low] if len(messages) > 1 else messages
        done = piece(
            x, dy, factors, table(0, 0), rows, low, high, got, last=devices if high == steps else 1, before=done
        )
    shard, squares = done

    total = lax.all_to_all(squares, ("dp", "section"), 0, 0, tiled=True)
    max_norm = math.sqrt(lax.axis_size("section") * stacked.size)
    new_param, new_first, new_second, own = update(
        total, shard, master[0], moment1[0], moment2[0], max_norm, rows
    )

    held = {0: own}
    other = {0: send(own, 0, 1)}
    for step in range(1, forth + 1):
        held[-step] = send(held[1 - step], 1)
        if step == 1:
            held[-1] = behind(held[-1], other[0])
        if step <= back:
            held[step] = send(held[step - 1], -1)
    for offset in held:
        if offset:
            other[offset] = send(held[offset], 0, 1)
    final = -forth
    pieces = [(held[o], table(o, 0)) for o in held] + [(other[o], table(o, 1)) for o in held if o != final]
    pieces.append((other[final], table(final, 1)))
    gathered = None
    for value, place in pieces:
        gathered = put(gathered, value, place, rows, stacked.shape[0])
    return new_param[None], new_first[None], new_second[None], gathered[None]


def local(weights, *rest):
    n = lax.axis_size("dp")
    height = weights.shape[1]
    fits = n % 2 == 0 and n > 2 and height % n == 0 and (height // n) % 128 == 0 and (height // 3) % 128 == 0
    return (paired if fits else plain)(weights, *rest)


def solution(mesh):
    whole = P("section", None, None)
    split = P("section", "dp", None)
    return jax.shard_map(
        local,
        mesh=mesh,
        in_specs=(whole, split, split, split, split, split),
        out_specs=(split, split, split, whole),
        check_vma=False,
    )
```

```python
import math

import jax
import jax.numpy as jnp
from jax import lax
from jax.experimental import pallas as pl
from jax.experimental.pallas import tpu as pltpu
from jax.sharding import PartitionSpec as P

MROWS = 256
STEP = 10
PAD = 16
POWER = 8
TOP = 32768.0
CHEAP = pl.CostEstimate(flops=1024, bytes_accessed=1024, transcendentals=0)


def forward_pieces(x_rows, dy_rows, w_gate, w_up, w_down):
    pre_gate = jnp.dot(x_rows, w_gate, preferred_element_type=jnp.float32)
    pre_up = jnp.dot(x_rows, w_up, preferred_element_type=jnp.float32)
    d_hidden = jnp.dot(dy_rows, w_down, preferred_element_type=jnp.float32)
    return activation(pre_gate, pre_up, d_hidden)


def activation(pre_gate, pre_up, d_hidden):
    sigma = jax.nn.sigmoid(pre_gate)
    silu_val = pre_gate * sigma
    hidden = (silu_val * pre_up).astype(jnp.bfloat16)
    d_gate = (d_hidden * pre_up * sigma * (1.0 + pre_gate * (1.0 - sigma))).astype(jnp.bfloat16)
    d_up = (d_hidden * silu_val).astype(jnp.bfloat16)
    return d_gate, d_up, hidden


def block_grads(x_rows, dy_rows, w_gate, w_up, w_down):
    d_gate, d_up, hidden = forward_pieces(x_rows, dy_rows, w_gate, w_up, w_down)
    g_gate = jnp.dot(x_rows.T, d_gate, preferred_element_type=jnp.float32)
    g_up = jnp.dot(x_rows.T, d_up, preferred_element_type=jnp.float32)
    g_down = jnp.dot(dy_rows.T, hidden, preferred_element_type=jnp.float32)
    return jnp.concatenate([g_gate, g_up, g_down], axis=0)


def adam(clip, shard, old_param, first, second):
    clipped = clip * shard
    new_first = 0.9 * first + 0.1 * clipped
    new_second = 0.95 * second + 0.05 * clipped * clipped
    first_fix = 1.0 / (1.0 - 0.9**STEP)
    second_fix = 1.0 / (1.0 - 0.95**STEP)
    update = new_first * first_fix / (jnp.sqrt(new_second * second_fix) + 1e-08) + 0.1 * old_param
    return old_param - 0.01 * update, new_first, new_second


def clip_of(total, max_norm):
    return jnp.minimum(jnp.float32(1.0), max_norm / (jnp.sqrt(total) + 1e-06))


def plain(weights, inputs, out_grads, master, moment1, moment2):
    stacked = weights[0]
    width = stacked.shape[0] // 3
    local_grad = jnp.zeros(stacked.shape, jnp.float32)
    for start in range(0, inputs.shape[1], MROWS):
        x_rows = inputs[0, start : start + MROWS]
        dy_rows = out_grads[0, start : start + MROWS]
        local_grad = local_grad + block_grads(
            x_rows, dy_rows, stacked[:width], stacked[width : 2 * width], stacked[2 * width :]
        )
    shard = lax.psum_scatter(local_grad, "dp", scatter_dimension=0, tiled=True)
    total = lax.psum(jnp.sum(shard * shard), ("dp", "section"))
    max_norm = jnp.sqrt(jnp.float32(lax.axis_size("section") * stacked.size))
    new_param, new_first, new_second = adam(clip_of(total, max_norm), shard, master[0], moment1[0], moment2[0])
    gathered = lax.all_gather(new_param.astype(jnp.bfloat16), "dp", axis=0, tiled=True)
    return new_param[None], new_first[None], new_second[None], gathered[None]


def encode(value):
    scale = jnp.max(jnp.abs(value), axis=0, keepdims=True)
    scale = jnp.maximum(scale, 1e-30).astype(jnp.bfloat16).astype(jnp.float32)
    v = value * (TOP / scale)
    v2 = v * v
    v4 = v2 * v2
    v8 = v4 * v4
    return jnp.where(v < 0.0, -v8, v8).astype(jnp.bfloat16), scale


def decode(code, scale):
    code = code.astype(jnp.float32)
    size = jnp.abs(code)
    root = jnp.exp(jnp.log(jnp.maximum(size, 1e-37)) * (1.0 / POWER)) * (scale * (1.0 / TOP))
    root = jnp.where(size > 0.0, root, 0.0)
    return jnp.where(code < 0.0, -root, root)


def lookup(table, index):
    out = jnp.int32(table[0])
    for at, value in enumerate(table[1:], 1):
        out = jnp.where(index == at, jnp.int32(value), out)
    return out


def message_rows(left, factor, out_ref, step, scales):
    rows = left.shape[1]
    total = lax.dot_general(left, factor, (((0,), (0,)), ((), ())), preferred_element_type=jnp.float32)
    code, scale = encode(total)
    out_ref[step * rows : (step + 1) * rows, :] = code
    row = lax.broadcasted_iota(jnp.int32, scales.shape, 0)
    return jnp.where(row == step, scale, scales)


def forward_kernel(owner, rows, x_hbm, dy_hbm, w_hbm, factors_ref, out_ref, x_ref, dy_ref, w_ref, sems):
    width = x_hbm.shape[1]
    half = width // 2

    def fetch(at, source, target, index):
        copy = pltpu.make_async_copy(source.at[index], target.at[index], sems.at[at])
        copy.start()
        return copy

    copies = []
    for columns in (pl.ds(0, half), pl.ds(half, half)):
        copies.append(fetch(len(copies), x_hbm, x_ref, (slice(None), columns)))
        copies.append(fetch(len(copies), w_hbm, w_ref, columns))
        copies.append(fetch(len(copies), w_hbm, w_ref, pl.ds(columns.start + width, half)))
    for columns in (pl.ds(0, half), pl.ds(half, half)):
        copies.append(fetch(len(copies), dy_hbm, dy_ref, (slice(None), columns)))
        copies.append(fetch(len(copies), w_hbm, w_ref, pl.ds(columns.start + 2 * width, half)))

    def product(left, start, which):
        weight = w_ref[which * width + start : which * width + start + half]
        return jnp.dot(left[:, start : start + half], weight, preferred_element_type=jnp.float32)

    for copy in copies[:3]:
        copy.wait()
    pre_gate = product(x_ref, 0, 0)
    pre_up = product(x_ref, 0, 1)
    for copy in copies[3:6]:
        copy.wait()
    pre_gate = pre_gate + product(x_ref, half, 0)
    pre_up = pre_up + product(x_ref, half, 1)
    for copy in copies[6:8]:
        copy.wait()
    d_hidden = product(dy_ref, 0, 2)
    for copy in copies[8:]:
        copy.wait()
    d_hidden = d_hidden + product(dy_ref, half, 2)
    d_gate, d_up, hidden = activation(pre_gate, pre_up, d_hidden)
    factors_ref[0] = d_gate
    factors_ref[1] = d_up
    factors_ref[2] = hidden
    steps = (out_ref.shape[0] - PAD) // rows
    scales = jnp.zeros((PAD, out_ref.shape[1]), jnp.float32)
    for step in range(steps):
        at = owner() * steps + step
        kind = lax.div(at, width // rows)
        column = pl.ds(pl.multiple_of(lax.rem(at, width // rows) * rows, rows), rows)
        left = jnp.where(kind == 2, dy_ref[:, column], x_ref[:, column])
        scales = message_rows(left, factors_ref[kind], out_ref, step, scales)
    out_ref[steps * rows :, :] = scales.astype(jnp.bfloat16)


def forward(x, dy, stacked, table, rows):
    tokens, width = x.shape
    hidden = stacked.shape[1]
    shard = stacked.shape[0] // len(table)

    def owner():
        return lookup(table, lax.axis_index("dp"))

    return pl.pallas_call(
        lambda *refs: forward_kernel(owner, rows, *refs),
        in_specs=[pl.BlockSpec(memory_space=pltpu.HBM)] * 3,
        out_shape=[
            jax.ShapeDtypeStruct((3, tokens, hidden), jnp.bfloat16),
            jax.ShapeDtypeStruct((shard + PAD, hidden), jnp.bfloat16),
        ],
        scratch_shapes=[
            pltpu.VMEM(x.shape, x.dtype),
            pltpu.VMEM(dy.shape, dy.dtype),
            pltpu.VMEM(stacked.shape, stacked.dtype),
            pltpu.SemaphoreType.DMA((10,)),
        ],
        compiler_params=pltpu.CompilerParams(vmem_limit_bytes=60 << 20),
        cost_estimate=CHEAP,
        name="forward",
    )(x, dy, stacked)


def piece_kernel(owner, per, steps, low, starts, extra, last, *refs):
    step = pl.program_id(0)
    x_ref, dy_ref, d_ref = refs[:3]
    got = refs[3 : 3 + 2 * len(starts)]
    before = refs[3 + 2 * len(starts) : 3 + 2 * len(starts) + extra]
    outs = refs[3 + 2 * len(starts) + extra :]
    rows = x_ref.shape[1]
    kind = lax.div(owner() * steps + low + step, per)
    left = jnp.where(kind == 2, dy_ref[...], x_ref[...])
    total = lax.dot_general(left, d_ref[0], (((0,), (0,)), ((), ())), preferred_element_type=jnp.float32)
    for at, start in enumerate(starts):
        scales = got[2 * at + 1][...].astype(jnp.float32)
        row = lax.broadcasted_iota(jnp.int32, scales.shape, 0)
        scale = jnp.sum(jnp.where(row == step + low - start, scales, 0.0), axis=0, keepdims=True)
        total = total + decode(got[2 * at][...], scale)
    if last:
        out_ref, squares = outs
        out_ref[...] = total
        tile = jnp.sum((total * total).reshape(rows // 8, 8, -1), axis=0)
        tile = sum(tile[:, at : at + 128] for at in range(0, tile.shape[1], 128))
        tile = tile + jnp.where(step == 0, before[1][...] if extra else 0.0, squares[:8])
        for at in range(0, squares.shape[0], 8):
            squares[at : at + 8] = tile
    else:
        out_ref, scales_ref = outs
        code, scale = encode(total)
        out_ref[pl.ds(pl.multiple_of(step * rows, rows), rows), :] = code
        row = lax.broadcasted_iota(jnp.int32, scales_ref.shape, 0)
        scales_ref[...] = jnp.where(row == step, scale, jnp.where(step == 0, 0.0, scales_ref[...]))
        out_ref[pl.ds(out_ref.shape[0] - PAD, PAD), :] = scales_ref[...].astype(jnp.bfloat16)


def piece(x, dy, factors, table, rows, low, high, got=(), after=None, last=0, before=None):
    tokens, width = x.shape
    hidden = factors.shape[2]
    per = width // rows
    shard = 3 * width // len(table)
    steps = shard // rows

    def owner():
        return lookup(table, lax.axis_index("dp"))

    def column(i):
        return (0, lax.rem(owner() * steps + low + i, per))

    in_specs = [
        pl.BlockSpec((tokens, rows), column),
        pl.BlockSpec((tokens, rows), column),
        pl.BlockSpec((1, tokens, hidden), lambda i: (lax.div(owner() * steps + low + i, per), 0, 0)),
    ]
    operands = [x, dy, factors]
    for message, start in got:
        blocks = (message.shape[0] - PAD) // PAD
        in_specs += [
            pl.BlockSpec((rows, hidden), lambda i, start=start: (i + low - start, 0)),
            pl.BlockSpec((PAD, hidden), lambda i, blocks=blocks: (blocks, 0)),
        ]
        operands += [message, message]
    aliases = {}
    extra = 0
    if before is not None:
        extra = 2
        aliases = {len(operands): 0}
        operands += before
        in_specs += [pl.BlockSpec(memory_space=pl.ANY), pl.BlockSpec((8, 128), lambda i: (0, 0))]
    elif after is not None:
        extra = 1
        operands.append(after)
        in_specs.append(pl.BlockSpec(memory_space=pl.ANY))
    if last:
        out_specs = [
            pl.BlockSpec((rows, hidden), lambda i: (i + low, 0)),
            pl.BlockSpec((8 * last, 128), lambda i: (0, 0)),
        ]
        out_shape = [
            jax.ShapeDtypeStruct((shard, hidden), jnp.float32),
            jax.ShapeDtypeStruct((8 * last, 128), jnp.float32),
        ]
        scratch = []
    else:
        out_specs = pl.BlockSpec(((high - low) * rows + PAD, hidden), lambda i: (0, 0))
        out_shape = jax.ShapeDtypeStruct(((high - low) * rows + PAD, hidden), jnp.bfloat16)
        scratch = [pltpu.VMEM((PAD, hidden), jnp.float32)]
    return pl.pallas_call(
        lambda *refs: piece_kernel(owner, per, steps, low, [s for _, s in got], extra, last, *refs),
        grid=(high - low,),
        in_specs=in_specs,
        out_specs=out_specs,
        out_shape=out_shape,
        scratch_shapes=scratch,
        input_output_aliases=aliases,
        compiler_params=pltpu.CompilerParams(vmem_limit_bytes=32 << 20),
        cost_estimate=CHEAP,
        name="piece",
    )(*operands)


def update_kernel(max_norm, total_ref, g_ref, p_ref, m1_ref, m2_ref, new_p, new_m1, new_m2, new_w):
    clip = clip_of(jnp.sum(total_ref[...], keepdims=True), max_norm)
    param, first, second = adam(clip, g_ref[...], p_ref[...], m1_ref[...], m2_ref[...])
    new_p[...] = param
    new_m1[...] = first
    new_m2[...] = second
    new_w[...] = param.astype(jnp.bfloat16)


def update(total, shard, param, first, second, max_norm, rows):
    block = pl.BlockSpec((rows, shard.shape[1]), lambda i: (i, 0))
    wide = jax.ShapeDtypeStruct(shard.shape, jnp.float32)
    return pl.pallas_call(
        lambda *refs: update_kernel(max_norm, *refs),
        grid=(shard.shape[0] // rows,),
        in_specs=[pl.BlockSpec(total.shape, lambda i: (0, 0))] + [block] * 4,
        out_specs=[block] * 4,
        out_shape=[wide] * 3 + [jax.ShapeDtypeStruct(shard.shape, jnp.bfloat16)],
        compiler_params=pltpu.CompilerParams(vmem_limit_bytes=32 << 20),
        cost_estimate=CHEAP,
        name="update",
    )(total, shard, param, first, second)


def behind(value, other):
    return pl.pallas_call(
        lambda *refs: None,
        in_specs=[pl.BlockSpec(memory_space=pl.ANY)] * 2,
        out_specs=pl.BlockSpec(memory_space=pl.ANY),
        out_shape=jax.ShapeDtypeStruct(value.shape, value.dtype),
        input_output_aliases={0: 0},
        cost_estimate=CHEAP,
        name="behind",
    )(value, other)


def paired(weights, inputs, out_grads, master, moment1, moment2):
    n = lax.axis_size("dp")
    pairs = n // 2
    ring = list(range(0, pairs, 2)) + list(range(pairs - 1 - pairs % 2, 0, -2))
    place = {pair: at for at, pair in enumerate(ring)}

    def at_offset(r, offset, flip):
        return 2 * ring[(place[r // 2] + offset) % pairs] + ((r % 2) ^ flip)

    def table(offset, flip):
        return [at_offset(r, offset, flip) for r in range(n)]

    def send(value, offset, flip=0):
        return lax.ppermute(value, "dp", [(r, at_offset(r, offset, flip)) for r in range(n)])

    stacked = weights[0]
    x, dy = inputs[0], out_grads[0]
    width = x.shape[1]
    shard_rows = stacked.shape[0] // n
    rows = math.gcd(math.gcd(shard_rows, width), 256)

    steps = shard_rows // rows
    forth = pairs // 2
    back = pairs - 1 - forth
    order = sorted(range(-back, forth + 1), key=lambda o: (-abs(o), o))
    cuts = {offset: [(0, steps)] for offset in order}
    if steps > 1:
        cuts[order[-2]] = [(0, steps - 1), (steps - 1, steps)]

    factors, message = forward(x, dy, stacked, table(order[0], 1), rows)
    crossed = {order[0]: send(message, 0, 1)}
    after = None
    for offset in order[1:]:
        after = piece(x, dy, factors, table(offset, 1), rows, 0, steps, after=after)
        crossed[offset] = send(after, 0, 1)

    arrived = {}
    devices = n * lax.axis_size("section")
    for offset in order[:-1]:
        way = 1 if offset > 0 else -1
        for low, high in cuts[offset]:
            got = [(crossed[offset], 0)] + arrived.get((offset, way), [])
            message = piece(x, dy, factors, table(offset, 0), rows, low, high, got)
            arrived.setdefault((offset - way, way), []).append((send(message, way), low))
    cut = cuts[order[-2]]
    whole = (crossed[0], 0)
    done = None
    for low, high in cut:
        got = [whole]
        for key in ((0, 1), (0, -1)):
            messages = arrived.get(key, [])
            got += [m for m in messages if m[1] == low] if len(messages) > 1 else messages
        done = piece(
            x, dy, factors, table(0, 0), rows, low, high, got, last=devices if high == steps else 1, before=done
        )
    shard, squares = done

    total = lax.all_to_all(squares, ("dp", "section"), 0, 0, tiled=True)
    max_norm = math.sqrt(lax.axis_size("section") * stacked.size)
    new_param, new_first, new_second, own = update(
        total, shard, master[0], moment1[0], moment2[0], max_norm, rows
    )

    held = {0: own}
    other = {0: send(own, 0, 1)}
    for step in range(1, forth + 1):
        forward_on = held[1 - step] if step == 1 else behind(held[1 - step], other[0])
        held[-step] = send(forward_on, 1)
        if step <= back:
            held[step] = send(held[step - 1], -1)
    for offset in held:
        if offset:
            other[offset] = send(held[offset], 0, 1)
    r = lax.axis_index("dp")
    gathered = jnp.zeros_like(stacked)
    for flip, values in enumerate((held, other)):
        for offset in sorted(held, key=lambda o: (abs(o), o)):
            start = lookup(table(offset, flip), r) * shard_rows
            gathered = lax.dynamic_update_slice(gathered, values[offset], (start, 0))
    return new_param[None], new_first[None], new_second[None], gathered[None]


def local(weights, *rest):
    n = lax.axis_size("dp")
    height = weights.shape[1]
    fits = n % 2 == 0 and n > 2 and height % n == 0 and (height // n) % 128 == 0 and (height // 3) % 128 == 0
    return (paired if fits else plain)(weights, *rest)


def solution(mesh):
    whole = P("section", None, None)
    split = P("section", "dp", None)
    return jax.shard_map(
        local,
        mesh=mesh,
        in_specs=(whole, split, split, split, split, split),
        out_specs=(split, split, split, whole),
        check_vma=False,
    )
```

```python
import math

import jax
import jax.numpy as jnp
from jax import lax
from jax.experimental import pallas as pl
from jax.experimental.pallas import tpu as pltpu
from jax.sharding import PartitionSpec as P

MROWS = 256
STEP = 10
PAD = 16
POWER = 8
TOP = 32768.0
CHEAP = pl.CostEstimate(flops=1024, bytes_accessed=1024, transcendentals=0)


def forward_pieces(x_rows, dy_rows, w_gate, w_up, w_down):
    pre_gate = jnp.dot(x_rows, w_gate, preferred_element_type=jnp.float32)
    pre_up = jnp.dot(x_rows, w_up, preferred_element_type=jnp.float32)
    d_hidden = jnp.dot(dy_rows, w_down, preferred_element_type=jnp.float32)
    return activation(pre_gate, pre_up, d_hidden)


def activation(pre_gate, pre_up, d_hidden):
    sigma = jax.nn.sigmoid(pre_gate)
    silu_val = pre_gate * sigma
    hidden = (silu_val * pre_up).astype(jnp.bfloat16)
    d_gate = (d_hidden * pre_up * sigma * (1.0 + pre_gate * (1.0 - sigma))).astype(jnp.bfloat16)
    d_up = (d_hidden * silu_val).astype(jnp.bfloat16)
    return d_gate, d_up, hidden


def block_grads(x_rows, dy_rows, w_gate, w_up, w_down):
    d_gate, d_up, hidden = forward_pieces(x_rows, dy_rows, w_gate, w_up, w_down)
    g_gate = jnp.dot(x_rows.T, d_gate, preferred_element_type=jnp.float32)
    g_up = jnp.dot(x_rows.T, d_up, preferred_element_type=jnp.float32)
    g_down = jnp.dot(dy_rows.T, hidden, preferred_element_type=jnp.float32)
    return jnp.concatenate([g_gate, g_up, g_down], axis=0)


def adam(clip, shard, old_param, first, second):
    clipped = clip * shard
    new_first = 0.9 * first + 0.1 * clipped
    new_second = 0.95 * second + 0.05 * clipped * clipped
    first_fix = 1.0 / (1.0 - 0.9**STEP)
    second_fix = 1.0 / (1.0 - 0.95**STEP)
    update = new_first * first_fix / (jnp.sqrt(new_second * second_fix) + 1e-08) + 0.1 * old_param
    return old_param - 0.01 * update, new_first, new_second


def clip_of(total, max_norm):
    return jnp.minimum(jnp.float32(1.0), max_norm / (jnp.sqrt(total) + 1e-06))


def plain(weights, inputs, out_grads, master, moment1, moment2):
    stacked = weights[0]
    width = stacked.shape[0] // 3
    local_grad = jnp.zeros(stacked.shape, jnp.float32)
    for start in range(0, inputs.shape[1], MROWS):
        x_rows = inputs[0, start : start + MROWS]
        dy_rows = out_grads[0, start : start + MROWS]
        local_grad = local_grad + block_grads(
            x_rows, dy_rows, stacked[:width], stacked[width : 2 * width], stacked[2 * width :]
        )
    shard = lax.psum_scatter(local_grad, "dp", scatter_dimension=0, tiled=True)
    total = lax.psum(jnp.sum(shard * shard), ("dp", "section"))
    max_norm = jnp.sqrt(jnp.float32(lax.axis_size("section") * stacked.size))
    new_param, new_first, new_second = adam(clip_of(total, max_norm), shard, master[0], moment1[0], moment2[0])
    gathered = lax.all_gather(new_param.astype(jnp.bfloat16), "dp", axis=0, tiled=True)
    return new_param[None], new_first[None], new_second[None], gathered[None]


def encode(value):
    scale = jnp.max(jnp.abs(value), axis=0, keepdims=True)
    scale = jnp.maximum(scale, 1e-30).astype(jnp.bfloat16).astype(jnp.float32)
    v = value * (TOP / scale)
    v2 = v * v
    v4 = v2 * v2
    v8 = v4 * v4
    return jnp.where(v < 0.0, -v8, v8).astype(jnp.bfloat16), scale


def decode(code, scale):
    code = code.astype(jnp.float32)
    size = jnp.abs(code)
    root = jnp.exp(jnp.log(jnp.maximum(size, 1e-37)) * (1.0 / POWER)) * (scale * (1.0 / TOP))
    root = jnp.where(size > 0.0, root, 0.0)
    return jnp.where(code < 0.0, -root, root)


def lookup(table, index):
    out = jnp.int32(table[0])
    for at, value in enumerate(table[1:], 1):
        out = jnp.where(index == at, jnp.int32(value), out)
    return out


def message_rows(left, factor, out_ref, step, scales):
    rows = left.shape[1]
    total = lax.dot_general(left, factor, (((0,), (0,)), ((), ())), preferred_element_type=jnp.float32)
    code, scale = encode(total)
    out_ref[step * rows : (step + 1) * rows, :] = code
    row = lax.broadcasted_iota(jnp.int32, scales.shape, 0)
    return jnp.where(row == step, scale, scales)


def forward_kernel(owner, rows, x_hbm, dy_hbm, w_hbm, factors_ref, out_ref, x_ref, dy_ref, w_ref, sems):
    width = x_hbm.shape[1]
    half = width // 2

    def fetch(at, source, target, index):
        copy = pltpu.make_async_copy(source.at[index], target.at[index], sems.at[at])
        copy.start()
        return copy

    copies = []
    for columns in (pl.ds(0, half), pl.ds(half, half)):
        copies.append(fetch(len(copies), x_hbm, x_ref, (slice(None), columns)))
        copies.append(fetch(len(copies), w_hbm, w_ref, columns))
        copies.append(fetch(len(copies), w_hbm, w_ref, pl.ds(columns.start + width, half)))
    for columns in (pl.ds(0, half), pl.ds(half, half)):
        copies.append(fetch(len(copies), dy_hbm, dy_ref, (slice(None), columns)))
        copies.append(fetch(len(copies), w_hbm, w_ref, pl.ds(columns.start + 2 * width, half)))

    def product(left, start, which):
        weight = w_ref[which * width + start : which * width + start + half]
        return jnp.dot(left[:, start : start + half], weight, preferred_element_type=jnp.float32)

    for copy in copies[:3]:
        copy.wait()
    pre_gate = product(x_ref, 0, 0)
    pre_up = product(x_ref, 0, 1)
    for copy in copies[3:6]:
        copy.wait()
    pre_gate = pre_gate + product(x_ref, half, 0)
    pre_up = pre_up + product(x_ref, half, 1)
    for copy in copies[6:8]:
        copy.wait()
    d_hidden = product(dy_ref, 0, 2)
    for copy in copies[8:]:
        copy.wait()
    d_hidden = d_hidden + product(dy_ref, half, 2)
    d_gate, d_up, hidden = activation(pre_gate, pre_up, d_hidden)
    factors_ref[0] = d_gate
    factors_ref[1] = d_up
    factors_ref[2] = hidden
    steps = (out_ref.shape[0] - PAD) // rows
    scales = jnp.zeros((PAD, out_ref.shape[1]), jnp.float32)
    for step in range(steps):
        at = owner() * steps + step
        kind = lax.div(at, width // rows)
        column = pl.ds(pl.multiple_of(lax.rem(at, width // rows) * rows, rows), rows)
        left = jnp.where(kind == 2, dy_ref[:, column], x_ref[:, column])
        scales = message_rows(left, factors_ref[kind], out_ref, step, scales)
    out_ref[steps * rows :, :] = scales.astype(jnp.bfloat16)


def forward(x, dy, stacked, table, rows):
    tokens, width = x.shape
    hidden = stacked.shape[1]
    shard = stacked.shape[0] // len(table)

    def owner():
        return lookup(table, lax.axis_index("dp"))

    return pl.pallas_call(
        lambda *refs: forward_kernel(owner, rows, *refs),
        in_specs=[pl.BlockSpec(memory_space=pltpu.HBM)] * 3,
        out_shape=[
            jax.ShapeDtypeStruct((3, tokens, hidden), jnp.bfloat16),
            jax.ShapeDtypeStruct((shard + PAD, hidden), jnp.bfloat16),
        ],
        scratch_shapes=[
            pltpu.VMEM(x.shape, x.dtype),
            pltpu.VMEM(dy.shape, dy.dtype),
            pltpu.VMEM(stacked.shape, stacked.dtype),
            pltpu.SemaphoreType.DMA((10,)),
        ],
        compiler_params=pltpu.CompilerParams(vmem_limit_bytes=60 << 20),
        cost_estimate=CHEAP,
        name="forward",
    )(x, dy, stacked)


def piece_kernel(owner, per, steps, low, starts, extra, last, *refs):
    step = pl.program_id(0)
    x_ref, dy_ref, d_ref = refs[:3]
    got = refs[3 : 3 + 2 * len(starts)]
    before = refs[3 + 2 * len(starts) : 3 + 2 * len(starts) + extra]
    outs = refs[3 + 2 * len(starts) + extra :]
    rows = x_ref.shape[1]
    kind = lax.div(owner() * steps + low + step, per)
    left = jnp.where(kind == 2, dy_ref[...], x_ref[...])
    total = lax.dot_general(left, d_ref[0], (((0,), (0,)), ((), ())), preferred_element_type=jnp.float32)
    for at, start in enumerate(starts):
        scales = got[2 * at + 1][...].astype(jnp.float32)
        row = lax.broadcasted_iota(jnp.int32, scales.shape, 0)
        scale = jnp.sum(jnp.where(row == step + low - start, scales, 0.0), axis=0, keepdims=True)
        total = total + decode(got[2 * at][...], scale)
    if last:
        out_ref, squares = outs
        out_ref[...] = total
        tile = jnp.sum((total * total).reshape(rows // 8, 8, -1), axis=0)
        tile = sum(tile[:, at : at + 128] for at in range(0, tile.shape[1], 128))
        tile = tile + jnp.where(step == 0, before[1][...] if extra else 0.0, squares[:8])
        for at in range(0, squares.shape[0], 8):
            squares[at : at + 8] = tile
    else:
        out_ref, scales_ref = outs
        code, scale = encode(total)
        out_ref[pl.ds(pl.multiple_of(step * rows, rows), rows), :] = code
        row = lax.broadcasted_iota(jnp.int32, scales_ref.shape, 0)
        scales_ref[...] = jnp.where(row == step, scale, jnp.where(step == 0, 0.0, scales_ref[...]))
        out_ref[pl.ds(out_ref.shape[0] - PAD, PAD), :] = scales_ref[...].astype(jnp.bfloat16)


def piece(x, dy, factors, table, rows, low, high, got=(), after=None, last=0, before=None):
    tokens, width = x.shape
    hidden = factors.shape[2]
    per = width // rows
    shard = 3 * width // len(table)
    steps = shard // rows

    def owner():
        return lookup(table, lax.axis_index("dp"))

    def column(i):
        return (0, lax.rem(owner() * steps + low + i, per))

    in_specs = [
        pl.BlockSpec((tokens, rows), column),
        pl.BlockSpec((tokens, rows), column),
        pl.BlockSpec((1, tokens, hidden), lambda i: (lax.div(owner() * steps + low + i, per), 0, 0)),
    ]
    operands = [x, dy, factors]
    for message, start in got:
        blocks = (message.shape[0] - PAD) // PAD
        in_specs += [
            pl.BlockSpec((rows, hidden), lambda i, start=start: (i + low - start, 0)),
            pl.BlockSpec((PAD, hidden), lambda i, blocks=blocks: (blocks, 0)),
        ]
        operands += [message, message]
    aliases = {}
    extra = 0
    if before is not None:
        extra = 2
        aliases = {len(operands): 0}
        operands += before
        in_specs += [pl.BlockSpec(memory_space=pl.ANY), pl.BlockSpec((8, 128), lambda i: (0, 0))]
    elif after is not None:
        extra = 1
        operands.append(after)
        in_specs.append(pl.BlockSpec(memory_space=pl.ANY))
    if last:
        out_specs = [
            pl.BlockSpec((rows, hidden), lambda i: (i + low, 0)),
            pl.BlockSpec((8 * last, 128), lambda i: (0, 0)),
        ]
        out_shape = [
            jax.ShapeDtypeStruct((shard, hidden), jnp.float32),
            jax.ShapeDtypeStruct((8 * last, 128), jnp.float32),
        ]
        scratch = []
    else:
        out_specs = pl.BlockSpec(((high - low) * rows + PAD, hidden), lambda i: (0, 0))
        out_shape = jax.ShapeDtypeStruct(((high - low) * rows + PAD, hidden), jnp.bfloat16)
        scratch = [pltpu.VMEM((PAD, hidden), jnp.float32)]
    return pl.pallas_call(
        lambda *refs: piece_kernel(owner, per, steps, low, [s for _, s in got], extra, last, *refs),
        grid=(high - low,),
        in_specs=in_specs,
        out_specs=out_specs,
        out_shape=out_shape,
        scratch_shapes=scratch,
        input_output_aliases=aliases,
        compiler_params=pltpu.CompilerParams(vmem_limit_bytes=32 << 20),
        cost_estimate=CHEAP,
        name="piece",
    )(*operands)


def update_kernel(max_norm, total_ref, g_ref, p_ref, m1_ref, m2_ref, new_p, new_m1, new_m2, new_w):
    clip = clip_of(jnp.sum(total_ref[...], keepdims=True), max_norm)
    param, first, second = adam(clip, g_ref[...], p_ref[...], m1_ref[...], m2_ref[...])
    new_p[...] = param
    new_m1[...] = first
    new_m2[...] = second
    new_w[...] = param.astype(jnp.bfloat16)


def update(total, shard, param, first, second, max_norm, rows):
    block = pl.BlockSpec((rows, shard.shape[1]), lambda i: (i, 0))
    wide = jax.ShapeDtypeStruct(shard.shape, jnp.float32)
    return pl.pallas_call(
        lambda *refs: update_kernel(max_norm, *refs),
        grid=(shard.shape[0] // rows,),
        in_specs=[pl.BlockSpec(total.shape, lambda i: (0, 0))] + [block] * 4,
        out_specs=[block] * 4,
        out_shape=[wide] * 3 + [jax.ShapeDtypeStruct(shard.shape, jnp.bfloat16)],
        compiler_params=pltpu.CompilerParams(vmem_limit_bytes=32 << 20),
        cost_estimate=CHEAP,
        name="update",
    )(total, shard, param, first, second)


def paired(weights, inputs, out_grads, master, moment1, moment2):
    n = lax.axis_size("dp")
    pairs = n // 2
    ring = list(range(0, pairs, 2)) + list(range(pairs - 1 - pairs % 2, 0, -2))
    place = {pair: at for at, pair in enumerate(ring)}

    def at_offset(r, offset, flip):
        return 2 * ring[(place[r // 2] + offset) % pairs] + ((r % 2) ^ flip)

    def table(offset, flip):
        return [at_offset(r, offset, flip) for r in range(n)]

    def send(value, offset, flip=0):
        return lax.ppermute(value, "dp", [(r, at_offset(r, offset, flip)) for r in range(n)])

    stacked = weights[0]
    x, dy = inputs[0], out_grads[0]
    width = x.shape[1]
    shard_rows = stacked.shape[0] // n
    rows = math.gcd(math.gcd(shard_rows, width), 256)

    steps = shard_rows // rows
    forth = pairs // 2
    back = pairs - 1 - forth
    order = sorted(range(-back, forth + 1), key=lambda o: (-abs(o), o))
    cuts = {offset: [(0, steps)] for offset in order}
    if steps > 1:
        cuts[order[-2]] = [(0, steps - 1), (steps - 1, steps)]

    factors, message = forward(x, dy, stacked, table(order[0], 1), rows)
    crossed = {order[0]: send(message, 0, 1)}
    after = None
    for offset in order[1:]:
        after = piece(x, dy, factors, table(offset, 1), rows, 0, steps, after=after)
        crossed[offset] = send(after, 0, 1)

    arrived = {}
    sections = lax.axis_size("section")
    for offset in order[:-1]:
        way = 1 if offset > 0 else -1
        for low, high in cuts[offset]:
            got = [(crossed[offset], 0)] + arrived.get((offset, way), [])
            message = piece(x, dy, factors, table(offset, 0), rows, low, high, got)
            arrived.setdefault((offset - way, way), []).append((send(message, way), low))
    cut = cuts[order[-2]]
    whole = (crossed[0], 0)
    done = None
    for low, high in cut:
        got = [whole]
        for key in ((0, 1), (0, -1)):
            messages = arrived.get(key, [])
            got += [m for m in messages if m[1] == low] if len(messages) > 1 else messages
        done = piece(
            x, dy, factors, table(0, 0), rows, low, high, got, last=sections if high == steps else 1, before=done
        )
    shard, squares = done

    total = lax.all_to_all(squares, "section", 0, 0, tiled=True)
    total = jnp.tile(jnp.sum(total.reshape(-1, 8, 128), axis=0), (n, 1))
    total = lax.all_to_all(total, "dp", 0, 0, tiled=True)
    max_norm = math.sqrt(lax.axis_size("section") * stacked.size)
    new_param, new_first, new_second, own = update(
        total, shard, master[0], moment1[0], moment2[0], max_norm, rows
    )

    r = lax.axis_index("dp")
    cut = shard_rows - rows

    def start(offset, flip):
        return lookup(table(offset, flip), r) * shard_rows

    def put(gathered, value, offset, flip, low=0):
        return lax.dynamic_update_slice(gathered, value, (start(offset, flip) + low, 0))

    def take(gathered, offset, flip, size):
        return lax.dynamic_slice(gathered, (start(offset, flip), 0), (size, stacked.shape[1]))

    other = send(own, 0, 1)
    held = {-1: send(own, 1)}
    tail = send(own[cut:], -1)
    gathered = put(jnp.zeros_like(stacked), own, 0, 0)
    gathered = put(gathered, other, 0, 1)
    gathered = put(gathered, held[-1], -1, 0)
    crosses = {-1: send(held[-1], 0, 1)}
    held[-2] = send(take(gathered, -1, 0, shard_rows), 1)
    gathered = put(gathered, tail, 1, 0, cut)
    tail_cross = send(tail, 0, 1)
    both = send(jnp.concatenate([take(gathered, 0, 0, cut), take(gathered, 0, 1, cut)]), -1)
    crosses[-2] = send(held[-2], 0, 1)
    gathered = put(gathered, crosses[-1], -1, 1)
    gathered = put(gathered, tail_cross, 1, 1, cut)
    gathered = put(gathered, held[-2], -2, 0)
    gathered = put(gathered, both[:cut], 1, 0)
    gathered = put(gathered, both[cut:], 1, 1)
    gathered = put(gathered, crosses[-2], -2, 1)
    return new_param[None], new_first[None], new_second[None], gathered[None]


def local(weights, *rest):
    n = lax.axis_size("dp")
    height = weights.shape[1]
    fits = n == 8 and height % n == 0 and (height // n) % 128 == 0 and (height // 3) % 128 == 0
    return (paired if fits else plain)(weights, *rest)


def solution(mesh):
    whole = P("section", None, None)
    split = P("section", "dp", None)
    return jax.shard_map(
        local,
        mesh=mesh,
        in_specs=(whole, split, split, split, split, split),
        out_specs=(split, split, split, whole),
        check_vma=False,
    )
```

```python
import math

import jax
import jax.numpy as jnp
from jax import lax
from jax.experimental import pallas as pl
from jax.experimental.pallas import tpu as pltpu
from jax.sharding import PartitionSpec as P

MROWS = 256
STEP = 10
PAD = 16
POWER = 8
TOP = 32768.0
PIECE = pl.CostEstimate(flops=2_000_000_000, bytes_accessed=1024, transcendentals=0)
CHEAP = pl.CostEstimate(flops=1024, bytes_accessed=1024, transcendentals=0)


def forward_pieces(x_rows, dy_rows, w_gate, w_up, w_down):
    pre_gate = jnp.dot(x_rows, w_gate, preferred_element_type=jnp.float32)
    pre_up = jnp.dot(x_rows, w_up, preferred_element_type=jnp.float32)
    d_hidden = jnp.dot(dy_rows, w_down, preferred_element_type=jnp.float32)
    return activation(pre_gate, pre_up, d_hidden)


def activation(pre_gate, pre_up, d_hidden):
    sigma = jax.nn.sigmoid(pre_gate)
    silu_val = pre_gate * sigma
    hidden = (silu_val * pre_up).astype(jnp.bfloat16)
    d_gate = (d_hidden * pre_up * sigma * (1.0 + pre_gate * (1.0 - sigma))).astype(jnp.bfloat16)
    d_up = (d_hidden * silu_val).astype(jnp.bfloat16)
    return d_gate, d_up, hidden


def block_grads(x_rows, dy_rows, w_gate, w_up, w_down):
    d_gate, d_up, hidden = forward_pieces(x_rows, dy_rows, w_gate, w_up, w_down)
    g_gate = jnp.dot(x_rows.T, d_gate, preferred_element_type=jnp.float32)
    g_up = jnp.dot(x_rows.T, d_up, preferred_element_type=jnp.float32)
    g_down = jnp.dot(dy_rows.T, hidden, preferred_element_type=jnp.float32)
    return jnp.concatenate([g_gate, g_up, g_down], axis=0)


def adam(clip, shard, old_param, first, second):
    clipped = clip * shard
    new_first = 0.9 * first + 0.1 * clipped
    new_second = 0.95 * second + 0.05 * clipped * clipped
    first_fix = 1.0 / (1.0 - 0.9**STEP)
    second_fix = 1.0 / (1.0 - 0.95**STEP)
    update = new_first * first_fix / (jnp.sqrt(new_second * second_fix) + 1e-08) + 0.1 * old_param
    return old_param - 0.01 * update, new_first, new_second


def clip_of(total, max_norm):
    return jnp.minimum(jnp.float32(1.0), max_norm / (jnp.sqrt(total) + 1e-06))


def plain(weights, inputs, out_grads, master, moment1, moment2):
    stacked = weights[0]
    width = stacked.shape[0] // 3
    local_grad = jnp.zeros(stacked.shape, jnp.float32)
    for start in range(0, inputs.shape[1], MROWS):
        x_rows = inputs[0, start : start + MROWS]
        dy_rows = out_grads[0, start : start + MROWS]
        local_grad = local_grad + block_grads(
            x_rows, dy_rows, stacked[:width], stacked[width : 2 * width], stacked[2 * width :]
        )
    shard = lax.psum_scatter(local_grad, "dp", scatter_dimension=0, tiled=True)
    total = lax.psum(jnp.sum(shard * shard), ("dp", "section"))
    max_norm = jnp.sqrt(jnp.float32(lax.axis_size("section") * stacked.size))
    new_param, new_first, new_second = adam(clip_of(total, max_norm), shard, master[0], moment1[0], moment2[0])
    gathered = lax.all_gather(new_param.astype(jnp.bfloat16), "dp", axis=0, tiled=True)
    return new_param[None], new_first[None], new_second[None], gathered[None]


def encode(value):
    scale = jnp.max(jnp.abs(value), axis=0, keepdims=True)
    scale = jnp.maximum(scale, 1e-30).astype(jnp.bfloat16).astype(jnp.float32)
    v = value * (TOP / scale)
    v2 = v * v
    v4 = v2 * v2
    v8 = v4 * v4
    return jnp.where(v < 0.0, -v8, v8).astype(jnp.bfloat16), scale


def decode(code, scale):
    code = code.astype(jnp.float32)
    size = jnp.abs(code)
    root = jnp.exp(jnp.log(jnp.maximum(size, 1e-37)) * (1.0 / POWER)) * (scale * (1.0 / TOP))
    root = jnp.where(size > 0.0, root, 0.0)
    return jnp.where(code < 0.0, -root, root)


def lookup(table, index):
    bits = max(max(table).bit_length(), 1)
    if bits * len(table) < 32:
        packed = sum(value << (bits * at) for at, value in enumerate(table))
        return jnp.bitwise_and(jnp.right_shift(jnp.int32(packed), index * bits), (1 << bits) - 1)
    out = jnp.int32(table[0])
    for at, value in enumerate(table[1:], 1):
        out = jnp.where(index == at, jnp.int32(value), out)
    return out


def message_rows(left, factor, out_ref, step, scales):
    rows = left.shape[1]
    total = lax.dot_general(left, factor, (((0,), (0,)), ((), ())), preferred_element_type=jnp.float32)
    code, scale = encode(total)
    out_ref[step * rows : (step + 1) * rows, :] = code
    row = lax.broadcasted_iota(jnp.int32, scales.shape, 0)
    return jnp.where(row == step, scale, scales)


def forward_kernel(owner, rows, x_hbm, dy_hbm, w_hbm, factors_ref, out_ref, x_ref, dy_ref, w_ref, sems):
    width = x_hbm.shape[1]
    half = width // 2

    def fetch(at, source, target, index):
        copy = pltpu.make_async_copy(source.at[index], target.at[index], sems.at[at])
        copy.start()
        return copy

    copies = []
    for columns in (pl.ds(0, half), pl.ds(half, half)):
        copies.append(fetch(len(copies), x_hbm, x_ref, (slice(None), columns)))
        copies.append(fetch(len(copies), w_hbm, w_ref, columns))
        copies.append(fetch(len(copies), w_hbm, w_ref, pl.ds(columns.start + width, half)))
    for columns in (pl.ds(0, half), pl.ds(half, half)):
        copies.append(fetch(len(copies), dy_hbm, dy_ref, (slice(None), columns)))
        copies.append(fetch(len(copies), w_hbm, w_ref, pl.ds(columns.start + 2 * width, half)))

    def product(left, start, which):
        weight = w_ref[which * width + start : which * width + start + half]
        return jnp.dot(left[:, start : start + half], weight, preferred_element_type=jnp.float32)

    for copy in copies[:3]:
        copy.wait()
    pre_gate = product(x_ref, 0, 0)
    pre_up = product(x_ref, 0, 1)
    for copy in copies[3:6]:
        copy.wait()
    pre_gate = pre_gate + product(x_ref, half, 0)
    pre_up = pre_up + product(x_ref, half, 1)
    for copy in copies[6:8]:
        copy.wait()
    d_hidden = product(dy_ref, 0, 2)
    for copy in copies[8:]:
        copy.wait()
    d_hidden = d_hidden + product(dy_ref, half, 2)
    d_gate, d_up, hidden = activation(pre_gate, pre_up, d_hidden)
    factors_ref[0] = d_gate
    factors_ref[1] = d_up
    factors_ref[2] = hidden
    steps = (out_ref.shape[0] - PAD) // rows
    scales = jnp.zeros((PAD, out_ref.shape[1]), jnp.float32)
    for step in range(steps):
        at = owner() * steps + step
        kind = lax.div(at, width // rows)
        column = pl.ds(pl.multiple_of(lax.rem(at, width // rows) * rows, rows), rows)
        left = jnp.where(kind == 2, dy_ref[:, column], x_ref[:, column])
        scales = message_rows(left, factors_ref[kind], out_ref, step, scales)
    out_ref[steps * rows :, :] = scales.astype(jnp.bfloat16)


def forward(x, dy, stacked, table, rows):
    tokens, width = x.shape
    hidden = stacked.shape[1]
    shard = stacked.shape[0] // len(table)

    def owner():
        return lookup(table, lax.axis_index("dp"))

    return pl.pallas_call(
        lambda *refs: forward_kernel(owner, rows, *refs),
        in_specs=[pl.BlockSpec(memory_space=pltpu.HBM)] * 3,
        out_shape=[
            jax.ShapeDtypeStruct((3, tokens, hidden), jnp.bfloat16),
            jax.ShapeDtypeStruct((shard + PAD, hidden), jnp.bfloat16),
        ],
        scratch_shapes=[
            pltpu.VMEM(x.shape, x.dtype),
            pltpu.VMEM(dy.shape, dy.dtype),
            pltpu.VMEM(stacked.shape, stacked.dtype),
            pltpu.SemaphoreType.DMA((10,)),
        ],
        compiler_params=pltpu.CompilerParams(vmem_limit_bytes=60 << 20),
        cost_estimate=CHEAP,
        name="forward",
    )(x, dy, stacked)


def pick(values, step):
    if all(value == values[0] + at for at, value in enumerate(values)):
        return step + values[0] if len(values) > 1 else jnp.int32(values[0])
    out = jnp.int32(values[0])
    for at, value in enumerate(values[1:], 1):
        out = jnp.where(step == at, value, out)
    return out


def piece_kernel(place, per, got, extra, last, *refs):
    step = pl.program_id(0)
    x_ref, dy_ref, d_ref = refs[:3]
    before = refs[3 + 2 * len(got) : 3 + 2 * len(got) + extra]
    outs = refs[3 + 2 * len(got) + extra :]
    rows = x_ref.shape[1]
    left = jnp.where(lax.div(place(step), per) == 2, dy_ref[...], x_ref[...])
    total = lax.dot_general(left, d_ref[0], (((0,), (0,)), ((), ())), preferred_element_type=jnp.float32)
    for at, blocks in enumerate(got):
        scales = refs[4 + 2 * at][...].astype(jnp.float32)
        row = lax.broadcasted_iota(jnp.int32, scales.shape, 0)
        here = pick([PAD if block is None else block for block in blocks], step)
        scale = jnp.sum(jnp.where(row == here, scales, 0.0), axis=0, keepdims=True)
        total = total + decode(refs[3 + 2 * at][...], scale)
    if last:
        out_ref, squares = outs
        out_ref[...] = total
        tile = jnp.sum((total * total).reshape(rows // 8, 8, -1), axis=0)
        tile = sum(tile[:, at : at + 128] for at in range(0, tile.shape[1], 128))
        tile = tile + jnp.where(step == 0, before[1][...] if extra else 0.0, squares[:8])
        for at in range(0, squares.shape[0], 8):
            squares[at : at + 8] = tile
    else:
        out_ref, scales_ref = outs
        code, scale = encode(total)
        out_ref[pl.ds(pl.multiple_of(step * rows, rows), rows), :] = code
        row = lax.broadcasted_iota(jnp.int32, scales_ref.shape, 0)
        scales_ref[...] = jnp.where(row == step, scale, jnp.where(step == 0, 0.0, scales_ref[...]))
        out_ref[pl.ds(out_ref.shape[0] - PAD, PAD), :] = scales_ref[...].astype(jnp.bfloat16)


def piece(x, dy, factors, rows, blocks, got=(), after=None, last=0, before=None):
    tokens, width = x.shape
    hidden = factors.shape[2]
    per = width // rows
    shard = 3 * width // len(blocks[0][0])
    steps = shard // rows
    tables = [table for table, _ in blocks]
    within = [block for _, block in blocks]

    def place(i):
        r = lax.axis_index("dp")
        owner = lookup(tables[0], r)
        for at, table in enumerate(tables[1:], 1):
            if table != tables[at - 1]:
                owner = jnp.where(i >= at, lookup(table, r), owner)
        return owner * steps + pick(within, i)

    def column(i):
        return (0, lax.rem(place(i), per))

    in_specs = [
        pl.BlockSpec((tokens, rows), column),
        pl.BlockSpec((tokens, rows), column),
        pl.BlockSpec((1, tokens, hidden), lambda i: (lax.div(place(i), per), 0, 0)),
    ]
    operands = [x, dy, factors]
    for message, parts in got:
        present = [part for part in parts if part is not None]
        nearest = [present[0] if part is None else part for part in parts]
        scales = (message.shape[0] - PAD) // PAD
        in_specs += [
            pl.BlockSpec((rows, hidden), lambda i, nearest=nearest: (pick(nearest, i), 0)),
            pl.BlockSpec((PAD, hidden), lambda i, scales=scales: (scales, 0)),
        ]
        operands += [message, message]
    aliases = {}
    extra = 0
    if before is not None:
        extra = 2
        aliases = {len(operands): 0}
        operands += before
        in_specs += [pl.BlockSpec(memory_space=pl.ANY), pl.BlockSpec((8, 128), lambda i: (0, 0))]
    elif after is not None:
        extra = 1
        operands.append(after)
        in_specs.append(pl.BlockSpec(memory_space=pl.ANY))
    if last:
        out_specs = [
            pl.BlockSpec((rows, hidden), lambda i: (pick(within, i), 0)),
            pl.BlockSpec((8 * last, 128), lambda i: (0, 0)),
        ]
        out_shape = [
            jax.ShapeDtypeStruct((shard, hidden), jnp.float32),
            jax.ShapeDtypeStruct((8 * last, 128), jnp.float32),
        ]
        scratch = []
    else:
        out_specs = pl.BlockSpec((len(blocks) * rows + PAD, hidden), lambda i: (0, 0))
        out_shape = jax.ShapeDtypeStruct((len(blocks) * rows + PAD, hidden), jnp.bfloat16)
        scratch = [pltpu.VMEM((PAD, hidden), jnp.float32)]
    return pl.pallas_call(
        lambda *refs: piece_kernel(place, per, [parts for _, parts in got], extra, last, *refs),
        grid=(len(blocks),),
        in_specs=in_specs,
        out_specs=out_specs,
        out_shape=out_shape,
        scratch_shapes=scratch,
        input_output_aliases=aliases,
        compiler_params=pltpu.CompilerParams(vmem_limit_bytes=32 << 20),
        cost_estimate=PIECE,
        name="piece",
    )(*operands)


def update_kernel(max_norm, states, total_ref, g_ref, p_ref, m1_ref, m2_ref, *outs):
    clip = clip_of(jnp.sum(total_ref[...], keepdims=True), max_norm)
    param, first, second = adam(clip, g_ref[...], p_ref[...], m1_ref[...], m2_ref[...])
    values = (param, first, second) if states else (param.astype(jnp.bfloat16),)
    for out, value in zip(outs, values):
        out[...] = value


def update(total, shard, param, first, second, max_norm, rows, states):
    block = pl.BlockSpec((rows, shard.shape[1]), lambda i: (i, 0))
    dtypes = [jnp.float32] * 3 if states else [jnp.bfloat16]
    return pl.pallas_call(
        lambda *refs: update_kernel(max_norm, states, *refs),
        grid=(shard.shape[0] // rows,),
        in_specs=[pl.BlockSpec(total.shape, lambda i: (0, 0))] + [block] * 4,
        out_specs=[block] * len(dtypes),
        out_shape=[jax.ShapeDtypeStruct(shard.shape, dtype) for dtype in dtypes],
        compiler_params=pltpu.CompilerParams(vmem_limit_bytes=32 << 20),
        cost_estimate=CHEAP,
        name="states" if states else "update",
    )(total, shard, param, first, second)


def tie(value, other):
    rows = min(PAD, value.shape[0], other.shape[0])
    columns = min(value.shape[1], other.shape[1])
    top = value[:rows, :columns]
    that = other[:rows, :columns].astype(value.dtype)
    return lax.dynamic_update_slice(value, jnp.where(that > jnp.inf, that, top), (0, 0))


def paired(weights, inputs, out_grads, master, moment1, moment2):
    n = lax.axis_size("dp")
    pairs = n // 2
    ring = list(range(0, pairs, 2)) + list(range(pairs - 1 - pairs % 2, 0, -2))
    place = {pair: at for at, pair in enumerate(ring)}

    def at_offset(r, offset, flip):
        return 2 * ring[(place[r // 2] + offset) % pairs] + ((r % 2) ^ flip)

    def table(offset, flip):
        return [at_offset(r, offset, flip) for r in range(n)]

    def send(value, offset, flip=0):
        return lax.ppermute(value, "dp", [(r, at_offset(r, offset, flip)) for r in range(n)])

    stacked = weights[0]
    x, dy = inputs[0], out_grads[0]
    width = x.shape[1]
    shard_rows = stacked.shape[0] // n
    rows = math.gcd(shard_rows, width, 256)

    steps = shard_rows // rows

    most, end = range(steps - 1), steps - 1

    def made(blocks, got=(), **more):
        return piece(x, dy, factors, rows, [(table(offset, flip), block) for offset, flip, block in blocks], got, **more)

    factors, message = forward(x, dy, stacked, table(2, 1), rows)
    cross_far = send(message, 0, 1)
    message = made([(-1, 0, end), (-1, 1, end)])
    ahead = send(message, -1)
    message = made([(-1, 1, block) for block in most] + [(1, 1, 0)], after=message)
    cross_a = send(message, 0, 1)
    message = made([(1, 1, block) for block in range(1, steps)] + [(0, 1, 0)], after=message)
    cross_b = send(message, 0, 1)
    message = made(
        [(0, 1, block) for block in range(1, steps)], [(ahead, [None] * (steps - 2) + [1])], after=message
    )
    cross_c = send(message, 0, 1)

    by_ring = send(made([(2, 0, block) for block in range(steps)], [(cross_far, list(range(steps)))]), 1)
    from_ahead = send(made([(-1, 0, block) for block in most], [(cross_a, list(most))]), -1)
    first = send(made([(1, 0, 0)], [(cross_a, [end]), (by_ring, [0])]), 1)
    rest = list(range(1, steps))
    others = send(made([(1, 0, block) for block in rest], [(cross_b, list(most)), (by_ring, rest)]), 1)
    done = made([(0, 0, 0)], [(cross_b, [end]), (from_ahead, [0]), (first, [0])], last=1)
    got = [
        (cross_c, list(most)),
        (from_ahead, rest[:-1] + [None]),
        (ahead, [None] * (steps - 2) + [0]),
        (others, list(most)),
    ]
    devices = n * lax.axis_size("section")
    done = made([(0, 0, block) for block in rest], got, last=devices, before=done)
    shard, squares = done

    total = lax.all_to_all(squares, ("dp", "section"), 0, 0, tiled=True)
    max_norm = math.sqrt(lax.axis_size("section") * stacked.size)
    states = (shard, master[0], moment1[0], moment2[0], max_norm, rows)
    (own,) = update(total, *states, False)

    r = lax.axis_index("dp")
    cut = shard_rows - rows

    def start(offset, flip):
        return lookup(table(offset, flip), r) * shard_rows

    def put(gathered, value, offset, flip, low=0):
        return lax.dynamic_update_slice(gathered, value, (start(offset, flip) + low, 0))

    def take(gathered, offset, flip, low, high):
        return lax.dynamic_slice(gathered, (start(offset, flip) + low, 0), (high - low, stacked.shape[1]))

    other = send(own, 0, 1)
    behind = tie(send(own, 1), other)
    tail = send(own[cut:], -1)
    behind_cross = send(behind, 0, 1)
    far = send(behind, 1)
    gathered = put(jnp.zeros_like(stacked), own, 0, 0)
    gathered = put(gathered, behind, -1, 0)
    gathered = put(gathered, other, 0, 1)
    gathered = put(gathered, tail, 1, 0, cut)
    tail_cross = send(take(gathered, 1, 0, cut, shard_rows), 0, 1)
    both = send(jnp.concatenate([take(gathered, 0, 0, 0, cut), take(gathered, 0, 1, 0, cut)]), -1)
    far_cross = send(far, 0, 1)
    new_param, new_first, new_second = update(tie(total, other), *states, True)
    gathered = put(gathered, behind_cross, -1, 1)
    gathered = put(gathered, tail_cross, 1, 1, cut)
    gathered = put(gathered, far, -2, 0)
    gathered = put(gathered, both[:cut], 1, 0)
    gathered = put(gathered, both[cut:], 1, 1)
    gathered = put(gathered, far_cross, -2, 1)
    return new_param[None], new_first[None], new_second[None], gathered[None]


def local(weights, *rest):
    n = lax.axis_size("dp")
    height = weights.shape[1]
    shard, width = height // n, height // 3
    fits = n == 8 and height % n == 0 and math.gcd(shard, width, 256) % 128 == 0 and shard // math.gcd(shard, width, 256) > 2
    return (paired if fits else plain)(weights, *rest)


def solution(mesh):
    whole = P("section", None, None)
    split = P("section", "dp", None)
    return jax.shard_map(
        local,
        mesh=mesh,
        in_specs=(whole, split, split, split, split, split),
        out_specs=(split, split, split, whole),
        check_vma=False,
    )
```

```python
import math

import jax
import jax.numpy as jnp
from jax import lax
from jax.experimental import pallas as pl
from jax.experimental.pallas import tpu as pltpu
from jax.sharding import PartitionSpec as P

MROWS = 256
STEP = 10
CHUNK = 32
PAD = 16
POWER = 8
TOP = 32768.0
PIECE = pl.CostEstimate(flops=2_000_000_000, bytes_accessed=1024, transcendentals=0)
CHEAP = pl.CostEstimate(flops=1024, bytes_accessed=1024, transcendentals=0)


def forward_pieces(x_rows, dy_rows, w_gate, w_up, w_down):
    pre_gate = jnp.dot(x_rows, w_gate, preferred_element_type=jnp.float32)
    pre_up = jnp.dot(x_rows, w_up, preferred_element_type=jnp.float32)
    d_hidden = jnp.dot(dy_rows, w_down, preferred_element_type=jnp.float32)
    return activation(pre_gate, pre_up, d_hidden)


def activation(pre_gate, pre_up, d_hidden):
    sigma = jax.nn.sigmoid(pre_gate)
    silu_val = pre_gate * sigma
    hidden = (silu_val * pre_up).astype(jnp.bfloat16)
    d_gate = (d_hidden * pre_up * sigma * (1.0 + pre_gate * (1.0 - sigma))).astype(jnp.bfloat16)
    d_up = (d_hidden * silu_val).astype(jnp.bfloat16)
    return d_gate, d_up, hidden


def block_grads(x_rows, dy_rows, w_gate, w_up, w_down):
    d_gate, d_up, hidden = forward_pieces(x_rows, dy_rows, w_gate, w_up, w_down)
    g_gate = jnp.dot(x_rows.T, d_gate, preferred_element_type=jnp.float32)
    g_up = jnp.dot(x_rows.T, d_up, preferred_element_type=jnp.float32)
    g_down = jnp.dot(dy_rows.T, hidden, preferred_element_type=jnp.float32)
    return jnp.concatenate([g_gate, g_up, g_down], axis=0)


def adam(clip, shard, old_param, first, second):
    clipped = clip * shard
    new_first = 0.9 * first + 0.1 * clipped
    new_second = 0.95 * second + 0.05 * clipped * clipped
    first_fix = 1.0 / (1.0 - 0.9**STEP)
    second_fix = 1.0 / (1.0 - 0.95**STEP)
    update = new_first * first_fix / (jnp.sqrt(new_second * second_fix) + 1e-08) + 0.1 * old_param
    return old_param - 0.01 * update, new_first, new_second


def clip_of(total, max_norm):
    return jnp.minimum(jnp.float32(1.0), max_norm / (jnp.sqrt(total) + 1e-06))


def plain(weights, inputs, out_grads, master, moment1, moment2):
    stacked = weights[0]
    width = stacked.shape[0] // 3
    local_grad = jnp.zeros(stacked.shape, jnp.float32)
    for start in range(0, inputs.shape[1], MROWS):
        x_rows = inputs[0, start : start + MROWS]
        dy_rows = out_grads[0, start : start + MROWS]
        local_grad = local_grad + block_grads(
            x_rows, dy_rows, stacked[:width], stacked[width : 2 * width], stacked[2 * width :]
        )
    shard = lax.psum_scatter(local_grad, "dp", scatter_dimension=0, tiled=True)
    total = lax.psum(jnp.sum(shard * shard), ("dp", "section"))
    max_norm = jnp.sqrt(jnp.float32(lax.axis_size("section") * stacked.size))
    new_param, new_first, new_second = adam(clip_of(total, max_norm), shard, master[0], moment1[0], moment2[0])
    gathered = lax.all_gather(new_param.astype(jnp.bfloat16), "dp", axis=0, tiled=True)
    return new_param[None], new_first[None], new_second[None], gathered[None]


def chunks(rows):
    return [slice(at, min(at + CHUNK, rows)) for at in range(0, rows, CHUNK)]


def fold(value):
    return jnp.max(jnp.abs(value).reshape(-1, 8, value.shape[1]), axis=0)


def scale_of(top):
    scale = jnp.max(top, axis=0, keepdims=True)
    return jnp.maximum(scale, 1e-30).astype(jnp.bfloat16).astype(jnp.float32)


def encode(value, factor):
    v = value * factor
    v2 = v * v
    v4 = v2 * v2
    v8 = v4 * v4
    return jnp.where(v < 0.0, -v8, v8).astype(jnp.bfloat16)


def decode(code, factor):
    code = code.astype(jnp.float32)
    size = jnp.abs(code)
    root = jnp.exp(jnp.log(jnp.maximum(size, 1e-37)) * (1.0 / POWER)) * factor
    root = jnp.where(size > 0.0, root, 0.0)
    return jnp.where(code < 0.0, -root, root)


def write_codes(total_ref, top, out_ref, first):
    scale = scale_of(top)
    factor = TOP / scale
    for part in chunks(total_ref.shape[0]):
        size = part.stop - part.start
        out_ref[pl.ds(first + part.start, size), :] = encode(total_ref[part, :], factor)
    return scale


def lookup(table, index):
    bits = max(max(table).bit_length(), 1)
    if bits * len(table) < 32:
        packed = sum(value << (bits * at) for at, value in enumerate(table))
        return jnp.bitwise_and(jnp.right_shift(jnp.int32(packed), index * bits), (1 << bits) - 1)
    out = jnp.int32(table[0])
    for at, value in enumerate(table[1:], 1):
        out = jnp.where(index == at, jnp.int32(value), out)
    return out


def forward_kernel(owner, rows, x_hbm, dy_hbm, w_hbm, factors_ref, out_ref, x_ref, dy_ref, w_ref, a_ref, b_ref, h_ref, total_ref, sems):
    width = x_hbm.shape[1]
    half = width // 2

    def fetch(at, source, target, index):
        copy = pltpu.make_async_copy(source.at[index], target.at[index], sems.at[at])
        copy.start()
        return copy

    copies = []
    for columns in (pl.ds(0, half), pl.ds(half, half)):
        copies.append(fetch(len(copies), x_hbm, x_ref, (slice(None), columns)))
        copies.append(fetch(len(copies), w_hbm, w_ref, columns))
        copies.append(fetch(len(copies), w_hbm, w_ref, pl.ds(columns.start + width, half)))
    for columns in (pl.ds(0, half), pl.ds(half, half)):
        copies.append(fetch(len(copies), dy_hbm, dy_ref, (slice(None), columns)))
        copies.append(fetch(len(copies), w_hbm, w_ref, pl.ds(columns.start + 2 * width, half)))

    def product(left, start, which):
        weight = w_ref[which * width + start : which * width + start + half]
        return jnp.dot(left[:, start : start + half], weight, preferred_element_type=jnp.float32)

    for copy in copies[:3]:
        copy.wait()
    a_ref[...] = product(x_ref, 0, 0)
    b_ref[...] = product(x_ref, 0, 1)
    for copy in copies[3:6]:
        copy.wait()
    a_ref[...] += product(x_ref, half, 0)
    b_ref[...] += product(x_ref, half, 1)
    for copy in copies[6:8]:
        copy.wait()
    h_ref[...] = product(dy_ref, 0, 2)
    for copy in copies[8:]:
        copy.wait()
    h_ref[...] += product(dy_ref, half, 2)
    for part in chunks(x_ref.shape[0]):
        d_gate, d_up, hidden = activation(a_ref[part, :], b_ref[part, :], h_ref[part, :])
        factors_ref[0, part, :] = d_gate
        factors_ref[1, part, :] = d_up
        factors_ref[2, part, :] = hidden
    steps = (out_ref.shape[0] - PAD) // rows
    scales = jnp.zeros((PAD, out_ref.shape[1]), jnp.float32)
    for step in range(steps):
        at = owner() * steps + step
        kind = lax.div(at, width // rows)
        column = pl.ds(pl.multiple_of(lax.rem(at, width // rows) * rows, rows), rows)
        left = jnp.where(kind == 2, dy_ref[:, column], x_ref[:, column])
        total_ref[...] = lax.dot_general(
            left, factors_ref[kind], (((0,), (0,)), ((), ())), preferred_element_type=jnp.float32
        )
        top = fold(total_ref[:CHUNK, :])
        for part in chunks(rows)[1:]:
            top = jnp.maximum(top, fold(total_ref[part, :]))
        scale = write_codes(total_ref, top, out_ref, step * rows)
        row = lax.broadcasted_iota(jnp.int32, scales.shape, 0)
        scales = jnp.where(row == step, scale, scales)
    out_ref[steps * rows :, :] = scales.astype(jnp.bfloat16)


def forward(x, dy, stacked, table, rows):
    tokens, width = x.shape
    hidden = stacked.shape[1]
    shard = stacked.shape[0] // len(table)

    def owner():
        return lookup(table, lax.axis_index("dp"))

    return pl.pallas_call(
        lambda *refs: forward_kernel(owner, rows, *refs),
        in_specs=[pl.BlockSpec(memory_space=pltpu.HBM)] * 3,
        out_shape=[
            jax.ShapeDtypeStruct((3, tokens, hidden), jnp.bfloat16),
            jax.ShapeDtypeStruct((shard + PAD, hidden), jnp.bfloat16),
        ],
        scratch_shapes=[
            pltpu.VMEM(x.shape, x.dtype),
            pltpu.VMEM(dy.shape, dy.dtype),
            pltpu.VMEM(stacked.shape, stacked.dtype),
            *[pltpu.VMEM((tokens, hidden), jnp.float32)] * 3,
            pltpu.VMEM((rows, hidden), jnp.float32),
            pltpu.SemaphoreType.DMA((10,)),
        ],
        compiler_params=pltpu.CompilerParams(vmem_limit_bytes=60 << 20),
        cost_estimate=CHEAP,
        name="forward",
    )(x, dy, stacked)


def pick(values, step):
    if all(value == values[0] + at for at, value in enumerate(values)):
        return step + values[0] if len(values) > 1 else jnp.int32(values[0])
    out = jnp.int32(values[0])
    for at, value in enumerate(values[1:], 1):
        out = jnp.where(step == at, value, out)
    return out


def piece_kernel(place, per, got, extra, last, *refs):
    step = pl.program_id(0)
    x_ref, dy_ref, d_ref = refs[:3]
    before = refs[3 + 2 * len(got) : 3 + 2 * len(got) + extra]
    outs = refs[3 + 2 * len(got) + extra :]
    rows = x_ref.shape[1]
    left = jnp.where(lax.div(place(step), per) == 2, dy_ref[...], x_ref[...])
    total_ref = outs[-1]
    total_ref[...] = lax.dot_general(left, d_ref[0], (((0,), (0,)), ((), ())), preferred_element_type=jnp.float32)
    factors = []
    for at, blocks in enumerate(got):
        scales = refs[4 + 2 * at][...].astype(jnp.float32)
        row = lax.broadcasted_iota(jnp.int32, scales.shape, 0)
        here = pick([PAD if block is None else block for block in blocks], step)
        factors.append(jnp.sum(jnp.where(row == here, scales, 0.0), axis=0, keepdims=True) * (1.0 / TOP))
    top = jnp.zeros((8, total_ref.shape[1]), jnp.float32)
    for part in chunks(rows):
        total = total_ref[part, :]
        for at, factor in enumerate(factors):
            total = total + decode(refs[3 + 2 * at][part, :], factor)
        if last:
            outs[0][part, :] = total
            top = top + jnp.sum((total * total).reshape(-1, 8, total.shape[1]), axis=0)
        else:
            if factors:
                total_ref[part, :] = total
            top = jnp.maximum(top, fold(total))
    if last:
        squares = outs[1]
        tile = sum(top[:, at : at + 128] for at in range(0, top.shape[1], 128))
        tile = tile + jnp.where(step == 0, before[1][...] if extra else 0.0, squares[:8])
        for at in range(0, squares.shape[0], 8):
            squares[at : at + 8] = tile
    else:
        out_ref, scales_ref = outs[:2]
        scale = write_codes(total_ref, top, out_ref, pl.multiple_of(step * rows, rows))
        row = lax.broadcasted_iota(jnp.int32, scales_ref.shape, 0)
        scales_ref[...] = jnp.where(row == step, scale, jnp.where(step == 0, 0.0, scales_ref[...]))
        out_ref[pl.ds(out_ref.shape[0] - PAD, PAD), :] = scales_ref[...].astype(jnp.bfloat16)


def piece(x, dy, factors, rows, blocks, got=(), after=None, last=0, before=None):
    tokens, width = x.shape
    hidden = factors.shape[2]
    per = width // rows
    shard = 3 * width // len(blocks[0][0])
    steps = shard // rows
    tables = [table for table, _ in blocks]
    within = [block for _, block in blocks]

    def place(i):
        r = lax.axis_index("dp")
        owner = lookup(tables[0], r)
        for at, table in enumerate(tables[1:], 1):
            if table != tables[at - 1]:
                owner = jnp.where(i >= at, lookup(table, r), owner)
        return owner * steps + pick(within, i)

    def column(i):
        return (0, lax.rem(place(i), per))

    in_specs = [
        pl.BlockSpec((tokens, rows), column),
        pl.BlockSpec((tokens, rows), column),
        pl.BlockSpec((1, tokens, hidden), lambda i: (lax.div(place(i), per), 0, 0)),
    ]
    operands = [x, dy, factors]
    for message, parts in got:
        present = [part for part in parts if part is not None]
        nearest = [present[0] if part is None else part for part in parts]
        scales = (message.shape[0] - PAD) // PAD
        in_specs += [
            pl.BlockSpec((rows, hidden), lambda i, nearest=nearest: (pick(nearest, i), 0)),
            pl.BlockSpec((PAD, hidden), lambda i, scales=scales: (scales, 0)),
        ]
        operands += [message, message]
    aliases = {}
    extra = 0
    if before is not None:
        extra = 2
        aliases = {len(operands): 0}
        operands += before
        in_specs += [pl.BlockSpec(memory_space=pl.ANY), pl.BlockSpec((8, 128), lambda i: (0, 0))]
    elif after is not None:
        extra = 1
        operands.append(after)
        in_specs.append(pl.BlockSpec(memory_space=pl.ANY))
    if last:
        out_specs = [
            pl.BlockSpec((rows, hidden), lambda i: (pick(within, i), 0)),
            pl.BlockSpec((8 * last, 128), lambda i: (0, 0)),
        ]
        out_shape = [
            jax.ShapeDtypeStruct((shard, hidden), jnp.float32),
            jax.ShapeDtypeStruct((8 * last, 128), jnp.float32),
        ]
        scratch = [pltpu.VMEM((rows, hidden), jnp.float32)]
    else:
        out_specs = pl.BlockSpec((len(blocks) * rows + PAD, hidden), lambda i: (0, 0))
        out_shape = jax.ShapeDtypeStruct((len(blocks) * rows + PAD, hidden), jnp.bfloat16)
        scratch = [pltpu.VMEM((PAD, hidden), jnp.float32), pltpu.VMEM((rows, hidden), jnp.float32)]
    return pl.pallas_call(
        lambda *refs: piece_kernel(place, per, [parts for _, parts in got], extra, last, *refs),
        grid=(len(blocks),),
        in_specs=in_specs,
        out_specs=out_specs,
        out_shape=out_shape,
        scratch_shapes=scratch,
        input_output_aliases=aliases,
        compiler_params=pltpu.CompilerParams(vmem_limit_bytes=32 << 20),
        cost_estimate=PIECE,
        name="piece",
    )(*operands)


def update_kernel(max_norm, states, total_ref, g_ref, p_ref, m1_ref, m2_ref, *outs):
    clip = clip_of(jnp.sum(total_ref[...], keepdims=True), max_norm)
    for part in chunks(g_ref.shape[0]):
        param, first, second = adam(clip, g_ref[part, :], p_ref[part, :], m1_ref[part, :], m2_ref[part, :])
        values = (param, first, second) if states else (param.astype(jnp.bfloat16),)
        for out, value in zip(outs, values):
            out[part, :] = value


def update(total, shard, param, first, second, max_norm, rows, states):
    block = pl.BlockSpec((rows, shard.shape[1]), lambda i: (i, 0))
    dtypes = [jnp.float32] * 3 if states else [jnp.bfloat16]
    return pl.pallas_call(
        lambda *refs: update_kernel(max_norm, states, *refs),
        grid=(shard.shape[0] // rows,),
        in_specs=[pl.BlockSpec(total.shape, lambda i: (0, 0))] + [block] * 4,
        out_specs=[block] * len(dtypes),
        out_shape=[jax.ShapeDtypeStruct(shard.shape, dtype) for dtype in dtypes],
        compiler_params=pltpu.CompilerParams(vmem_limit_bytes=32 << 20),
        cost_estimate=CHEAP,
        name="states" if states else "update",
    )(total, shard, param, first, second)


def tie(value, other):
    rows = min(PAD, value.shape[0], other.shape[0])
    columns = min(value.shape[1], other.shape[1])
    top = value[:rows, :columns]
    that = other[:rows, :columns].astype(value.dtype)
    return lax.dynamic_update_slice(value, jnp.where(that > jnp.inf, that, top), (0, 0))


def behind_of(value, other):
    return pl.pallas_call(
        lambda *refs: None,
        grid=(1,),
        in_specs=[pl.BlockSpec(memory_space=pl.ANY), pl.BlockSpec((PAD, 128), lambda i: (0, 0))],
        out_specs=pl.BlockSpec(memory_space=pl.ANY),
        out_shape=jax.ShapeDtypeStruct(value.shape, value.dtype),
        input_output_aliases={0: 0},
        cost_estimate=CHEAP,
        name="behind",
    )(value, other)


def paired(weights, inputs, out_grads, master, moment1, moment2):
    n = lax.axis_size("dp")
    pairs = n // 2
    ring = list(range(0, pairs, 2)) + list(range(pairs - 1 - pairs % 2, 0, -2))
    place = {pair: at for at, pair in enumerate(ring)}

    def at_offset(r, offset, flip):
        return 2 * ring[(place[r // 2] + offset) % pairs] + ((r % 2) ^ flip)

    def table(offset, flip):
        return [at_offset(r, offset, flip) for r in range(n)]

    def send(value, offset, flip=0):
        return lax.ppermute(value, "dp", [(r, at_offset(r, offset, flip)) for r in range(n)])

    stacked = weights[0]
    x, dy = inputs[0], out_grads[0]
    width = x.shape[1]
    shard_rows = stacked.shape[0] // n
    rows = math.gcd(shard_rows, width, 256)

    steps = shard_rows // rows

    most, end = range(steps - 1), steps - 1

    def made(blocks, got=(), **more):
        return piece(x, dy, factors, rows, [(table(offset, flip), block) for offset, flip, block in blocks], got, **more)

    factors, message = forward(x, dy, stacked, table(2, 1), rows)
    cross_far = send(message, 0, 1)
    message = made([(-1, 0, end), (-1, 1, end)])
    ahead = send(message, -1)
    message = made([(-1, 1, block) for block in most] + [(1, 1, 0)], after=message)
    cross_a = send(message, 0, 1)
    message = made([(1, 1, block) for block in range(1, steps)] + [(0, 1, 0)], after=message)
    cross_b = send(message, 0, 1)
    message = made(
        [(0, 1, block) for block in range(1, steps)], [(ahead, [None] * (steps - 2) + [1])], after=message
    )
    cross_c = send(message, 0, 1)

    by_ring = send(made([(2, 0, block) for block in range(steps)], [(cross_far, list(range(steps)))]), 1)
    from_ahead = send(made([(-1, 0, block) for block in most], [(cross_a, list(most))]), -1)
    first = send(made([(1, 0, 0)], [(cross_a, [end]), (by_ring, [0])]), 1)
    rest = list(range(1, steps))
    others = send(made([(1, 0, block) for block in rest], [(cross_b, list(most)), (by_ring, rest)]), 1)
    done = made([(0, 0, 0)], [(cross_b, [end]), (from_ahead, [0]), (first, [0])], last=1)
    got = [
        (cross_c, list(most)),
        (from_ahead, rest[:-1] + [None]),
        (ahead, [None] * (steps - 2) + [0]),
        (others, list(most)),
    ]
    devices = n * lax.axis_size("section")
    done = made([(0, 0, block) for block in rest], got, last=devices, before=done)
    shard, squares = done

    total = lax.all_to_all(squares, ("dp", "section"), 0, 0, tiled=True)
    max_norm = math.sqrt(lax.axis_size("section") * stacked.size)
    states = (shard, master[0], moment1[0], moment2[0], max_norm, rows)
    (own,) = update(total, *states, False)

    r = lax.axis_index("dp")
    cut = shard_rows - rows

    def start(offset, flip):
        return lookup(table(offset, flip), r) * shard_rows

    def put(gathered, value, offset, flip, low=0):
        return lax.dynamic_update_slice(gathered, value, (start(offset, flip) + low, 0))

    def take(gathered, offset, flip, low, high):
        return lax.dynamic_slice(gathered, (start(offset, flip) + low, 0), (high - low, stacked.shape[1]))

    other = send(own, 0, 1)
    behind = behind_of(send(own, 1), other)
    tail = send(own[cut:], -1)
    behind_cross = send(behind, 0, 1)
    far = send(behind, 1)
    gathered = put(jnp.zeros_like(stacked), own, 0, 0)
    gathered = put(gathered, behind, -1, 0)
    gathered = put(gathered, other, 0, 1)
    gathered = put(gathered, tail, 1, 0, cut)
    tail_cross = send(take(gathered, 1, 0, cut, shard_rows), 0, 1)
    both = send(jnp.concatenate([take(gathered, 0, 0, 0, cut), take(gathered, 0, 1, 0, cut)]), -1)
    far_cross = send(far, 0, 1)
    new_param, new_first, new_second = update(tie(total, other), *states, True)
    gathered = put(gathered, behind_cross, -1, 1)
    gathered = put(gathered, tail_cross, 1, 1, cut)
    gathered = put(gathered, far, -2, 0)
    gathered = put(gathered, both[:cut], 1, 0)
    gathered = put(gathered, both[cut:], 1, 1)
    gathered = put(gathered, far_cross, -2, 1)
    return new_param[None], new_first[None], new_second[None], gathered[None]


def local(weights, *rest):
    n = lax.axis_size("dp")
    height = weights.shape[1]
    shard, width = height // n, height // 3
    fits = n == 8 and height % n == 0 and math.gcd(shard, width, 256) % 128 == 0 and shard // math.gcd(shard, width, 256) > 2
    return (paired if fits else plain)(weights, *rest)


def solution(mesh):
    whole = P("section", None, None)
    split = P("section", "dp", None)
    return jax.shard_map(
        local,
        mesh=mesh,
        in_specs=(whole, split, split, split, split, split),
        out_specs=(split, split, split, whole),
        check_vma=False,
    )
```

```python
import math

import jax
import jax.numpy as jnp
from jax import lax
from jax.experimental import pallas as pl
from jax.experimental.pallas import tpu as pltpu
from jax.sharding import PartitionSpec as P

MROWS = 256
STEP = 10
LITTLE = 16 << 20
CHUNK = 32
PAD = 16
POWER = 8
TOP = 32768.0
PIECE = pl.CostEstimate(flops=2_000_000_000, bytes_accessed=1024, transcendentals=0)
CHEAP = pl.CostEstimate(flops=1024, bytes_accessed=1024, transcendentals=0)


def forward_pieces(x_rows, dy_rows, w_gate, w_up, w_down):
    pre_gate = jnp.dot(x_rows, w_gate, preferred_element_type=jnp.float32)
    pre_up = jnp.dot(x_rows, w_up, preferred_element_type=jnp.float32)
    d_hidden = jnp.dot(dy_rows, w_down, preferred_element_type=jnp.float32)
    return activation(pre_gate, pre_up, d_hidden)


def activation(pre_gate, pre_up, d_hidden):
    sigma = jax.nn.sigmoid(pre_gate)
    silu_val = pre_gate * sigma
    hidden = (silu_val * pre_up).astype(jnp.bfloat16)
    d_gate = (d_hidden * pre_up * sigma * (1.0 + pre_gate * (1.0 - sigma))).astype(jnp.bfloat16)
    d_up = (d_hidden * silu_val).astype(jnp.bfloat16)
    return d_gate, d_up, hidden


def block_grads(x_rows, dy_rows, w_gate, w_up, w_down):
    d_gate, d_up, hidden = forward_pieces(x_rows, dy_rows, w_gate, w_up, w_down)
    g_gate = jnp.dot(x_rows.T, d_gate, preferred_element_type=jnp.float32)
    g_up = jnp.dot(x_rows.T, d_up, preferred_element_type=jnp.float32)
    g_down = jnp.dot(dy_rows.T, hidden, preferred_element_type=jnp.float32)
    return jnp.concatenate([g_gate, g_up, g_down], axis=0)


def adam(clip, shard, old_param, first, second):
    clipped = clip * shard
    new_first = 0.9 * first + 0.1 * clipped
    new_second = 0.95 * second + 0.05 * clipped * clipped
    first_fix = 1.0 / (1.0 - 0.9**STEP)
    second_fix = 1.0 / (1.0 - 0.95**STEP)
    update = new_first * first_fix / (jnp.sqrt(new_second * second_fix) + 1e-08) + 0.1 * old_param
    return old_param - 0.01 * update, new_first, new_second


def clip_of(total, max_norm):
    return jnp.minimum(jnp.float32(1.0), max_norm / (jnp.sqrt(total) + 1e-06))


def plain(weights, inputs, out_grads, master, moment1, moment2):
    stacked = weights[0]
    width = stacked.shape[0] // 3
    local_grad = jnp.zeros(stacked.shape, jnp.float32)
    for start in range(0, inputs.shape[1], MROWS):
        x_rows = inputs[0, start : start + MROWS]
        dy_rows = out_grads[0, start : start + MROWS]
        local_grad = local_grad + block_grads(
            x_rows, dy_rows, stacked[:width], stacked[width : 2 * width], stacked[2 * width :]
        )
    shard = lax.psum_scatter(local_grad, "dp", scatter_dimension=0, tiled=True)
    total = lax.psum(jnp.sum(shard * shard), ("dp", "section"))
    max_norm = jnp.sqrt(jnp.float32(lax.axis_size("section") * stacked.size))
    new_param, new_first, new_second = adam(clip_of(total, max_norm), shard, master[0], moment1[0], moment2[0])
    gathered = lax.all_gather(new_param.astype(jnp.bfloat16), "dp", axis=0, tiled=True)
    return new_param[None], new_first[None], new_second[None], gathered[None]


def chunks(rows):
    return [slice(at, min(at + CHUNK, rows)) for at in range(0, rows, CHUNK)]


def fold(value):
    return jnp.max(jnp.abs(value).reshape(-1, 8, value.shape[1]), axis=0)


def scale_of(top):
    scale = jnp.max(top, axis=0, keepdims=True)
    return jnp.maximum(scale, 1e-30).astype(jnp.bfloat16).astype(jnp.float32)


def encode(value, factor):
    v = value * factor
    v2 = v * v
    v4 = v2 * v2
    v8 = v4 * v4
    return jnp.where(v < 0.0, -v8, v8).astype(jnp.bfloat16)


def decode(code, factor):
    code = code.astype(jnp.float32)
    size = jnp.abs(code)
    root = jnp.exp(jnp.log(jnp.maximum(size, 1e-37)) * (1.0 / POWER)) * factor
    root = jnp.where(size > 0.0, root, 0.0)
    return jnp.where(code < 0.0, -root, root)


def write_codes(total_ref, top, out_ref, first):
    scale = scale_of(top)
    factor = TOP / scale
    for part in chunks(total_ref.shape[0]):
        size = part.stop - part.start
        out_ref[pl.ds(first + part.start, size), :] = encode(total_ref[part, :], factor)
    return scale


def lookup(table, index):
    bits = max(max(table).bit_length(), 1)
    if bits * len(table) < 32:
        packed = sum(value << (bits * at) for at, value in enumerate(table))
        return jnp.bitwise_and(jnp.right_shift(jnp.int32(packed), index * bits), (1 << bits) - 1)
    out = jnp.int32(table[0])
    for at, value in enumerate(table[1:], 1):
        out = jnp.where(index == at, jnp.int32(value), out)
    return out


def forward_kernel(messages, rows, x_hbm, dy_hbm, w_hbm, factors_ref, *refs):
    outs = refs[: len(messages)]
    x_ref, dy_ref, w_ref, a_ref, b_ref, h_ref, total_ref, sems = refs[len(messages) :]
    width = x_hbm.shape[1]
    half = width // 2

    def fetch(at, source, target, index):
        copy = pltpu.make_async_copy(source.at[index], target.at[index], sems.at[at])
        copy.start()
        return copy

    copies = []
    for columns in (pl.ds(0, half), pl.ds(half, half)):
        copies.append(fetch(len(copies), x_hbm, x_ref, (slice(None), columns)))
        copies.append(fetch(len(copies), w_hbm, w_ref, columns))
        copies.append(fetch(len(copies), w_hbm, w_ref, pl.ds(columns.start + width, half)))
    for columns in (pl.ds(0, half), pl.ds(half, half)):
        copies.append(fetch(len(copies), dy_hbm, dy_ref, (slice(None), columns)))
        copies.append(fetch(len(copies), w_hbm, w_ref, pl.ds(columns.start + 2 * width, half)))

    def product(left, start, which):
        weight = w_ref[which * width + start : which * width + start + half]
        return jnp.dot(left[:, start : start + half], weight, preferred_element_type=jnp.float32)

    for copy in copies[:3]:
        copy.wait()
    a_ref[...] = product(x_ref, 0, 0)
    b_ref[...] = product(x_ref, 0, 1)
    for copy in copies[3:6]:
        copy.wait()
    a_ref[...] += product(x_ref, half, 0)
    b_ref[...] += product(x_ref, half, 1)
    for copy in copies[6:8]:
        copy.wait()
    h_ref[...] = product(dy_ref, 0, 2)
    for copy in copies[8:]:
        copy.wait()
    h_ref[...] += product(dy_ref, half, 2)
    for part in chunks(x_ref.shape[0]):
        d_gate, d_up, hidden = activation(a_ref[part, :], b_ref[part, :], h_ref[part, :])
        factors_ref[0, part, :] = d_gate
        factors_ref[1, part, :] = d_up
        factors_ref[2, part, :] = hidden
    per = width // rows
    for places, out_ref in zip(messages, outs):
        scales = jnp.zeros((PAD, out_ref.shape[1]), jnp.float32)
        for step, place in enumerate(places):
            at = place()
            kind = lax.div(at, per)
            column = pl.ds(pl.multiple_of(lax.rem(at, per) * rows, rows), rows)
            left = jnp.where(kind == 2, dy_ref[:, column], x_ref[:, column])
            total_ref[...] = lax.dot_general(
                left, factors_ref[kind], (((0,), (0,)), ((), ())), preferred_element_type=jnp.float32
            )
            top = fold(total_ref[:CHUNK, :])
            for part in chunks(rows)[1:]:
                top = jnp.maximum(top, fold(total_ref[part, :]))
            scale = write_codes(total_ref, top, out_ref, step * rows)
            row = lax.broadcasted_iota(jnp.int32, scales.shape, 0)
            scales = jnp.where(row == step, scale, scales)
        out_ref[len(places) * rows :, :] = scales.astype(jnp.bfloat16)


def forward(x, dy, stacked, messages, rows):
    tokens, width = x.shape
    hidden = stacked.shape[1]

    def place_of(table, block):
        steps = stacked.shape[0] // len(table) // rows
        return lambda: lookup(table, lax.axis_index("dp")) * steps + block

    places = [[place_of(*block) for block in blocks] for blocks in messages]
    return pl.pallas_call(
        lambda *refs: forward_kernel(places, rows, *refs),
        in_specs=[pl.BlockSpec(memory_space=pltpu.HBM)] * 3,
        out_shape=[jax.ShapeDtypeStruct((3, tokens, hidden), jnp.bfloat16)]
        + [jax.ShapeDtypeStruct((len(blocks) * rows + PAD, hidden), jnp.bfloat16) for blocks in messages],
        scratch_shapes=[
            pltpu.VMEM(x.shape, x.dtype),
            pltpu.VMEM(dy.shape, dy.dtype),
            pltpu.VMEM(stacked.shape, stacked.dtype),
            *[pltpu.VMEM((tokens, hidden), jnp.float32)] * 3,
            pltpu.VMEM((rows, hidden), jnp.float32),
            pltpu.SemaphoreType.DMA((10,)),
        ],
        compiler_params=pltpu.CompilerParams(vmem_limit_bytes=60 << 20),
        cost_estimate=CHEAP,
        name="forward",
    )(x, dy, stacked)


def pick(values, step):
    if all(value == values[0] + at for at, value in enumerate(values)):
        return step + values[0] if len(values) > 1 else jnp.int32(values[0])
    out = jnp.int32(values[0])
    for at, value in enumerate(values[1:], 1):
        out = jnp.where(step == at, value, out)
    return out


def piece_kernel(place, per, got, extra, last, *refs):
    step = pl.program_id(0)
    x_ref, dy_ref, d_ref = refs[:3]
    outs = refs[3 + 2 * len(got) + extra :]
    rows = x_ref.shape[1]
    left = jnp.where(lax.div(place(step), per) == 2, dy_ref[...], x_ref[...])
    total_ref = outs[-1]
    total_ref[...] = lax.dot_general(left, d_ref[0], (((0,), (0,)), ((), ())), preferred_element_type=jnp.float32)
    factors = []
    for at, blocks in enumerate(got):
        scales = refs[4 + 2 * at][...].astype(jnp.float32)
        row = lax.broadcasted_iota(jnp.int32, scales.shape, 0)
        here = pick([PAD if block is None else block for block in blocks], step)
        factors.append(jnp.sum(jnp.where(row == here, scales, 0.0), axis=0, keepdims=True) * (1.0 / TOP))
    top = jnp.zeros((8, total_ref.shape[1]), jnp.float32)
    for part in chunks(rows):
        total = total_ref[part, :]
        for at, factor in enumerate(factors):
            total = total + decode(refs[3 + 2 * at][part, :], factor)
        if last:
            outs[0][part, :] = total
        else:
            if factors:
                total_ref[part, :] = total
            top = jnp.maximum(top, fold(total))
    if not last:
        out_ref, scales_ref = outs[:2]
        scale = write_codes(total_ref, top, out_ref, pl.multiple_of(step * rows, rows))
        row = lax.broadcasted_iota(jnp.int32, scales_ref.shape, 0)
        scales_ref[...] = jnp.where(row == step, scale, jnp.where(step == 0, 0.0, scales_ref[...]))
        out_ref[pl.ds(out_ref.shape[0] - PAD, PAD), :] = scales_ref[...].astype(jnp.bfloat16)


def piece(x, dy, factors, rows, blocks, got=(), after=None, last=False):
    tokens, width = x.shape
    hidden = factors.shape[2]
    per = width // rows
    shard = 3 * width // len(blocks[0][0])
    steps = shard // rows
    tables = [table for table, _ in blocks]
    within = [block for _, block in blocks]

    def place(i):
        r = lax.axis_index("dp")
        owner = lookup(tables[0], r)
        for at, table in enumerate(tables[1:], 1):
            if table != tables[at - 1]:
                owner = jnp.where(i >= at, lookup(table, r), owner)
        return owner * steps + pick(within, i)

    def column(i):
        return (0, lax.rem(place(i), per))

    in_specs = [
        pl.BlockSpec((tokens, rows), column),
        pl.BlockSpec((tokens, rows), column),
        pl.BlockSpec((1, tokens, hidden), lambda i: (lax.div(place(i), per), 0, 0)),
    ]
    operands = [x, dy, factors]
    for message, parts in got:
        present = [part for part in parts if part is not None]
        nearest = [present[0] if part is None else part for part in parts]
        scales = (message.shape[0] - PAD) // PAD
        in_specs += [
            pl.BlockSpec((rows, hidden), lambda i, nearest=nearest: (pick(nearest, i), 0)),
            pl.BlockSpec((PAD, hidden), lambda i, scales=scales: (scales, 0)),
        ]
        operands += [message, message]
    extra = 0
    if after is not None:
        extra = 1
        operands.append(after)
        in_specs.append(pl.BlockSpec(memory_space=pl.ANY))
    if last:
        out_specs = pl.BlockSpec((rows, hidden), lambda i: (i, 0))
        out_shape = jax.ShapeDtypeStruct((len(blocks) * rows, hidden), jnp.float32)
        scratch = [pltpu.VMEM((rows, hidden), jnp.float32)]
    else:
        out_specs = pl.BlockSpec((len(blocks) * rows + PAD, hidden), lambda i: (0, 0))
        out_shape = jax.ShapeDtypeStruct((len(blocks) * rows + PAD, hidden), jnp.bfloat16)
        scratch = [pltpu.VMEM((PAD, hidden), jnp.float32), pltpu.VMEM((rows, hidden), jnp.float32)]
    return pl.pallas_call(
        lambda *refs: piece_kernel(place, per, [parts for _, parts in got], extra, last, *refs),
        grid=(len(blocks),),
        in_specs=in_specs,
        out_specs=out_specs,
        out_shape=out_shape,
        scratch_shapes=scratch,
        compiler_params=pltpu.CompilerParams(vmem_limit_bytes=LITTLE),
        cost_estimate=PIECE,
        name="piece",
    )(*operands)


def finish_kernel(count, sum_ref, code_ref, scales_ref, out_ref, squares_ref):
    step = pl.program_id(0)
    scales = scales_ref[...].astype(jnp.float32)
    row = lax.broadcasted_iota(jnp.int32, scales.shape, 0)
    factor = jnp.sum(jnp.where(row == step, scales, 0.0), axis=0, keepdims=True) * (1.0 / TOP)
    top = jnp.zeros((8, out_ref.shape[1]), jnp.float32)
    for part in chunks(out_ref.shape[0]):
        total = sum_ref[part, :] + decode(code_ref[part, :], factor)
        out_ref[part, :] = total
        top = top + jnp.sum((total * total).reshape(-1, 8, total.shape[1]), axis=0)
    tile = sum(top[:, at : at + 128] for at in range(0, top.shape[1], 128))
    tile = tile + jnp.where(step == 0, 0.0, squares_ref[:8])
    for at in range(0, squares_ref.shape[0], 8):
        squares_ref[at : at + 8] = tile


def finish(partial, message, rows, count):
    height, hidden = partial.shape
    block = pl.BlockSpec((rows, hidden), lambda i: (i, 0))
    return pl.pallas_call(
        lambda *refs: finish_kernel(count, *refs),
        grid=(height // rows,),
        in_specs=[block, block, pl.BlockSpec((PAD, hidden), lambda i: (height // PAD, 0))],
        out_specs=[block, pl.BlockSpec((8 * count, 128), lambda i: (0, 0))],
        out_shape=[
            jax.ShapeDtypeStruct(partial.shape, jnp.float32),
            jax.ShapeDtypeStruct((8 * count, 128), jnp.float32),
        ],
        compiler_params=pltpu.CompilerParams(vmem_limit_bytes=LITTLE),
        cost_estimate=PIECE,
        name="finish",
    )(partial, message, message)


def update_kernel(max_norm, states, total_ref, g_ref, p_ref, m1_ref, m2_ref, *outs):
    clip = clip_of(jnp.sum(total_ref[...], keepdims=True), max_norm)
    for part in chunks(g_ref.shape[0]):
        param, first, second = adam(clip, g_ref[part, :], p_ref[part, :], m1_ref[part, :], m2_ref[part, :])
        values = (param, first, second) if states else (param.astype(jnp.bfloat16),)
        for out, value in zip(outs, values):
            out[part, :] = value


def update(total, shard, param, first, second, max_norm, rows, states):
    block = pl.BlockSpec((rows, shard.shape[1]), lambda i: (i, 0))
    dtypes = [jnp.float32] * 3 if states else [jnp.bfloat16]
    return pl.pallas_call(
        lambda *refs: update_kernel(max_norm, states, *refs),
        grid=(shard.shape[0] // rows,),
        in_specs=[pl.BlockSpec(total.shape, lambda i: (0, 0))] + [block] * 4,
        out_specs=[block] * len(dtypes),
        out_shape=[jax.ShapeDtypeStruct(shard.shape, dtype) for dtype in dtypes],
        compiler_params=pltpu.CompilerParams(vmem_limit_bytes=LITTLE),
        cost_estimate=CHEAP,
        name="states" if states else "update",
    )(total, shard, param, first, second)


def behind_of(value, other):
    return pl.pallas_call(
        lambda *refs: None,
        grid=(1,),
        in_specs=[pl.BlockSpec(memory_space=pl.ANY), pl.BlockSpec((PAD, 128), lambda i: (0, 0))],
        out_specs=pl.BlockSpec(memory_space=pl.ANY),
        out_shape=jax.ShapeDtypeStruct(value.shape, value.dtype),
        input_output_aliases={0: 0},
        compiler_params=pltpu.CompilerParams(vmem_limit_bytes=LITTLE),
        cost_estimate=CHEAP,
        name="behind",
    )(value, other)


def both_of(own, other, tail, after, rows, cut):
    columns = own.shape[1]
    steps = cut // rows

    def kernel(own_ref, other_ref, tail_ref, after_ref, both_ref, tail_out):
        step = pl.program_id(0)

        @pl.when(step < steps)
        def _():
            both_ref[...] = own_ref[...]

        @pl.when(step >= steps)
        def _():
            both_ref[...] = other_ref[...]

        tail_out[...] = tail_ref[...]

    return pl.pallas_call(
        kernel,
        grid=(2 * steps,),
        in_specs=[
            pl.BlockSpec((rows, columns), lambda i: (jnp.minimum(i, steps - 1), 0)),
            pl.BlockSpec((rows, columns), lambda i: (jnp.maximum(i - steps, 0), 0)),
            pl.BlockSpec(tail.shape, lambda i: (0, 0)),
            pl.BlockSpec((PAD, 128), lambda i: (0, 0)),
        ],
        out_specs=[
            pl.BlockSpec((rows, columns), lambda i: (i, 0)),
            pl.BlockSpec(tail.shape, lambda i: (0, 0)),
        ],
        out_shape=[
            jax.ShapeDtypeStruct((2 * cut, columns), own.dtype),
            jax.ShapeDtypeStruct(tail.shape, own.dtype),
        ],
        compiler_params=pltpu.CompilerParams(vmem_limit_bytes=LITTLE),
        cost_estimate=PIECE,
        name="both",
    )(own, other, tail, after)


def fill_kernel(moves, count, *refs):
    out, sems = refs[-2:]
    r = lax.axis_index("dp")
    copies = []
    for at, (source, low, size, table, shard, first) in enumerate(moves):
        to = pl.multiple_of(lookup(table, r) * shard + first, PAD)
        copies.append(pltpu.make_async_copy(refs[source].at[low : low + size], out.at[pl.ds(to, size)], sems.at[at]))
        copies[-1].start()
    for copy in copies:
        copy.wait()


def fill(buffer, values, moves, height):
    columns = values[0].shape[1]
    return pl.pallas_call(
        lambda *refs: fill_kernel(moves, len(values), *refs),
        in_specs=[pl.BlockSpec(memory_space=pltpu.VMEM)] * len(values)
        + [pl.BlockSpec(memory_space=pltpu.HBM)] * (buffer is not None),
        out_specs=pl.BlockSpec(memory_space=pltpu.HBM),
        out_shape=jax.ShapeDtypeStruct((height, columns), values[0].dtype),
        input_output_aliases={} if buffer is None else {len(values): 0},
        scratch_shapes=[pltpu.SemaphoreType.DMA((len(moves),))],
        compiler_params=pltpu.CompilerParams(vmem_limit_bytes=LITTLE),
        cost_estimate=CHEAP,
        name="fill",
    )(*values, *([] if buffer is None else [buffer]))


def paired(weights, inputs, out_grads, master, moment1, moment2):
    n = lax.axis_size("dp")
    pairs = n // 2
    ring = list(range(0, pairs, 2)) + list(range(pairs - 1 - pairs % 2, 0, -2))
    place = {pair: at for at, pair in enumerate(ring)}

    def at_offset(r, offset, flip):
        return 2 * ring[(place[r // 2] + offset) % pairs] + ((r % 2) ^ flip)

    def table(offset, flip):
        return [at_offset(r, offset, flip) for r in range(n)]

    def send(value, offset, flip=0):
        return lax.ppermute(value, "dp", [(r, at_offset(r, offset, flip)) for r in range(n)])

    stacked = weights[0]
    x, dy = inputs[0], out_grads[0]
    width = x.shape[1]
    shard_rows = stacked.shape[0] // n
    rows = math.gcd(shard_rows, width, 256)

    steps = shard_rows // rows

    every, most, rest, end = list(range(steps)), list(range(steps - 1)), list(range(1, steps)), steps - 1

    def at(*blocks):
        return [(table(offset, flip), block) for offset, flip, block in blocks]

    def made(blocks, got=(), **more):
        return piece(x, dy, factors, rows, blocks, got, **more)

    factors, message, ring_message = forward(
        x, dy, stacked, [at(*[(2, 1, b) for b in every]), at((-1, 0, end), (-1, 1, end))], rows
    )
    cross_far = send(message, 0, 1)
    ahead = send(ring_message, -1)
    message = made(at(*[(-1, 1, b) for b in most], (1, 1, 0)))
    cross_a = send(message, 0, 1)
    message = made(at(*[(1, 1, b) for b in rest]), after=message)
    cross_b = send(message, 0, 1)
    message = made(at(*[(0, 1, b) for b in every]), [(ahead, [None] * end + [1])], after=message)
    cross_c = send(message, 0, 1)

    by_ring = send(made(at(*[(2, 0, b) for b in every]), [(cross_far, every)]), 1)
    from_ahead = send(made(at(*[(-1, 0, b) for b in most]), [(cross_a, most)]), -1)
    first = send(made(at((1, 0, 0)), [(cross_a, [end]), (by_ring, [0])]), 1)
    others = send(made(at(*[(1, 0, b) for b in rest]), [(cross_b, most), (by_ring, rest)]), 1)
    got = [
        (from_ahead, most + [None]),
        (ahead, [None] * end + [0]),
        (first, [0] + [None] * end),
        (others, [None] + most),
    ]
    partial = made(at(*[(0, 0, b) for b in every]), got, last=True)
    shard, squares = finish(partial, cross_c, rows, n * lax.axis_size("section"))

    total = lax.all_to_all(squares, ("dp", "section"), 0, 0, tiled=True)
    max_norm = math.sqrt(lax.axis_size("section") * stacked.size)
    states = (shard, master[0], moment1[0], moment2[0], max_norm, rows)
    (own,) = update(total, *states, False)

    cut = shard_rows - rows
    other = send(own, 0, 1)
    behind = behind_of(send(own, 1), other)
    tail = send(own[cut:], -1)
    behind_cross = send(behind, 0, 1)
    far = send(behind, 1)
    both, tail = both_of(own, other, tail, behind, rows, cut)
    both = send(both, -1)
    tail_cross = send(tail, 0, 1)
    far = behind_of(far, behind_cross)
    far_cross = send(far, 0, 1)
    new_param, new_first, new_second = update(total, *states, True)

    def move(value, offset, flip, low=0, first=0, size=shard_rows):
        return (value, low, size, table(offset, flip), shard_rows, first)

    gathered = fill(
        None,
        [own, other, behind, tail, behind_cross, tail_cross, far],
        [
            move(0, 0, 0),
            move(1, 0, 1),
            move(2, -1, 0),
            move(3, 1, 0, 0, cut, rows),
            move(4, -1, 1),
            move(5, 1, 1, 0, cut, rows),
            move(6, -2, 0),
        ],
        stacked.shape[0],
    )
    gathered = fill(
        gathered,
        [both, far_cross],
        [move(0, 1, 0, 0, 0, cut), move(0, 1, 1, cut, 0, cut), move(1, -2, 1)],
        stacked.shape[0],
    )
    return new_param[None], new_first[None], new_second[None], gathered[None]


def local(weights, *rest):
    n = lax.axis_size("dp")
    height = weights.shape[1]
    shard, width = height // n, height // 3
    fits = n == 8 and height % n == 0 and math.gcd(shard, width, 256) % 128 == 0 and shard // math.gcd(shard, width, 256) > 2
    return (paired if fits else plain)(weights, *rest)


def solution(mesh):
    whole = P("section", None, None)
    split = P("section", "dp", None)
    return jax.shard_map(
        local,
        mesh=mesh,
        in_specs=(whole, split, split, split, split, split),
        out_specs=(split, split, split, whole),
        check_vma=False,
    )
```

```python
import math

import jax
import jax.numpy as jnp
from jax import lax
from jax.experimental import pallas as pl
from jax.experimental.pallas import tpu as pltpu
from jax.sharding import PartitionSpec as P

MROWS = 256
STEP = 10
LITTLE = 16 << 20
CHUNK = 32
PAD = 16
POWER = 8
TOP = 32768.0


def cost_of(micros):
    return pl.CostEstimate(flops=int(micros * 1.18e9), bytes_accessed=1024, transcendentals=0)


PIECE = cost_of(1.7)
CHEAP = pl.CostEstimate(flops=1024, bytes_accessed=1024, transcendentals=0)


def forward_pieces(x_rows, dy_rows, w_gate, w_up, w_down):
    pre_gate = jnp.dot(x_rows, w_gate, preferred_element_type=jnp.float32)
    pre_up = jnp.dot(x_rows, w_up, preferred_element_type=jnp.float32)
    d_hidden = jnp.dot(dy_rows, w_down, preferred_element_type=jnp.float32)
    return activation(pre_gate, pre_up, d_hidden)


def activation(pre_gate, pre_up, d_hidden):
    sigma = jax.nn.sigmoid(pre_gate)
    silu_val = pre_gate * sigma
    hidden = (silu_val * pre_up).astype(jnp.bfloat16)
    d_gate = (d_hidden * pre_up * sigma * (1.0 + pre_gate * (1.0 - sigma))).astype(jnp.bfloat16)
    d_up = (d_hidden * silu_val).astype(jnp.bfloat16)
    return d_gate, d_up, hidden


def block_grads(x_rows, dy_rows, w_gate, w_up, w_down):
    d_gate, d_up, hidden = forward_pieces(x_rows, dy_rows, w_gate, w_up, w_down)
    g_gate = jnp.dot(x_rows.T, d_gate, preferred_element_type=jnp.float32)
    g_up = jnp.dot(x_rows.T, d_up, preferred_element_type=jnp.float32)
    g_down = jnp.dot(dy_rows.T, hidden, preferred_element_type=jnp.float32)
    return jnp.concatenate([g_gate, g_up, g_down], axis=0)


def adam(clip, shard, old_param, first, second):
    clipped = clip * shard
    new_first = 0.9 * first + 0.1 * clipped
    new_second = 0.95 * second + 0.05 * clipped * clipped
    first_fix = 1.0 / (1.0 - 0.9**STEP)
    second_fix = 1.0 / (1.0 - 0.95**STEP)
    update = new_first * first_fix / (jnp.sqrt(new_second * second_fix) + 1e-08) + 0.1 * old_param
    return old_param - 0.01 * update, new_first, new_second


def clip_of(total, max_norm):
    return jnp.minimum(jnp.float32(1.0), max_norm / (jnp.sqrt(total) + 1e-06))


def plain(weights, inputs, out_grads, master, moment1, moment2):
    stacked = weights[0]
    width = stacked.shape[0] // 3
    local_grad = jnp.zeros(stacked.shape, jnp.float32)
    for start in range(0, inputs.shape[1], MROWS):
        x_rows = inputs[0, start : start + MROWS]
        dy_rows = out_grads[0, start : start + MROWS]
        local_grad = local_grad + block_grads(
            x_rows, dy_rows, stacked[:width], stacked[width : 2 * width], stacked[2 * width :]
        )
    shard = lax.psum_scatter(local_grad, "dp", scatter_dimension=0, tiled=True)
    total = lax.psum(jnp.sum(shard * shard), ("dp", "section"))
    max_norm = jnp.sqrt(jnp.float32(lax.axis_size("section") * stacked.size))
    new_param, new_first, new_second = adam(clip_of(total, max_norm), shard, master[0], moment1[0], moment2[0])
    gathered = lax.all_gather(new_param.astype(jnp.bfloat16), "dp", axis=0, tiled=True)
    return new_param[None], new_first[None], new_second[None], gathered[None]


def chunks(rows):
    return [slice(at, min(at + CHUNK, rows)) for at in range(0, rows, CHUNK)]


def fold(value):
    return jnp.max(jnp.abs(value).reshape(-1, 8, value.shape[1]), axis=0)


def scale_of(top):
    scale = jnp.max(top, axis=0, keepdims=True)
    return jnp.maximum(scale, 1e-30).astype(jnp.bfloat16).astype(jnp.float32)


def encode(value, factor):
    v = value * factor
    v2 = v * v
    v4 = v2 * v2
    v8 = v4 * v4
    return jnp.where(v < 0.0, -v8, v8).astype(jnp.bfloat16)


def decode(code, factor):
    code = code.astype(jnp.float32)
    size = jnp.abs(code)
    root = jnp.exp(jnp.log(jnp.maximum(size, 1e-37)) * (1.0 / POWER)) * factor
    root = jnp.where(size > 0.0, root, 0.0)
    return jnp.where(code < 0.0, -root, root)


def write_codes(total_ref, top, out_ref, first):
    scale = scale_of(top)
    factor = TOP / scale
    for part in chunks(total_ref.shape[0]):
        size = part.stop - part.start
        out_ref[pl.ds(first + part.start, size), :] = encode(total_ref[part, :], factor)
    return scale


def lookup(table, index):
    bits = max(max(table).bit_length(), 1)
    if bits * len(table) < 32:
        packed = sum(value << (bits * at) for at, value in enumerate(table))
        return jnp.bitwise_and(jnp.right_shift(jnp.int32(packed), index * bits), (1 << bits) - 1)
    out = jnp.int32(table[0])
    for at, value in enumerate(table[1:], 1):
        out = jnp.where(index == at, jnp.int32(value), out)
    return out


def forward_kernel(messages, rows, x_hbm, dy_hbm, w_hbm, factors_ref, *refs):
    outs = refs[: len(messages)]
    x_ref, dy_ref, w_ref, a_ref, b_ref, h_ref, total_ref, sems = refs[len(messages) :]
    width = x_hbm.shape[1]
    half = width // 2

    def fetch(at, source, target, index):
        copy = pltpu.make_async_copy(source.at[index], target.at[index], sems.at[at])
        copy.start()
        return copy

    copies = []
    for columns in (pl.ds(0, half), pl.ds(half, half)):
        copies.append(fetch(len(copies), x_hbm, x_ref, (slice(None), columns)))
        copies.append(fetch(len(copies), w_hbm, w_ref, columns))
        copies.append(fetch(len(copies), w_hbm, w_ref, pl.ds(columns.start + width, half)))
    for columns in (pl.ds(0, half), pl.ds(half, half)):
        copies.append(fetch(len(copies), dy_hbm, dy_ref, (slice(None), columns)))
        copies.append(fetch(len(copies), w_hbm, w_ref, pl.ds(columns.start + 2 * width, half)))

    def product(left, start, which):
        weight = w_ref[which * width + start : which * width + start + half]
        return jnp.dot(left[:, start : start + half], weight, preferred_element_type=jnp.float32)

    for copy in copies[:3]:
        copy.wait()
    a_ref[...] = product(x_ref, 0, 0)
    b_ref[...] = product(x_ref, 0, 1)
    for copy in copies[3:6]:
        copy.wait()
    a_ref[...] += product(x_ref, half, 0)
    b_ref[...] += product(x_ref, half, 1)
    for copy in copies[6:8]:
        copy.wait()
    h_ref[...] = product(dy_ref, 0, 2)
    for copy in copies[8:]:
        copy.wait()
    h_ref[...] += product(dy_ref, half, 2)
    for part in chunks(x_ref.shape[0]):
        d_gate, d_up, hidden = activation(a_ref[part, :], b_ref[part, :], h_ref[part, :])
        factors_ref[0, part, :] = d_gate
        factors_ref[1, part, :] = d_up
        factors_ref[2, part, :] = hidden
    per = width // rows
    for places, out_ref in zip(messages, outs):
        scales = jnp.zeros((PAD, out_ref.shape[1]), jnp.float32)
        for step, place in enumerate(places):
            at = place()
            kind = lax.div(at, per)
            column = pl.ds(pl.multiple_of(lax.rem(at, per) * rows, rows), rows)
            left = jnp.where(kind == 2, dy_ref[:, column], x_ref[:, column])
            total_ref[...] = lax.dot_general(
                left, factors_ref[kind], (((0,), (0,)), ((), ())), preferred_element_type=jnp.float32
            )
            top = fold(total_ref[:CHUNK, :])
            for part in chunks(rows)[1:]:
                top = jnp.maximum(top, fold(total_ref[part, :]))
            scale = write_codes(total_ref, top, out_ref, step * rows)
            row = lax.broadcasted_iota(jnp.int32, scales.shape, 0)
            scales = jnp.where(row == step, scale, scales)
        out_ref[len(places) * rows :, :] = scales.astype(jnp.bfloat16)


def forward(x, dy, stacked, messages, rows):
    tokens, width = x.shape
    hidden = stacked.shape[1]

    def place_of(table, block):
        steps = stacked.shape[0] // len(table) // rows
        return lambda: lookup(table, lax.axis_index("dp")) * steps + block

    places = [[place_of(*block) for block in blocks] for blocks in messages]
    return pl.pallas_call(
        lambda *refs: forward_kernel(places, rows, *refs),
        in_specs=[pl.BlockSpec(memory_space=pltpu.HBM)] * 3,
        out_shape=[jax.ShapeDtypeStruct((3, tokens, hidden), jnp.bfloat16)]
        + [jax.ShapeDtypeStruct((len(blocks) * rows + PAD, hidden), jnp.bfloat16) for blocks in messages],
        scratch_shapes=[
            pltpu.VMEM(x.shape, x.dtype),
            pltpu.VMEM(dy.shape, dy.dtype),
            pltpu.VMEM(stacked.shape, stacked.dtype),
            *[pltpu.VMEM((tokens, hidden), jnp.float32)] * 3,
            pltpu.VMEM((rows, hidden), jnp.float32),
            pltpu.SemaphoreType.DMA((10,)),
        ],
        compiler_params=pltpu.CompilerParams(vmem_limit_bytes=60 << 20),
        cost_estimate=CHEAP,
        name="forward",
    )(x, dy, stacked)


def pick(values, step):
    if all(value == values[0] + at for at, value in enumerate(values)):
        return step + values[0] if len(values) > 1 else jnp.int32(values[0])
    out = jnp.int32(values[0])
    for at, value in enumerate(values[1:], 1):
        out = jnp.where(step == at, value, out)
    return out


def piece_kernel(place, per, got, extra, last, *refs):
    step = pl.program_id(0)
    x_ref, dy_ref, d_ref = refs[:3]
    outs = refs[3 + 2 * len(got) + extra :]
    rows = x_ref.shape[1]
    left = jnp.where(lax.div(place(step), per) == 2, dy_ref[...], x_ref[...])
    total_ref = outs[-1]
    total_ref[...] = lax.dot_general(left, d_ref[0], (((0,), (0,)), ((), ())), preferred_element_type=jnp.float32)
    factors = []
    for at, blocks in enumerate(got):
        scales = refs[4 + 2 * at][...].astype(jnp.float32)
        row = lax.broadcasted_iota(jnp.int32, scales.shape, 0)
        here = pick([PAD if block is None else block for block in blocks], step)
        factors.append(jnp.sum(jnp.where(row == here, scales, 0.0), axis=0, keepdims=True) * (1.0 / TOP))
    top = jnp.zeros((8, total_ref.shape[1]), jnp.float32)
    for part in chunks(rows):
        total = total_ref[part, :]
        for at, factor in enumerate(factors):
            total = total + decode(refs[3 + 2 * at][part, :], factor)
        if last:
            outs[0][part, :] = total
        else:
            if factors:
                total_ref[part, :] = total
            top = jnp.maximum(top, fold(total))
    if not last:
        out_ref, scales_ref = outs[:2]
        scale = write_codes(total_ref, top, out_ref, pl.multiple_of(step * rows, rows))
        row = lax.broadcasted_iota(jnp.int32, scales_ref.shape, 0)
        scales_ref[...] = jnp.where(row == step, scale, jnp.where(step == 0, 0.0, scales_ref[...]))
        out_ref[pl.ds(out_ref.shape[0] - PAD, PAD), :] = scales_ref[...].astype(jnp.bfloat16)


def piece(x, dy, factors, rows, blocks, got=(), after=None, last=False, cost=PIECE):
    tokens, width = x.shape
    hidden = factors.shape[2]
    per = width // rows
    shard = 3 * width // len(blocks[0][0])
    steps = shard // rows
    tables = [table for table, _ in blocks]
    within = [block for _, block in blocks]

    def place(i):
        r = lax.axis_index("dp")
        owner = lookup(tables[0], r)
        for at, table in enumerate(tables[1:], 1):
            if table != tables[at - 1]:
                owner = jnp.where(i >= at, lookup(table, r), owner)
        return owner * steps + pick(within, i)

    def column(i):
        return (0, lax.rem(place(i), per))

    in_specs = [
        pl.BlockSpec((tokens, rows), column),
        pl.BlockSpec((tokens, rows), column),
        pl.BlockSpec((1, tokens, hidden), lambda i: (lax.div(place(i), per), 0, 0)),
    ]
    operands = [x, dy, factors]
    for message, parts in got:
        present = [part for part in parts if part is not None]
        nearest = [present[0] if part is None else part for part in parts]
        scales = (message.shape[0] - PAD) // PAD
        in_specs += [
            pl.BlockSpec((rows, hidden), lambda i, nearest=nearest: (pick(nearest, i), 0)),
            pl.BlockSpec((PAD, hidden), lambda i, scales=scales: (scales, 0)),
        ]
        operands += [message, message]
    extra = 0
    if after is not None:
        extra = 1
        operands.append(after)
        in_specs.append(pl.BlockSpec(memory_space=pl.ANY))
    if last:
        out_specs = pl.BlockSpec((rows, hidden), lambda i: (i, 0))
        out_shape = jax.ShapeDtypeStruct((len(blocks) * rows, hidden), jnp.float32)
        scratch = [pltpu.VMEM((rows, hidden), jnp.float32)]
    else:
        out_specs = pl.BlockSpec((len(blocks) * rows + PAD, hidden), lambda i: (0, 0))
        out_shape = jax.ShapeDtypeStruct((len(blocks) * rows + PAD, hidden), jnp.bfloat16)
        scratch = [pltpu.VMEM((PAD, hidden), jnp.float32), pltpu.VMEM((rows, hidden), jnp.float32)]
    return pl.pallas_call(
        lambda *refs: piece_kernel(place, per, [parts for _, parts in got], extra, last, *refs),
        grid=(len(blocks),),
        in_specs=in_specs,
        out_specs=out_specs,
        out_shape=out_shape,
        scratch_shapes=scratch,
        compiler_params=pltpu.CompilerParams(vmem_limit_bytes=LITTLE),
        cost_estimate=cost,
        name="piece",
    )(*operands)


def finish_kernel(sum_ref, *refs):
    step = pl.program_id(0)
    out_ref, squares_ref = refs[-2:]
    factors = []
    for scales_ref in refs[1:-2:2]:
        scales = scales_ref[...].astype(jnp.float32)
        row = lax.broadcasted_iota(jnp.int32, scales.shape, 0)
        factors.append(jnp.sum(jnp.where(row == step, scales, 0.0), axis=0, keepdims=True) * (1.0 / TOP))
    top = jnp.zeros((8, out_ref.shape[1]), jnp.float32)
    for part in chunks(out_ref.shape[0]):
        total = sum_ref[part, :]
        for code_ref, factor in zip(refs[:-2:2], factors):
            total = total + decode(code_ref[part, :], factor)
        out_ref[part, :] = total
        top = top + jnp.sum((total * total).reshape(-1, 8, total.shape[1]), axis=0)
    tile = sum(top[:, at : at + 128] for at in range(0, top.shape[1], 128))
    tile = tile + jnp.where(step == 0, 0.0, squares_ref[:8])
    for at in range(0, squares_ref.shape[0], 8):
        squares_ref[at : at + 8] = tile


def finish(partial, messages, rows, count):
    height, hidden = partial.shape
    block = pl.BlockSpec((rows, hidden), lambda i: (i, 0))
    scales = pl.BlockSpec((PAD, hidden), lambda i: (height // PAD, 0))
    return pl.pallas_call(
        finish_kernel,
        grid=(height // rows,),
        in_specs=[block] + [block, scales] * len(messages),
        out_specs=[block, pl.BlockSpec((8 * count, 128), lambda i: (0, 0))],
        out_shape=[
            jax.ShapeDtypeStruct(partial.shape, jnp.float32),
            jax.ShapeDtypeStruct((8 * count, 128), jnp.float32),
        ],
        compiler_params=pltpu.CompilerParams(vmem_limit_bytes=LITTLE),
        cost_estimate=PIECE,
        name="finish",
    )(partial, *[m for message in messages for m in (message, message)])


def update_kernel(max_norm, states, total_ref, g_ref, p_ref, m1_ref, m2_ref, *outs):
    clip = clip_of(jnp.sum(total_ref[...], keepdims=True), max_norm)
    for part in chunks(g_ref.shape[0]):
        param, first, second = adam(clip, g_ref[part, :], p_ref[part, :], m1_ref[part, :], m2_ref[part, :])
        values = (param, first, second) if states else (param.astype(jnp.bfloat16),)
        for out, value in zip(outs, values):
            out[part, :] = value


def update(total, shard, param, first, second, max_norm, rows, states):
    block = pl.BlockSpec((rows, shard.shape[1]), lambda i: (i, 0))
    dtypes = [jnp.float32] * 3 if states else [jnp.bfloat16]
    return pl.pallas_call(
        lambda *refs: update_kernel(max_norm, states, *refs),
        grid=(shard.shape[0] // rows,),
        in_specs=[pl.BlockSpec(total.shape, lambda i: (0, 0))] + [block] * 4,
        out_specs=[block] * len(dtypes),
        out_shape=[jax.ShapeDtypeStruct(shard.shape, dtype) for dtype in dtypes],
        compiler_params=pltpu.CompilerParams(vmem_limit_bytes=LITTLE),
        cost_estimate=CHEAP,
        name="states" if states else "update",
    )(total, shard, param, first, second)


def behind_of(value, other, cost=CHEAP):
    return pl.pallas_call(
        lambda *refs: None,
        grid=(1,),
        in_specs=[pl.BlockSpec(memory_space=pl.ANY), pl.BlockSpec((PAD, 128), lambda i: (0, 0))],
        out_specs=pl.BlockSpec(memory_space=pl.ANY),
        out_shape=jax.ShapeDtypeStruct(value.shape, value.dtype),
        input_output_aliases={0: 0},
        compiler_params=pltpu.CompilerParams(vmem_limit_bytes=LITTLE),
        cost_estimate=cost,
        name="behind",
    )(value, other)


def both_of(own, other, after, rows, cut):
    columns = own.shape[1]
    steps = cut // rows

    def kernel(own_ref, other_ref, after_ref, both_ref):
        both_ref[...] = jnp.where(pl.program_id(0) < steps, own_ref[...], other_ref[...])

    return pl.pallas_call(
        kernel,
        grid=(2 * steps,),
        in_specs=[
            pl.BlockSpec((rows, columns), lambda i: (jnp.minimum(i, steps - 1), 0)),
            pl.BlockSpec((rows, columns), lambda i: (jnp.maximum(i - steps, 0), 0)),
            pl.BlockSpec((PAD, 128), lambda i: (0, 0)),
        ],
        out_specs=pl.BlockSpec((rows, columns), lambda i: (i, 0)),
        out_shape=jax.ShapeDtypeStruct((2 * cut, columns), own.dtype),
        compiler_params=pltpu.CompilerParams(vmem_limit_bytes=LITTLE),
        cost_estimate=PIECE,
        name="both",
    )(own, other, after)


def fill_kernel(moves, count, *refs):
    out, sems = refs[-2:]
    r = lax.axis_index("dp")
    copies = []
    for at, (source, low, size, table, shard, first) in enumerate(moves):
        to = pl.multiple_of(lookup(table, r) * shard + first, PAD)
        copies.append(pltpu.make_async_copy(refs[source].at[low : low + size], out.at[pl.ds(to, size)], sems.at[at]))
        copies[-1].start()
    for copy in copies:
        copy.wait()


def fill(buffer, values, moves, height):
    columns = values[0].shape[1]
    return pl.pallas_call(
        lambda *refs: fill_kernel(moves, len(values), *refs),
        in_specs=[pl.BlockSpec(memory_space=pltpu.VMEM)] * len(values)
        + [pl.BlockSpec(memory_space=pltpu.HBM)] * (buffer is not None),
        out_specs=pl.BlockSpec(memory_space=pltpu.HBM),
        out_shape=jax.ShapeDtypeStruct((height, columns), values[0].dtype),
        input_output_aliases={} if buffer is None else {len(values): 0},
        scratch_shapes=[pltpu.SemaphoreType.DMA((len(moves),))],
        compiler_params=pltpu.CompilerParams(vmem_limit_bytes=LITTLE),
        cost_estimate=CHEAP,
        name="fill",
    )(*values, *([] if buffer is None else [buffer]))


def paired(weights, inputs, out_grads, master, moment1, moment2):
    n = lax.axis_size("dp")
    pairs = n // 2
    ring = list(range(0, pairs, 2)) + list(range(pairs - 1 - pairs % 2, 0, -2))
    place = {pair: at for at, pair in enumerate(ring)}

    def at_offset(r, offset, flip):
        return 2 * ring[(place[r // 2] + offset) % pairs] + ((r % 2) ^ flip)

    def table(offset, flip):
        return [at_offset(r, offset, flip) for r in range(n)]

    def send(value, offset, flip=0):
        return lax.ppermute(value, "dp", [(r, at_offset(r, offset, flip)) for r in range(n)])

    stacked = weights[0]
    x, dy = inputs[0], out_grads[0]
    width = x.shape[1]
    shard_rows = stacked.shape[0] // n
    rows = math.gcd(shard_rows, width, 256)

    steps = shard_rows // rows

    every, most, rest, end = list(range(steps)), list(range(steps - 1)), list(range(1, steps)), steps - 1

    def at(*blocks):
        return [(table(offset, flip), block) for offset, flip, block in blocks]

    def made(blocks, got=(), **more):
        return piece(x, dy, factors, rows, blocks, got, **more)

    factors, message, ring_message = forward(
        x, dy, stacked, [at(*[(2, 1, b) for b in every]), at((-1, 0, end), (-1, 1, end))], rows
    )
    cross_far = send(message, 0, 1)
    ahead = send(ring_message, -1)
    message = made(at(*[(-1, 1, b) for b in most]))
    cross_back = send(message, 0, 1)
    message = made(at(*[(1, 1, b) for b in every]), after=message)
    cross_next = send(message, 0, 1)
    message = made(at(*[(0, 1, b) for b in every]), [(ahead, [None] * end + [1])], after=message)
    cross_own = send(message, 0, 1)

    by_ring = send(made(at(*[(2, 0, b) for b in every]), [(cross_far, every)]), 1)
    from_ahead = send(made(at(*[(-1, 0, b) for b in most]), [(cross_back, most)]), -1)
    from_behind = send(made(at(*[(1, 0, b) for b in every]), [(cross_next, every), (by_ring, every)]), 1)
    partial = made(at(*[(0, 0, b) for b in every]), [(from_ahead, most + [None]), (ahead, [None] * end + [0])], last=True)
    shard, squares = finish(partial, [cross_own, from_behind], rows, n * lax.axis_size("section"))

    total = lax.all_to_all(squares, ("dp", "section"), 0, 0, tiled=True)
    max_norm = math.sqrt(lax.axis_size("section") * stacked.size)
    states = (shard, master[0], moment1[0], moment2[0], max_norm, rows)
    (own,) = update(total, *states, False)

    cut = shard_rows - rows
    other = send(own, 0, 1)
    behind = behind_of(send(own, 1), other)
    tail = send(own[cut:], -1)
    behind_cross = send(behind, 0, 1)
    far = send(behind, 1)
    tail = behind_of(tail, behind, cost_of(3.4))
    tail_cross = send(tail, 0, 1)
    both = send(both_of(own, other, behind_cross, rows, cut), -1)
    far = behind_of(behind_of(far, behind_cross), tail_cross)
    far_cross = send(far, 0, 1)
    new_param, new_first, new_second = update(total, *states, True)

    def move(value, offset, flip, low=0, first=0, size=shard_rows):
        return (value, low, size, table(offset, flip), shard_rows, first)

    gathered = fill(
        None,
        [own, other, behind, tail, behind_cross, tail_cross, far],
        [
            move(0, 0, 0),
            move(1, 0, 1),
            move(2, -1, 0),
            move(3, 1, 0, 0, cut, rows),
            move(4, -1, 1),
            move(5, 1, 1, 0, cut, rows),
            move(6, -2, 0),
        ],
        stacked.shape[0],
    )
    gathered = fill(
        gathered,
        [both, far_cross],
        [move(0, 1, 0, 0, 0, cut), move(0, 1, 1, cut, 0, cut), move(1, -2, 1)],
        stacked.shape[0],
    )
    return new_param[None], new_first[None], new_second[None], gathered[None]


def local(weights, *rest):
    n = lax.axis_size("dp")
    height = weights.shape[1]
    shard, width = height // n, height // 3
    fits = n == 8 and height % n == 0 and math.gcd(shard, width, 256) % 128 == 0 and shard // math.gcd(shard, width, 256) > 2
    return (paired if fits else plain)(weights, *rest)


def solution(mesh):
    whole = P("section", None, None)
    split = P("section", "dp", None)
    return jax.shard_map(
        local,
        mesh=mesh,
        in_specs=(whole, split, split, split, split, split),
        out_specs=(split, split, split, whole),
        check_vma=False,
    )
```

```python
import math

import jax
import jax.numpy as jnp
from jax import lax
from jax.experimental import pallas as pl
from jax.experimental.pallas import tpu as pltpu
from jax.sharding import PartitionSpec as P

MROWS = 256
STEP = 10
LITTLE = 16 << 20
CHUNK = 32
PAD = 16
POWER = 8
TOP = 32768.0


def cost_of(micros):
    return pl.CostEstimate(flops=int(micros * 1.18e9), bytes_accessed=1024, transcendentals=0)


PIECE = cost_of(1.7)
CHEAP = pl.CostEstimate(flops=1024, bytes_accessed=1024, transcendentals=0)


def forward_pieces(x_rows, dy_rows, w_gate, w_up, w_down):
    pre_gate = jnp.dot(x_rows, w_gate, preferred_element_type=jnp.float32)
    pre_up = jnp.dot(x_rows, w_up, preferred_element_type=jnp.float32)
    d_hidden = jnp.dot(dy_rows, w_down, preferred_element_type=jnp.float32)
    return activation(pre_gate, pre_up, d_hidden)


def activation(pre_gate, pre_up, d_hidden):
    sigma = jax.nn.sigmoid(pre_gate)
    silu_val = pre_gate * sigma
    hidden = (silu_val * pre_up).astype(jnp.bfloat16)
    d_gate = (d_hidden * pre_up * sigma * (1.0 + pre_gate * (1.0 - sigma))).astype(jnp.bfloat16)
    d_up = (d_hidden * silu_val).astype(jnp.bfloat16)
    return d_gate, d_up, hidden


def block_grads(x_rows, dy_rows, w_gate, w_up, w_down):
    d_gate, d_up, hidden = forward_pieces(x_rows, dy_rows, w_gate, w_up, w_down)
    g_gate = jnp.dot(x_rows.T, d_gate, preferred_element_type=jnp.float32)
    g_up = jnp.dot(x_rows.T, d_up, preferred_element_type=jnp.float32)
    g_down = jnp.dot(dy_rows.T, hidden, preferred_element_type=jnp.float32)
    return jnp.concatenate([g_gate, g_up, g_down], axis=0)


def adam(clip, shard, old_param, first, second):
    clipped = clip * shard
    new_first = 0.9 * first + 0.1 * clipped
    new_second = 0.95 * second + 0.05 * clipped * clipped
    first_fix = 1.0 / (1.0 - 0.9**STEP)
    second_fix = 1.0 / (1.0 - 0.95**STEP)
    update = new_first * first_fix / (jnp.sqrt(new_second * second_fix) + 1e-08) + 0.1 * old_param
    return old_param - 0.01 * update, new_first, new_second


def clip_of(total, max_norm):
    return jnp.minimum(jnp.float32(1.0), max_norm / (jnp.sqrt(total) + 1e-06))


def plain(weights, inputs, out_grads, master, moment1, moment2):
    stacked = weights[0]
    width = stacked.shape[0] // 3
    local_grad = jnp.zeros(stacked.shape, jnp.float32)
    for start in range(0, inputs.shape[1], MROWS):
        x_rows = inputs[0, start : start + MROWS]
        dy_rows = out_grads[0, start : start + MROWS]
        local_grad = local_grad + block_grads(
            x_rows, dy_rows, stacked[:width], stacked[width : 2 * width], stacked[2 * width :]
        )
    shard = lax.psum_scatter(local_grad, "dp", scatter_dimension=0, tiled=True)
    total = lax.psum(jnp.sum(shard * shard), ("dp", "section"))
    max_norm = jnp.sqrt(jnp.float32(lax.axis_size("section") * stacked.size))
    new_param, new_first, new_second = adam(clip_of(total, max_norm), shard, master[0], moment1[0], moment2[0])
    gathered = lax.all_gather(new_param.astype(jnp.bfloat16), "dp", axis=0, tiled=True)
    return new_param[None], new_first[None], new_second[None], gathered[None]


def chunks(rows):
    return [slice(at, min(at + CHUNK, rows)) for at in range(0, rows, CHUNK)]


def fold(value):
    return jnp.max(jnp.abs(value).reshape(-1, 8, value.shape[1]), axis=0)


def scale_of(top):
    scale = jnp.max(top, axis=0, keepdims=True)
    return jnp.maximum(scale, 1e-30).astype(jnp.bfloat16).astype(jnp.float32)


def encode(value, factor):
    v = value * factor
    v2 = v * v
    v4 = v2 * v2
    v8 = v4 * v4
    return jnp.where(v < 0.0, -v8, v8).astype(jnp.bfloat16)


def decode(code, factor):
    code = code.astype(jnp.float32)
    size = jnp.abs(code)
    root = jnp.exp(jnp.log(jnp.maximum(size, 1e-37)) * (1.0 / POWER)) * factor
    root = jnp.where(size > 0.0, root, 0.0)
    return jnp.where(code < 0.0, -root, root)


def write_codes(total_ref, top, out_ref, first):
    scale = scale_of(top)
    factor = TOP / scale
    for part in chunks(total_ref.shape[0]):
        size = part.stop - part.start
        out_ref[pl.ds(first + part.start, size), :] = encode(total_ref[part, :], factor)
    return scale


def lookup(table, index):
    bits = max(max(table).bit_length(), 1)
    if bits * len(table) < 32:
        packed = sum(value << (bits * at) for at, value in enumerate(table))
        return jnp.bitwise_and(jnp.right_shift(jnp.int32(packed), index * bits), (1 << bits) - 1)
    out = jnp.int32(table[0])
    for at, value in enumerate(table[1:], 1):
        out = jnp.where(index == at, jnp.int32(value), out)
    return out


def forward_kernel(messages, rows, x_hbm, dy_hbm, w_hbm, factors_ref, *refs):
    outs = refs[: len(messages)]
    x_ref, dy_ref, w_ref, a_ref, b_ref, h_ref, total_ref, sems = refs[len(messages) :]
    width = x_hbm.shape[1]
    half = width // 2

    def fetch(at, source, target, index):
        copy = pltpu.make_async_copy(source.at[index], target.at[index], sems.at[at])
        copy.start()
        return copy

    copies = []
    for columns in (pl.ds(0, half), pl.ds(half, half)):
        copies.append(fetch(len(copies), x_hbm, x_ref, (slice(None), columns)))
        copies.append(fetch(len(copies), w_hbm, w_ref, columns))
        copies.append(fetch(len(copies), w_hbm, w_ref, pl.ds(columns.start + width, half)))
    for columns in (pl.ds(0, half), pl.ds(half, half)):
        copies.append(fetch(len(copies), dy_hbm, dy_ref, (slice(None), columns)))
        copies.append(fetch(len(copies), w_hbm, w_ref, pl.ds(columns.start + 2 * width, half)))

    def product(left, start, which):
        weight = w_ref[which * width + start : which * width + start + half]
        return jnp.dot(left[:, start : start + half], weight, preferred_element_type=jnp.float32)

    for copy in copies[:3]:
        copy.wait()
    a_ref[...] = product(x_ref, 0, 0)
    b_ref[...] = product(x_ref, 0, 1)
    for copy in copies[3:6]:
        copy.wait()
    a_ref[...] += product(x_ref, half, 0)
    b_ref[...] += product(x_ref, half, 1)
    for copy in copies[6:8]:
        copy.wait()
    h_ref[...] = product(dy_ref, 0, 2)
    for copy in copies[8:]:
        copy.wait()
    h_ref[...] += product(dy_ref, half, 2)
    for part in chunks(x_ref.shape[0]):
        d_gate, d_up, hidden = activation(a_ref[part, :], b_ref[part, :], h_ref[part, :])
        factors_ref[0, part, :] = d_gate
        factors_ref[1, part, :] = d_up
        factors_ref[2, part, :] = hidden
    per = width // rows
    for places, out_ref in zip(messages, outs):
        scales = jnp.zeros((PAD, out_ref.shape[1]), jnp.float32)
        for step, place in enumerate(places):
            at = place()
            kind = lax.div(at, per)
            column = pl.ds(pl.multiple_of(lax.rem(at, per) * rows, rows), rows)
            left = jnp.where(kind == 2, dy_ref[:, column], x_ref[:, column])
            total_ref[...] = lax.dot_general(
                left, factors_ref[kind], (((0,), (0,)), ((), ())), preferred_element_type=jnp.float32
            )
            top = fold(total_ref[:CHUNK, :])
            for part in chunks(rows)[1:]:
                top = jnp.maximum(top, fold(total_ref[part, :]))
            scale = write_codes(total_ref, top, out_ref, step * rows)
            row = lax.broadcasted_iota(jnp.int32, scales.shape, 0)
            scales = jnp.where(row == step, scale, scales)
        out_ref[len(places) * rows :, :] = scales.astype(jnp.bfloat16)


def forward(x, dy, stacked, messages, rows):
    tokens, width = x.shape
    hidden = stacked.shape[1]

    def place_of(table, block):
        steps = stacked.shape[0] // len(table) // rows
        return lambda: lookup(table, lax.axis_index("dp")) * steps + block

    places = [[place_of(*block) for block in blocks] for blocks in messages]
    return pl.pallas_call(
        lambda *refs: forward_kernel(places, rows, *refs),
        in_specs=[pl.BlockSpec(memory_space=pltpu.HBM)] * 3,
        out_shape=[jax.ShapeDtypeStruct((3, tokens, hidden), jnp.bfloat16)]
        + [jax.ShapeDtypeStruct((len(blocks) * rows + PAD, hidden), jnp.bfloat16) for blocks in messages],
        scratch_shapes=[
            pltpu.VMEM(x.shape, x.dtype),
            pltpu.VMEM(dy.shape, dy.dtype),
            pltpu.VMEM(stacked.shape, stacked.dtype),
            *[pltpu.VMEM((tokens, hidden), jnp.float32)] * 3,
            pltpu.VMEM((rows, hidden), jnp.float32),
            pltpu.SemaphoreType.DMA((10,)),
        ],
        compiler_params=pltpu.CompilerParams(vmem_limit_bytes=60 << 20),
        cost_estimate=CHEAP,
        name="forward",
    )(x, dy, stacked)


def pick(values, step):
    if all(value == values[0] + at for at, value in enumerate(values)):
        return step + values[0] if len(values) > 1 else jnp.int32(values[0])
    out = jnp.int32(values[0])
    for at, value in enumerate(values[1:], 1):
        out = jnp.where(step == at, value, out)
    return out


def piece_kernel(place, per, got, extra, last, *refs):
    step = pl.program_id(0)
    x_ref, dy_ref, d_ref = refs[:3]
    outs = refs[3 + 2 * len(got) + extra :]
    rows = x_ref.shape[1]
    left = jnp.where(lax.div(place(step), per) == 2, dy_ref[...], x_ref[...])
    total_ref = outs[-1]
    total_ref[...] = lax.dot_general(left, d_ref[0], (((0,), (0,)), ((), ())), preferred_element_type=jnp.float32)
    factors = []
    for at, blocks in enumerate(got):
        scales = refs[4 + 2 * at][...].astype(jnp.float32)
        row = lax.broadcasted_iota(jnp.int32, scales.shape, 0)
        here = pick([PAD if block is None else block for block in blocks], step)
        factors.append(jnp.sum(jnp.where(row == here, scales, 0.0), axis=0, keepdims=True) * (1.0 / TOP))
    top = jnp.zeros((8, total_ref.shape[1]), jnp.float32)
    for part in chunks(rows):
        total = total_ref[part, :]
        for at, factor in enumerate(factors):
            total = total + decode(refs[3 + 2 * at][part, :], factor)
        if last:
            outs[0][part, :] = total
        else:
            if factors:
                total_ref[part, :] = total
            top = jnp.maximum(top, fold(total))
    if not last:
        out_ref, scales_ref = outs[:2]
        scale = write_codes(total_ref, top, out_ref, pl.multiple_of(step * rows, rows))
        row = lax.broadcasted_iota(jnp.int32, scales_ref.shape, 0)
        scales_ref[...] = jnp.where(row == step, scale, jnp.where(step == 0, 0.0, scales_ref[...]))
        out_ref[pl.ds(out_ref.shape[0] - PAD, PAD), :] = scales_ref[...].astype(jnp.bfloat16)


def piece(x, dy, factors, rows, blocks, got=(), after=None, last=False, cost=PIECE):
    tokens, width = x.shape
    hidden = factors.shape[2]
    per = width // rows
    shard = 3 * width // len(blocks[0][0])
    steps = shard // rows
    tables = [table for table, _ in blocks]
    within = [block for _, block in blocks]

    def place(i):
        r = lax.axis_index("dp")
        owner = lookup(tables[0], r)
        for at, table in enumerate(tables[1:], 1):
            if table != tables[at - 1]:
                owner = jnp.where(i >= at, lookup(table, r), owner)
        return owner * steps + pick(within, i)

    def column(i):
        return (0, lax.rem(place(i), per))

    in_specs = [
        pl.BlockSpec((tokens, rows), column),
        pl.BlockSpec((tokens, rows), column),
        pl.BlockSpec((1, tokens, hidden), lambda i: (lax.div(place(i), per), 0, 0)),
    ]
    operands = [x, dy, factors]
    for message, parts in got:
        present = [part for part in parts if part is not None]
        nearest = [present[0] if part is None else part for part in parts]
        scales = (message.shape[0] - PAD) // PAD
        in_specs += [
            pl.BlockSpec((rows, hidden), lambda i, nearest=nearest: (pick(nearest, i), 0)),
            pl.BlockSpec((PAD, hidden), lambda i, scales=scales: (scales, 0)),
        ]
        operands += [message, message]
    extra = 0
    if after is not None:
        extra = 1
        operands.append(after)
        in_specs.append(pl.BlockSpec(memory_space=pl.ANY))
    if last:
        out_specs = pl.BlockSpec((rows, hidden), lambda i: (i, 0))
        out_shape = jax.ShapeDtypeStruct((len(blocks) * rows, hidden), jnp.float32)
        scratch = [pltpu.VMEM((rows, hidden), jnp.float32)]
    else:
        out_specs = pl.BlockSpec((len(blocks) * rows + PAD, hidden), lambda i: (0, 0))
        out_shape = jax.ShapeDtypeStruct((len(blocks) * rows + PAD, hidden), jnp.bfloat16)
        scratch = [pltpu.VMEM((PAD, hidden), jnp.float32), pltpu.VMEM((rows, hidden), jnp.float32)]
    return pl.pallas_call(
        lambda *refs: piece_kernel(place, per, [parts for _, parts in got], extra, last, *refs),
        grid=(len(blocks),),
        in_specs=in_specs,
        out_specs=out_specs,
        out_shape=out_shape,
        scratch_shapes=scratch,
        compiler_params=pltpu.CompilerParams(vmem_limit_bytes=LITTLE),
        cost_estimate=cost,
        name="piece",
    )(*operands)


def finish_kernel(sum_ref, *refs):
    step = pl.program_id(0)
    out_ref, squares_ref = refs[-2:]
    factors = []
    for scales_ref in refs[1:-2:2]:
        scales = scales_ref[...].astype(jnp.float32)
        row = lax.broadcasted_iota(jnp.int32, scales.shape, 0)
        factors.append(jnp.sum(jnp.where(row == step, scales, 0.0), axis=0, keepdims=True) * (1.0 / TOP))
    top = jnp.zeros((8, out_ref.shape[1]), jnp.float32)
    for part in chunks(out_ref.shape[0]):
        total = sum_ref[part, :]
        for code_ref, factor in zip(refs[:-2:2], factors):
            total = total + decode(code_ref[part, :], factor)
        out_ref[part, :] = total
        top = top + jnp.sum((total * total).reshape(-1, 8, total.shape[1]), axis=0)
    row = jnp.sum(sum(top[:, at : at + 128] for at in range(0, top.shape[1], 128)), axis=0, keepdims=True)
    squares_ref[...] = jnp.broadcast_to(row, squares_ref.shape) + jnp.where(step == 0, 0.0, squares_ref[...])


def finish(partial, messages, rows, count):
    height, hidden = partial.shape
    block = pl.BlockSpec((rows, hidden), lambda i: (i, 0))
    scales = pl.BlockSpec((PAD, hidden), lambda i: (height // PAD, 0))
    return pl.pallas_call(
        finish_kernel,
        grid=(height // rows,),
        in_specs=[block] + [block, scales] * len(messages),
        out_specs=[block, pl.BlockSpec((count, 128), lambda i: (0, 0))],
        out_shape=[
            jax.ShapeDtypeStruct(partial.shape, jnp.float32),
            jax.ShapeDtypeStruct((count, 128), jnp.float32),
        ],
        compiler_params=pltpu.CompilerParams(vmem_limit_bytes=LITTLE),
        cost_estimate=PIECE,
        name="finish",
    )(partial, *[m for message in messages for m in (message, message)])


def join_kernel(sum_ref, code_ref, scales_ref, out_ref, total_ref, out_scales_ref):
    step = pl.program_id(0)
    rows = sum_ref.shape[0]
    scales = scales_ref[...].astype(jnp.float32)
    row = lax.broadcasted_iota(jnp.int32, scales.shape, 0)
    factor = jnp.sum(jnp.where(row == step, scales, 0.0), axis=0, keepdims=True) * (1.0 / TOP)
    top = jnp.zeros((8, sum_ref.shape[1]), jnp.float32)
    for part in chunks(rows):
        total = sum_ref[part, :] + decode(code_ref[part, :], factor)
        total_ref[part, :] = total
        top = jnp.maximum(top, fold(total))
    scale = write_codes(total_ref, top, out_ref, pl.multiple_of(step * rows, rows))
    out_scales_ref[...] = jnp.where(row == step, scale, jnp.where(step == 0, 0.0, out_scales_ref[...]))
    out_ref[pl.ds(out_ref.shape[0] - PAD, PAD), :] = out_scales_ref[...].astype(jnp.bfloat16)


def join(partial, message, rows):
    height, hidden = partial.shape
    block = pl.BlockSpec((rows, hidden), lambda i: (i, 0))
    return pl.pallas_call(
        join_kernel,
        grid=(height // rows,),
        in_specs=[block, block, pl.BlockSpec((PAD, hidden), lambda i: (height // PAD, 0))],
        out_specs=pl.BlockSpec(message.shape, lambda i: (0, 0)),
        out_shape=jax.ShapeDtypeStruct(message.shape, message.dtype),
        scratch_shapes=[pltpu.VMEM((rows, hidden), jnp.float32), pltpu.VMEM((PAD, hidden), jnp.float32)],
        compiler_params=pltpu.CompilerParams(vmem_limit_bytes=LITTLE),
        cost_estimate=PIECE,
        name="join",
    )(partial, message, message)


def update_kernel(max_norm, states, total_ref, g_ref, p_ref, m1_ref, m2_ref, *outs):
    clip = clip_of(jnp.sum(total_ref[...], keepdims=True), max_norm)
    for part in chunks(g_ref.shape[0]):
        param, first, second = adam(clip, g_ref[part, :], p_ref[part, :], m1_ref[part, :], m2_ref[part, :])
        values = (param, first, second) if states else (param.astype(jnp.bfloat16),)
        for out, value in zip(outs, values):
            out[part, :] = value


def update(total, shard, param, first, second, max_norm, rows, states):
    block = pl.BlockSpec((rows, shard.shape[1]), lambda i: (i, 0))
    dtypes = [jnp.float32] * 3 if states else [jnp.bfloat16]
    return pl.pallas_call(
        lambda *refs: update_kernel(max_norm, states, *refs),
        grid=(shard.shape[0] // rows,),
        in_specs=[pl.BlockSpec(total.shape, lambda i: (0, 0))] + [block] * 4,
        out_specs=[block] * len(dtypes),
        out_shape=[jax.ShapeDtypeStruct(shard.shape, dtype) for dtype in dtypes],
        compiler_params=pltpu.CompilerParams(vmem_limit_bytes=LITTLE),
        cost_estimate=CHEAP,
        name="states" if states else "update",
    )(total, shard, param, first, second)


def behind_of(value, other, cost=CHEAP):
    return pl.pallas_call(
        lambda *refs: None,
        grid=(1,),
        in_specs=[pl.BlockSpec(memory_space=pl.ANY), pl.BlockSpec((PAD, 128), lambda i: (0, 0))],
        out_specs=pl.BlockSpec(memory_space=pl.ANY),
        out_shape=jax.ShapeDtypeStruct(value.shape, value.dtype),
        input_output_aliases={0: 0},
        compiler_params=pltpu.CompilerParams(vmem_limit_bytes=LITTLE),
        cost_estimate=cost,
        name="behind",
    )(value, other)


def both_of(own, other, after, rows, cut):
    columns = own.shape[1]
    steps = cut // rows

    def kernel(own_ref, other_ref, after_ref, both_ref):
        both_ref[...] = jnp.where(pl.program_id(0) < steps, own_ref[...], other_ref[...])

    return pl.pallas_call(
        kernel,
        grid=(2 * steps,),
        in_specs=[
            pl.BlockSpec((rows, columns), lambda i: (jnp.minimum(i, steps - 1), 0)),
            pl.BlockSpec((rows, columns), lambda i: (jnp.maximum(i - steps, 0), 0)),
            pl.BlockSpec((PAD, 128), lambda i: (0, 0)),
        ],
        out_specs=pl.BlockSpec((rows, columns), lambda i: (i, 0)),
        out_shape=jax.ShapeDtypeStruct((2 * cut, columns), own.dtype),
        compiler_params=pltpu.CompilerParams(vmem_limit_bytes=LITTLE),
        cost_estimate=PIECE,
        name="both",
    )(own, other, after)


def fill_kernel(moves, count, *refs):
    out, sems = refs[-2:]
    r = lax.axis_index("dp")
    copies = []
    for at, (source, low, size, table, shard, first) in enumerate(moves):
        to = pl.multiple_of(lookup(table, r) * shard + first, PAD)
        copies.append(pltpu.make_async_copy(refs[source].at[low : low + size], out.at[pl.ds(to, size)], sems.at[at]))
        copies[-1].start()
    for copy in copies:
        copy.wait()


def fill(buffer, values, moves, height):
    columns = values[0].shape[1]
    return pl.pallas_call(
        lambda *refs: fill_kernel(moves, len(values), *refs),
        in_specs=[pl.BlockSpec(memory_space=pltpu.VMEM)] * len(values)
        + [pl.BlockSpec(memory_space=pltpu.HBM)] * (buffer is not None),
        out_specs=pl.BlockSpec(memory_space=pltpu.HBM),
        out_shape=jax.ShapeDtypeStruct((height, columns), values[0].dtype),
        input_output_aliases={} if buffer is None else {len(values): 0},
        scratch_shapes=[pltpu.SemaphoreType.DMA((len(moves),))],
        compiler_params=pltpu.CompilerParams(vmem_limit_bytes=LITTLE),
        cost_estimate=CHEAP,
        name="fill",
    )(*values, *([] if buffer is None else [buffer]))


def paired(weights, inputs, out_grads, master, moment1, moment2):
    n = lax.axis_size("dp")
    pairs = n // 2
    ring = list(range(0, pairs, 2)) + list(range(pairs - 1 - pairs % 2, 0, -2))
    place = {pair: at for at, pair in enumerate(ring)}

    def at_offset(r, offset, flip):
        return 2 * ring[(place[r // 2] + offset) % pairs] + ((r % 2) ^ flip)

    def table(offset, flip):
        return [at_offset(r, offset, flip) for r in range(n)]

    def send(value, offset, flip=0):
        return lax.ppermute(value, "dp", [(r, at_offset(r, offset, flip)) for r in range(n)])

    stacked = weights[0]
    x, dy = inputs[0], out_grads[0]
    width = x.shape[1]
    shard_rows = stacked.shape[0] // n
    rows = math.gcd(shard_rows, width, 256)

    steps = shard_rows // rows

    every, most, rest, end = list(range(steps)), list(range(steps - 1)), list(range(1, steps)), steps - 1

    def at(*blocks):
        return [(table(offset, flip), block) for offset, flip, block in blocks]

    def made(blocks, got=(), **more):
        return piece(x, dy, factors, rows, blocks, got, **more)

    factors, message = forward(x, dy, stacked, [at(*[(2, 1, b) for b in every])], rows)
    cross_far = send(message, 0, 1)
    message = made(at((-1, 0, end), (-1, 1, end)))
    ahead = send(message, -1)
    message = made(at(*[(-1, 1, b) for b in most]), after=message)
    cross_back = send(message, 0, 1)
    message = made(at(*[(1, 1, b) for b in every]), after=message)
    cross_next = send(message, 0, 1)
    message = made(at(*[(0, 1, b) for b in every]), [(ahead, [None] * end + [1])], after=message)
    cross_own = send(message, 0, 1)

    by_ring = send(made(at(*[(2, 0, b) for b in every]), [(cross_far, every)]), 1)
    from_ahead = send(made(at(*[(-1, 0, b) for b in most]), [(cross_back, most)]), -1)
    from_behind = send(join(made(at(*[(1, 0, b) for b in every]), [(by_ring, every)], last=True), cross_next, rows), 1)
    partial = made(at(*[(0, 0, b) for b in every]), [(from_ahead, most + [None]), (ahead, [None] * end + [0])], last=True)
    shard, squares = finish(partial, [cross_own, from_behind], rows, n * lax.axis_size("section"))

    total = lax.all_to_all(squares, ("dp", "section"), 0, 0, tiled=True)
    max_norm = math.sqrt(lax.axis_size("section") * stacked.size)
    states = (shard, master[0], moment1[0], moment2[0], max_norm, rows)
    (own,) = update(total, *states, False)

    cut = shard_rows - rows
    other = send(own, 0, 1)
    behind = behind_of(send(own, 1), other)
    tail = send(own[cut:], -1)
    behind_cross = send(behind, 0, 1)
    far = send(behind, 1)
    tail = behind_of(tail, behind, cost_of(3.4))
    tail_cross = send(tail, 0, 1)
    both = send(both_of(own, other, behind_cross, rows, cut), -1)
    far = behind_of(behind_of(far, behind_cross), tail_cross)
    far_cross = send(far, 0, 1)
    new_param, new_first, new_second = update(total, *states, True)

    def move(value, offset, flip, low=0, first=0, size=shard_rows):
        return (value, low, size, table(offset, flip), shard_rows, first)

    gathered = fill(
        None,
        [own, other, behind, tail, behind_cross, tail_cross, far],
        [
            move(0, 0, 0),
            move(1, 0, 1),
            move(2, -1, 0),
            move(3, 1, 0, 0, cut, rows),
            move(4, -1, 1),
            move(5, 1, 1, 0, cut, rows),
            move(6, -2, 0),
        ],
        stacked.shape[0],
    )
    gathered = fill(
        gathered,
        [both, far_cross],
        [move(0, 1, 0, 0, 0, cut), move(0, 1, 1, cut, 0, cut), move(1, -2, 1)],
        stacked.shape[0],
    )
    return new_param[None], new_first[None], new_second[None], gathered[None]


def local(weights, *rest):
    n = lax.axis_size("dp")
    height = weights.shape[1]
    shard, width = height // n, height // 3
    fits = n == 8 and height % n == 0 and math.gcd(shard, width, 256) % 128 == 0 and shard // math.gcd(shard, width, 256) > 2
    return (paired if fits else plain)(weights, *rest)


def solution(mesh):
    whole = P("section", None, None)
    split = P("section", "dp", None)
    return jax.shard_map(
        local,
        mesh=mesh,
        in_specs=(whole, split, split, split, split, split),
        out_specs=(split, split, split, whole),
        check_vma=False,
    )
```

```python
import math

import jax
import jax.numpy as jnp
from jax import lax
from jax.experimental import pallas as pl
from jax.experimental.pallas import tpu as pltpu
from jax.sharding import PartitionSpec as P

MROWS = 256
STEP = 10
LITTLE = 16 << 20
CHUNK = 32
PAD = 16
POWER = 8
TOP = 32768.0


def cost_of(micros):
    return pl.CostEstimate(flops=int(micros * 1.18e9), bytes_accessed=1024, transcendentals=0)


PIECE = cost_of(1.7)
CHEAP = pl.CostEstimate(flops=1024, bytes_accessed=1024, transcendentals=0)


def forward_pieces(x_rows, dy_rows, w_gate, w_up, w_down):
    pre_gate = jnp.dot(x_rows, w_gate, preferred_element_type=jnp.float32)
    pre_up = jnp.dot(x_rows, w_up, preferred_element_type=jnp.float32)
    d_hidden = jnp.dot(dy_rows, w_down, preferred_element_type=jnp.float32)
    return activation(pre_gate, pre_up, d_hidden)


def activation(pre_gate, pre_up, d_hidden):
    sigma = jax.nn.sigmoid(pre_gate)
    silu_val = pre_gate * sigma
    hidden = (silu_val * pre_up).astype(jnp.bfloat16)
    d_gate = (d_hidden * pre_up * sigma * (1.0 + pre_gate * (1.0 - sigma))).astype(jnp.bfloat16)
    d_up = (d_hidden * silu_val).astype(jnp.bfloat16)
    return d_gate, d_up, hidden


def block_grads(x_rows, dy_rows, w_gate, w_up, w_down):
    d_gate, d_up, hidden = forward_pieces(x_rows, dy_rows, w_gate, w_up, w_down)
    g_gate = jnp.dot(x_rows.T, d_gate, preferred_element_type=jnp.float32)
    g_up = jnp.dot(x_rows.T, d_up, preferred_element_type=jnp.float32)
    g_down = jnp.dot(dy_rows.T, hidden, preferred_element_type=jnp.float32)
    return jnp.concatenate([g_gate, g_up, g_down], axis=0)


def adam(clip, shard, old_param, first, second):
    clipped = clip * shard
    new_first = 0.9 * first + 0.1 * clipped
    new_second = 0.95 * second + 0.05 * clipped * clipped
    first_fix = 1.0 / (1.0 - 0.9**STEP)
    second_fix = 1.0 / (1.0 - 0.95**STEP)
    update = new_first * first_fix / (jnp.sqrt(new_second * second_fix) + 1e-08) + 0.1 * old_param
    return old_param - 0.01 * update, new_first, new_second


def clip_of(total, max_norm):
    return jnp.minimum(jnp.float32(1.0), max_norm / (jnp.sqrt(total) + 1e-06))


def plain(weights, inputs, out_grads, master, moment1, moment2):
    stacked = weights[0]
    width = stacked.shape[0] // 3
    local_grad = jnp.zeros(stacked.shape, jnp.float32)
    for start in range(0, inputs.shape[1], MROWS):
        x_rows = inputs[0, start : start + MROWS]
        dy_rows = out_grads[0, start : start + MROWS]
        local_grad = local_grad + block_grads(
            x_rows, dy_rows, stacked[:width], stacked[width : 2 * width], stacked[2 * width :]
        )
    shard = lax.psum_scatter(local_grad, "dp", scatter_dimension=0, tiled=True)
    total = lax.psum(jnp.sum(shard * shard), ("dp", "section"))
    max_norm = jnp.sqrt(jnp.float32(lax.axis_size("section") * stacked.size))
    new_param, new_first, new_second = adam(clip_of(total, max_norm), shard, master[0], moment1[0], moment2[0])
    gathered = lax.all_gather(new_param.astype(jnp.bfloat16), "dp", axis=0, tiled=True)
    return new_param[None], new_first[None], new_second[None], gathered[None]


def chunks(rows):
    return [slice(at, min(at + CHUNK, rows)) for at in range(0, rows, CHUNK)]


def fold(value):
    return jnp.max(jnp.abs(value).reshape(-1, 8, value.shape[1]), axis=0)


def scale_of(top):
    scale = jnp.max(top, axis=0, keepdims=True)
    return jnp.maximum(scale, 1e-30).astype(jnp.bfloat16).astype(jnp.float32)


def encode(value, factor):
    v = value * factor
    v2 = v * v
    v4 = v2 * v2
    v8 = v4 * v4
    return jnp.where(v < 0.0, -v8, v8).astype(jnp.bfloat16)


def decode(code, factor):
    code = code.astype(jnp.float32)
    size = jnp.abs(code)
    root = jnp.exp(jnp.log(jnp.maximum(size, 1e-37)) * (1.0 / POWER)) * factor
    root = jnp.where(size > 0.0, root, 0.0)
    return jnp.where(code < 0.0, -root, root)


def write_codes(total_ref, top, out_ref, first):
    scale = scale_of(top)
    factor = TOP / scale
    for part in chunks(total_ref.shape[0]):
        size = part.stop - part.start
        out_ref[pl.ds(first + part.start, size), :] = encode(total_ref[part, :], factor)
    return scale


def lookup(table, index):
    bits = max(max(table).bit_length(), 1)
    if bits * len(table) < 32:
        packed = sum(value << (bits * at) for at, value in enumerate(table))
        return jnp.bitwise_and(jnp.right_shift(jnp.int32(packed), index * bits), (1 << bits) - 1)
    out = jnp.int32(table[0])
    for at, value in enumerate(table[1:], 1):
        out = jnp.where(index == at, jnp.int32(value), out)
    return out


def forward_kernel(places, rows, x_hbm, dy_hbm, w_hbm, factors_ref, out_ref, *refs):
    x_ref, dy_ref, w_ref, left_ref, a_ref, b_ref, h_ref, total_ref, sems = refs
    width = x_hbm.shape[1]
    weights = [pl.ds(part * width, width) for part in range(3)]
    copies = [
        pltpu.make_async_copy(x_hbm, x_ref, sems.at[0]),
        pltpu.make_async_copy(dy_hbm, dy_ref, sems.at[1]),
        *[pltpu.make_async_copy(w_hbm.at[part], w_ref.at[part], sems.at[2 + at]) for at, part in enumerate(weights)],
    ]
    for copy in copies:
        copy.start()
    per = width // rows
    copies[0].wait()
    copies[1].wait()
    for step, place in enumerate(places):
        at = place()
        column = pl.ds(pl.multiple_of(lax.rem(at, per) * rows, rows), rows)
        left_ref[step] = jnp.where(lax.div(at, per) == 2, dy_ref[:, column], x_ref[:, column]).T
    for copy, part, left, product in zip(copies[2:], weights, (x_ref, x_ref, dy_ref), (a_ref, b_ref, h_ref)):
        copy.wait()
        product[...] = jnp.dot(left[...], w_ref[part], preferred_element_type=jnp.float32)
    for part in chunks(x_ref.shape[0]):
        d_gate, d_up, hidden = activation(a_ref[part, :], b_ref[part, :], h_ref[part, :])
        factors_ref[0, part, :] = d_gate
        factors_ref[1, part, :] = d_up
        factors_ref[2, part, :] = hidden
    scales = jnp.zeros((PAD, out_ref.shape[1]), jnp.float32)
    for step, place in enumerate(places):
        factor = factors_ref[lax.div(place(), per)]
        total_ref[...] = jnp.dot(left_ref[step], factor, preferred_element_type=jnp.float32)
        top = fold(total_ref[:CHUNK, :])
        for part in chunks(rows)[1:]:
            top = jnp.maximum(top, fold(total_ref[part, :]))
        scale = write_codes(total_ref, top, out_ref, step * rows)
        row = lax.broadcasted_iota(jnp.int32, scales.shape, 0)
        scales = jnp.where(row == step, scale, scales)
    out_ref[len(places) * rows :, :] = scales.astype(jnp.bfloat16)


def forward(x, dy, stacked, blocks, rows):
    tokens, width = x.shape
    hidden = stacked.shape[1]

    def place_of(table, block):
        steps = stacked.shape[0] // len(table) // rows
        return lambda: lookup(table, lax.axis_index("dp")) * steps + block

    places = [place_of(*block) for block in blocks]
    return pl.pallas_call(
        lambda *refs: forward_kernel(places, rows, *refs),
        in_specs=[pl.BlockSpec(memory_space=pltpu.HBM)] * 3,
        out_shape=[
            jax.ShapeDtypeStruct((3, tokens, hidden), jnp.bfloat16),
            jax.ShapeDtypeStruct((len(blocks) * rows + PAD, hidden), jnp.bfloat16),
        ],
        scratch_shapes=[
            pltpu.VMEM(x.shape, x.dtype),
            pltpu.VMEM(dy.shape, dy.dtype),
            pltpu.VMEM(stacked.shape, stacked.dtype),
            pltpu.VMEM((len(blocks), rows, tokens), x.dtype),
            *[pltpu.VMEM((tokens, hidden), jnp.float32)] * 3,
            pltpu.VMEM((rows, hidden), jnp.float32),
            pltpu.SemaphoreType.DMA((5,)),
        ],
        compiler_params=pltpu.CompilerParams(vmem_limit_bytes=60 << 20),
        cost_estimate=CHEAP,
        name="forward",
    )(x, dy, stacked)


def pick(values, step):
    if all(value == values[0] + at for at, value in enumerate(values)):
        return step + values[0] if len(values) > 1 else jnp.int32(values[0])
    out = jnp.int32(values[0])
    for at, value in enumerate(values[1:], 1):
        out = jnp.where(step == at, value, out)
    return out


def piece_kernel(place, per, got, extra, last, *refs):
    step = pl.program_id(0)
    x_ref, dy_ref, d_ref = refs[:3]
    outs = refs[3 + 2 * len(got) + extra :]
    rows = x_ref.shape[1]
    left = jnp.where(lax.div(place(step), per) == 2, dy_ref[...], x_ref[...])
    total_ref = outs[-1]
    total_ref[...] = lax.dot_general(left, d_ref[0], (((0,), (0,)), ((), ())), preferred_element_type=jnp.float32)
    factors = []
    for at, blocks in enumerate(got):
        scales = refs[4 + 2 * at][...].astype(jnp.float32)
        row = lax.broadcasted_iota(jnp.int32, scales.shape, 0)
        here = pick([PAD if block is None else block for block in blocks], step)
        factors.append(jnp.sum(jnp.where(row == here, scales, 0.0), axis=0, keepdims=True) * (1.0 / TOP))
    top = jnp.zeros((8, total_ref.shape[1]), jnp.float32)
    for part in chunks(rows):
        total = total_ref[part, :]
        for at, factor in enumerate(factors):
            total = total + decode(refs[3 + 2 * at][part, :], factor)
        if last:
            outs[0][part, :] = total
        else:
            if factors:
                total_ref[part, :] = total
            top = jnp.maximum(top, fold(total))
    if not last:
        out_ref, scales_ref = outs[:2]
        scale = write_codes(total_ref, top, out_ref, pl.multiple_of(step * rows, rows))
        row = lax.broadcasted_iota(jnp.int32, scales_ref.shape, 0)
        scales_ref[...] = jnp.where(row == step, scale, jnp.where(step == 0, 0.0, scales_ref[...]))
        out_ref[pl.ds(out_ref.shape[0] - PAD, PAD), :] = scales_ref[...].astype(jnp.bfloat16)


def piece(x, dy, factors, rows, blocks, got=(), after=None, last=False, cost=PIECE):
    tokens, width = x.shape
    hidden = factors.shape[2]
    per = width // rows
    shard = 3 * width // len(blocks[0][0])
    steps = shard // rows
    tables = [table for table, _ in blocks]
    within = [block for _, block in blocks]

    def place(i):
        r = lax.axis_index("dp")
        owner = lookup(tables[0], r)
        for at, table in enumerate(tables[1:], 1):
            if table != tables[at - 1]:
                owner = jnp.where(i >= at, lookup(table, r), owner)
        return owner * steps + pick(within, i)

    def column(i):
        return (0, lax.rem(place(i), per))

    in_specs = [
        pl.BlockSpec((tokens, rows), column),
        pl.BlockSpec((tokens, rows), column),
        pl.BlockSpec((1, tokens, hidden), lambda i: (lax.div(place(i), per), 0, 0)),
    ]
    operands = [x, dy, factors]
    for message, parts in got:
        present = [part for part in parts if part is not None]
        nearest = [present[0] if part is None else part for part in parts]
        scales = (message.shape[0] - PAD) // PAD
        in_specs += [
            pl.BlockSpec((rows, hidden), lambda i, nearest=nearest: (pick(nearest, i), 0)),
            pl.BlockSpec((PAD, hidden), lambda i, scales=scales: (scales, 0)),
        ]
        operands += [message, message]
    extra = 0
    if after is not None:
        extra = 1
        operands.append(after)
        in_specs.append(pl.BlockSpec(memory_space=pl.ANY))
    if last:
        out_specs = pl.BlockSpec((rows, hidden), lambda i: (i, 0))
        out_shape = jax.ShapeDtypeStruct((len(blocks) * rows, hidden), jnp.float32)
        scratch = [pltpu.VMEM((rows, hidden), jnp.float32)]
    else:
        out_specs = pl.BlockSpec((len(blocks) * rows + PAD, hidden), lambda i: (0, 0))
        out_shape = jax.ShapeDtypeStruct((len(blocks) * rows + PAD, hidden), jnp.bfloat16)
        scratch = [pltpu.VMEM((PAD, hidden), jnp.float32), pltpu.VMEM((rows, hidden), jnp.float32)]
    return pl.pallas_call(
        lambda *refs: piece_kernel(place, per, [parts for _, parts in got], extra, last, *refs),
        grid=(len(blocks),),
        in_specs=in_specs,
        out_specs=out_specs,
        out_shape=out_shape,
        scratch_shapes=scratch,
        compiler_params=pltpu.CompilerParams(vmem_limit_bytes=LITTLE),
        cost_estimate=cost,
        name="piece",
    )(*operands)


def finish_kernel(sum_ref, *refs):
    step = pl.program_id(0)
    out_ref, squares_ref = refs[-2:]
    factors = []
    for scales_ref in refs[1:-2:2]:
        scales = scales_ref[...].astype(jnp.float32)
        row = lax.broadcasted_iota(jnp.int32, scales.shape, 0)
        factors.append(jnp.sum(jnp.where(row == step, scales, 0.0), axis=0, keepdims=True) * (1.0 / TOP))
    top = jnp.zeros((8, out_ref.shape[1]), jnp.float32)
    for part in chunks(out_ref.shape[0]):
        total = sum_ref[part, :]
        for code_ref, factor in zip(refs[:-2:2], factors):
            total = total + decode(code_ref[part, :], factor)
        out_ref[part, :] = total
        top = top + jnp.sum((total * total).reshape(-1, 8, total.shape[1]), axis=0)
    row = jnp.sum(sum(top[:, at : at + 128] for at in range(0, top.shape[1], 128)), axis=0, keepdims=True)
    squares_ref[...] = jnp.broadcast_to(row, squares_ref.shape) + jnp.where(step == 0, 0.0, squares_ref[...])


def finish(partial, messages, rows, count):
    height, hidden = partial.shape
    block = pl.BlockSpec((rows, hidden), lambda i: (i, 0))
    scales = pl.BlockSpec((PAD, hidden), lambda i: (height // PAD, 0))
    return pl.pallas_call(
        finish_kernel,
        grid=(height // rows,),
        in_specs=[block] + [block, scales] * len(messages),
        out_specs=[block, pl.BlockSpec((count, 128), lambda i: (0, 0))],
        out_shape=[
            jax.ShapeDtypeStruct(partial.shape, jnp.float32),
            jax.ShapeDtypeStruct((count, 128), jnp.float32),
        ],
        compiler_params=pltpu.CompilerParams(vmem_limit_bytes=LITTLE),
        cost_estimate=PIECE,
        name="finish",
    )(partial, *[m for message in messages for m in (message, message)])


def join_kernel(sum_ref, code_ref, scales_ref, out_ref, total_ref, out_scales_ref):
    step = pl.program_id(0)
    rows = sum_ref.shape[0]
    scales = scales_ref[...].astype(jnp.float32)
    row = lax.broadcasted_iota(jnp.int32, scales.shape, 0)
    factor = jnp.sum(jnp.where(row == step, scales, 0.0), axis=0, keepdims=True) * (1.0 / TOP)
    top = jnp.zeros((8, sum_ref.shape[1]), jnp.float32)
    for part in chunks(rows):
        total = sum_ref[part, :] + decode(code_ref[part, :], factor)
        total_ref[part, :] = total
        top = jnp.maximum(top, fold(total))
    scale = write_codes(total_ref, top, out_ref, pl.multiple_of(step * rows, rows))
    out_scales_ref[...] = jnp.where(row == step, scale, jnp.where(step == 0, 0.0, out_scales_ref[...]))
    out_ref[pl.ds(out_ref.shape[0] - PAD, PAD), :] = out_scales_ref[...].astype(jnp.bfloat16)


def join(partial, message, rows):
    height, hidden = partial.shape
    block = pl.BlockSpec((rows, hidden), lambda i: (i, 0))
    return pl.pallas_call(
        join_kernel,
        grid=(height // rows,),
        in_specs=[block, block, pl.BlockSpec((PAD, hidden), lambda i: (height // PAD, 0))],
        out_specs=pl.BlockSpec(message.shape, lambda i: (0, 0)),
        out_shape=jax.ShapeDtypeStruct(message.shape, message.dtype),
        scratch_shapes=[pltpu.VMEM((rows, hidden), jnp.float32), pltpu.VMEM((PAD, hidden), jnp.float32)],
        compiler_params=pltpu.CompilerParams(vmem_limit_bytes=LITTLE),
        cost_estimate=PIECE,
        name="join",
    )(partial, message, message)


def update_kernel(max_norm, states, total_ref, g_ref, p_ref, m1_ref, m2_ref, *outs):
    clip = clip_of(jnp.sum(total_ref[...], keepdims=True), max_norm)
    for part in chunks(g_ref.shape[0]):
        param, first, second = adam(clip, g_ref[part, :], p_ref[part, :], m1_ref[part, :], m2_ref[part, :])
        values = (param, first, second) if states else (param.astype(jnp.bfloat16),)
        for out, value in zip(outs, values):
            out[part, :] = value


def update(total, shard, param, first, second, max_norm, rows, states):
    block = pl.BlockSpec((rows, shard.shape[1]), lambda i: (i, 0))
    dtypes = [jnp.float32] * 3 if states else [jnp.bfloat16]
    return pl.pallas_call(
        lambda *refs: update_kernel(max_norm, states, *refs),
        grid=(shard.shape[0] // rows,),
        in_specs=[pl.BlockSpec(total.shape, lambda i: (0, 0))] + [block] * 4,
        out_specs=[block] * len(dtypes),
        out_shape=[jax.ShapeDtypeStruct(shard.shape, dtype) for dtype in dtypes],
        compiler_params=pltpu.CompilerParams(vmem_limit_bytes=LITTLE),
        cost_estimate=CHEAP,
        name="states" if states else "update",
    )(total, shard, param, first, second)


def behind_of(value, other, cost=CHEAP):
    return pl.pallas_call(
        lambda *refs: None,
        grid=(1,),
        in_specs=[pl.BlockSpec(memory_space=pl.ANY), pl.BlockSpec((PAD, 128), lambda i: (0, 0))],
        out_specs=pl.BlockSpec(memory_space=pl.ANY),
        out_shape=jax.ShapeDtypeStruct(value.shape, value.dtype),
        input_output_aliases={0: 0},
        compiler_params=pltpu.CompilerParams(vmem_limit_bytes=LITTLE),
        cost_estimate=cost,
        name="behind",
    )(value, other)


def both_of(own, other, after, rows, cut):
    columns = own.shape[1]
    steps = cut // rows

    def kernel(own_ref, other_ref, after_ref, both_ref):
        both_ref[...] = jnp.where(pl.program_id(0) < steps, own_ref[...], other_ref[...])

    return pl.pallas_call(
        kernel,
        grid=(2 * steps,),
        in_specs=[
            pl.BlockSpec((rows, columns), lambda i: (jnp.minimum(i, steps - 1), 0)),
            pl.BlockSpec((rows, columns), lambda i: (jnp.maximum(i - steps, 0), 0)),
            pl.BlockSpec((PAD, 128), lambda i: (0, 0)),
        ],
        out_specs=pl.BlockSpec((rows, columns), lambda i: (i, 0)),
        out_shape=jax.ShapeDtypeStruct((2 * cut, columns), own.dtype),
        compiler_params=pltpu.CompilerParams(vmem_limit_bytes=LITTLE),
        cost_estimate=PIECE,
        name="both",
    )(own, other, after)


def fill_kernel(moves, count, *refs):
    out, sems = refs[-2:]
    r = lax.axis_index("dp")
    copies = []
    for at, (source, low, size, table, shard, first) in enumerate(moves):
        to = pl.multiple_of(lookup(table, r) * shard + first, PAD)
        copies.append(pltpu.make_async_copy(refs[source].at[low : low + size], out.at[pl.ds(to, size)], sems.at[at]))
        copies[-1].start()
    for copy in copies:
        copy.wait()


def fill(buffer, values, moves, height):
    columns = values[0].shape[1]
    return pl.pallas_call(
        lambda *refs: fill_kernel(moves, len(values), *refs),
        in_specs=[pl.BlockSpec(memory_space=pltpu.VMEM)] * len(values)
        + [pl.BlockSpec(memory_space=pltpu.HBM)] * (buffer is not None),
        out_specs=pl.BlockSpec(memory_space=pltpu.HBM),
        out_shape=jax.ShapeDtypeStruct((height, columns), values[0].dtype),
        input_output_aliases={} if buffer is None else {len(values): 0},
        scratch_shapes=[pltpu.SemaphoreType.DMA((len(moves),))],
        compiler_params=pltpu.CompilerParams(vmem_limit_bytes=LITTLE),
        cost_estimate=CHEAP,
        name="fill",
    )(*values, *([] if buffer is None else [buffer]))


def paired(weights, inputs, out_grads, master, moment1, moment2):
    n = lax.axis_size("dp")
    pairs = n // 2
    ring = list(range(0, pairs, 2)) + list(range(pairs - 1 - pairs % 2, 0, -2))
    place = {pair: at for at, pair in enumerate(ring)}

    def at_offset(r, offset, flip):
        return 2 * ring[(place[r // 2] + offset) % pairs] + ((r % 2) ^ flip)

    def table(offset, flip):
        return [at_offset(r, offset, flip) for r in range(n)]

    def send(value, offset, flip=0):
        return lax.ppermute(value, "dp", [(r, at_offset(r, offset, flip)) for r in range(n)])

    stacked = weights[0]
    x, dy = inputs[0], out_grads[0]
    width = x.shape[1]
    shard_rows = stacked.shape[0] // n
    rows = math.gcd(shard_rows, width, 256)

    steps = shard_rows // rows

    every, most, rest, end = list(range(steps)), list(range(steps - 1)), list(range(1, steps)), steps - 1

    def at(*blocks):
        return [(table(offset, flip), block) for offset, flip, block in blocks]

    def made(blocks, got=(), **more):
        return piece(x, dy, factors, rows, blocks, got, **more)

    factors, message = forward(x, dy, stacked, at(*[(2, 1, b) for b in every]), rows)
    cross_far = send(message, 0, 1)
    message = made(at((-1, 0, end), (-1, 1, end)))
    ahead = send(message, -1)
    message = made(at(*[(-1, 1, b) for b in most]), after=message)
    cross_back = send(message, 0, 1)
    message = made(at(*[(1, 1, b) for b in every]), after=message)
    cross_next = send(message, 0, 1)
    third = message
    message = made(at(*[(0, 1, b) for b in every]), [(ahead, [None] * end + [1])], after=message)
    cross_own = send(message, 0, 1)

    by_ring = send(made(at(*[(2, 0, b) for b in every]), [(cross_far, every)], after=third), 1)
    from_ahead = send(made(at(*[(-1, 0, b) for b in most]), [(cross_back, most)]), -1)
    from_behind = send(join(made(at(*[(1, 0, b) for b in every]), [(by_ring, every)], last=True), cross_next, rows), 1)
    partial = made(at(*[(0, 0, b) for b in every]), [(from_ahead, most + [None]), (ahead, [None] * end + [0])], last=True)
    shard, squares = finish(partial, [cross_own, from_behind], rows, n * lax.axis_size("section"))

    total = lax.all_to_all(squares, ("dp", "section"), 0, 0, tiled=True)
    max_norm = math.sqrt(lax.axis_size("section") * stacked.size)
    states = (shard, master[0], moment1[0], moment2[0], max_norm, rows)
    (own,) = update(total, *states, False)

    cut = shard_rows - rows
    other = send(own, 0, 1)
    behind = behind_of(send(own, 1), other)
    tail = send(own[cut:], -1)
    behind_cross = send(behind, 0, 1)
    far = send(behind, 1)
    tail = behind_of(tail, behind, cost_of(3.4))
    tail_cross = send(tail, 0, 1)
    both = send(both_of(own, other, behind_cross, rows, cut), -1)
    far = behind_of(behind_of(far, behind_cross), tail_cross)
    far_cross = send(far, 0, 1)
    new_param, new_first, new_second = update(total, *states, True)

    def move(value, offset, flip, low=0, first=0, size=shard_rows):
        return (value, low, size, table(offset, flip), shard_rows, first)

    gathered = fill(
        None,
        [own, other, behind, tail, behind_cross, tail_cross, far],
        [
            move(0, 0, 0),
            move(1, 0, 1),
            move(2, -1, 0),
            move(3, 1, 0, 0, cut, rows),
            move(4, -1, 1),
            move(5, 1, 1, 0, cut, rows),
            move(6, -2, 0),
        ],
        stacked.shape[0],
    )
    gathered = fill(
        gathered,
        [both, far_cross],
        [move(0, 1, 0, 0, 0, cut), move(0, 1, 1, cut, 0, cut), move(1, -2, 1)],
        stacked.shape[0],
    )
    return new_param[None], new_first[None], new_second[None], gathered[None]


def local(weights, *rest):
    n = lax.axis_size("dp")
    height = weights.shape[1]
    shard, width = height // n, height // 3
    fits = n == 8 and height % n == 0 and math.gcd(shard, width, 256) % 128 == 0 and shard // math.gcd(shard, width, 256) > 2
    return (paired if fits else plain)(weights, *rest)


def solution(mesh):
    whole = P("section", None, None)
    split = P("section", "dp", None)
    return jax.shard_map(
        local,
        mesh=mesh,
        in_specs=(whole, split, split, split, split, split),
        out_specs=(split, split, split, whole),
        check_vma=False,
    )
```

```python
import math

import jax
import jax.numpy as jnp
from jax import lax
from jax.experimental import pallas as pl
from jax.experimental.pallas import tpu as pltpu
from jax.sharding import PartitionSpec as P

MROWS = 256
STEP = 10
LITTLE = 16 << 20
CHUNK = 32
PAD = 16
POWER = 8
TOP = 32768.0


def cost_of(micros):
    return pl.CostEstimate(flops=int(micros * 1.18e9), bytes_accessed=1024, transcendentals=0)


PIECE = cost_of(1.7)
CHEAP = pl.CostEstimate(flops=1024, bytes_accessed=1024, transcendentals=0)


def forward_pieces(x_rows, dy_rows, w_gate, w_up, w_down):
    pre_gate = jnp.dot(x_rows, w_gate, preferred_element_type=jnp.float32)
    pre_up = jnp.dot(x_rows, w_up, preferred_element_type=jnp.float32)
    d_hidden = jnp.dot(dy_rows, w_down, preferred_element_type=jnp.float32)
    return activation(pre_gate, pre_up, d_hidden)


def activation(pre_gate, pre_up, d_hidden):
    sigma = jax.nn.sigmoid(pre_gate)
    silu_val = pre_gate * sigma
    hidden = (silu_val * pre_up).astype(jnp.bfloat16)
    d_gate = (d_hidden * pre_up * sigma * (1.0 + pre_gate * (1.0 - sigma))).astype(jnp.bfloat16)
    d_up = (d_hidden * silu_val).astype(jnp.bfloat16)
    return d_gate, d_up, hidden


def block_grads(x_rows, dy_rows, w_gate, w_up, w_down):
    d_gate, d_up, hidden = forward_pieces(x_rows, dy_rows, w_gate, w_up, w_down)
    g_gate = jnp.dot(x_rows.T, d_gate, preferred_element_type=jnp.float32)
    g_up = jnp.dot(x_rows.T, d_up, preferred_element_type=jnp.float32)
    g_down = jnp.dot(dy_rows.T, hidden, preferred_element_type=jnp.float32)
    return jnp.concatenate([g_gate, g_up, g_down], axis=0)


def adam(clip, shard, old_param, first, second):
    clipped = clip * shard
    new_first = 0.9 * first + 0.1 * clipped
    new_second = 0.95 * second + 0.05 * clipped * clipped
    first_fix = 1.0 / (1.0 - 0.9**STEP)
    second_fix = 1.0 / (1.0 - 0.95**STEP)
    update = new_first * first_fix / (jnp.sqrt(new_second * second_fix) + 1e-08) + 0.1 * old_param
    return old_param - 0.01 * update, new_first, new_second


def clip_of(total, max_norm):
    return jnp.minimum(jnp.float32(1.0), max_norm / (jnp.sqrt(total) + 1e-06))


def plain(weights, inputs, out_grads, master, moment1, moment2):
    stacked = weights[0]
    width = stacked.shape[0] // 3
    local_grad = jnp.zeros(stacked.shape, jnp.float32)
    for start in range(0, inputs.shape[1], MROWS):
        x_rows = inputs[0, start : start + MROWS]
        dy_rows = out_grads[0, start : start + MROWS]
        local_grad = local_grad + block_grads(
            x_rows, dy_rows, stacked[:width], stacked[width : 2 * width], stacked[2 * width :]
        )
    shard = lax.psum_scatter(local_grad, "dp", scatter_dimension=0, tiled=True)
    total = lax.psum(jnp.sum(shard * shard), ("dp", "section"))
    max_norm = jnp.sqrt(jnp.float32(lax.axis_size("section") * stacked.size))
    new_param, new_first, new_second = adam(clip_of(total, max_norm), shard, master[0], moment1[0], moment2[0])
    gathered = lax.all_gather(new_param.astype(jnp.bfloat16), "dp", axis=0, tiled=True)
    return new_param[None], new_first[None], new_second[None], gathered[None]


def chunks(rows):
    return [slice(at, min(at + CHUNK, rows)) for at in range(0, rows, CHUNK)]


def fold(value):
    return jnp.max(jnp.abs(value).reshape(-1, 8, value.shape[1]), axis=0)


def scale_of(top):
    scale = jnp.max(top, axis=0, keepdims=True)
    return jnp.maximum(scale, 1e-30).astype(jnp.bfloat16).astype(jnp.float32)


def encode(value, factor):
    v = value * factor
    v2 = v * v
    v4 = v2 * v2
    v8 = v4 * v4
    return jnp.where(v < 0.0, -v8, v8).astype(jnp.bfloat16)


def decode(code, factor):
    code = code.astype(jnp.float32)
    size = jnp.abs(code)
    root = jnp.exp(jnp.log(jnp.maximum(size, 1e-37)) * (1.0 / POWER)) * factor
    root = jnp.where(size > 0.0, root, 0.0)
    return jnp.where(code < 0.0, -root, root)


def write_codes(total_ref, top, out_ref, first):
    scale = scale_of(top)
    factor = TOP / scale
    for part in chunks(total_ref.shape[0]):
        size = part.stop - part.start
        out_ref[pl.ds(first + part.start, size), :] = encode(total_ref[part, :], factor)
    return scale


def lookup(table, index):
    bits = max(max(table).bit_length(), 1)
    if bits * len(table) < 32:
        packed = sum(value << (bits * at) for at, value in enumerate(table))
        return jnp.bitwise_and(jnp.right_shift(jnp.int32(packed), index * bits), (1 << bits) - 1)
    out = jnp.int32(table[0])
    for at, value in enumerate(table[1:], 1):
        out = jnp.where(index == at, jnp.int32(value), out)
    return out


def forward_kernel(messages, rows, x_hbm, dy_hbm, w_hbm, factors_ref, *refs):
    outs = refs[: len(messages)]
    x_ref, dy_ref, w_ref, a_ref, b_ref, h_ref, total_ref, sems = refs[len(messages) :]
    width = x_hbm.shape[1]
    half = width // 2

    def fetch(at, source, target, index):
        copy = pltpu.make_async_copy(source.at[index], target.at[index], sems.at[at])
        copy.start()
        return copy

    copies = []
    for columns in (pl.ds(0, half), pl.ds(half, half)):
        copies.append(fetch(len(copies), x_hbm, x_ref, (slice(None), columns)))
        copies.append(fetch(len(copies), w_hbm, w_ref, columns))
        copies.append(fetch(len(copies), w_hbm, w_ref, pl.ds(columns.start + width, half)))
    for columns in (pl.ds(0, half), pl.ds(half, half)):
        copies.append(fetch(len(copies), dy_hbm, dy_ref, (slice(None), columns)))
        copies.append(fetch(len(copies), w_hbm, w_ref, pl.ds(columns.start + 2 * width, half)))

    def product(left, start, which):
        weight = w_ref[which * width + start : which * width + start + half]
        return jnp.dot(left[:, start : start + half], weight, preferred_element_type=jnp.float32)

    for copy in copies[:3]:
        copy.wait()
    a_ref[...] = product(x_ref, 0, 0)
    b_ref[...] = product(x_ref, 0, 1)
    for copy in copies[3:6]:
        copy.wait()
    a_ref[...] += product(x_ref, half, 0)
    b_ref[...] += product(x_ref, half, 1)
    for copy in copies[6:8]:
        copy.wait()
    h_ref[...] = product(dy_ref, 0, 2)
    for copy in copies[8:]:
        copy.wait()
    h_ref[...] += product(dy_ref, half, 2)
    for part in chunks(x_ref.shape[0]):
        d_gate, d_up, hidden = activation(a_ref[part, :], b_ref[part, :], h_ref[part, :])
        factors_ref[0, part, :] = d_gate
        factors_ref[1, part, :] = d_up
        factors_ref[2, part, :] = hidden
    per = width // rows
    for places, out_ref in zip(messages, outs):
        scales = jnp.zeros((PAD, out_ref.shape[1]), jnp.float32)
        for step, place in enumerate(places):
            at = place()
            kind = lax.div(at, per)
            column = pl.ds(pl.multiple_of(lax.rem(at, per) * rows, rows), rows)
            left = jnp.where(kind == 2, dy_ref[:, column], x_ref[:, column])
            total_ref[...] = lax.dot_general(
                left, factors_ref[kind], (((0,), (0,)), ((), ())), preferred_element_type=jnp.float32
            )
            top = fold(total_ref[:CHUNK, :])
            for part in chunks(rows)[1:]:
                top = jnp.maximum(top, fold(total_ref[part, :]))
            scale = write_codes(total_ref, top, out_ref, step * rows)
            row = lax.broadcasted_iota(jnp.int32, scales.shape, 0)
            scales = jnp.where(row == step, scale, scales)
        out_ref[len(places) * rows :, :] = scales.astype(jnp.bfloat16)


def forward(x, dy, stacked, messages, rows):
    tokens, width = x.shape
    hidden = stacked.shape[1]

    def place_of(table, block):
        steps = stacked.shape[0] // len(table) // rows
        return lambda: lookup(table, lax.axis_index("dp")) * steps + block

    places = [[place_of(*block) for block in blocks] for blocks in messages]
    return pl.pallas_call(
        lambda *refs: forward_kernel(places, rows, *refs),
        in_specs=[pl.BlockSpec(memory_space=pltpu.HBM)] * 3,
        out_shape=[jax.ShapeDtypeStruct((3, tokens, hidden), jnp.bfloat16)]
        + [jax.ShapeDtypeStruct((len(blocks) * rows + PAD, hidden), jnp.bfloat16) for blocks in messages],
        scratch_shapes=[
            pltpu.VMEM(x.shape, x.dtype),
            pltpu.VMEM(dy.shape, dy.dtype),
            pltpu.VMEM(stacked.shape, stacked.dtype),
            *[pltpu.VMEM((tokens, hidden), jnp.float32)] * 3,
            pltpu.VMEM((rows, hidden), jnp.float32),
            pltpu.SemaphoreType.DMA((10,)),
        ],
        compiler_params=pltpu.CompilerParams(vmem_limit_bytes=60 << 20),
        cost_estimate=CHEAP,
        name="forward",
    )(x, dy, stacked)


def pick(values, step):
    if all(value == values[0] + at for at, value in enumerate(values)):
        return step + values[0] if len(values) > 1 else jnp.int32(values[0])
    out = jnp.int32(values[0])
    for at, value in enumerate(values[1:], 1):
        out = jnp.where(step == at, value, out)
    return out


def piece_kernel(place, per, got, extra, last, *refs):
    step = pl.program_id(0)
    x_ref, dy_ref, d_ref = refs[:3]
    outs = refs[3 + 2 * len(got) + extra :]
    rows = x_ref.shape[1]
    left = jnp.where(lax.div(place(step), per) == 2, dy_ref[...], x_ref[...])
    total_ref = outs[-1]
    total_ref[...] = lax.dot_general(left, d_ref[0], (((0,), (0,)), ((), ())), preferred_element_type=jnp.float32)
    factors = []
    for at, blocks in enumerate(got):
        scales = refs[4 + 2 * at][...].astype(jnp.float32)
        row = lax.broadcasted_iota(jnp.int32, scales.shape, 0)
        here = pick([PAD if block is None else block for block in blocks], step)
        factors.append(jnp.sum(jnp.where(row == here, scales, 0.0), axis=0, keepdims=True) * (1.0 / TOP))
    top = jnp.zeros((8, total_ref.shape[1]), jnp.float32)
    for part in chunks(rows):
        total = total_ref[part, :]
        for at, factor in enumerate(factors):
            total = total + decode(refs[3 + 2 * at][part, :], factor)
        if last:
            outs[0][part, :] = total
        else:
            if factors:
                total_ref[part, :] = total
            top = jnp.maximum(top, fold(total))
    if not last:
        out_ref, scales_ref = outs[:2]
        scale = write_codes(total_ref, top, out_ref, pl.multiple_of(step * rows, rows))
        row = lax.broadcasted_iota(jnp.int32, scales_ref.shape, 0)
        scales_ref[...] = jnp.where(row == step, scale, jnp.where(step == 0, 0.0, scales_ref[...]))
        out_ref[pl.ds(out_ref.shape[0] - PAD, PAD), :] = scales_ref[...].astype(jnp.bfloat16)


def piece(x, dy, factors, rows, blocks, got=(), after=None, last=False, cost=PIECE):
    tokens, width = x.shape
    hidden = factors.shape[2]
    per = width // rows
    shard = 3 * width // len(blocks[0][0])
    steps = shard // rows
    tables = [table for table, _ in blocks]
    within = [block for _, block in blocks]

    def place(i):
        r = lax.axis_index("dp")
        owner = lookup(tables[0], r)
        for at, table in enumerate(tables[1:], 1):
            if table != tables[at - 1]:
                owner = jnp.where(i >= at, lookup(table, r), owner)
        return owner * steps + pick(within, i)

    def column(i):
        return (0, lax.rem(place(i), per))

    in_specs = [
        pl.BlockSpec((tokens, rows), column),
        pl.BlockSpec((tokens, rows), column),
        pl.BlockSpec((1, tokens, hidden), lambda i: (lax.div(place(i), per), 0, 0)),
    ]
    operands = [x, dy, factors]
    for message, parts in got:
        present = [part for part in parts if part is not None]
        nearest = [present[0] if part is None else part for part in parts]
        scales = (message.shape[0] - PAD) // PAD
        in_specs += [
            pl.BlockSpec((rows, hidden), lambda i, nearest=nearest: (pick(nearest, i), 0)),
            pl.BlockSpec((PAD, hidden), lambda i, scales=scales: (scales, 0)),
        ]
        operands += [message, message]
    extra = 0
    if after is not None:
        extra = 1
        operands.append(after)
        in_specs.append(pl.BlockSpec(memory_space=pl.ANY))
    if last:
        out_specs = pl.BlockSpec((rows, hidden), lambda i: (i, 0))
        out_shape = jax.ShapeDtypeStruct((len(blocks) * rows, hidden), jnp.float32)
        scratch = [pltpu.VMEM((rows, hidden), jnp.float32)]
    else:
        out_specs = pl.BlockSpec((len(blocks) * rows + PAD, hidden), lambda i: (0, 0))
        out_shape = jax.ShapeDtypeStruct((len(blocks) * rows + PAD, hidden), jnp.bfloat16)
        scratch = [pltpu.VMEM((PAD, hidden), jnp.float32), pltpu.VMEM((rows, hidden), jnp.float32)]
    return pl.pallas_call(
        lambda *refs: piece_kernel(place, per, [parts for _, parts in got], extra, last, *refs),
        grid=(len(blocks),),
        in_specs=in_specs,
        out_specs=out_specs,
        out_shape=out_shape,
        scratch_shapes=scratch,
        compiler_params=pltpu.CompilerParams(vmem_limit_bytes=LITTLE),
        cost_estimate=cost,
        name="piece",
    )(*operands)


def finish_kernel(sum_ref, *refs):
    step = pl.program_id(0)
    out_ref, squares_ref = refs[-2:]
    factors = []
    for scales_ref in refs[1:-2:2]:
        scales = scales_ref[...].astype(jnp.float32)
        row = lax.broadcasted_iota(jnp.int32, scales.shape, 0)
        factors.append(jnp.sum(jnp.where(row == step, scales, 0.0), axis=0, keepdims=True) * (1.0 / TOP))
    top = jnp.zeros((8, out_ref.shape[1]), jnp.float32)
    for part in chunks(out_ref.shape[0]):
        total = sum_ref[part, :]
        for code_ref, factor in zip(refs[:-2:2], factors):
            total = total + decode(code_ref[part, :], factor)
        out_ref[part, :] = total
        top = top + jnp.sum((total * total).reshape(-1, 8, total.shape[1]), axis=0)
    row = jnp.sum(sum(top[:, at : at + 128] for at in range(0, top.shape[1], 128)), axis=0, keepdims=True)
    squares_ref[...] = jnp.broadcast_to(row, squares_ref.shape) + jnp.where(step == 0, 0.0, squares_ref[...])


def finish(partial, messages, rows, count):
    height, hidden = partial.shape
    block = pl.BlockSpec((rows, hidden), lambda i: (i, 0))
    scales = pl.BlockSpec((PAD, hidden), lambda i: (height // PAD, 0))
    return pl.pallas_call(
        finish_kernel,
        grid=(height // rows,),
        in_specs=[block] + [block, scales] * len(messages),
        out_specs=[block, pl.BlockSpec((count, 128), lambda i: (0, 0))],
        out_shape=[
            jax.ShapeDtypeStruct(partial.shape, jnp.float32),
            jax.ShapeDtypeStruct((count, 128), jnp.float32),
        ],
        compiler_params=pltpu.CompilerParams(vmem_limit_bytes=LITTLE),
        cost_estimate=PIECE,
        name="finish",
    )(partial, *[m for message in messages for m in (message, message)])


def join_kernel(sum_ref, code_ref, scales_ref, out_ref, total_ref, out_scales_ref):
    step = pl.program_id(0)
    rows = sum_ref.shape[0]
    scales = scales_ref[...].astype(jnp.float32)
    row = lax.broadcasted_iota(jnp.int32, scales.shape, 0)
    factor = jnp.sum(jnp.where(row == step, scales, 0.0), axis=0, keepdims=True) * (1.0 / TOP)
    top = jnp.zeros((8, sum_ref.shape[1]), jnp.float32)
    for part in chunks(rows):
        total = sum_ref[part, :] + decode(code_ref[part, :], factor)
        total_ref[part, :] = total
        top = jnp.maximum(top, fold(total))
    scale = write_codes(total_ref, top, out_ref, pl.multiple_of(step * rows, rows))
    out_scales_ref[...] = jnp.where(row == step, scale, jnp.where(step == 0, 0.0, out_scales_ref[...]))
    out_ref[pl.ds(out_ref.shape[0] - PAD, PAD), :] = out_scales_ref[...].astype(jnp.bfloat16)


def join(partial, message, rows):
    height, hidden = partial.shape
    block = pl.BlockSpec((rows, hidden), lambda i: (i, 0))
    return pl.pallas_call(
        join_kernel,
        grid=(height // rows,),
        in_specs=[block, block, pl.BlockSpec((PAD, hidden), lambda i: (height // PAD, 0))],
        out_specs=pl.BlockSpec(message.shape, lambda i: (0, 0)),
        out_shape=jax.ShapeDtypeStruct(message.shape, message.dtype),
        scratch_shapes=[pltpu.VMEM((rows, hidden), jnp.float32), pltpu.VMEM((PAD, hidden), jnp.float32)],
        compiler_params=pltpu.CompilerParams(vmem_limit_bytes=LITTLE),
        cost_estimate=PIECE,
        name="join",
    )(partial, message, message)


def update_kernel(max_norm, states, total_ref, g_ref, p_ref, m1_ref, m2_ref, *outs):
    clip = clip_of(jnp.sum(total_ref[...], keepdims=True), max_norm)
    for part in chunks(g_ref.shape[0]):
        param, first, second = adam(clip, g_ref[part, :], p_ref[part, :], m1_ref[part, :], m2_ref[part, :])
        values = (param, first, second) if states else (param.astype(jnp.bfloat16),)
        for out, value in zip(outs, values):
            out[part, :] = value


def update(total, shard, param, first, second, max_norm, rows, states):
    block = pl.BlockSpec((rows, shard.shape[1]), lambda i: (i, 0))
    dtypes = [jnp.float32] * 3 if states else [jnp.bfloat16]
    return pl.pallas_call(
        lambda *refs: update_kernel(max_norm, states, *refs),
        grid=(shard.shape[0] // rows,),
        in_specs=[pl.BlockSpec(total.shape, lambda i: (0, 0))] + [block] * 4,
        out_specs=[block] * len(dtypes),
        out_shape=[jax.ShapeDtypeStruct(shard.shape, dtype) for dtype in dtypes],
        compiler_params=pltpu.CompilerParams(vmem_limit_bytes=LITTLE),
        cost_estimate=CHEAP,
        name="states" if states else "update",
    )(total, shard, param, first, second)


def behind_of(value, other, cost=CHEAP):
    return pl.pallas_call(
        lambda *refs: None,
        grid=(1,),
        in_specs=[pl.BlockSpec(memory_space=pl.ANY), pl.BlockSpec((PAD, 128), lambda i: (0, 0))],
        out_specs=pl.BlockSpec(memory_space=pl.ANY),
        out_shape=jax.ShapeDtypeStruct(value.shape, value.dtype),
        input_output_aliases={0: 0},
        compiler_params=pltpu.CompilerParams(vmem_limit_bytes=LITTLE),
        cost_estimate=cost,
        name="behind",
    )(value, other)


def both_of(own, other, after, rows, cut):
    columns = own.shape[1]
    steps = cut // rows

    def kernel(own_ref, other_ref, after_ref, both_ref):
        both_ref[...] = jnp.where(pl.program_id(0) < steps, own_ref[...], other_ref[...])

    return pl.pallas_call(
        kernel,
        grid=(2 * steps,),
        in_specs=[
            pl.BlockSpec((rows, columns), lambda i: (jnp.minimum(i, steps - 1), 0)),
            pl.BlockSpec((rows, columns), lambda i: (jnp.maximum(i - steps, 0), 0)),
            pl.BlockSpec((PAD, 128), lambda i: (0, 0)),
        ],
        out_specs=pl.BlockSpec((rows, columns), lambda i: (i, 0)),
        out_shape=jax.ShapeDtypeStruct((2 * cut, columns), own.dtype),
        compiler_params=pltpu.CompilerParams(vmem_limit_bytes=LITTLE),
        cost_estimate=PIECE,
        name="both",
    )(own, other, after)


def fill_kernel(moves, count, *refs):
    out, sems = refs[-2:]
    r = lax.axis_index("dp")
    copies = []
    for at, (source, low, size, table, shard, first) in enumerate(moves):
        to = pl.multiple_of(lookup(table, r) * shard + first, PAD)
        copies.append(pltpu.make_async_copy(refs[source].at[low : low + size], out.at[pl.ds(to, size)], sems.at[at]))
        copies[-1].start()
    for copy in copies:
        copy.wait()


def fill(buffer, values, moves, height):
    columns = values[0].shape[1]
    return pl.pallas_call(
        lambda *refs: fill_kernel(moves, len(values), *refs),
        in_specs=[pl.BlockSpec(memory_space=pltpu.VMEM)] * len(values)
        + [pl.BlockSpec(memory_space=pltpu.HBM)] * (buffer is not None),
        out_specs=pl.BlockSpec(memory_space=pltpu.HBM),
        out_shape=jax.ShapeDtypeStruct((height, columns), values[0].dtype),
        input_output_aliases={} if buffer is None else {len(values): 0},
        scratch_shapes=[pltpu.SemaphoreType.DMA((len(moves),))],
        compiler_params=pltpu.CompilerParams(vmem_limit_bytes=LITTLE),
        cost_estimate=CHEAP,
        name="fill",
    )(*values, *([] if buffer is None else [buffer]))


def paired(weights, inputs, out_grads, master, moment1, moment2):
    n = lax.axis_size("dp")
    pairs = n // 2
    ring = list(range(0, pairs, 2)) + list(range(pairs - 1 - pairs % 2, 0, -2))
    place = {pair: at for at, pair in enumerate(ring)}

    def at_offset(r, offset, flip):
        return 2 * ring[(place[r // 2] + offset) % pairs] + ((r % 2) ^ flip)

    def table(offset, flip):
        return [at_offset(r, offset, flip) for r in range(n)]

    def send(value, offset, flip=0):
        return lax.ppermute(value, "dp", [(r, at_offset(r, offset, flip)) for r in range(n)])

    stacked = weights[0]
    x, dy = inputs[0], out_grads[0]
    width = x.shape[1]
    shard_rows = stacked.shape[0] // n
    rows = math.gcd(shard_rows, width, 256)

    steps = shard_rows // rows

    every, most, rest, end = list(range(steps)), list(range(steps - 1)), list(range(1, steps)), steps - 1

    def at(*blocks):
        return [(table(offset, flip), block) for offset, flip, block in blocks]

    def made(blocks, got=(), **more):
        return piece(x, dy, factors, rows, blocks, got, **more)

    factors, message = forward(x, dy, stacked, [at(*[(2, 1, b) for b in every])], rows)
    cross_far = send(message, 0, 1)
    message = made(at((-1, 0, end), (-1, 1, end)))
    ahead = send(message, -1)
    message = made(at(*[(-1, 1, b) for b in most]), after=message)
    cross_back = send(message, 0, 1)
    own_far = made(at(*[(2, 0, b) for b in every]), after=message, last=True)
    message = made(at(*[(1, 1, b) for b in every]), after=own_far)
    cross_next = send(message, 0, 1)
    message = made(at(*[(0, 1, b) for b in every]), [(ahead, [None] * end + [1])], after=message)
    cross_own = send(message, 0, 1)

    by_ring = send(join(own_far, cross_far, rows), 1)
    from_ahead = send(made(at(*[(-1, 0, b) for b in most]), [(cross_back, most)]), -1)
    from_behind = send(join(made(at(*[(1, 0, b) for b in every]), [(by_ring, every)], last=True), cross_next, rows), 1)
    partial = made(at(*[(0, 0, b) for b in every]), [(from_ahead, most + [None]), (ahead, [None] * end + [0])], last=True)
    shard, squares = finish(partial, [cross_own, from_behind], rows, n * lax.axis_size("section"))

    total = lax.all_to_all(squares, ("dp", "section"), 0, 0, tiled=True)
    max_norm = math.sqrt(lax.axis_size("section") * stacked.size)
    states = (shard, master[0], moment1[0], moment2[0], max_norm, rows)
    (own,) = update(total, *states, False)

    cut = shard_rows - rows
    other = send(own, 0, 1)
    behind = behind_of(send(own, 1), other)
    tail = send(own[cut:], -1)
    behind_cross = send(behind, 0, 1)
    far = send(behind, 1)
    tail = behind_of(tail, behind, cost_of(3.4))
    tail_cross = send(tail, 0, 1)
    both = send(both_of(own, other, behind_cross, rows, cut), -1)
    far = behind_of(behind_of(far, behind_cross), tail_cross)
    far_cross = send(far, 0, 1)
    new_param, new_first, new_second = update(total, *states, True)

    def move(value, offset, flip, low=0, first=0, size=shard_rows):
        return (value, low, size, table(offset, flip), shard_rows, first)

    gathered = fill(
        None,
        [own, other, behind, tail, behind_cross, tail_cross, far],
        [
            move(0, 0, 0),
            move(1, 0, 1),
            move(2, -1, 0),
            move(3, 1, 0, 0, cut, rows),
            move(4, -1, 1),
            move(5, 1, 1, 0, cut, rows),
            move(6, -2, 0),
        ],
        stacked.shape[0],
    )
    gathered = fill(
        gathered,
        [both, far_cross],
        [move(0, 1, 0, 0, 0, cut), move(0, 1, 1, cut, 0, cut), move(1, -2, 1)],
        stacked.shape[0],
    )
    return new_param[None], new_first[None], new_second[None], gathered[None]


def local(weights, *rest):
    n = lax.axis_size("dp")
    height = weights.shape[1]
    shard, width = height // n, height // 3
    fits = n == 8 and height % n == 0 and math.gcd(shard, width, 256) % 128 == 0 and shard // math.gcd(shard, width, 256) > 2
    return (paired if fits else plain)(weights, *rest)


def solution(mesh):
    whole = P("section", None, None)
    split = P("section", "dp", None)
    return jax.shard_map(
        local,
        mesh=mesh,
        in_specs=(whole, split, split, split, split, split),
        out_specs=(split, split, split, whole),
        check_vma=False,
    )
```

```python
import math

import jax
import jax.numpy as jnp
from jax import lax
from jax.experimental import pallas as pl
from jax.experimental.pallas import tpu as pltpu
from jax.sharding import PartitionSpec as P

MROWS = 256
STEP = 10
LITTLE = 16 << 20
CHUNK = 32
PAD = 16
POWER = 8
TOP = 32768.0


def cost_of(micros):
    return pl.CostEstimate(flops=int(micros * 1.18e9), bytes_accessed=1024, transcendentals=0)


PIECE = cost_of(1.2)
CHEAP = pl.CostEstimate(flops=1024, bytes_accessed=1024, transcendentals=0)


def forward_pieces(x_rows, dy_rows, w_gate, w_up, w_down):
    pre_gate = jnp.dot(x_rows, w_gate, preferred_element_type=jnp.float32)
    pre_up = jnp.dot(x_rows, w_up, preferred_element_type=jnp.float32)
    d_hidden = jnp.dot(dy_rows, w_down, preferred_element_type=jnp.float32)
    return activation(pre_gate, pre_up, d_hidden)


def activation(pre_gate, pre_up, d_hidden):
    sigma = jax.nn.sigmoid(pre_gate)
    silu_val = pre_gate * sigma
    hidden = (silu_val * pre_up).astype(jnp.bfloat16)
    d_gate = (d_hidden * pre_up * sigma * (1.0 + pre_gate * (1.0 - sigma))).astype(jnp.bfloat16)
    d_up = (d_hidden * silu_val).astype(jnp.bfloat16)
    return d_gate, d_up, hidden


def block_grads(x_rows, dy_rows, w_gate, w_up, w_down):
    d_gate, d_up, hidden = forward_pieces(x_rows, dy_rows, w_gate, w_up, w_down)
    g_gate = jnp.dot(x_rows.T, d_gate, preferred_element_type=jnp.float32)
    g_up = jnp.dot(x_rows.T, d_up, preferred_element_type=jnp.float32)
    g_down = jnp.dot(dy_rows.T, hidden, preferred_element_type=jnp.float32)
    return jnp.concatenate([g_gate, g_up, g_down], axis=0)


def adam(clip, shard, old_param, first, second):
    clipped = clip * shard
    new_first = 0.9 * first + 0.1 * clipped
    new_second = 0.95 * second + 0.05 * clipped * clipped
    first_fix = 1.0 / (1.0 - 0.9**STEP)
    second_fix = 1.0 / (1.0 - 0.95**STEP)
    update = new_first * first_fix / (jnp.sqrt(new_second * second_fix) + 1e-08) + 0.1 * old_param
    return old_param - 0.01 * update, new_first, new_second


def clip_of(total, max_norm):
    return jnp.minimum(jnp.float32(1.0), max_norm / (jnp.sqrt(total) + 1e-06))


def plain(weights, inputs, out_grads, master, moment1, moment2):
    stacked = weights[0]
    width = stacked.shape[0] // 3
    local_grad = jnp.zeros(stacked.shape, jnp.float32)
    for start in range(0, inputs.shape[1], MROWS):
        x_rows = inputs[0, start : start + MROWS]
        dy_rows = out_grads[0, start : start + MROWS]
        local_grad = local_grad + block_grads(
            x_rows, dy_rows, stacked[:width], stacked[width : 2 * width], stacked[2 * width :]
        )
    shard = lax.psum_scatter(local_grad, "dp", scatter_dimension=0, tiled=True)
    total = lax.psum(jnp.sum(shard * shard), ("dp", "section"))
    max_norm = jnp.sqrt(jnp.float32(lax.axis_size("section") * stacked.size))
    new_param, new_first, new_second = adam(clip_of(total, max_norm), shard, master[0], moment1[0], moment2[0])
    gathered = lax.all_gather(new_param.astype(jnp.bfloat16), "dp", axis=0, tiled=True)
    return new_param[None], new_first[None], new_second[None], gathered[None]


def chunks(rows):
    return [slice(at, min(at + CHUNK, rows)) for at in range(0, rows, CHUNK)]


def fold(value):
    return jnp.max(jnp.abs(value).reshape(-1, 8, value.shape[1]), axis=0)


def scale_of(top):
    scale = jnp.max(top, axis=0, keepdims=True)
    return jnp.maximum(scale, 1e-30).astype(jnp.bfloat16).astype(jnp.float32)


def encode(value, factor):
    v = value * factor
    v2 = v * v
    v4 = v2 * v2
    v8 = v4 * v4
    return jnp.where(v < 0.0, -v8, v8).astype(jnp.bfloat16)


def decode(code, factor):
    code = code.astype(jnp.float32)
    size = jnp.abs(code)
    root = jnp.exp(jnp.log(jnp.maximum(size, 1e-37)) * (1.0 / POWER)) * factor
    root = jnp.where(size > 0.0, root, 0.0)
    return jnp.where(code < 0.0, -root, root)


def write_codes(total_ref, top, out_ref, first):
    scale = scale_of(top)
    factor = TOP / scale
    for part in chunks(total_ref.shape[0]):
        size = part.stop - part.start
        out_ref[pl.ds(first + part.start, size), :] = encode(total_ref[part, :], factor)
    return scale


def lookup(table, index):
    bits = max(max(table).bit_length(), 1)
    if bits * len(table) < 32:
        packed = sum(value << (bits * at) for at, value in enumerate(table))
        return jnp.bitwise_and(jnp.right_shift(jnp.int32(packed), index * bits), (1 << bits) - 1)
    out = jnp.int32(table[0])
    for at, value in enumerate(table[1:], 1):
        out = jnp.where(index == at, jnp.int32(value), out)
    return out


def forward_kernel(messages, rows, x_hbm, dy_hbm, w_hbm, factors_ref, *refs):
    outs = refs[: len(messages)]
    x_ref, dy_ref, w_ref, a_ref, b_ref, h_ref, total_ref, sems = refs[len(messages) :]
    width = x_hbm.shape[1]
    half = width // 2

    def fetch(at, source, target, index):
        copy = pltpu.make_async_copy(source.at[index], target.at[index], sems.at[at])
        copy.start()
        return copy

    copies = []
    for columns in (pl.ds(0, half), pl.ds(half, half)):
        copies.append(fetch(len(copies), x_hbm, x_ref, (slice(None), columns)))
        copies.append(fetch(len(copies), w_hbm, w_ref, columns))
        copies.append(fetch(len(copies), w_hbm, w_ref, pl.ds(columns.start + width, half)))
    for columns in (pl.ds(0, half), pl.ds(half, half)):
        copies.append(fetch(len(copies), dy_hbm, dy_ref, (slice(None), columns)))
        copies.append(fetch(len(copies), w_hbm, w_ref, pl.ds(columns.start + 2 * width, half)))

    def product(left, start, which):
        weight = w_ref[which * width + start : which * width + start + half]
        return jnp.dot(left[:, start : start + half], weight, preferred_element_type=jnp.float32)

    for copy in copies[:3]:
        copy.wait()
    a_ref[...] = product(x_ref, 0, 0)
    b_ref[...] = product(x_ref, 0, 1)
    for copy in copies[3:6]:
        copy.wait()
    a_ref[...] += product(x_ref, half, 0)
    b_ref[...] += product(x_ref, half, 1)
    for copy in copies[6:8]:
        copy.wait()
    h_ref[...] = product(dy_ref, 0, 2)
    for copy in copies[8:]:
        copy.wait()
    h_ref[...] += product(dy_ref, half, 2)
    for part in chunks(x_ref.shape[0]):
        d_gate, d_up, hidden = activation(a_ref[part, :], b_ref[part, :], h_ref[part, :])
        factors_ref[0, part, :] = d_gate
        factors_ref[1, part, :] = d_up
        factors_ref[2, part, :] = hidden
    per = width // rows
    for places, out_ref in zip(messages, outs):
        scales = jnp.zeros((PAD, out_ref.shape[1]), jnp.float32)
        for step, place in enumerate(places):
            at = place()
            kind = lax.div(at, per)
            column = pl.ds(pl.multiple_of(lax.rem(at, per) * rows, rows), rows)
            left = jnp.where(kind == 2, dy_ref[:, column], x_ref[:, column])
            total_ref[...] = lax.dot_general(
                left, factors_ref[kind], (((0,), (0,)), ((), ())), preferred_element_type=jnp.float32
            )
            top = fold(total_ref[:CHUNK, :])
            for part in chunks(rows)[1:]:
                top = jnp.maximum(top, fold(total_ref[part, :]))
            scale = write_codes(total_ref, top, out_ref, step * rows)
            row = lax.broadcasted_iota(jnp.int32, scales.shape, 0)
            scales = jnp.where(row == step, scale, scales)
        out_ref[len(places) * rows :, :] = scales.astype(jnp.bfloat16)


def forward(x, dy, stacked, messages, rows):
    tokens, width = x.shape
    hidden = stacked.shape[1]

    def place_of(table, block):
        steps = stacked.shape[0] // len(table) // rows
        return lambda: lookup(table, lax.axis_index("dp")) * steps + block

    places = [[place_of(*block) for block in blocks] for blocks in messages]
    return pl.pallas_call(
        lambda *refs: forward_kernel(places, rows, *refs),
        in_specs=[pl.BlockSpec(memory_space=pltpu.HBM)] * 3,
        out_shape=[jax.ShapeDtypeStruct((3, tokens, hidden), jnp.bfloat16)]
        + [jax.ShapeDtypeStruct((len(blocks) * rows + PAD, hidden), jnp.bfloat16) for blocks in messages],
        scratch_shapes=[
            pltpu.VMEM(x.shape, x.dtype),
            pltpu.VMEM(dy.shape, dy.dtype),
            pltpu.VMEM(stacked.shape, stacked.dtype),
            *[pltpu.VMEM((tokens, hidden), jnp.float32)] * 3,
            pltpu.VMEM((rows, hidden), jnp.float32),
            pltpu.SemaphoreType.DMA((10,)),
        ],
        compiler_params=pltpu.CompilerParams(vmem_limit_bytes=60 << 20),
        cost_estimate=CHEAP,
        name="forward",
    )(x, dy, stacked)


def pick(values, step):
    if all(value == values[0] + at for at, value in enumerate(values)):
        return step + values[0] if len(values) > 1 else jnp.int32(values[0])
    out = jnp.int32(values[0])
    for at, value in enumerate(values[1:], 1):
        out = jnp.where(step == at, value, out)
    return out


def piece_kernel(place, per, got, extra, last, *refs):
    step = pl.program_id(0)
    x_ref, dy_ref, d_ref = refs[:3]
    outs = refs[3 + 2 * len(got) + extra :]
    rows = x_ref.shape[1]
    left = jnp.where(lax.div(place(step), per) == 2, dy_ref[...], x_ref[...])
    total_ref = outs[-1]
    total_ref[...] = lax.dot_general(left, d_ref[0], (((0,), (0,)), ((), ())), preferred_element_type=jnp.float32)
    factors = []
    for at, blocks in enumerate(got):
        scales = refs[4 + 2 * at][...].astype(jnp.float32)
        row = lax.broadcasted_iota(jnp.int32, scales.shape, 0)
        here = pick([PAD if block is None else block for block in blocks], step)
        factors.append(jnp.sum(jnp.where(row == here, scales, 0.0), axis=0, keepdims=True) * (1.0 / TOP))
    top = jnp.zeros((8, total_ref.shape[1]), jnp.float32)
    for part in chunks(rows):
        total = total_ref[part, :]
        for at, factor in enumerate(factors):
            total = total + decode(refs[3 + 2 * at][part, :], factor)
        if last:
            outs[0][part, :] = total
        else:
            if factors:
                total_ref[part, :] = total
            top = jnp.maximum(top, fold(total))
    if not last:
        out_ref, scales_ref = outs[:2]
        scale = write_codes(total_ref, top, out_ref, pl.multiple_of(step * rows, rows))
        row = lax.broadcasted_iota(jnp.int32, scales_ref.shape, 0)
        scales_ref[...] = jnp.where(row == step, scale, jnp.where(step == 0, 0.0, scales_ref[...]))
        out_ref[pl.ds(out_ref.shape[0] - PAD, PAD), :] = scales_ref[...].astype(jnp.bfloat16)


def piece(x, dy, factors, rows, blocks, got=(), after=None, last=False, cost=PIECE):
    tokens, width = x.shape
    hidden = factors.shape[2]
    per = width // rows
    shard = 3 * width // len(blocks[0][0])
    steps = shard // rows
    tables = [table for table, _ in blocks]
    within = [block for _, block in blocks]

    def place(i):
        r = lax.axis_index("dp")
        owner = lookup(tables[0], r)
        for at, table in enumerate(tables[1:], 1):
            if table != tables[at - 1]:
                owner = jnp.where(i >= at, lookup(table, r), owner)
        return owner * steps + pick(within, i)

    def column(i):
        return (0, lax.rem(place(i), per))

    in_specs = [
        pl.BlockSpec((tokens, rows), column),
        pl.BlockSpec((tokens, rows), column),
        pl.BlockSpec((1, tokens, hidden), lambda i: (lax.div(place(i), per), 0, 0)),
    ]
    operands = [x, dy, factors]
    for message, parts in got:
        present = [part for part in parts if part is not None]
        nearest = [present[0] if part is None else part for part in parts]
        scales = (message.shape[0] - PAD) // PAD
        in_specs += [
            pl.BlockSpec((rows, hidden), lambda i, nearest=nearest: (pick(nearest, i), 0)),
            pl.BlockSpec((PAD, hidden), lambda i, scales=scales: (scales, 0)),
        ]
        operands += [message, message]
    extra = 0
    if after is not None:
        extra = 1
        operands.append(after)
        in_specs.append(pl.BlockSpec(memory_space=pl.ANY))
    if last:
        out_specs = pl.BlockSpec((rows, hidden), lambda i: (i, 0))
        out_shape = jax.ShapeDtypeStruct((len(blocks) * rows, hidden), jnp.float32)
        scratch = [pltpu.VMEM((rows, hidden), jnp.float32)]
    else:
        out_specs = pl.BlockSpec((len(blocks) * rows + PAD, hidden), lambda i: (0, 0))
        out_shape = jax.ShapeDtypeStruct((len(blocks) * rows + PAD, hidden), jnp.bfloat16)
        scratch = [pltpu.VMEM((PAD, hidden), jnp.float32), pltpu.VMEM((rows, hidden), jnp.float32)]
    return pl.pallas_call(
        lambda *refs: piece_kernel(place, per, [parts for _, parts in got], extra, last, *refs),
        grid=(len(blocks),),
        in_specs=in_specs,
        out_specs=out_specs,
        out_shape=out_shape,
        scratch_shapes=scratch,
        compiler_params=pltpu.CompilerParams(vmem_limit_bytes=LITTLE),
        cost_estimate=cost,
        name="piece",
    )(*operands)


def finish_kernel(sum_ref, *refs):
    step = pl.program_id(0)
    out_ref, squares_ref = refs[-2:]
    factors = []
    for scales_ref in refs[1:-2:2]:
        scales = scales_ref[...].astype(jnp.float32)
        row = lax.broadcasted_iota(jnp.int32, scales.shape, 0)
        factors.append(jnp.sum(jnp.where(row == step, scales, 0.0), axis=0, keepdims=True) * (1.0 / TOP))
    top = jnp.zeros((8, out_ref.shape[1]), jnp.float32)
    for part in chunks(out_ref.shape[0]):
        total = sum_ref[part, :]
        for code_ref, factor in zip(refs[:-2:2], factors):
            total = total + decode(code_ref[part, :], factor)
        out_ref[part, :] = total
        top = top + jnp.sum((total * total).reshape(-1, 8, total.shape[1]), axis=0)
    row = jnp.sum(sum(top[:, at : at + 128] for at in range(0, top.shape[1], 128)), axis=0, keepdims=True)
    squares_ref[...] = jnp.broadcast_to(row, squares_ref.shape) + jnp.where(step == 0, 0.0, squares_ref[...])


def finish(partial, messages, rows, count):
    height, hidden = partial.shape
    block = pl.BlockSpec((rows, hidden), lambda i: (i, 0))
    scales = pl.BlockSpec((PAD, hidden), lambda i: (height // PAD, 0))
    return pl.pallas_call(
        finish_kernel,
        grid=(height // rows,),
        in_specs=[block] + [block, scales] * len(messages),
        out_specs=[block, pl.BlockSpec((count, 128), lambda i: (0, 0))],
        out_shape=[
            jax.ShapeDtypeStruct(partial.shape, jnp.float32),
            jax.ShapeDtypeStruct((count, 128), jnp.float32),
        ],
        compiler_params=pltpu.CompilerParams(vmem_limit_bytes=LITTLE),
        cost_estimate=PIECE,
        name="finish",
    )(partial, *[m for message in messages for m in (message, message)])


def join_kernel(sum_ref, code_ref, scales_ref, out_ref, total_ref, out_scales_ref):
    step = pl.program_id(0)
    rows = sum_ref.shape[0]
    scales = scales_ref[...].astype(jnp.float32)
    row = lax.broadcasted_iota(jnp.int32, scales.shape, 0)
    factor = jnp.sum(jnp.where(row == step, scales, 0.0), axis=0, keepdims=True) * (1.0 / TOP)
    top = jnp.zeros((8, sum_ref.shape[1]), jnp.float32)
    for part in chunks(rows):
        total = sum_ref[part, :] + decode(code_ref[part, :], factor)
        total_ref[part, :] = total
        top = jnp.maximum(top, fold(total))
    scale = write_codes(total_ref, top, out_ref, pl.multiple_of(step * rows, rows))
    out_scales_ref[...] = jnp.where(row == step, scale, jnp.where(step == 0, 0.0, out_scales_ref[...]))
    out_ref[pl.ds(out_ref.shape[0] - PAD, PAD), :] = out_scales_ref[...].astype(jnp.bfloat16)


def join(partial, message, rows):
    height, hidden = partial.shape
    block = pl.BlockSpec((rows, hidden), lambda i: (i, 0))
    return pl.pallas_call(
        join_kernel,
        grid=(height // rows,),
        in_specs=[block, block, pl.BlockSpec((PAD, hidden), lambda i: (height // PAD, 0))],
        out_specs=pl.BlockSpec(message.shape, lambda i: (0, 0)),
        out_shape=jax.ShapeDtypeStruct(message.shape, message.dtype),
        scratch_shapes=[pltpu.VMEM((rows, hidden), jnp.float32), pltpu.VMEM((PAD, hidden), jnp.float32)],
        compiler_params=pltpu.CompilerParams(vmem_limit_bytes=LITTLE),
        cost_estimate=PIECE,
        name="join",
    )(partial, message, message)


def update_kernel(max_norm, states, total_ref, g_ref, p_ref, m1_ref, m2_ref, *outs):
    clip = clip_of(jnp.sum(total_ref[...], keepdims=True), max_norm)
    for part in chunks(g_ref.shape[0]):
        param, first, second = adam(clip, g_ref[part, :], p_ref[part, :], m1_ref[part, :], m2_ref[part, :])
        values = (param, first, second) if states else (param.astype(jnp.bfloat16),)
        for out, value in zip(outs, values):
            out[part, :] = value


def update(total, shard, param, first, second, max_norm, rows, states):
    block = pl.BlockSpec((rows, shard.shape[1]), lambda i: (i, 0))
    dtypes = [jnp.float32] * 3 if states else [jnp.bfloat16]
    return pl.pallas_call(
        lambda *refs: update_kernel(max_norm, states, *refs),
        grid=(shard.shape[0] // rows,),
        in_specs=[pl.BlockSpec(total.shape, lambda i: (0, 0))] + [block] * 4,
        out_specs=[block] * len(dtypes),
        out_shape=[jax.ShapeDtypeStruct(shard.shape, dtype) for dtype in dtypes],
        compiler_params=pltpu.CompilerParams(vmem_limit_bytes=LITTLE),
        cost_estimate=CHEAP,
        name="states" if states else "update",
    )(total, shard, param, first, second)


def behind_of(value, other, cost=CHEAP):
    return pl.pallas_call(
        lambda *refs: None,
        grid=(1,),
        in_specs=[pl.BlockSpec(memory_space=pl.ANY), pl.BlockSpec((PAD, 128), lambda i: (0, 0))],
        out_specs=pl.BlockSpec(memory_space=pl.ANY),
        out_shape=jax.ShapeDtypeStruct(value.shape, value.dtype),
        input_output_aliases={0: 0},
        compiler_params=pltpu.CompilerParams(vmem_limit_bytes=LITTLE),
        cost_estimate=cost,
        name="behind",
    )(value, other)


def both_of(own, other, after, cut):
    columns = own.shape[1]

    def kernel(own_ref, other_ref, after_ref, both_ref):
        both_ref[...] = jnp.where(pl.program_id(0) == 0, own_ref[...], other_ref[...])

    return pl.pallas_call(
        kernel,
        grid=(2,),
        in_specs=[
            pl.BlockSpec((cut, columns), lambda i: (0, 0)),
            pl.BlockSpec((cut, columns), lambda i: (0, 0)),
            pl.BlockSpec((PAD, 128), lambda i: (0, 0)),
        ],
        out_specs=pl.BlockSpec((cut, columns), lambda i: (i, 0)),
        out_shape=jax.ShapeDtypeStruct((2 * cut, columns), own.dtype),
        compiler_params=pltpu.CompilerParams(vmem_limit_bytes=LITTLE),
        cost_estimate=PIECE,
        name="both",
    )(own, other, after)


def fill_kernel(moves, count, *refs):
    out, sems = refs[-2:]
    r = lax.axis_index("dp")
    copies = []
    for at, (source, low, size, table, shard, first) in enumerate(moves):
        to = pl.multiple_of(lookup(table, r) * shard + first, PAD)
        copies.append(pltpu.make_async_copy(refs[source].at[low : low + size], out.at[pl.ds(to, size)], sems.at[at]))
        copies[-1].start()
    for copy in copies:
        copy.wait()


def fill(buffer, values, moves, height):
    columns = values[0].shape[1]
    return pl.pallas_call(
        lambda *refs: fill_kernel(moves, len(values), *refs),
        in_specs=[pl.BlockSpec(memory_space=pltpu.VMEM)] * len(values)
        + [pl.BlockSpec(memory_space=pltpu.HBM)] * (buffer is not None),
        out_specs=pl.BlockSpec(memory_space=pltpu.HBM),
        out_shape=jax.ShapeDtypeStruct((height, columns), values[0].dtype),
        input_output_aliases={} if buffer is None else {len(values): 0},
        scratch_shapes=[pltpu.SemaphoreType.DMA((len(moves),))],
        compiler_params=pltpu.CompilerParams(vmem_limit_bytes=LITTLE),
        cost_estimate=CHEAP,
        name="fill",
    )(*values, *([] if buffer is None else [buffer]))


def paired(weights, inputs, out_grads, master, moment1, moment2):
    n = lax.axis_size("dp")
    pairs = n // 2
    ring = list(range(0, pairs, 2)) + list(range(pairs - 1 - pairs % 2, 0, -2))
    place = {pair: at for at, pair in enumerate(ring)}

    def at_offset(r, offset, flip):
        return 2 * ring[(place[r // 2] + offset) % pairs] + ((r % 2) ^ flip)

    def table(offset, flip):
        return [at_offset(r, offset, flip) for r in range(n)]

    def send(value, offset, flip=0):
        return lax.ppermute(value, "dp", [(r, at_offset(r, offset, flip)) for r in range(n)])

    stacked = weights[0]
    x, dy = inputs[0], out_grads[0]
    width = x.shape[1]
    shard_rows = stacked.shape[0] // n
    rows = math.gcd(shard_rows, width, 256)

    steps = shard_rows // rows

    every, most, rest, end = list(range(steps)), list(range(steps - 1)), list(range(1, steps)), steps - 1

    def at(*blocks):
        return [(table(offset, flip), block) for offset, flip, block in blocks]

    def made(blocks, got=(), **more):
        return piece(x, dy, factors, rows, blocks, got, **more)

    factors, message = forward(x, dy, stacked, [at(*[(2, 1, b) for b in every])], rows)
    cross_far = send(message, 0, 1)
    message = made(at((-1, 0, end), (-1, 1, end)))
    ahead = send(message, -1)
    message = made(at(*[(-1, 1, b) for b in most]), after=message)
    cross_back = send(message, 0, 1)
    message = made(at(*[(1, 1, b) for b in every]), after=message)
    own_far = made(at(*[(2, 0, b) for b in every]), after=message, last=True)
    cross_next = send(message, 0, 1)
    message = made(at(*[(0, 1, b) for b in every]), [(ahead, [None] * end + [1])], after=message)
    cross_own = send(message, 0, 1)

    by_ring = send(join(own_far, cross_far, rows), 1)
    from_ahead = send(made(at(*[(-1, 0, b) for b in most]), [(cross_back, most)]), -1)
    from_behind = send(join(made(at(*[(1, 0, b) for b in every]), [(by_ring, every)], last=True), cross_next, rows), 1)
    partial = made(at(*[(0, 0, b) for b in every]), [(from_ahead, most + [None]), (ahead, [None] * end + [0])], last=True)
    shard, squares = finish(partial, [cross_own, from_behind], rows, n * lax.axis_size("section"))

    total = lax.all_to_all(squares, ("dp", "section"), 0, 0, tiled=True)
    max_norm = math.sqrt(lax.axis_size("section") * stacked.size)
    states = (shard, master[0], moment1[0], moment2[0], max_norm, rows)
    (own,) = update(total, *states, False)

    cut = shard_rows * 7 // 12 // PAD * PAD
    other = send(own, 0, 1)
    behind = behind_of(send(own, 1), other)
    tail = send(own[cut:], -1)
    behind_cross = send(behind, 0, 1)
    far = send(behind, 1)
    tail = behind_of(tail, behind, cost_of(3.4))
    tail_cross = send(tail, 0, 1)
    both = send(both_of(own, other, behind_cross, cut), -1)
    far = behind_of(behind_of(far, behind_cross), tail_cross)
    far_cross = send(far, 0, 1)
    new_param, new_first, new_second = update(total, *states, True)

    def move(value, offset, flip, low=0, first=0, size=shard_rows):
        return (value, low, size, table(offset, flip), shard_rows, first)

    gathered = fill(
        None,
        [own, other, behind, tail, behind_cross, tail_cross, far],
        [
            move(0, 0, 0),
            move(1, 0, 1),
            move(2, -1, 0),
            move(3, 1, 0, 0, cut, shard_rows - cut),
            move(4, -1, 1),
            move(5, 1, 1, 0, cut, shard_rows - cut),
            move(6, -2, 0),
        ],
        stacked.shape[0],
    )
    gathered = fill(
        gathered,
        [both, far_cross],
        [move(0, 1, 0, 0, 0, cut), move(0, 1, 1, cut, 0, cut), move(1, -2, 1)],
        stacked.shape[0],
    )
    return new_param[None], new_first[None], new_second[None], gathered[None]


def local(weights, *rest):
    n = lax.axis_size("dp")
    height = weights.shape[1]
    shard, width = height // n, height // 3
    fits = n == 8 and height % n == 0 and math.gcd(shard, width, 256) % 128 == 0 and shard // math.gcd(shard, width, 256) > 2
    return (paired if fits else plain)(weights, *rest)


def solution(mesh):
    whole = P("section", None, None)
    split = P("section", "dp", None)
    return jax.shard_map(
        local,
        mesh=mesh,
        in_specs=(whole, split, split, split, split, split),
        out_specs=(split, split, split, whole),
        check_vma=False,
    )
```

```python
import math

import jax
import jax.numpy as jnp
from jax import lax
from jax.experimental import pallas as pl
from jax.experimental.pallas import tpu as pltpu
from jax.sharding import PartitionSpec as P

MROWS = 256
STEP = 10
LITTLE = 16 << 20
CHUNK = 32
PAD = 16
POWER = 8
TOP = 32768.0


def cost_of(micros):
    return pl.CostEstimate(flops=int(micros * 1.18e9), bytes_accessed=1024, transcendentals=0)


PIECE = cost_of(1.7)
CHEAP = pl.CostEstimate(flops=1024, bytes_accessed=1024, transcendentals=0)


def forward_pieces(x_rows, dy_rows, w_gate, w_up, w_down):
    pre_gate = jnp.dot(x_rows, w_gate, preferred_element_type=jnp.float32)
    pre_up = jnp.dot(x_rows, w_up, preferred_element_type=jnp.float32)
    d_hidden = jnp.dot(dy_rows, w_down, preferred_element_type=jnp.float32)
    return activation(pre_gate, pre_up, d_hidden)


def activation(pre_gate, pre_up, d_hidden):
    sigma = jax.nn.sigmoid(pre_gate)
    silu_val = pre_gate * sigma
    hidden = (silu_val * pre_up).astype(jnp.bfloat16)
    d_gate = (d_hidden * pre_up * sigma * (1.0 + pre_gate * (1.0 - sigma))).astype(jnp.bfloat16)
    d_up = (d_hidden * silu_val).astype(jnp.bfloat16)
    return d_gate, d_up, hidden


def block_grads(x_rows, dy_rows, w_gate, w_up, w_down):
    d_gate, d_up, hidden = forward_pieces(x_rows, dy_rows, w_gate, w_up, w_down)
    g_gate = jnp.dot(x_rows.T, d_gate, preferred_element_type=jnp.float32)
    g_up = jnp.dot(x_rows.T, d_up, preferred_element_type=jnp.float32)
    g_down = jnp.dot(dy_rows.T, hidden, preferred_element_type=jnp.float32)
    return jnp.concatenate([g_gate, g_up, g_down], axis=0)


def adam(clip, shard, old_param, first, second):
    clipped = clip * shard
    new_first = 0.9 * first + 0.1 * clipped
    new_second = 0.95 * second + 0.05 * clipped * clipped
    first_fix = 1.0 / (1.0 - 0.9**STEP)
    second_fix = 1.0 / (1.0 - 0.95**STEP)
    update = new_first * first_fix / (jnp.sqrt(new_second * second_fix) + 1e-08) + 0.1 * old_param
    return old_param - 0.01 * update, new_first, new_second


def clip_of(total, max_norm):
    return jnp.minimum(jnp.float32(1.0), max_norm / (jnp.sqrt(total) + 1e-06))


def plain(weights, inputs, out_grads, master, moment1, moment2):
    stacked = weights[0]
    width = stacked.shape[0] // 3
    local_grad = jnp.zeros(stacked.shape, jnp.float32)
    for start in range(0, inputs.shape[1], MROWS):
        x_rows = inputs[0, start : start + MROWS]
        dy_rows = out_grads[0, start : start + MROWS]
        local_grad = local_grad + block_grads(
            x_rows, dy_rows, stacked[:width], stacked[width : 2 * width], stacked[2 * width :]
        )
    shard = lax.psum_scatter(local_grad, "dp", scatter_dimension=0, tiled=True)
    total = lax.psum(jnp.sum(shard * shard), ("dp", "section"))
    max_norm = jnp.sqrt(jnp.float32(lax.axis_size("section") * stacked.size))
    new_param, new_first, new_second = adam(clip_of(total, max_norm), shard, master[0], moment1[0], moment2[0])
    gathered = lax.all_gather(new_param.astype(jnp.bfloat16), "dp", axis=0, tiled=True)
    return new_param[None], new_first[None], new_second[None], gathered[None]


def chunks(rows):
    return [slice(at, min(at + CHUNK, rows)) for at in range(0, rows, CHUNK)]


def fold(value):
    return jnp.max(jnp.abs(value).reshape(-1, 8, value.shape[1]), axis=0)


def scale_of(top):
    scale = jnp.max(top, axis=0, keepdims=True)
    return jnp.maximum(scale, 1e-30).astype(jnp.bfloat16).astype(jnp.float32)


def encode(value, factor):
    v = value * factor
    v2 = v * v
    v4 = v2 * v2
    v8 = v4 * v4
    return jnp.where(v < 0.0, -v8, v8).astype(jnp.bfloat16)


def decode(code, factor):
    code = code.astype(jnp.float32)
    size = jnp.abs(code)
    root = jnp.exp(jnp.log(jnp.maximum(size, 1e-37)) * (1.0 / POWER)) * factor
    root = jnp.where(size > 0.0, root, 0.0)
    return jnp.where(code < 0.0, -root, root)


def write_codes(total_ref, top, out_ref, first):
    scale = scale_of(top)
    factor = TOP / scale
    for part in chunks(total_ref.shape[0]):
        size = part.stop - part.start
        out_ref[pl.ds(first + part.start, size), :] = encode(total_ref[part, :], factor)
    return scale


def lookup(table, index):
    bits = max(max(table).bit_length(), 1)
    if bits * len(table) < 32:
        packed = sum(value << (bits * at) for at, value in enumerate(table))
        return jnp.bitwise_and(jnp.right_shift(jnp.int32(packed), index * bits), (1 << bits) - 1)
    out = jnp.int32(table[0])
    for at, value in enumerate(table[1:], 1):
        out = jnp.where(index == at, jnp.int32(value), out)
    return out


def forward_kernel(messages, rows, x_hbm, dy_hbm, w_hbm, factors_ref, *refs):
    outs = refs[: len(messages)]
    x_ref, dy_ref, w_ref, a_ref, b_ref, h_ref, total_ref, sems = refs[len(messages) :]
    width = x_hbm.shape[1]
    half = width // 2

    def fetch(at, source, target, index):
        copy = pltpu.make_async_copy(source.at[index], target.at[index], sems.at[at])
        copy.start()
        return copy

    copies = []
    for columns in (pl.ds(0, half), pl.ds(half, half)):
        copies.append(fetch(len(copies), x_hbm, x_ref, (slice(None), columns)))
        copies.append(fetch(len(copies), w_hbm, w_ref, columns))
        copies.append(fetch(len(copies), w_hbm, w_ref, pl.ds(columns.start + width, half)))
    for columns in (pl.ds(0, half), pl.ds(half, half)):
        copies.append(fetch(len(copies), dy_hbm, dy_ref, (slice(None), columns)))
        copies.append(fetch(len(copies), w_hbm, w_ref, pl.ds(columns.start + 2 * width, half)))

    def product(left, start, which):
        weight = w_ref[which * width + start : which * width + start + half]
        return jnp.dot(left[:, start : start + half], weight, preferred_element_type=jnp.float32)

    for copy in copies[:3]:
        copy.wait()
    a_ref[...] = product(x_ref, 0, 0)
    b_ref[...] = product(x_ref, 0, 1)
    for copy in copies[3:6]:
        copy.wait()
    a_ref[...] += product(x_ref, half, 0)
    b_ref[...] += product(x_ref, half, 1)
    for copy in copies[6:8]:
        copy.wait()
    h_ref[...] = product(dy_ref, 0, 2)
    for copy in copies[8:]:
        copy.wait()
    h_ref[...] += product(dy_ref, half, 2)
    for part in chunks(x_ref.shape[0]):
        d_gate, d_up, hidden = activation(a_ref[part, :], b_ref[part, :], h_ref[part, :])
        factors_ref[0, part, :] = d_gate
        factors_ref[1, part, :] = d_up
        factors_ref[2, part, :] = hidden
    per = width // rows
    for places, out_ref in zip(messages, outs):
        scales = jnp.zeros((PAD, out_ref.shape[1]), jnp.float32)
        for step, place in enumerate(places):
            at = place()
            kind = lax.div(at, per)
            column = pl.ds(pl.multiple_of(lax.rem(at, per) * rows, rows), rows)
            left = jnp.where(kind == 2, dy_ref[:, column], x_ref[:, column])
            total_ref[...] = lax.dot_general(
                left, factors_ref[kind], (((0,), (0,)), ((), ())), preferred_element_type=jnp.float32
            )
            top = fold(total_ref[:CHUNK, :])
            for part in chunks(rows)[1:]:
                top = jnp.maximum(top, fold(total_ref[part, :]))
            scale = write_codes(total_ref, top, out_ref, step * rows)
            row = lax.broadcasted_iota(jnp.int32, scales.shape, 0)
            scales = jnp.where(row == step, scale, scales)
        out_ref[len(places) * rows :, :] = scales.astype(jnp.bfloat16)


def forward(x, dy, stacked, messages, rows):
    tokens, width = x.shape
    hidden = stacked.shape[1]

    def place_of(table, block):
        steps = stacked.shape[0] // len(table) // rows
        return lambda: lookup(table, lax.axis_index("dp")) * steps + block

    places = [[place_of(*block) for block in blocks] for blocks in messages]
    return pl.pallas_call(
        lambda *refs: forward_kernel(places, rows, *refs),
        in_specs=[pl.BlockSpec(memory_space=pltpu.HBM)] * 3,
        out_shape=[jax.ShapeDtypeStruct((3, tokens, hidden), jnp.bfloat16)]
        + [jax.ShapeDtypeStruct((len(blocks) * rows + PAD, hidden), jnp.bfloat16) for blocks in messages],
        scratch_shapes=[
            pltpu.VMEM(x.shape, x.dtype),
            pltpu.VMEM(dy.shape, dy.dtype),
            pltpu.VMEM(stacked.shape, stacked.dtype),
            *[pltpu.VMEM((tokens, hidden), jnp.float32)] * 3,
            pltpu.VMEM((rows, hidden), jnp.float32),
            pltpu.SemaphoreType.DMA((10,)),
        ],
        compiler_params=pltpu.CompilerParams(vmem_limit_bytes=60 << 20),
        cost_estimate=CHEAP,
        name="forward",
    )(x, dy, stacked)


def pick(values, step):
    if all(value == values[0] + at for at, value in enumerate(values)):
        return step + values[0] if len(values) > 1 else jnp.int32(values[0])
    out = jnp.int32(values[0])
    for at, value in enumerate(values[1:], 1):
        out = jnp.where(step == at, value, out)
    return out


def piece_kernel(place, per, got, extra, last, *refs):
    step = pl.program_id(0)
    x_ref, dy_ref, d_ref = refs[:3]
    outs = refs[3 + 2 * len(got) + extra :]
    rows = x_ref.shape[1]
    left = jnp.where(lax.div(place(step), per) == 2, dy_ref[...], x_ref[...])
    total_ref = outs[-1]
    total_ref[...] = lax.dot_general(left, d_ref[0], (((0,), (0,)), ((), ())), preferred_element_type=jnp.float32)
    factors = []
    for at, blocks in enumerate(got):
        scales = refs[4 + 2 * at][...].astype(jnp.float32)
        row = lax.broadcasted_iota(jnp.int32, scales.shape, 0)
        here = pick([PAD if block is None else block for block in blocks], step)
        factors.append(jnp.sum(jnp.where(row == here, scales, 0.0), axis=0, keepdims=True) * (1.0 / TOP))
    top = jnp.zeros((8, total_ref.shape[1]), jnp.float32)
    for part in chunks(rows):
        total = total_ref[part, :]
        for at, factor in enumerate(factors):
            total = total + decode(refs[3 + 2 * at][part, :], factor)
        if last:
            outs[0][part, :] = total
        else:
            if factors:
                total_ref[part, :] = total
            top = jnp.maximum(top, fold(total))
    if not last:
        out_ref, scales_ref = outs[:2]
        scale = write_codes(total_ref, top, out_ref, pl.multiple_of(step * rows, rows))
        row = lax.broadcasted_iota(jnp.int32, scales_ref.shape, 0)
        scales_ref[...] = jnp.where(row == step, scale, jnp.where(step == 0, 0.0, scales_ref[...]))
        out_ref[pl.ds(out_ref.shape[0] - PAD, PAD), :] = scales_ref[...].astype(jnp.bfloat16)


def piece(x, dy, factors, rows, blocks, got=(), after=None, last=False, cost=PIECE):
    tokens, width = x.shape
    hidden = factors.shape[2]
    per = width // rows
    shard = 3 * width // len(blocks[0][0])
    steps = shard // rows
    tables = [table for table, _ in blocks]
    within = [block for _, block in blocks]

    def place(i):
        r = lax.axis_index("dp")
        owner = lookup(tables[0], r)
        for at, table in enumerate(tables[1:], 1):
            if table != tables[at - 1]:
                owner = jnp.where(i >= at, lookup(table, r), owner)
        return owner * steps + pick(within, i)

    def column(i):
        return (0, lax.rem(place(i), per))

    in_specs = [
        pl.BlockSpec((tokens, rows), column),
        pl.BlockSpec((tokens, rows), column),
        pl.BlockSpec((1, tokens, hidden), lambda i: (lax.div(place(i), per), 0, 0)),
    ]
    operands = [x, dy, factors]
    for message, parts in got:
        present = [part for part in parts if part is not None]
        nearest = [present[0] if part is None else part for part in parts]
        scales = (message.shape[0] - PAD) // PAD
        in_specs += [
            pl.BlockSpec((rows, hidden), lambda i, nearest=nearest: (pick(nearest, i), 0)),
            pl.BlockSpec((PAD, hidden), lambda i, scales=scales: (scales, 0)),
        ]
        operands += [message, message]
    extra = 0
    if after is not None:
        extra = 1
        operands.append(after)
        in_specs.append(pl.BlockSpec(memory_space=pl.ANY))
    if last:
        out_specs = pl.BlockSpec((rows, hidden), lambda i: (i, 0))
        out_shape = jax.ShapeDtypeStruct((len(blocks) * rows, hidden), jnp.float32)
        scratch = [pltpu.VMEM((rows, hidden), jnp.float32)]
    else:
        out_specs = pl.BlockSpec((len(blocks) * rows + PAD, hidden), lambda i: (0, 0))
        out_shape = jax.ShapeDtypeStruct((len(blocks) * rows + PAD, hidden), jnp.bfloat16)
        scratch = [pltpu.VMEM((PAD, hidden), jnp.float32), pltpu.VMEM((rows, hidden), jnp.float32)]
    return pl.pallas_call(
        lambda *refs: piece_kernel(place, per, [parts for _, parts in got], extra, last, *refs),
        grid=(len(blocks),),
        in_specs=in_specs,
        out_specs=out_specs,
        out_shape=out_shape,
        scratch_shapes=scratch,
        compiler_params=pltpu.CompilerParams(vmem_limit_bytes=LITTLE),
        cost_estimate=cost,
        name="piece",
    )(*operands)


def finish_kernel(sum_ref, *refs):
    step = pl.program_id(0)
    out_ref, squares_ref = refs[-2:]
    factors = []
    for scales_ref in refs[1:-2:2]:
        scales = scales_ref[...].astype(jnp.float32)
        row = lax.broadcasted_iota(jnp.int32, scales.shape, 0)
        factors.append(jnp.sum(jnp.where(row == step, scales, 0.0), axis=0, keepdims=True) * (1.0 / TOP))
    top = jnp.zeros((8, out_ref.shape[1]), jnp.float32)
    for part in chunks(out_ref.shape[0]):
        total = sum_ref[part, :]
        for code_ref, factor in zip(refs[:-2:2], factors):
            total = total + decode(code_ref[part, :], factor)
        out_ref[part, :] = total
        top = top + jnp.sum((total * total).reshape(-1, 8, total.shape[1]), axis=0)
    row = jnp.sum(sum(top[:, at : at + 128] for at in range(0, top.shape[1], 128)), axis=0, keepdims=True)
    squares_ref[...] = jnp.broadcast_to(row, squares_ref.shape) + jnp.where(step == 0, 0.0, squares_ref[...])


def finish(partial, messages, rows, count):
    height, hidden = partial.shape
    block = pl.BlockSpec((rows, hidden), lambda i: (i, 0))
    scales = pl.BlockSpec((PAD, hidden), lambda i: (height // PAD, 0))
    return pl.pallas_call(
        finish_kernel,
        grid=(height // rows,),
        in_specs=[block] + [block, scales] * len(messages),
        out_specs=[block, pl.BlockSpec((count, 128), lambda i: (0, 0))],
        out_shape=[
            jax.ShapeDtypeStruct(partial.shape, jnp.float32),
            jax.ShapeDtypeStruct((count, 128), jnp.float32),
        ],
        compiler_params=pltpu.CompilerParams(vmem_limit_bytes=LITTLE),
        cost_estimate=PIECE,
        name="finish",
    )(partial, *[m for message in messages for m in (message, message)])


def join_kernel(sum_ref, code_ref, scales_ref, out_ref, total_ref, out_scales_ref):
    step = pl.program_id(0)
    rows = sum_ref.shape[0]
    scales = scales_ref[...].astype(jnp.float32)
    row = lax.broadcasted_iota(jnp.int32, scales.shape, 0)
    factor = jnp.sum(jnp.where(row == step, scales, 0.0), axis=0, keepdims=True) * (1.0 / TOP)
    top = jnp.zeros((8, sum_ref.shape[1]), jnp.float32)
    for part in chunks(rows):
        total = sum_ref[part, :] + decode(code_ref[part, :], factor)
        total_ref[part, :] = total
        top = jnp.maximum(top, fold(total))
    scale = write_codes(total_ref, top, out_ref, pl.multiple_of(step * rows, rows))
    out_scales_ref[...] = jnp.where(row == step, scale, jnp.where(step == 0, 0.0, out_scales_ref[...]))
    out_ref[pl.ds(out_ref.shape[0] - PAD, PAD), :] = out_scales_ref[...].astype(jnp.bfloat16)


def join(partial, message, rows):
    height, hidden = partial.shape
    block = pl.BlockSpec((rows, hidden), lambda i: (i, 0))
    return pl.pallas_call(
        join_kernel,
        grid=(height // rows,),
        in_specs=[block, block, pl.BlockSpec((PAD, hidden), lambda i: (height // PAD, 0))],
        out_specs=pl.BlockSpec(message.shape, lambda i: (0, 0)),
        out_shape=jax.ShapeDtypeStruct(message.shape, message.dtype),
        scratch_shapes=[pltpu.VMEM((rows, hidden), jnp.float32), pltpu.VMEM((PAD, hidden), jnp.float32)],
        compiler_params=pltpu.CompilerParams(vmem_limit_bytes=LITTLE),
        cost_estimate=PIECE,
        name="join",
    )(partial, message, message)


def update_kernel(max_norm, states, total_ref, g_ref, p_ref, m1_ref, m2_ref, *outs):
    clip = clip_of(jnp.sum(total_ref[...], keepdims=True), max_norm)
    for part in chunks(g_ref.shape[0]):
        param, first, second = adam(clip, g_ref[part, :], p_ref[part, :], m1_ref[part, :], m2_ref[part, :])
        values = (param, first, second) if states else (param.astype(jnp.bfloat16),)
        for out, value in zip(outs, values):
            out[part, :] = value


def update(total, shard, param, first, second, max_norm, rows, states):
    block = pl.BlockSpec((rows, shard.shape[1]), lambda i: (i, 0))
    dtypes = [jnp.float32] * 3 if states else [jnp.bfloat16]
    return pl.pallas_call(
        lambda *refs: update_kernel(max_norm, states, *refs),
        grid=(shard.shape[0] // rows,),
        in_specs=[pl.BlockSpec(total.shape, lambda i: (0, 0))] + [block] * 4,
        out_specs=[block] * len(dtypes),
        out_shape=[jax.ShapeDtypeStruct(shard.shape, dtype) for dtype in dtypes],
        compiler_params=pltpu.CompilerParams(vmem_limit_bytes=LITTLE),
        cost_estimate=CHEAP,
        name="states" if states else "update",
    )(total, shard, param, first, second)


def behind_of(value, other, cost=CHEAP):
    return pl.pallas_call(
        lambda *refs: None,
        grid=(1,),
        in_specs=[pl.BlockSpec(memory_space=pl.ANY), pl.BlockSpec((PAD, 128), lambda i: (0, 0))],
        out_specs=pl.BlockSpec(memory_space=pl.ANY),
        out_shape=jax.ShapeDtypeStruct(value.shape, value.dtype),
        input_output_aliases={0: 0},
        compiler_params=pltpu.CompilerParams(vmem_limit_bytes=LITTLE),
        cost_estimate=cost,
        name="behind",
    )(value, other)


def both_of(own, other, after, cut):
    columns = own.shape[1]

    def kernel(own_ref, other_ref, after_ref, both_ref):
        both_ref[...] = jnp.where(pl.program_id(0) == 0, own_ref[...], other_ref[...])

    return pl.pallas_call(
        kernel,
        grid=(2,),
        in_specs=[
            pl.BlockSpec((cut, columns), lambda i: (0, 0)),
            pl.BlockSpec((cut, columns), lambda i: (0, 0)),
            pl.BlockSpec((PAD, 128), lambda i: (0, 0)),
        ],
        out_specs=pl.BlockSpec((cut, columns), lambda i: (i, 0)),
        out_shape=jax.ShapeDtypeStruct((2 * cut, columns), own.dtype),
        compiler_params=pltpu.CompilerParams(vmem_limit_bytes=LITTLE),
        cost_estimate=PIECE,
        name="both",
    )(own, other, after)


def fill_kernel(moves, count, *refs):
    out, sems = refs[-2:]
    r = lax.axis_index("dp")
    copies = []
    for at, (source, low, size, table, shard, first) in enumerate(moves):
        to = pl.multiple_of(lookup(table, r) * shard + first, PAD)
        copies.append(pltpu.make_async_copy(refs[source].at[low : low + size], out.at[pl.ds(to, size)], sems.at[at]))
        copies[-1].start()
    for copy in copies:
        copy.wait()


def fill(buffer, values, moves, height):
    columns = values[0].shape[1]
    return pl.pallas_call(
        lambda *refs: fill_kernel(moves, len(values), *refs),
        in_specs=[pl.BlockSpec(memory_space=pltpu.VMEM)] * len(values)
        + [pl.BlockSpec(memory_space=pltpu.HBM)] * (buffer is not None),
        out_specs=pl.BlockSpec(memory_space=pltpu.HBM),
        out_shape=jax.ShapeDtypeStruct((height, columns), values[0].dtype),
        input_output_aliases={} if buffer is None else {len(values): 0},
        scratch_shapes=[pltpu.SemaphoreType.DMA((len(moves),))],
        compiler_params=pltpu.CompilerParams(vmem_limit_bytes=LITTLE),
        cost_estimate=CHEAP,
        name="fill",
    )(*values, *([] if buffer is None else [buffer]))


def paired(weights, inputs, out_grads, master, moment1, moment2):
    n = lax.axis_size("dp")
    pairs = n // 2
    ring = list(range(0, pairs, 2)) + list(range(pairs - 1 - pairs % 2, 0, -2))
    place = {pair: at for at, pair in enumerate(ring)}

    def at_offset(r, offset, flip):
        return 2 * ring[(place[r // 2] + offset) % pairs] + ((r % 2) ^ flip)

    def table(offset, flip):
        return [at_offset(r, offset, flip) for r in range(n)]

    def send(value, offset, flip=0):
        return lax.ppermute(value, "dp", [(r, at_offset(r, offset, flip)) for r in range(n)])

    stacked = weights[0]
    x, dy = inputs[0], out_grads[0]
    width = x.shape[1]
    shard_rows = stacked.shape[0] // n
    rows = math.gcd(shard_rows, width, 256)

    steps = shard_rows // rows

    every, most, rest, end = list(range(steps)), list(range(steps - 1)), list(range(1, steps)), steps - 1

    def at(*blocks):
        return [(table(offset, flip), block) for offset, flip, block in blocks]

    def made(blocks, got=(), **more):
        return piece(x, dy, factors, rows, blocks, got, **more)

    factors, message = forward(x, dy, stacked, [at(*[(2, 1, b) for b in every])], rows)
    cross_far = send(message, 0, 1)
    message = made(at((-1, 0, end), (-1, 1, end)))
    ahead = send(message, -1)
    message = made(at(*[(-1, 1, b) for b in most]), after=message)
    cross_back = send(message, 0, 1)
    own_far = made(at(*[(2, 0, b) for b in every]), after=message, last=True)
    message = made(at(*[(1, 1, b) for b in every]), after=own_far)
    cross_next = send(message, 0, 1)
    message = made(at(*[(0, 1, b) for b in every]), [(ahead, [None] * end + [1])], after=message)
    cross_own = send(message, 0, 1)

    by_ring = send(join(own_far, cross_far, rows), 1)
    from_ahead = send(made(at(*[(-1, 0, b) for b in most]), [(cross_back, most)]), -1)
    from_behind = send(join(made(at(*[(1, 0, b) for b in every]), [(by_ring, every)], last=True), cross_next, rows), 1)
    partial = made(at(*[(0, 0, b) for b in every]), [(from_ahead, most + [None]), (ahead, [None] * end + [0])], last=True)
    shard, squares = finish(partial, [cross_own, from_behind], rows, n * lax.axis_size("section"))

    total = lax.all_to_all(squares, ("dp", "section"), 0, 0, tiled=True)
    max_norm = math.sqrt(lax.axis_size("section") * stacked.size)
    states = (shard, master[0], moment1[0], moment2[0], max_norm, rows // 2)
    (own,) = update(total, *states, False)

    cut = shard_rows * 7 // 12 // PAD * PAD
    other = send(own, 0, 1)
    behind = behind_of(send(own, 1), other)
    tail = send(own[cut:], -1)
    behind_cross = send(behind, 0, 1)
    far = send(behind, 1)
    tail = behind_of(tail, behind, cost_of(3.4))
    tail_cross = send(tail, 0, 1)
    both = send(both_of(own, other, behind_cross, cut), -1)
    far = behind_of(behind_of(far, behind_cross), tail_cross)
    far_cross = send(far, 0, 1)
    new_param, new_first, new_second = update(total, *states, True)

    def move(value, offset, flip, low=0, first=0, size=shard_rows):
        return (value, low, size, table(offset, flip), shard_rows, first)

    gathered = fill(
        None,
        [own, other, behind, tail, behind_cross, tail_cross, far],
        [
            move(0, 0, 0),
            move(1, 0, 1),
            move(2, -1, 0),
            move(3, 1, 0, 0, cut, shard_rows - cut),
            move(4, -1, 1),
            move(5, 1, 1, 0, cut, shard_rows - cut),
            move(6, -2, 0),
        ],
        stacked.shape[0],
    )
    gathered = fill(
        gathered,
        [both, far_cross],
        [move(0, 1, 0, 0, 0, cut), move(0, 1, 1, cut, 0, cut), move(1, -2, 1)],
        stacked.shape[0],
    )
    return new_param[None], new_first[None], new_second[None], gathered[None]


def local(weights, *rest):
    n = lax.axis_size("dp")
    height = weights.shape[1]
    shard, width = height // n, height // 3
    fits = n == 8 and height % n == 0 and math.gcd(shard, width, 256) % 128 == 0 and shard // math.gcd(shard, width, 256) > 2
    return (paired if fits else plain)(weights, *rest)


def solution(mesh):
    whole = P("section", None, None)
    split = P("section", "dp", None)
    return jax.shard_map(
        local,
        mesh=mesh,
        in_specs=(whole, split, split, split, split, split),
        out_specs=(split, split, split, whole),
        check_vma=False,
    )
```

```python
import math

import jax
import jax.numpy as jnp
from jax import lax
from jax.experimental import pallas as pl
from jax.experimental.pallas import tpu as pltpu
from jax.sharding import PartitionSpec as P

MROWS = 256
STEP = 10
LITTLE = 16 << 20
CHUNK = 32
PAD = 16
POWER = 8
TOP = 32768.0


def cost_of(micros):
    return pl.CostEstimate(flops=int(micros * 1.18e9), bytes_accessed=1024, transcendentals=0)


PIECE = cost_of(1.7)
CHEAP = pl.CostEstimate(flops=1024, bytes_accessed=1024, transcendentals=0)


def forward_pieces(x_rows, dy_rows, w_gate, w_up, w_down):
    pre_gate = jnp.dot(x_rows, w_gate, preferred_element_type=jnp.float32)
    pre_up = jnp.dot(x_rows, w_up, preferred_element_type=jnp.float32)
    d_hidden = jnp.dot(dy_rows, w_down, preferred_element_type=jnp.float32)
    return activation(pre_gate, pre_up, d_hidden)


def activation(pre_gate, pre_up, d_hidden):
    sigma = jax.nn.sigmoid(pre_gate)
    silu_val = pre_gate * sigma
    hidden = (silu_val * pre_up).astype(jnp.bfloat16)
    d_gate = (d_hidden * pre_up * sigma * (1.0 + pre_gate * (1.0 - sigma))).astype(jnp.bfloat16)
    d_up = (d_hidden * silu_val).astype(jnp.bfloat16)
    return d_gate, d_up, hidden


def block_grads(x_rows, dy_rows, w_gate, w_up, w_down):
    d_gate, d_up, hidden = forward_pieces(x_rows, dy_rows, w_gate, w_up, w_down)
    g_gate = jnp.dot(x_rows.T, d_gate, preferred_element_type=jnp.float32)
    g_up = jnp.dot(x_rows.T, d_up, preferred_element_type=jnp.float32)
    g_down = jnp.dot(dy_rows.T, hidden, preferred_element_type=jnp.float32)
    return jnp.concatenate([g_gate, g_up, g_down], axis=0)


def adam(clip, shard, old_param, first, second):
    clipped = clip * shard
    new_first = 0.9 * first + 0.1 * clipped
    new_second = 0.95 * second + 0.05 * clipped * clipped
    first_fix = 1.0 / (1.0 - 0.9**STEP)
    second_fix = 1.0 / (1.0 - 0.95**STEP)
    update = new_first * first_fix / (jnp.sqrt(new_second * second_fix) + 1e-08) + 0.1 * old_param
    return old_param - 0.01 * update, new_first, new_second


def clip_of(total, max_norm):
    return jnp.minimum(jnp.float32(1.0), max_norm / (jnp.sqrt(total) + 1e-06))


def plain(weights, inputs, out_grads, master, moment1, moment2):
    stacked = weights[0]
    width = stacked.shape[0] // 3
    local_grad = jnp.zeros(stacked.shape, jnp.float32)
    for start in range(0, inputs.shape[1], MROWS):
        x_rows = inputs[0, start : start + MROWS]
        dy_rows = out_grads[0, start : start + MROWS]
        local_grad = local_grad + block_grads(
            x_rows, dy_rows, stacked[:width], stacked[width : 2 * width], stacked[2 * width :]
        )
    shard = lax.psum_scatter(local_grad, "dp", scatter_dimension=0, tiled=True)
    total = lax.psum(jnp.sum(shard * shard), ("dp", "section"))
    max_norm = jnp.sqrt(jnp.float32(lax.axis_size("section") * stacked.size))
    new_param, new_first, new_second = adam(clip_of(total, max_norm), shard, master[0], moment1[0], moment2[0])
    gathered = lax.all_gather(new_param.astype(jnp.bfloat16), "dp", axis=0, tiled=True)
    return new_param[None], new_first[None], new_second[None], gathered[None]


def chunks(rows):
    return [slice(at, min(at + CHUNK, rows)) for at in range(0, rows, CHUNK)]


def fold(value):
    return jnp.max(jnp.abs(value).reshape(-1, 8, value.shape[1]), axis=0)


def scale_of(top):
    scale = jnp.max(top, axis=0, keepdims=True)
    return jnp.maximum(scale, 1e-30).astype(jnp.bfloat16).astype(jnp.float32)


def encode(value, factor):
    v = value * factor
    v2 = v * v
    v4 = v2 * v2
    v8 = v4 * v4
    return jnp.where(v < 0.0, -v8, v8).astype(jnp.bfloat16)


def decode(code, factor):
    code = code.astype(jnp.float32)
    size = jnp.abs(code)
    root = jnp.exp(jnp.log(jnp.maximum(size, 1e-37)) * (1.0 / POWER)) * factor
    root = jnp.where(size > 0.0, root, 0.0)
    return jnp.where(code < 0.0, -root, root)


def write_codes(total_ref, top, out_ref, first):
    scale = scale_of(top)
    factor = TOP / scale
    for part in chunks(total_ref.shape[0]):
        size = part.stop - part.start
        out_ref[pl.ds(first + part.start, size), :] = encode(total_ref[part, :], factor)
    return scale


def lookup(table, index):
    bits = max(max(table).bit_length(), 1)
    if bits * len(table) < 32:
        packed = sum(value << (bits * at) for at, value in enumerate(table))
        return jnp.bitwise_and(jnp.right_shift(jnp.int32(packed), index * bits), (1 << bits) - 1)
    out = jnp.int32(table[0])
    for at, value in enumerate(table[1:], 1):
        out = jnp.where(index == at, jnp.int32(value), out)
    return out


def forward_kernel(messages, rows, x_hbm, dy_hbm, w_hbm, factors_ref, *refs):
    outs = refs[: len(messages)]
    x_ref, dy_ref, w_ref, a_ref, b_ref, h_ref, total_ref, sems = refs[len(messages) :]
    width = x_hbm.shape[1]
    half = width // 2

    def fetch(at, source, target, index):
        copy = pltpu.make_async_copy(source.at[index], target.at[index], sems.at[at])
        copy.start()
        return copy

    copies = []
    for columns in (pl.ds(0, half), pl.ds(half, half)):
        copies.append(fetch(len(copies), x_hbm, x_ref, (slice(None), columns)))
        copies.append(fetch(len(copies), w_hbm, w_ref, columns))
        copies.append(fetch(len(copies), w_hbm, w_ref, pl.ds(columns.start + width, half)))
    for columns in (pl.ds(0, half), pl.ds(half, half)):
        copies.append(fetch(len(copies), dy_hbm, dy_ref, (slice(None), columns)))
        copies.append(fetch(len(copies), w_hbm, w_ref, pl.ds(columns.start + 2 * width, half)))

    def product(left, start, which):
        weight = w_ref[which * width + start : which * width + start + half]
        return jnp.dot(left[:, start : start + half], weight, preferred_element_type=jnp.float32)

    for copy in copies[:3]:
        copy.wait()
    a_ref[...] = product(x_ref, 0, 0)
    b_ref[...] = product(x_ref, 0, 1)
    for copy in copies[3:6]:
        copy.wait()
    a_ref[...] += product(x_ref, half, 0)
    b_ref[...] += product(x_ref, half, 1)
    for copy in copies[6:8]:
        copy.wait()
    h_ref[...] = product(dy_ref, 0, 2)
    for copy in copies[8:]:
        copy.wait()
    h_ref[...] += product(dy_ref, half, 2)
    for part in chunks(x_ref.shape[0]):
        d_gate, d_up, hidden = activation(a_ref[part, :], b_ref[part, :], h_ref[part, :])
        factors_ref[0, part, :] = d_gate
        factors_ref[1, part, :] = d_up
        factors_ref[2, part, :] = hidden
    per = width // rows
    for places, out_ref in zip(messages, outs):
        scales = jnp.zeros((PAD, out_ref.shape[1]), jnp.float32)
        for step, place in enumerate(places):
            at = place()
            kind = lax.div(at, per)
            column = pl.ds(pl.multiple_of(lax.rem(at, per) * rows, rows), rows)
            left = jnp.where(kind == 2, dy_ref[:, column], x_ref[:, column])
            total_ref[...] = lax.dot_general(
                left, factors_ref[kind], (((0,), (0,)), ((), ())), preferred_element_type=jnp.float32
            )
            top = fold(total_ref[:CHUNK, :])
            for part in chunks(rows)[1:]:
                top = jnp.maximum(top, fold(total_ref[part, :]))
            scale = write_codes(total_ref, top, out_ref, step * rows)
            row = lax.broadcasted_iota(jnp.int32, scales.shape, 0)
            scales = jnp.where(row == step, scale, scales)
        out_ref[len(places) * rows :, :] = scales.astype(jnp.bfloat16)


def forward(x, dy, stacked, messages, rows):
    tokens, width = x.shape
    hidden = stacked.shape[1]

    def place_of(table, block):
        steps = stacked.shape[0] // len(table) // rows
        return lambda: lookup(table, lax.axis_index("dp")) * steps + block

    places = [[place_of(*block) for block in blocks] for blocks in messages]
    return pl.pallas_call(
        lambda *refs: forward_kernel(places, rows, *refs),
        in_specs=[pl.BlockSpec(memory_space=pltpu.HBM)] * 3,
        out_shape=[jax.ShapeDtypeStruct((3, tokens, hidden), jnp.bfloat16)]
        + [jax.ShapeDtypeStruct((len(blocks) * rows + PAD, hidden), jnp.bfloat16) for blocks in messages],
        scratch_shapes=[
            pltpu.VMEM(x.shape, x.dtype),
            pltpu.VMEM(dy.shape, dy.dtype),
            pltpu.VMEM(stacked.shape, stacked.dtype),
            *[pltpu.VMEM((tokens, hidden), jnp.float32)] * 3,
            pltpu.VMEM((rows, hidden), jnp.float32),
            pltpu.SemaphoreType.DMA((10,)),
        ],
        compiler_params=pltpu.CompilerParams(vmem_limit_bytes=60 << 20),
        cost_estimate=CHEAP,
        name="forward",
    )(x, dy, stacked)


def pick(values, step):
    if all(value == values[0] + at for at, value in enumerate(values)):
        return step + values[0] if len(values) > 1 else jnp.int32(values[0])
    out = jnp.int32(values[0])
    for at, value in enumerate(values[1:], 1):
        out = jnp.where(step == at, value, out)
    return out


def piece_kernel(place, per, got, extra, last, *refs):
    step = pl.program_id(0)
    x_ref, dy_ref, d_ref = refs[:3]
    outs = refs[3 + 2 * len(got) + extra :]
    rows = x_ref.shape[1]
    left = jnp.where(lax.div(place(step), per) == 2, dy_ref[...], x_ref[...])
    total_ref = outs[-1]
    total_ref[...] = lax.dot_general(left, d_ref[0], (((0,), (0,)), ((), ())), preferred_element_type=jnp.float32)
    factors = []
    for at, blocks in enumerate(got):
        scales = refs[4 + 2 * at][...].astype(jnp.float32)
        row = lax.broadcasted_iota(jnp.int32, scales.shape, 0)
        here = pick([PAD if block is None else block for block in blocks], step)
        factors.append(jnp.sum(jnp.where(row == here, scales, 0.0), axis=0, keepdims=True) * (1.0 / TOP))
    top = jnp.zeros((8, total_ref.shape[1]), jnp.float32)
    for part in chunks(rows):
        total = total_ref[part, :]
        for at, factor in enumerate(factors):
            total = total + decode(refs[3 + 2 * at][part, :], factor)
        if last:
            outs[0][part, :] = total
        else:
            if factors:
                total_ref[part, :] = total
            top = jnp.maximum(top, fold(total))
    if not last:
        out_ref, scales_ref = outs[:2]
        scale = write_codes(total_ref, top, out_ref, pl.multiple_of(step * rows, rows))
        row = lax.broadcasted_iota(jnp.int32, scales_ref.shape, 0)
        scales_ref[...] = jnp.where(row == step, scale, jnp.where(step == 0, 0.0, scales_ref[...]))
        out_ref[pl.ds(out_ref.shape[0] - PAD, PAD), :] = scales_ref[...].astype(jnp.bfloat16)


def piece(x, dy, factors, rows, blocks, got=(), after=None, last=False, cost=PIECE):
    tokens, width = x.shape
    hidden = factors.shape[2]
    per = width // rows
    shard = 3 * width // len(blocks[0][0])
    steps = shard // rows
    tables = [table for table, _ in blocks]
    within = [block for _, block in blocks]

    def place(i):
        r = lax.axis_index("dp")
        owner = lookup(tables[0], r)
        for at, table in enumerate(tables[1:], 1):
            if table != tables[at - 1]:
                owner = jnp.where(i >= at, lookup(table, r), owner)
        return owner * steps + pick(within, i)

    def column(i):
        return (0, lax.rem(place(i), per))

    in_specs = [
        pl.BlockSpec((tokens, rows), column),
        pl.BlockSpec((tokens, rows), column),
        pl.BlockSpec((1, tokens, hidden), lambda i: (lax.div(place(i), per), 0, 0)),
    ]
    operands = [x, dy, factors]
    for message, parts in got:
        present = [part for part in parts if part is not None]
        nearest = [present[0] if part is None else part for part in parts]
        scales = (message.shape[0] - PAD) // PAD
        in_specs += [
            pl.BlockSpec((rows, hidden), lambda i, nearest=nearest: (pick(nearest, i), 0)),
            pl.BlockSpec((PAD, hidden), lambda i, scales=scales: (scales, 0)),
        ]
        operands += [message, message]
    extra = 0
    if after is not None:
        extra = 1
        operands.append(after)
        in_specs.append(pl.BlockSpec(memory_space=pl.ANY))
    if last:
        out_specs = pl.BlockSpec((rows, hidden), lambda i: (i, 0))
        out_shape = jax.ShapeDtypeStruct((len(blocks) * rows, hidden), jnp.float32)
        scratch = [pltpu.VMEM((rows, hidden), jnp.float32)]
    else:
        out_specs = pl.BlockSpec((len(blocks) * rows + PAD, hidden), lambda i: (0, 0))
        out_shape = jax.ShapeDtypeStruct((len(blocks) * rows + PAD, hidden), jnp.bfloat16)
        scratch = [pltpu.VMEM((PAD, hidden), jnp.float32), pltpu.VMEM((rows, hidden), jnp.float32)]
    return pl.pallas_call(
        lambda *refs: piece_kernel(place, per, [parts for _, parts in got], extra, last, *refs),
        grid=(len(blocks),),
        in_specs=in_specs,
        out_specs=out_specs,
        out_shape=out_shape,
        scratch_shapes=scratch,
        compiler_params=pltpu.CompilerParams(vmem_limit_bytes=LITTLE),
        cost_estimate=cost,
        name="piece",
    )(*operands)


def finish_kernel(rows, sum_ref, *refs):
    out_ref, squares_ref = refs[-2:]
    height, hidden = out_ref.shape
    codes = refs[:-2]
    scales = [code[height:, :].astype(jnp.float32) * (1.0 / TOP) for code in codes]
    top = jnp.zeros((8, hidden), jnp.float32)
    for part in chunks(height):
        block = part.start // rows
        total = sum_ref[part, :]
        for code, factor in zip(codes, scales):
            total = total + decode(code[part, :], factor[block : block + 1])
        out_ref[part, :] = total
        top = top + jnp.sum((total * total).reshape(-1, 8, hidden), axis=0)
    row = jnp.sum(sum(top[:, at : at + 128] for at in range(0, hidden, 128)), axis=0, keepdims=True)
    squares_ref[...] = jnp.broadcast_to(row, squares_ref.shape)


def finish(partial, messages, rows, count):
    whole = pl.BlockSpec(partial.shape, lambda i: (0, 0))
    return pl.pallas_call(
        lambda *refs: finish_kernel(rows, *refs),
        grid=(1,),
        in_specs=[whole] + [pl.BlockSpec(message.shape, lambda i: (0, 0)) for message in messages],
        out_specs=[whole, pl.BlockSpec((count, 128), lambda i: (0, 0))],
        out_shape=[
            jax.ShapeDtypeStruct(partial.shape, jnp.float32),
            jax.ShapeDtypeStruct((count, 128), jnp.float32),
        ],
        compiler_params=pltpu.CompilerParams(vmem_limit_bytes=LITTLE),
        cost_estimate=PIECE,
        name="finish",
    )(partial, *messages)


def join_kernel(rows, sum_ref, code_ref, out_ref, total_ref):
    height, hidden = sum_ref.shape
    scales = code_ref[height:, :].astype(jnp.float32) * (1.0 / TOP)
    row = lax.broadcasted_iota(jnp.int32, scales.shape, 0)
    new_scales = jnp.zeros_like(scales)
    for block in range(height // rows):
        top = jnp.zeros((8, hidden), jnp.float32)
        for part in chunks(rows):
            here = slice(block * rows + part.start, block * rows + part.stop)
            total = sum_ref[here, :] + decode(code_ref[here, :], scales[block : block + 1])
            total_ref[part, :] = total
            top = jnp.maximum(top, fold(total))
        scale = write_codes(total_ref, top, out_ref, block * rows)
        new_scales = jnp.where(row == block, scale, new_scales)
    out_ref[height:, :] = new_scales.astype(jnp.bfloat16)


def join(partial, message, rows):
    whole = pl.BlockSpec(message.shape, lambda i: (0, 0))
    return pl.pallas_call(
        lambda *refs: join_kernel(rows, *refs),
        grid=(1,),
        in_specs=[pl.BlockSpec(partial.shape, lambda i: (0, 0)), whole],
        out_specs=whole,
        out_shape=jax.ShapeDtypeStruct(message.shape, message.dtype),
        scratch_shapes=[pltpu.VMEM((rows, partial.shape[1]), jnp.float32)],
        compiler_params=pltpu.CompilerParams(vmem_limit_bytes=LITTLE),
        cost_estimate=PIECE,
        name="join",
    )(partial, message)


def update_kernel(max_norm, states, total_ref, g_ref, p_ref, m1_ref, m2_ref, *outs):
    clip = clip_of(jnp.sum(total_ref[...], keepdims=True), max_norm)
    for part in chunks(g_ref.shape[0]):
        param, first, second = adam(clip, g_ref[part, :], p_ref[part, :], m1_ref[part, :], m2_ref[part, :])
        values = (param, first, second) if states else (param.astype(jnp.bfloat16),)
        for out, value in zip(outs, values):
            out[part, :] = value


def update(total, shard, param, first, second, max_norm, rows, states):
    block = pl.BlockSpec((rows, shard.shape[1]), lambda i: (i, 0))
    dtypes = [jnp.float32] * 3 if states else [jnp.bfloat16]
    return pl.pallas_call(
        lambda *refs: update_kernel(max_norm, states, *refs),
        grid=(shard.shape[0] // rows,),
        in_specs=[pl.BlockSpec(total.shape, lambda i: (0, 0))] + [block] * 4,
        out_specs=[block] * len(dtypes),
        out_shape=[jax.ShapeDtypeStruct(shard.shape, dtype) for dtype in dtypes],
        compiler_params=pltpu.CompilerParams(vmem_limit_bytes=LITTLE),
        cost_estimate=CHEAP,
        name="states" if states else "update",
    )(total, shard, param, first, second)


def behind_of(value, other, cost=CHEAP):
    return pl.pallas_call(
        lambda *refs: None,
        grid=(1,),
        in_specs=[pl.BlockSpec(memory_space=pl.ANY), pl.BlockSpec((PAD, 128), lambda i: (0, 0))],
        out_specs=pl.BlockSpec(memory_space=pl.ANY),
        out_shape=jax.ShapeDtypeStruct(value.shape, value.dtype),
        input_output_aliases={0: 0},
        compiler_params=pltpu.CompilerParams(vmem_limit_bytes=LITTLE),
        cost_estimate=cost,
        name="behind",
    )(value, other)


def both_of(own, other, after, cut):
    columns = own.shape[1]

    def kernel(own_ref, other_ref, after_ref, both_ref):
        both_ref[...] = jnp.where(pl.program_id(0) == 0, own_ref[...], other_ref[...])

    return pl.pallas_call(
        kernel,
        grid=(2,),
        in_specs=[
            pl.BlockSpec((cut, columns), lambda i: (0, 0)),
            pl.BlockSpec((cut, columns), lambda i: (0, 0)),
            pl.BlockSpec((PAD, 128), lambda i: (0, 0)),
        ],
        out_specs=pl.BlockSpec((cut, columns), lambda i: (i, 0)),
        out_shape=jax.ShapeDtypeStruct((2 * cut, columns), own.dtype),
        compiler_params=pltpu.CompilerParams(vmem_limit_bytes=LITTLE),
        cost_estimate=PIECE,
        name="both",
    )(own, other, after)


def fill_kernel(moves, count, *refs):
    out, sems = refs[-2:]
    r = lax.axis_index("dp")
    copies = []
    for at, (source, low, size, table, shard, first) in enumerate(moves):
        to = pl.multiple_of(lookup(table, r) * shard + first, PAD)
        copies.append(pltpu.make_async_copy(refs[source].at[low : low + size], out.at[pl.ds(to, size)], sems.at[at]))
        copies[-1].start()
    for copy in copies:
        copy.wait()


def fill(buffer, values, moves, height):
    columns = values[0].shape[1]
    return pl.pallas_call(
        lambda *refs: fill_kernel(moves, len(values), *refs),
        in_specs=[pl.BlockSpec(memory_space=pltpu.VMEM)] * len(values)
        + [pl.BlockSpec(memory_space=pltpu.HBM)] * (buffer is not None),
        out_specs=pl.BlockSpec(memory_space=pltpu.HBM),
        out_shape=jax.ShapeDtypeStruct((height, columns), values[0].dtype),
        input_output_aliases={} if buffer is None else {len(values): 0},
        scratch_shapes=[pltpu.SemaphoreType.DMA((len(moves),))],
        compiler_params=pltpu.CompilerParams(vmem_limit_bytes=LITTLE),
        cost_estimate=CHEAP,
        name="fill",
    )(*values, *([] if buffer is None else [buffer]))


def paired(weights, inputs, out_grads, master, moment1, moment2):
    n = lax.axis_size("dp")
    pairs = n // 2
    ring = list(range(0, pairs, 2)) + list(range(pairs - 1 - pairs % 2, 0, -2))
    place = {pair: at for at, pair in enumerate(ring)}

    def at_offset(r, offset, flip):
        return 2 * ring[(place[r // 2] + offset) % pairs] + ((r % 2) ^ flip)

    def table(offset, flip):
        return [at_offset(r, offset, flip) for r in range(n)]

    def send(value, offset, flip=0):
        return lax.ppermute(value, "dp", [(r, at_offset(r, offset, flip)) for r in range(n)])

    stacked = weights[0]
    x, dy = inputs[0], out_grads[0]
    width = x.shape[1]
    shard_rows = stacked.shape[0] // n
    rows = math.gcd(shard_rows, width, 256)

    steps = shard_rows // rows

    every, most, rest, end = list(range(steps)), list(range(steps - 1)), list(range(1, steps)), steps - 1

    def at(*blocks):
        return [(table(offset, flip), block) for offset, flip, block in blocks]

    def made(blocks, got=(), **more):
        return piece(x, dy, factors, rows, blocks, got, **more)

    factors, message = forward(x, dy, stacked, [at(*[(2, 1, b) for b in every])], rows)
    cross_far = send(message, 0, 1)
    message = made(at((-1, 0, end), (-1, 1, end)))
    ahead = send(message, -1)
    message = made(at(*[(-1, 1, b) for b in most]), after=message)
    cross_back = send(message, 0, 1)
    own_far = made(at(*[(2, 0, b) for b in every]), after=message, last=True)
    message = made(at(*[(1, 1, b) for b in every]), after=own_far)
    cross_next = send(message, 0, 1)
    message = made(at(*[(0, 1, b) for b in every]), [(ahead, [None] * end + [1])], after=message)
    cross_own = send(message, 0, 1)

    by_ring = send(join(own_far, cross_far, rows), 1)
    from_ahead = send(made(at(*[(-1, 0, b) for b in most]), [(cross_back, most)]), -1)
    from_behind = send(join(made(at(*[(1, 0, b) for b in every]), [(by_ring, every)], last=True), cross_next, rows), 1)
    partial = made(at(*[(0, 0, b) for b in every]), [(from_ahead, most + [None]), (ahead, [None] * end + [0])], last=True)
    shard, squares = finish(partial, [cross_own, from_behind], rows, n * lax.axis_size("section"))

    total = lax.all_to_all(squares, ("dp", "section"), 0, 0, tiled=True)
    max_norm = math.sqrt(lax.axis_size("section") * stacked.size)
    states = (shard, master[0], moment1[0], moment2[0], max_norm)
    (own,) = update(total, *states, shard_rows, False)

    cut = shard_rows * 7 // 12 // PAD * PAD
    other = send(own, 0, 1)
    behind = behind_of(send(own, 1), other)
    tail = send(own[cut:], -1)
    behind_cross = send(behind, 0, 1)
    far = send(behind, 1)
    tail = behind_of(tail, behind, cost_of(3.4))
    tail_cross = send(tail, 0, 1)
    both = send(both_of(own, other, behind_cross, cut), -1)
    far = behind_of(behind_of(far, behind_cross), tail_cross)
    far_cross = send(far, 0, 1)
    new_param, new_first, new_second = update(total, *states, rows, True)

    def move(value, offset, flip, low=0, first=0, size=shard_rows):
        return (value, low, size, table(offset, flip), shard_rows, first)

    gathered = fill(
        None,
        [own, other, behind, tail, behind_cross, tail_cross, far],
        [
            move(0, 0, 0),
            move(1, 0, 1),
            move(2, -1, 0),
            move(3, 1, 0, 0, cut, shard_rows - cut),
            move(4, -1, 1),
            move(5, 1, 1, 0, cut, shard_rows - cut),
            move(6, -2, 0),
        ],
        stacked.shape[0],
    )
    gathered = fill(
        gathered,
        [both, far_cross],
        [move(0, 1, 0, 0, 0, cut), move(0, 1, 1, cut, 0, cut), move(1, -2, 1)],
        stacked.shape[0],
    )
    return new_param[None], new_first[None], new_second[None], gathered[None]


def local(weights, *rest):
    n = lax.axis_size("dp")
    height = weights.shape[1]
    shard, width = height // n, height // 3
    fits = n == 8 and height % n == 0 and math.gcd(shard, width, 256) % 128 == 0 and shard // math.gcd(shard, width, 256) > 2
    return (paired if fits else plain)(weights, *rest)


def solution(mesh):
    whole = P("section", None, None)
    split = P("section", "dp", None)
    return jax.shard_map(
        local,
        mesh=mesh,
        in_specs=(whole, split, split, split, split, split),
        out_specs=(split, split, split, whole),
        check_vma=False,
    )
```

```python
import math

import jax
import jax.numpy as jnp
from jax import lax
from jax.experimental import pallas as pl
from jax.experimental.pallas import tpu as pltpu
from jax.sharding import PartitionSpec as P

MROWS = 256
STEP = 10
LITTLE = 16 << 20
CHUNK = 64
PAD = 16
POWER = 8
TOP = 32768.0


def cost_of(micros):
    return pl.CostEstimate(flops=int(micros * 1.18e9), bytes_accessed=1024, transcendentals=0)


PIECE = cost_of(1.7)
CHEAP = pl.CostEstimate(flops=1024, bytes_accessed=1024, transcendentals=0)


def forward_pieces(x_rows, dy_rows, w_gate, w_up, w_down):
    pre_gate = jnp.dot(x_rows, w_gate, preferred_element_type=jnp.float32)
    pre_up = jnp.dot(x_rows, w_up, preferred_element_type=jnp.float32)
    d_hidden = jnp.dot(dy_rows, w_down, preferred_element_type=jnp.float32)
    return activation(pre_gate, pre_up, d_hidden)


def activation(pre_gate, pre_up, d_hidden):
    sigma = jax.nn.sigmoid(pre_gate)
    silu_val = pre_gate * sigma
    hidden = (silu_val * pre_up).astype(jnp.bfloat16)
    d_gate = (d_hidden * pre_up * sigma * (1.0 + pre_gate * (1.0 - sigma))).astype(jnp.bfloat16)
    d_up = (d_hidden * silu_val).astype(jnp.bfloat16)
    return d_gate, d_up, hidden


def block_grads(x_rows, dy_rows, w_gate, w_up, w_down):
    d_gate, d_up, hidden = forward_pieces(x_rows, dy_rows, w_gate, w_up, w_down)
    g_gate = jnp.dot(x_rows.T, d_gate, preferred_element_type=jnp.float32)
    g_up = jnp.dot(x_rows.T, d_up, preferred_element_type=jnp.float32)
    g_down = jnp.dot(dy_rows.T, hidden, preferred_element_type=jnp.float32)
    return jnp.concatenate([g_gate, g_up, g_down], axis=0)


def adam(clip, shard, old_param, first, second):
    clipped = clip * shard
    new_first = 0.9 * first + 0.1 * clipped
    new_second = 0.95 * second + 0.05 * clipped * clipped
    first_fix = 1.0 / (1.0 - 0.9**STEP)
    second_fix = 1.0 / (1.0 - 0.95**STEP)
    update = new_first * first_fix / (jnp.sqrt(new_second * second_fix) + 1e-08) + 0.1 * old_param
    return old_param - 0.01 * update, new_first, new_second


def clip_of(total, max_norm):
    return jnp.minimum(jnp.float32(1.0), max_norm / (jnp.sqrt(total) + 1e-06))


def plain(weights, inputs, out_grads, master, moment1, moment2):
    stacked = weights[0]
    width = stacked.shape[0] // 3
    local_grad = jnp.zeros(stacked.shape, jnp.float32)
    for start in range(0, inputs.shape[1], MROWS):
        x_rows = inputs[0, start : start + MROWS]
        dy_rows = out_grads[0, start : start + MROWS]
        local_grad = local_grad + block_grads(
            x_rows, dy_rows, stacked[:width], stacked[width : 2 * width], stacked[2 * width :]
        )
    shard = lax.psum_scatter(local_grad, "dp", scatter_dimension=0, tiled=True)
    total = lax.psum(jnp.sum(shard * shard), ("dp", "section"))
    max_norm = jnp.sqrt(jnp.float32(lax.axis_size("section") * stacked.size))
    new_param, new_first, new_second = adam(clip_of(total, max_norm), shard, master[0], moment1[0], moment2[0])
    gathered = lax.all_gather(new_param.astype(jnp.bfloat16), "dp", axis=0, tiled=True)
    return new_param[None], new_first[None], new_second[None], gathered[None]


def chunks(rows):
    return [slice(at, min(at + CHUNK, rows)) for at in range(0, rows, CHUNK)]


def fold(value):
    return jnp.max(jnp.abs(value).reshape(-1, 8, value.shape[1]), axis=0)


def scale_of(top):
    scale = jnp.max(top, axis=0, keepdims=True)
    return jnp.maximum(scale, 1e-30).astype(jnp.bfloat16).astype(jnp.float32)


def encode(value, factor):
    v = value * factor
    v2 = v * v
    v4 = v2 * v2
    v8 = v4 * v4
    return jnp.where(v < 0.0, -v8, v8).astype(jnp.bfloat16)


def decode(code, factor):
    code = code.astype(jnp.float32)
    size = jnp.abs(code)
    root = jnp.exp(jnp.log(jnp.maximum(size, 1e-37)) * (1.0 / POWER)) * factor
    root = jnp.where(size > 0.0, root, 0.0)
    return jnp.where(code < 0.0, -root, root)


def write_codes(total_ref, top, out_ref, first):
    scale = scale_of(top)
    factor = TOP / scale
    for part in chunks(total_ref.shape[0]):
        size = part.stop - part.start
        out_ref[pl.ds(first + part.start, size), :] = encode(total_ref[part, :], factor)
    return scale


def lookup(table, index):
    bits = max(max(table).bit_length(), 1)
    if bits * len(table) < 32:
        packed = sum(value << (bits * at) for at, value in enumerate(table))
        return jnp.bitwise_and(jnp.right_shift(jnp.int32(packed), index * bits), (1 << bits) - 1)
    out = jnp.int32(table[0])
    for at, value in enumerate(table[1:], 1):
        out = jnp.where(index == at, jnp.int32(value), out)
    return out


def forward_kernel(messages, rows, x_hbm, dy_hbm, w_hbm, factors_ref, *refs):
    outs = refs[: len(messages)]
    x_ref, dy_ref, w_ref, a_ref, b_ref, h_ref, total_ref, sems = refs[len(messages) :]
    width = x_hbm.shape[1]
    half = width // 2

    def fetch(at, source, target, index):
        copy = pltpu.make_async_copy(source.at[index], target.at[index], sems.at[at])
        copy.start()
        return copy

    copies = []
    for columns in (pl.ds(0, half), pl.ds(half, half)):
        copies.append(fetch(len(copies), x_hbm, x_ref, (slice(None), columns)))
        copies.append(fetch(len(copies), w_hbm, w_ref, columns))
        copies.append(fetch(len(copies), w_hbm, w_ref, pl.ds(columns.start + width, half)))
    for columns in (pl.ds(0, half), pl.ds(half, half)):
        copies.append(fetch(len(copies), dy_hbm, dy_ref, (slice(None), columns)))
        copies.append(fetch(len(copies), w_hbm, w_ref, pl.ds(columns.start + 2 * width, half)))

    def product(left, start, which):
        weight = w_ref[which * width + start : which * width + start + half]
        return jnp.dot(left[:, start : start + half], weight, preferred_element_type=jnp.float32)

    for copy in copies[:3]:
        copy.wait()
    a_ref[...] = product(x_ref, 0, 0)
    b_ref[...] = product(x_ref, 0, 1)
    for copy in copies[3:6]:
        copy.wait()
    a_ref[...] += product(x_ref, half, 0)
    b_ref[...] += product(x_ref, half, 1)
    for copy in copies[6:8]:
        copy.wait()
    h_ref[...] = product(dy_ref, 0, 2)
    for copy in copies[8:]:
        copy.wait()
    h_ref[...] += product(dy_ref, half, 2)
    for part in chunks(x_ref.shape[0]):
        d_gate, d_up, hidden = activation(a_ref[part, :], b_ref[part, :], h_ref[part, :])
        factors_ref[0, part, :] = d_gate
        factors_ref[1, part, :] = d_up
        factors_ref[2, part, :] = hidden
    per = width // rows
    for places, out_ref in zip(messages, outs):
        scales = jnp.zeros((PAD, out_ref.shape[1]), jnp.float32)
        for step, place in enumerate(places):
            at = place()
            kind = lax.div(at, per)
            column = pl.ds(pl.multiple_of(lax.rem(at, per) * rows, rows), rows)
            left = jnp.where(kind == 2, dy_ref[:, column], x_ref[:, column])
            total_ref[...] = lax.dot_general(
                left, factors_ref[kind], (((0,), (0,)), ((), ())), preferred_element_type=jnp.float32
            )
            top = fold(total_ref[:CHUNK, :])
            for part in chunks(rows)[1:]:
                top = jnp.maximum(top, fold(total_ref[part, :]))
            scale = write_codes(total_ref, top, out_ref, step * rows)
            row = lax.broadcasted_iota(jnp.int32, scales.shape, 0)
            scales = jnp.where(row == step, scale, scales)
        out_ref[len(places) * rows :, :] = scales.astype(jnp.bfloat16)


def forward(x, dy, stacked, messages, rows):
    tokens, width = x.shape
    hidden = stacked.shape[1]

    def place_of(table, block):
        steps = stacked.shape[0] // len(table) // rows
        return lambda: lookup(table, lax.axis_index("dp")) * steps + block

    places = [[place_of(*block) for block in blocks] for blocks in messages]
    return pl.pallas_call(
        lambda *refs: forward_kernel(places, rows, *refs),
        in_specs=[pl.BlockSpec(memory_space=pltpu.HBM)] * 3,
        out_shape=[jax.ShapeDtypeStruct((3, tokens, hidden), jnp.bfloat16)]
        + [jax.ShapeDtypeStruct((len(blocks) * rows + PAD, hidden), jnp.bfloat16) for blocks in messages],
        scratch_shapes=[
            pltpu.VMEM(x.shape, x.dtype),
            pltpu.VMEM(dy.shape, dy.dtype),
            pltpu.VMEM(stacked.shape, stacked.dtype),
            *[pltpu.VMEM((tokens, hidden), jnp.float32)] * 3,
            pltpu.VMEM((rows, hidden), jnp.float32),
            pltpu.SemaphoreType.DMA((10,)),
        ],
        compiler_params=pltpu.CompilerParams(vmem_limit_bytes=60 << 20),
        cost_estimate=CHEAP,
        name="forward",
    )(x, dy, stacked)


def pick(values, step):
    if all(value == values[0] + at for at, value in enumerate(values)):
        return step + values[0] if len(values) > 1 else jnp.int32(values[0])
    out = jnp.int32(values[0])
    for at, value in enumerate(values[1:], 1):
        out = jnp.where(step == at, value, out)
    return out


def piece_kernel(place, per, got, extra, last, *refs):
    step = pl.program_id(0)
    x_ref, dy_ref, d_ref = refs[:3]
    outs = refs[3 + 2 * len(got) + extra :]
    rows = x_ref.shape[1]
    left = jnp.where(lax.div(place(step), per) == 2, dy_ref[...], x_ref[...])
    total_ref = outs[-1]
    total_ref[...] = lax.dot_general(left, d_ref[0], (((0,), (0,)), ((), ())), preferred_element_type=jnp.float32)
    factors = []
    for at, blocks in enumerate(got):
        scales = refs[4 + 2 * at][...].astype(jnp.float32)
        row = lax.broadcasted_iota(jnp.int32, scales.shape, 0)
        here = pick([PAD if block is None else block for block in blocks], step)
        factors.append(jnp.sum(jnp.where(row == here, scales, 0.0), axis=0, keepdims=True) * (1.0 / TOP))
    top = jnp.zeros((8, total_ref.shape[1]), jnp.float32)
    for part in chunks(rows):
        total = total_ref[part, :]
        for at, factor in enumerate(factors):
            total = total + decode(refs[3 + 2 * at][part, :], factor)
        if last:
            outs[0][part, :] = total
        else:
            if factors:
                total_ref[part, :] = total
            top = jnp.maximum(top, fold(total))
    if not last:
        out_ref, scales_ref = outs[:2]
        scale = write_codes(total_ref, top, out_ref, pl.multiple_of(step * rows, rows))
        row = lax.broadcasted_iota(jnp.int32, scales_ref.shape, 0)
        scales_ref[...] = jnp.where(row == step, scale, jnp.where(step == 0, 0.0, scales_ref[...]))
        out_ref[pl.ds(out_ref.shape[0] - PAD, PAD), :] = scales_ref[...].astype(jnp.bfloat16)


def piece(x, dy, factors, rows, blocks, got=(), after=None, last=False, cost=PIECE):
    tokens, width = x.shape
    hidden = factors.shape[2]
    per = width // rows
    shard = 3 * width // len(blocks[0][0])
    steps = shard // rows
    tables = [table for table, _ in blocks]
    within = [block for _, block in blocks]

    def place(i):
        r = lax.axis_index("dp")
        owner = lookup(tables[0], r)
        for at, table in enumerate(tables[1:], 1):
            if table != tables[at - 1]:
                owner = jnp.where(i >= at, lookup(table, r), owner)
        return owner * steps + pick(within, i)

    def column(i):
        return (0, lax.rem(place(i), per))

    in_specs = [
        pl.BlockSpec((tokens, rows), column),
        pl.BlockSpec((tokens, rows), column),
        pl.BlockSpec((1, tokens, hidden), lambda i: (lax.div(place(i), per), 0, 0)),
    ]
    operands = [x, dy, factors]
    for message, parts in got:
        present = [part for part in parts if part is not None]
        nearest = [present[0] if part is None else part for part in parts]
        scales = (message.shape[0] - PAD) // PAD
        in_specs += [
            pl.BlockSpec((rows, hidden), lambda i, nearest=nearest: (pick(nearest, i), 0)),
            pl.BlockSpec((PAD, hidden), lambda i, scales=scales: (scales, 0)),
        ]
        operands += [message, message]
    extra = 0
    if after is not None:
        extra = 1
        operands.append(after)
        in_specs.append(pl.BlockSpec(memory_space=pl.ANY))
    if last:
        out_specs = pl.BlockSpec((rows, hidden), lambda i: (i, 0))
        out_shape = jax.ShapeDtypeStruct((len(blocks) * rows, hidden), jnp.float32)
        scratch = [pltpu.VMEM((rows, hidden), jnp.float32)]
    else:
        out_specs = pl.BlockSpec((len(blocks) * rows + PAD, hidden), lambda i: (0, 0))
        out_shape = jax.ShapeDtypeStruct((len(blocks) * rows + PAD, hidden), jnp.bfloat16)
        scratch = [pltpu.VMEM((PAD, hidden), jnp.float32), pltpu.VMEM((rows, hidden), jnp.float32)]
    return pl.pallas_call(
        lambda *refs: piece_kernel(place, per, [parts for _, parts in got], extra, last, *refs),
        grid=(len(blocks),),
        in_specs=in_specs,
        out_specs=out_specs,
        out_shape=out_shape,
        scratch_shapes=scratch,
        compiler_params=pltpu.CompilerParams(vmem_limit_bytes=LITTLE),
        cost_estimate=cost,
        name="piece",
    )(*operands)


def finish_kernel(rows, sum_ref, *refs):
    out_ref, squares_ref = refs[-2:]
    height, hidden = out_ref.shape
    codes = refs[:-2]
    scales = [code[height:, :].astype(jnp.float32) * (1.0 / TOP) for code in codes]
    top = jnp.zeros((8, hidden), jnp.float32)
    for part in chunks(height):
        block = part.start // rows
        total = sum_ref[part, :]
        for code, factor in zip(codes, scales):
            total = total + decode(code[part, :], factor[block : block + 1])
        out_ref[part, :] = total
        top = top + jnp.sum((total * total).reshape(-1, 8, hidden), axis=0)
    row = jnp.sum(sum(top[:, at : at + 128] for at in range(0, hidden, 128)), axis=0, keepdims=True)
    squares_ref[...] = jnp.broadcast_to(row, squares_ref.shape)


def finish(partial, messages, rows, count):
    whole = pl.BlockSpec(partial.shape, lambda i: (0, 0))
    return pl.pallas_call(
        lambda *refs: finish_kernel(rows, *refs),
        grid=(1,),
        in_specs=[whole] + [pl.BlockSpec(message.shape, lambda i: (0, 0)) for message in messages],
        out_specs=[whole, pl.BlockSpec((count, 128), lambda i: (0, 0))],
        out_shape=[
            jax.ShapeDtypeStruct(partial.shape, jnp.float32),
            jax.ShapeDtypeStruct((count, 128), jnp.float32),
        ],
        compiler_params=pltpu.CompilerParams(vmem_limit_bytes=LITTLE),
        cost_estimate=PIECE,
        name="finish",
    )(partial, *messages)


def join_kernel(rows, sum_ref, code_ref, out_ref, total_ref):
    height, hidden = sum_ref.shape
    scales = code_ref[height:, :].astype(jnp.float32) * (1.0 / TOP)
    row = lax.broadcasted_iota(jnp.int32, scales.shape, 0)
    new_scales = jnp.zeros_like(scales)
    for block in range(height // rows):
        top = jnp.zeros((8, hidden), jnp.float32)
        for part in chunks(rows):
            here = slice(block * rows + part.start, block * rows + part.stop)
            total = sum_ref[here, :] + decode(code_ref[here, :], scales[block : block + 1])
            total_ref[part, :] = total
            top = jnp.maximum(top, fold(total))
        scale = write_codes(total_ref, top, out_ref, block * rows)
        new_scales = jnp.where(row == block, scale, new_scales)
    out_ref[height:, :] = new_scales.astype(jnp.bfloat16)


def join(partial, message, rows):
    whole = pl.BlockSpec(message.shape, lambda i: (0, 0))
    return pl.pallas_call(
        lambda *refs: join_kernel(rows, *refs),
        grid=(1,),
        in_specs=[pl.BlockSpec(partial.shape, lambda i: (0, 0)), whole],
        out_specs=whole,
        out_shape=jax.ShapeDtypeStruct(message.shape, message.dtype),
        scratch_shapes=[pltpu.VMEM((rows, partial.shape[1]), jnp.float32)],
        compiler_params=pltpu.CompilerParams(vmem_limit_bytes=LITTLE),
        cost_estimate=PIECE,
        name="join",
    )(partial, message)


def update_kernel(max_norm, states, total_ref, g_ref, p_ref, m1_ref, m2_ref, *outs):
    clip = clip_of(jnp.sum(total_ref[...], keepdims=True), max_norm)
    for part in chunks(g_ref.shape[0]):
        param, first, second = adam(clip, g_ref[part, :], p_ref[part, :], m1_ref[part, :], m2_ref[part, :])
        values = (param, first, second) if states else (param.astype(jnp.bfloat16),)
        for out, value in zip(outs, values):
            out[part, :] = value


def update(total, shard, param, first, second, max_norm, rows, states):
    block = pl.BlockSpec((rows, shard.shape[1]), lambda i: (i, 0))
    dtypes = [jnp.float32] * 3 if states else [jnp.bfloat16]
    return pl.pallas_call(
        lambda *refs: update_kernel(max_norm, states, *refs),
        grid=(shard.shape[0] // rows,),
        in_specs=[pl.BlockSpec(total.shape, lambda i: (0, 0))] + [block] * 4,
        out_specs=[block] * len(dtypes),
        out_shape=[jax.ShapeDtypeStruct(shard.shape, dtype) for dtype in dtypes],
        compiler_params=pltpu.CompilerParams(vmem_limit_bytes=LITTLE),
        cost_estimate=CHEAP,
        name="states" if states else "update",
    )(total, shard, param, first, second)


def behind_of(value, other, cost=CHEAP):
    return pl.pallas_call(
        lambda *refs: None,
        grid=(1,),
        in_specs=[pl.BlockSpec(memory_space=pl.ANY), pl.BlockSpec((PAD, 128), lambda i: (0, 0))],
        out_specs=pl.BlockSpec(memory_space=pl.ANY),
        out_shape=jax.ShapeDtypeStruct(value.shape, value.dtype),
        input_output_aliases={0: 0},
        compiler_params=pltpu.CompilerParams(vmem_limit_bytes=LITTLE),
        cost_estimate=cost,
        name="behind",
    )(value, other)


def both_of(own, other, after, cut):
    columns = own.shape[1]

    def kernel(own_ref, other_ref, after_ref, both_ref):
        both_ref[...] = jnp.where(pl.program_id(0) == 0, own_ref[...], other_ref[...])

    return pl.pallas_call(
        kernel,
        grid=(2,),
        in_specs=[
            pl.BlockSpec((cut, columns), lambda i: (0, 0)),
            pl.BlockSpec((cut, columns), lambda i: (0, 0)),
            pl.BlockSpec((PAD, 128), lambda i: (0, 0)),
        ],
        out_specs=pl.BlockSpec((cut, columns), lambda i: (i, 0)),
        out_shape=jax.ShapeDtypeStruct((2 * cut, columns), own.dtype),
        compiler_params=pltpu.CompilerParams(vmem_limit_bytes=LITTLE),
        cost_estimate=PIECE,
        name="both",
    )(own, other, after)


def fill_kernel(moves, count, *refs):
    out, sems = refs[-2:]
    r = lax.axis_index("dp")
    copies = []
    for at, (source, low, size, table, shard, first) in enumerate(moves):
        to = pl.multiple_of(lookup(table, r) * shard + first, PAD)
        copies.append(pltpu.make_async_copy(refs[source].at[low : low + size], out.at[pl.ds(to, size)], sems.at[at]))
        copies[-1].start()
    for copy in copies:
        copy.wait()


def fill(buffer, values, moves, height):
    columns = values[0].shape[1]
    return pl.pallas_call(
        lambda *refs: fill_kernel(moves, len(values), *refs),
        in_specs=[pl.BlockSpec(memory_space=pltpu.VMEM)] * len(values)
        + [pl.BlockSpec(memory_space=pltpu.HBM)] * (buffer is not None),
        out_specs=pl.BlockSpec(memory_space=pltpu.HBM),
        out_shape=jax.ShapeDtypeStruct((height, columns), values[0].dtype),
        input_output_aliases={} if buffer is None else {len(values): 0},
        scratch_shapes=[pltpu.SemaphoreType.DMA((len(moves),))],
        compiler_params=pltpu.CompilerParams(vmem_limit_bytes=LITTLE),
        cost_estimate=CHEAP,
        name="fill",
    )(*values, *([] if buffer is None else [buffer]))


def paired(weights, inputs, out_grads, master, moment1, moment2):
    n = lax.axis_size("dp")
    pairs = n // 2
    ring = list(range(0, pairs, 2)) + list(range(pairs - 1 - pairs % 2, 0, -2))
    place = {pair: at for at, pair in enumerate(ring)}

    def at_offset(r, offset, flip):
        return 2 * ring[(place[r // 2] + offset) % pairs] + ((r % 2) ^ flip)

    def table(offset, flip):
        return [at_offset(r, offset, flip) for r in range(n)]

    def send(value, offset, flip=0):
        return lax.ppermute(value, "dp", [(r, at_offset(r, offset, flip)) for r in range(n)])

    stacked = weights[0]
    x, dy = inputs[0], out_grads[0]
    width = x.shape[1]
    shard_rows = stacked.shape[0] // n
    rows = math.gcd(shard_rows, width, 256)

    steps = shard_rows // rows

    every, most, rest, end = list(range(steps)), list(range(steps - 1)), list(range(1, steps)), steps - 1

    def at(*blocks):
        return [(table(offset, flip), block) for offset, flip, block in blocks]

    def made(blocks, got=(), **more):
        return piece(x, dy, factors, rows, blocks, got, **more)

    factors, message = forward(x, dy, stacked, [at(*[(2, 1, b) for b in every])], rows)
    cross_far = send(message, 0, 1)
    message = made(at((-1, 0, end), (-1, 1, end)))
    ahead = send(message, -1)
    message = made(at(*[(-1, 1, b) for b in most]), after=message)
    cross_back = send(message, 0, 1)
    own_far = made(at(*[(2, 0, b) for b in every]), after=message, last=True)
    message = made(at(*[(1, 1, b) for b in every]), after=own_far)
    cross_next = send(message, 0, 1)
    message = made(at(*[(0, 1, b) for b in every]), [(ahead, [None] * end + [1])], after=message)
    cross_own = send(message, 0, 1)

    by_ring = send(join(own_far, cross_far, rows), 1)
    from_ahead = send(made(at(*[(-1, 0, b) for b in most]), [(cross_back, most)]), -1)
    from_behind = send(join(made(at(*[(1, 0, b) for b in every]), [(by_ring, every)], last=True), cross_next, rows), 1)
    partial = made(at(*[(0, 0, b) for b in every]), [(from_ahead, most + [None]), (ahead, [None] * end + [0])], last=True)
    shard, squares = finish(partial, [cross_own, from_behind], rows, n * lax.axis_size("section"))

    total = lax.all_to_all(squares, ("dp", "section"), 0, 0, tiled=True)
    max_norm = math.sqrt(lax.axis_size("section") * stacked.size)
    states = (shard, master[0], moment1[0], moment2[0], max_norm)
    (own,) = update(total, *states, shard_rows, False)

    cut = shard_rows * 7 // 12 // PAD * PAD
    other = send(own, 0, 1)
    behind = behind_of(send(own, 1), other)
    tail = send(own[cut:], -1)
    behind_cross = send(behind, 0, 1)
    far = send(behind, 1)
    tail = behind_of(tail, behind, cost_of(3.4))
    tail_cross = send(tail, 0, 1)
    both = send(both_of(own, other, behind_cross, cut), -1)
    far = behind_of(behind_of(far, behind_cross), tail_cross)
    far_cross = send(far, 0, 1)
    new_param, new_first, new_second = update(total, *states, rows, True)

    def move(value, offset, flip, low=0, first=0, size=shard_rows):
        return (value, low, size, table(offset, flip), shard_rows, first)

    gathered = fill(
        None,
        [own, other, behind, tail, behind_cross, tail_cross, far],
        [
            move(0, 0, 0),
            move(1, 0, 1),
            move(2, -1, 0),
            move(3, 1, 0, 0, cut, shard_rows - cut),
            move(4, -1, 1),
            move(5, 1, 1, 0, cut, shard_rows - cut),
            move(6, -2, 0),
        ],
        stacked.shape[0],
    )
    gathered = fill(
        gathered,
        [both, far_cross],
        [move(0, 1, 0, 0, 0, cut), move(0, 1, 1, cut, 0, cut), move(1, -2, 1)],
        stacked.shape[0],
    )
    return new_param[None], new_first[None], new_second[None], gathered[None]


def local(weights, *rest):
    n = lax.axis_size("dp")
    height = weights.shape[1]
    shard, width = height // n, height // 3
    fits = n == 8 and height % n == 0 and math.gcd(shard, width, 256) % 128 == 0 and shard // math.gcd(shard, width, 256) > 2
    return (paired if fits else plain)(weights, *rest)


def solution(mesh):
    whole = P("section", None, None)
    split = P("section", "dp", None)
    return jax.shard_map(
        local,
        mesh=mesh,
        in_specs=(whole, split, split, split, split, split),
        out_specs=(split, split, split, whole),
        check_vma=False,
    )
```

```python
import math

import jax
import jax.numpy as jnp
from jax import lax
from jax.experimental import pallas as pl
from jax.experimental.pallas import tpu as pltpu
from jax.sharding import PartitionSpec as P

MROWS = 256
STEP = 10
LITTLE = 16 << 20
CHUNK = 32
PAD = 16
POWER = 8
TOP = 32768.0


def cost_of(micros):
    return pl.CostEstimate(flops=int(micros * 1.18e9), bytes_accessed=1024, transcendentals=0)


PIECE = cost_of(1.2)
CHEAP = pl.CostEstimate(flops=1024, bytes_accessed=1024, transcendentals=0)


def forward_pieces(x_rows, dy_rows, w_gate, w_up, w_down):
    pre_gate = jnp.dot(x_rows, w_gate, preferred_element_type=jnp.float32)
    pre_up = jnp.dot(x_rows, w_up, preferred_element_type=jnp.float32)
    d_hidden = jnp.dot(dy_rows, w_down, preferred_element_type=jnp.float32)
    return activation(pre_gate, pre_up, d_hidden)


def activation(pre_gate, pre_up, d_hidden):
    sigma = jax.nn.sigmoid(pre_gate)
    silu_val = pre_gate * sigma
    hidden = (silu_val * pre_up).astype(jnp.bfloat16)
    d_gate = (d_hidden * pre_up * sigma * (1.0 + pre_gate * (1.0 - sigma))).astype(jnp.bfloat16)
    d_up = (d_hidden * silu_val).astype(jnp.bfloat16)
    return d_gate, d_up, hidden


def block_grads(x_rows, dy_rows, w_gate, w_up, w_down):
    d_gate, d_up, hidden = forward_pieces(x_rows, dy_rows, w_gate, w_up, w_down)
    g_gate = jnp.dot(x_rows.T, d_gate, preferred_element_type=jnp.float32)
    g_up = jnp.dot(x_rows.T, d_up, preferred_element_type=jnp.float32)
    g_down = jnp.dot(dy_rows.T, hidden, preferred_element_type=jnp.float32)
    return jnp.concatenate([g_gate, g_up, g_down], axis=0)


def adam(clip, shard, old_param, first, second):
    clipped = clip * shard
    new_first = 0.9 * first + 0.1 * clipped
    new_second = 0.95 * second + 0.05 * clipped * clipped
    first_fix = 1.0 / (1.0 - 0.9**STEP)
    second_fix = 1.0 / (1.0 - 0.95**STEP)
    update = new_first * first_fix / (jnp.sqrt(new_second * second_fix) + 1e-08) + 0.1 * old_param
    return old_param - 0.01 * update, new_first, new_second


def clip_of(total, max_norm):
    return jnp.minimum(jnp.float32(1.0), max_norm / (jnp.sqrt(total) + 1e-06))


def plain(weights, inputs, out_grads, master, moment1, moment2):
    stacked = weights[0]
    width = stacked.shape[0] // 3
    local_grad = jnp.zeros(stacked.shape, jnp.float32)
    for start in range(0, inputs.shape[1], MROWS):
        x_rows = inputs[0, start : start + MROWS]
        dy_rows = out_grads[0, start : start + MROWS]
        local_grad = local_grad + block_grads(
            x_rows, dy_rows, stacked[:width], stacked[width : 2 * width], stacked[2 * width :]
        )
    shard = lax.psum_scatter(local_grad, "dp", scatter_dimension=0, tiled=True)
    total = lax.psum(jnp.sum(shard * shard), ("dp", "section"))
    max_norm = jnp.sqrt(jnp.float32(lax.axis_size("section") * stacked.size))
    new_param, new_first, new_second = adam(clip_of(total, max_norm), shard, master[0], moment1[0], moment2[0])
    gathered = lax.all_gather(new_param.astype(jnp.bfloat16), "dp", axis=0, tiled=True)
    return new_param[None], new_first[None], new_second[None], gathered[None]


def chunks(rows):
    return [slice(at, min(at + CHUNK, rows)) for at in range(0, rows, CHUNK)]


def fold(value):
    return jnp.max(jnp.abs(value).reshape(-1, 8, value.shape[1]), axis=0)


def scale_of(top):
    scale = jnp.max(top, axis=0, keepdims=True)
    return jnp.maximum(scale, 1e-30).astype(jnp.bfloat16).astype(jnp.float32)


def encode(value, factor):
    v = value * factor
    v2 = v * v
    v4 = v2 * v2
    v8 = v4 * v4
    return jnp.where(v < 0.0, -v8, v8).astype(jnp.bfloat16)


def decode(code, factor):
    code = code.astype(jnp.float32)
    size = jnp.abs(code)
    root = jnp.exp(jnp.log(jnp.maximum(size, 1e-37)) * (1.0 / POWER)) * factor
    root = jnp.where(size > 0.0, root, 0.0)
    return jnp.where(code < 0.0, -root, root)


def write_codes(total_ref, top, out_ref, first):
    scale = scale_of(top)
    factor = TOP / scale
    for part in chunks(total_ref.shape[0]):
        size = part.stop - part.start
        out_ref[pl.ds(first + part.start, size), :] = encode(total_ref[part, :], factor)
    return scale


def lookup(table, index):
    bits = max(max(table).bit_length(), 1)
    if bits * len(table) < 32:
        packed = sum(value << (bits * at) for at, value in enumerate(table))
        return jnp.bitwise_and(jnp.right_shift(jnp.int32(packed), index * bits), (1 << bits) - 1)
    out = jnp.int32(table[0])
    for at, value in enumerate(table[1:], 1):
        out = jnp.where(index == at, jnp.int32(value), out)
    return out


def forward_kernel(messages, rows, x_hbm, dy_hbm, w_hbm, factors_ref, *refs):
    outs = refs[: len(messages)]
    x_ref, dy_ref, w_ref, a_ref, b_ref, h_ref, total_ref, sems = refs[len(messages) :]
    width = x_hbm.shape[1]
    half = width // 2

    def fetch(at, source, target, index):
        copy = pltpu.make_async_copy(source.at[index], target.at[index], sems.at[at])
        copy.start()
        return copy

    copies = []
    for columns in (pl.ds(0, half), pl.ds(half, half)):
        copies.append(fetch(len(copies), x_hbm, x_ref, (slice(None), columns)))
        copies.append(fetch(len(copies), w_hbm, w_ref, columns))
        copies.append(fetch(len(copies), w_hbm, w_ref, pl.ds(columns.start + width, half)))
    for columns in (pl.ds(0, half), pl.ds(half, half)):
        copies.append(fetch(len(copies), dy_hbm, dy_ref, (slice(None), columns)))
        copies.append(fetch(len(copies), w_hbm, w_ref, pl.ds(columns.start + 2 * width, half)))

    def product(left, start, which):
        weight = w_ref[which * width + start : which * width + start + half]
        return jnp.dot(left[:, start : start + half], weight, preferred_element_type=jnp.float32)

    for copy in copies[:3]:
        copy.wait()
    a_ref[...] = product(x_ref, 0, 0)
    b_ref[...] = product(x_ref, 0, 1)
    for copy in copies[3:6]:
        copy.wait()
    a_ref[...] += product(x_ref, half, 0)
    b_ref[...] += product(x_ref, half, 1)
    for copy in copies[6:8]:
        copy.wait()
    h_ref[...] = product(dy_ref, 0, 2)
    for copy in copies[8:]:
        copy.wait()
    h_ref[...] += product(dy_ref, half, 2)
    for part in chunks(x_ref.shape[0]):
        d_gate, d_up, hidden = activation(a_ref[part, :], b_ref[part, :], h_ref[part, :])
        factors_ref[0, part, :] = d_gate
        factors_ref[1, part, :] = d_up
        factors_ref[2, part, :] = hidden
    per = width // rows
    for places, out_ref in zip(messages, outs):
        scales = jnp.zeros((PAD, out_ref.shape[1]), jnp.float32)
        for step, place in enumerate(places):
            at = place()
            kind = lax.div(at, per)
            column = pl.ds(pl.multiple_of(lax.rem(at, per) * rows, rows), rows)
            left = jnp.where(kind == 2, dy_ref[:, column], x_ref[:, column])
            total_ref[...] = lax.dot_general(
                left, factors_ref[kind], (((0,), (0,)), ((), ())), preferred_element_type=jnp.float32
            )
            top = fold(total_ref[:CHUNK, :])
            for part in chunks(rows)[1:]:
                top = jnp.maximum(top, fold(total_ref[part, :]))
            scale = write_codes(total_ref, top, out_ref, step * rows)
            row = lax.broadcasted_iota(jnp.int32, scales.shape, 0)
            scales = jnp.where(row == step, scale, scales)
        out_ref[len(places) * rows :, :] = scales.astype(jnp.bfloat16)


def forward(x, dy, stacked, messages, rows):
    tokens, width = x.shape
    hidden = stacked.shape[1]

    def place_of(table, block):
        steps = stacked.shape[0] // len(table) // rows
        return lambda: lookup(table, lax.axis_index("dp")) * steps + block

    places = [[place_of(*block) for block in blocks] for blocks in messages]
    return pl.pallas_call(
        lambda *refs: forward_kernel(places, rows, *refs),
        in_specs=[pl.BlockSpec(memory_space=pltpu.HBM)] * 3,
        out_shape=[jax.ShapeDtypeStruct((3, tokens, hidden), jnp.bfloat16)]
        + [jax.ShapeDtypeStruct((len(blocks) * rows + PAD, hidden), jnp.bfloat16) for blocks in messages],
        scratch_shapes=[
            pltpu.VMEM(x.shape, x.dtype),
            pltpu.VMEM(dy.shape, dy.dtype),
            pltpu.VMEM(stacked.shape, stacked.dtype),
            *[pltpu.VMEM((tokens, hidden), jnp.float32)] * 3,
            pltpu.VMEM((rows, hidden), jnp.float32),
            pltpu.SemaphoreType.DMA((10,)),
        ],
        compiler_params=pltpu.CompilerParams(vmem_limit_bytes=60 << 20),
        cost_estimate=CHEAP,
        name="forward",
    )(x, dy, stacked)


def pick(values, step):
    if all(value == values[0] + at for at, value in enumerate(values)):
        return step + values[0] if len(values) > 1 else jnp.int32(values[0])
    out = jnp.int32(values[0])
    for at, value in enumerate(values[1:], 1):
        out = jnp.where(step == at, value, out)
    return out


def piece_kernel(place, per, got, extra, last, *refs):
    step = pl.program_id(0)
    x_ref, dy_ref, d_ref = refs[:3]
    outs = refs[3 + 2 * len(got) + extra :]
    rows = x_ref.shape[1]
    left = jnp.where(lax.div(place(step), per) == 2, dy_ref[...], x_ref[...])
    total_ref = outs[-1]
    total_ref[...] = lax.dot_general(left, d_ref[0], (((0,), (0,)), ((), ())), preferred_element_type=jnp.float32)
    factors = []
    for at, blocks in enumerate(got):
        scales = refs[4 + 2 * at][...].astype(jnp.float32)
        row = lax.broadcasted_iota(jnp.int32, scales.shape, 0)
        here = pick([PAD if block is None else block for block in blocks], step)
        factors.append(jnp.sum(jnp.where(row == here, scales, 0.0), axis=0, keepdims=True) * (1.0 / TOP))
    top = jnp.zeros((8, total_ref.shape[1]), jnp.float32)
    for part in chunks(rows):
        total = total_ref[part, :]
        for at, factor in enumerate(factors):
            total = total + decode(refs[3 + 2 * at][part, :], factor)
        if last:
            outs[0][part, :] = total
        else:
            if factors:
                total_ref[part, :] = total
            top = jnp.maximum(top, fold(total))
    if not last:
        out_ref, scales_ref = outs[:2]
        scale = write_codes(total_ref, top, out_ref, pl.multiple_of(step * rows, rows))
        row = lax.broadcasted_iota(jnp.int32, scales_ref.shape, 0)
        scales_ref[...] = jnp.where(row == step, scale, jnp.where(step == 0, 0.0, scales_ref[...]))
        out_ref[pl.ds(out_ref.shape[0] - PAD, PAD), :] = scales_ref[...].astype(jnp.bfloat16)


def piece(x, dy, factors, rows, blocks, got=(), after=None, last=False, cost=PIECE):
    tokens, width = x.shape
    hidden = factors.shape[2]
    per = width // rows
    shard = 3 * width // len(blocks[0][0])
    steps = shard // rows
    tables = [table for table, _ in blocks]
    within = [block for _, block in blocks]

    def place(i):
        r = lax.axis_index("dp")
        owner = lookup(tables[0], r)
        for at, table in enumerate(tables[1:], 1):
            if table != tables[at - 1]:
                owner = jnp.where(i >= at, lookup(table, r), owner)
        return owner * steps + pick(within, i)

    def column(i):
        return (0, lax.rem(place(i), per))

    in_specs = [
        pl.BlockSpec((tokens, rows), column),
        pl.BlockSpec((tokens, rows), column),
        pl.BlockSpec((1, tokens, hidden), lambda i: (lax.div(place(i), per), 0, 0)),
    ]
    operands = [x, dy, factors]
    for message, parts in got:
        present = [part for part in parts if part is not None]
        nearest = [present[0] if part is None else part for part in parts]
        scales = (message.shape[0] - PAD) // PAD
        in_specs += [
            pl.BlockSpec((rows, hidden), lambda i, nearest=nearest: (pick(nearest, i), 0)),
            pl.BlockSpec((PAD, hidden), lambda i, scales=scales: (scales, 0)),
        ]
        operands += [message, message]
    extra = 0
    if after is not None:
        extra = 1
        operands.append(after)
        in_specs.append(pl.BlockSpec(memory_space=pl.ANY))
    if last:
        out_specs = pl.BlockSpec((rows, hidden), lambda i: (i, 0))
        out_shape = jax.ShapeDtypeStruct((len(blocks) * rows, hidden), jnp.float32)
        scratch = [pltpu.VMEM((rows, hidden), jnp.float32)]
    else:
        out_specs = pl.BlockSpec((len(blocks) * rows + PAD, hidden), lambda i: (0, 0))
        out_shape = jax.ShapeDtypeStruct((len(blocks) * rows + PAD, hidden), jnp.bfloat16)
        scratch = [pltpu.VMEM((PAD, hidden), jnp.float32), pltpu.VMEM((rows, hidden), jnp.float32)]
    return pl.pallas_call(
        lambda *refs: piece_kernel(place, per, [parts for _, parts in got], extra, last, *refs),
        grid=(len(blocks),),
        in_specs=in_specs,
        out_specs=out_specs,
        out_shape=out_shape,
        scratch_shapes=scratch,
        compiler_params=pltpu.CompilerParams(vmem_limit_bytes=LITTLE),
        cost_estimate=cost,
        name="piece",
    )(*operands)


def finish_kernel(rows, sum_ref, *refs):
    out_ref, squares_ref = refs[-2:]
    height, hidden = out_ref.shape
    codes = refs[:-2]
    scales = [code[height:, :].astype(jnp.float32) * (1.0 / TOP) for code in codes]
    top = jnp.zeros((8, hidden), jnp.float32)
    for part in chunks(height):
        block = part.start // rows
        total = sum_ref[part, :]
        for code, factor in zip(codes, scales):
            total = total + decode(code[part, :], factor[block : block + 1])
        out_ref[part, :] = total
        top = top + jnp.sum((total * total).reshape(-1, 8, hidden), axis=0)
    row = jnp.sum(sum(top[:, at : at + 128] for at in range(0, hidden, 128)), axis=0, keepdims=True)
    squares_ref[...] = jnp.broadcast_to(row, squares_ref.shape)


def finish(partial, messages, rows, count):
    whole = pl.BlockSpec(partial.shape, lambda i: (0, 0))
    return pl.pallas_call(
        lambda *refs: finish_kernel(rows, *refs),
        grid=(1,),
        in_specs=[whole] + [pl.BlockSpec(message.shape, lambda i: (0, 0)) for message in messages],
        out_specs=[whole, pl.BlockSpec((count, 128), lambda i: (0, 0))],
        out_shape=[
            jax.ShapeDtypeStruct(partial.shape, jnp.float32),
            jax.ShapeDtypeStruct((count, 128), jnp.float32),
        ],
        compiler_params=pltpu.CompilerParams(vmem_limit_bytes=LITTLE),
        cost_estimate=PIECE,
        name="finish",
    )(partial, *messages)


def join_kernel(rows, sum_ref, code_ref, out_ref, total_ref):
    height, hidden = sum_ref.shape
    scales = code_ref[height:, :].astype(jnp.float32) * (1.0 / TOP)
    row = lax.broadcasted_iota(jnp.int32, scales.shape, 0)
    new_scales = jnp.zeros_like(scales)
    for block in range(height // rows):
        top = jnp.zeros((8, hidden), jnp.float32)
        for part in chunks(rows):
            here = slice(block * rows + part.start, block * rows + part.stop)
            total = sum_ref[here, :] + decode(code_ref[here, :], scales[block : block + 1])
            total_ref[part, :] = total
            top = jnp.maximum(top, fold(total))
        scale = write_codes(total_ref, top, out_ref, block * rows)
        new_scales = jnp.where(row == block, scale, new_scales)
    out_ref[height:, :] = new_scales.astype(jnp.bfloat16)


def join(partial, message, rows):
    whole = pl.BlockSpec(message.shape, lambda i: (0, 0))
    return pl.pallas_call(
        lambda *refs: join_kernel(rows, *refs),
        grid=(1,),
        in_specs=[pl.BlockSpec(partial.shape, lambda i: (0, 0)), whole],
        out_specs=whole,
        out_shape=jax.ShapeDtypeStruct(message.shape, message.dtype),
        scratch_shapes=[pltpu.VMEM((rows, partial.shape[1]), jnp.float32)],
        compiler_params=pltpu.CompilerParams(vmem_limit_bytes=LITTLE),
        cost_estimate=PIECE,
        name="join",
    )(partial, message)


def update_kernel(max_norm, states, total_ref, g_ref, p_ref, m1_ref, m2_ref, *outs):
    clip = clip_of(jnp.sum(total_ref[...], keepdims=True), max_norm)
    for part in chunks(g_ref.shape[0]):
        param, first, second = adam(clip, g_ref[part, :], p_ref[part, :], m1_ref[part, :], m2_ref[part, :])
        values = (param, first, second) if states else (param.astype(jnp.bfloat16),)
        for out, value in zip(outs, values):
            out[part, :] = value


def update(total, shard, param, first, second, max_norm, rows, states):
    block = pl.BlockSpec((rows, shard.shape[1]), lambda i: (i, 0))
    dtypes = [jnp.float32] * 3 if states else [jnp.bfloat16]
    return pl.pallas_call(
        lambda *refs: update_kernel(max_norm, states, *refs),
        grid=(shard.shape[0] // rows,),
        in_specs=[pl.BlockSpec(total.shape, lambda i: (0, 0))] + [block] * 4,
        out_specs=[block] * len(dtypes),
        out_shape=[jax.ShapeDtypeStruct(shard.shape, dtype) for dtype in dtypes],
        compiler_params=pltpu.CompilerParams(vmem_limit_bytes=LITTLE),
        cost_estimate=CHEAP,
        name="states" if states else "update",
    )(total, shard, param, first, second)


def behind_of(value, other, cost=CHEAP):
    return pl.pallas_call(
        lambda *refs: None,
        grid=(1,),
        in_specs=[pl.BlockSpec(memory_space=pl.ANY), pl.BlockSpec((PAD, 128), lambda i: (0, 0))],
        out_specs=pl.BlockSpec(memory_space=pl.ANY),
        out_shape=jax.ShapeDtypeStruct(value.shape, value.dtype),
        input_output_aliases={0: 0},
        compiler_params=pltpu.CompilerParams(vmem_limit_bytes=LITTLE),
        cost_estimate=cost,
        name="behind",
    )(value, other)


def both_of(own, other, after, cut):
    columns = own.shape[1]

    def kernel(own_ref, other_ref, after_ref, both_ref):
        both_ref[...] = jnp.where(pl.program_id(0) == 0, own_ref[...], other_ref[...])

    return pl.pallas_call(
        kernel,
        grid=(2,),
        in_specs=[
            pl.BlockSpec((cut, columns), lambda i: (0, 0)),
            pl.BlockSpec((cut, columns), lambda i: (0, 0)),
            pl.BlockSpec((PAD, 128), lambda i: (0, 0)),
        ],
        out_specs=pl.BlockSpec((cut, columns), lambda i: (i, 0)),
        out_shape=jax.ShapeDtypeStruct((2 * cut, columns), own.dtype),
        compiler_params=pltpu.CompilerParams(vmem_limit_bytes=LITTLE),
        cost_estimate=PIECE,
        name="both",
    )(own, other, after)


def fill_kernel(moves, count, *refs):
    out, sems = refs[-2:]
    r = lax.axis_index("dp")
    copies = []
    for at, (source, low, size, table, shard, first) in enumerate(moves):
        to = pl.multiple_of(lookup(table, r) * shard + first, PAD)
        copies.append(pltpu.make_async_copy(refs[source].at[low : low + size], out.at[pl.ds(to, size)], sems.at[at]))
        copies[-1].start()
    for copy in copies:
        copy.wait()


def fill(buffer, values, moves, height):
    columns = values[0].shape[1]
    return pl.pallas_call(
        lambda *refs: fill_kernel(moves, len(values), *refs),
        in_specs=[pl.BlockSpec(memory_space=pltpu.VMEM)] * len(values)
        + [pl.BlockSpec(memory_space=pltpu.HBM)] * (buffer is not None),
        out_specs=pl.BlockSpec(memory_space=pltpu.HBM),
        out_shape=jax.ShapeDtypeStruct((height, columns), values[0].dtype),
        input_output_aliases={} if buffer is None else {len(values): 0},
        scratch_shapes=[pltpu.SemaphoreType.DMA((len(moves),))],
        compiler_params=pltpu.CompilerParams(vmem_limit_bytes=LITTLE),
        cost_estimate=CHEAP,
        name="fill",
    )(*values, *([] if buffer is None else [buffer]))


def paired(weights, inputs, out_grads, master, moment1, moment2):
    n = lax.axis_size("dp")
    pairs = n // 2
    ring = list(range(0, pairs, 2)) + list(range(pairs - 1 - pairs % 2, 0, -2))
    place = {pair: at for at, pair in enumerate(ring)}

    def at_offset(r, offset, flip):
        return 2 * ring[(place[r // 2] + offset) % pairs] + ((r % 2) ^ flip)

    def table(offset, flip):
        return [at_offset(r, offset, flip) for r in range(n)]

    def send(value, offset, flip=0):
        return lax.ppermute(value, "dp", [(r, at_offset(r, offset, flip)) for r in range(n)])

    stacked = weights[0]
    x, dy = inputs[0], out_grads[0]
    width = x.shape[1]
    shard_rows = stacked.shape[0] // n
    rows = math.gcd(shard_rows, width, 256)

    steps = shard_rows // rows

    every, most, rest, end = list(range(steps)), list(range(steps - 1)), list(range(1, steps)), steps - 1

    def at(*blocks):
        return [(table(offset, flip), block) for offset, flip, block in blocks]

    def made(blocks, got=(), **more):
        return piece(x, dy, factors, rows, blocks, got, **more)

    factors, message = forward(x, dy, stacked, [at(*[(2, 1, b) for b in every])], rows)
    cross_far = send(message, 0, 1)
    message = made(at((-1, 0, end), (-1, 1, end)))
    ahead = send(message, -1)
    message = made(at(*[(-1, 1, b) for b in most]), after=message)
    cross_back = send(message, 0, 1)
    own_far = made(at(*[(2, 0, b) for b in every]), after=message, last=True)
    message = made(at(*[(1, 1, b) for b in every]), after=own_far)
    cross_next = send(message, 0, 1)
    own_back = made(at(*[(-1, 0, b) for b in most]), after=message, last=True)
    by_ring = send(join(own_far, cross_far, rows), 1)
    message = join(own_back, cross_back, rows)
    from_ahead = send(message, -1)
    message = made(at(*[(0, 1, b) for b in every]), [(ahead, [None] * end + [1])], after=message)
    cross_own = send(message, 0, 1)
    from_behind = send(join(made(at(*[(1, 0, b) for b in every]), [(by_ring, every)], last=True), cross_next, rows), 1)
    partial = made(at(*[(0, 0, b) for b in every]), [(from_ahead, most + [None]), (ahead, [None] * end + [0])], last=True)
    shard, squares = finish(partial, [cross_own, from_behind], rows, n * lax.axis_size("section"))

    total = lax.all_to_all(squares, ("dp", "section"), 0, 0, tiled=True)
    max_norm = math.sqrt(lax.axis_size("section") * stacked.size)
    states = (shard, master[0], moment1[0], moment2[0], max_norm)
    (own,) = update(total, *states, shard_rows, False)

    cut = shard_rows * 7 // 12 // PAD * PAD
    other = send(own, 0, 1)
    behind = behind_of(send(own, 1), other)
    tail = send(own[cut:], -1)
    behind_cross = send(behind, 0, 1)
    far = send(behind, 1)
    tail = behind_of(tail, behind, cost_of(3.4))
    tail_cross = send(tail, 0, 1)
    both = send(both_of(own, other, behind_cross, cut), -1)
    far = behind_of(behind_of(far, behind_cross), tail_cross)
    far_cross = send(far, 0, 1)
    new_param, new_first, new_second = update(total, *states, rows, True)

    def move(value, offset, flip, low=0, first=0, size=shard_rows):
        return (value, low, size, table(offset, flip), shard_rows, first)

    gathered = fill(
        None,
        [own, other, behind, tail, behind_cross, tail_cross, far],
        [
            move(0, 0, 0),
            move(1, 0, 1),
            move(2, -1, 0),
            move(3, 1, 0, 0, cut, shard_rows - cut),
            move(4, -1, 1),
            move(5, 1, 1, 0, cut, shard_rows - cut),
            move(6, -2, 0),
        ],
        stacked.shape[0],
    )
    gathered = fill(
        gathered,
        [both, far_cross],
        [move(0, 1, 0, 0, 0, cut), move(0, 1, 1, cut, 0, cut), move(1, -2, 1)],
        stacked.shape[0],
    )
    return new_param[None], new_first[None], new_second[None], gathered[None]


def local(weights, *rest):
    n = lax.axis_size("dp")
    height = weights.shape[1]
    shard, width = height // n, height // 3
    fits = n == 8 and height % n == 0 and math.gcd(shard, width, 256) % 128 == 0 and shard // math.gcd(shard, width, 256) > 2
    return (paired if fits else plain)(weights, *rest)


def solution(mesh):
    whole = P("section", None, None)
    split = P("section", "dp", None)
    return jax.shard_map(
        local,
        mesh=mesh,
        in_specs=(whole, split, split, split, split, split),
        out_specs=(split, split, split, whole),
        check_vma=False,
    )
```

```python
import math

import jax
import jax.numpy as jnp
from jax import lax
from jax.experimental import pallas as pl
from jax.experimental.pallas import tpu as pltpu
from jax.sharding import PartitionSpec as P

MROWS = 256
STEP = 10
LITTLE = 16 << 20
CHUNK = 32
PAD = 16
POWER = 8
TOP = 32768.0


def cost_of(micros):
    return pl.CostEstimate(flops=int(micros * 1.18e9), bytes_accessed=1024, transcendentals=0)


PIECE = cost_of(1.2)
CHEAP = pl.CostEstimate(flops=1024, bytes_accessed=1024, transcendentals=0)


def forward_pieces(x_rows, dy_rows, w_gate, w_up, w_down):
    pre_gate = jnp.dot(x_rows, w_gate, preferred_element_type=jnp.float32)
    pre_up = jnp.dot(x_rows, w_up, preferred_element_type=jnp.float32)
    d_hidden = jnp.dot(dy_rows, w_down, preferred_element_type=jnp.float32)
    return activation(pre_gate, pre_up, d_hidden)


def activation(pre_gate, pre_up, d_hidden):
    sigma = jax.nn.sigmoid(pre_gate)
    silu_val = pre_gate * sigma
    hidden = (silu_val * pre_up).astype(jnp.bfloat16)
    d_gate = (d_hidden * pre_up * sigma * (1.0 + pre_gate * (1.0 - sigma))).astype(jnp.bfloat16)
    d_up = (d_hidden * silu_val).astype(jnp.bfloat16)
    return d_gate, d_up, hidden


def block_grads(x_rows, dy_rows, w_gate, w_up, w_down):
    d_gate, d_up, hidden = forward_pieces(x_rows, dy_rows, w_gate, w_up, w_down)
    g_gate = jnp.dot(x_rows.T, d_gate, preferred_element_type=jnp.float32)
    g_up = jnp.dot(x_rows.T, d_up, preferred_element_type=jnp.float32)
    g_down = jnp.dot(dy_rows.T, hidden, preferred_element_type=jnp.float32)
    return jnp.concatenate([g_gate, g_up, g_down], axis=0)


def adam(clip, shard, old_param, first, second):
    clipped = clip * shard
    new_first = 0.9 * first + 0.1 * clipped
    new_second = 0.95 * second + 0.05 * clipped * clipped
    first_fix = 1.0 / (1.0 - 0.9**STEP)
    second_fix = 1.0 / (1.0 - 0.95**STEP)
    update = new_first * first_fix / (jnp.sqrt(new_second * second_fix) + 1e-08) + 0.1 * old_param
    return old_param - 0.01 * update, new_first, new_second


def clip_of(total, max_norm):
    return jnp.minimum(jnp.float32(1.0), max_norm / (jnp.sqrt(total) + 1e-06))


def plain(weights, inputs, out_grads, master, moment1, moment2):
    stacked = weights[0]
    width = stacked.shape[0] // 3
    local_grad = jnp.zeros(stacked.shape, jnp.float32)
    for start in range(0, inputs.shape[1], MROWS):
        x_rows = inputs[0, start : start + MROWS]
        dy_rows = out_grads[0, start : start + MROWS]
        local_grad = local_grad + block_grads(
            x_rows, dy_rows, stacked[:width], stacked[width : 2 * width], stacked[2 * width :]
        )
    shard = lax.psum_scatter(local_grad, "dp", scatter_dimension=0, tiled=True)
    total = lax.psum(jnp.sum(shard * shard), ("dp", "section"))
    max_norm = jnp.sqrt(jnp.float32(lax.axis_size("section") * stacked.size))
    new_param, new_first, new_second = adam(clip_of(total, max_norm), shard, master[0], moment1[0], moment2[0])
    gathered = lax.all_gather(new_param.astype(jnp.bfloat16), "dp", axis=0, tiled=True)
    return new_param[None], new_first[None], new_second[None], gathered[None]


def chunks(rows):
    return [slice(at, min(at + CHUNK, rows)) for at in range(0, rows, CHUNK)]


def fold(value):
    return jnp.max(jnp.abs(value).reshape(-1, 8, value.shape[1]), axis=0)


def scale_of(top):
    scale = jnp.max(top, axis=0, keepdims=True)
    return jnp.maximum(scale, 1e-30).astype(jnp.bfloat16).astype(jnp.float32)


def encode(value, factor):
    v = value * factor
    v2 = v * v
    v4 = v2 * v2
    v8 = v4 * v4
    return jnp.where(v < 0.0, -v8, v8).astype(jnp.bfloat16)


def decode(code, factor):
    code = code.astype(jnp.float32)
    size = jnp.abs(code)
    root = jnp.exp(jnp.log(jnp.maximum(size, 1e-37)) * (1.0 / POWER)) * factor
    root = jnp.where(size > 0.0, root, 0.0)
    return jnp.where(code < 0.0, -root, root)


def write_codes(total_ref, top, out_ref, first):
    scale = scale_of(top)
    factor = TOP / scale
    for part in chunks(total_ref.shape[0]):
        size = part.stop - part.start
        out_ref[pl.ds(first + part.start, size), :] = encode(total_ref[part, :], factor)
    return scale


def lookup(table, index):
    bits = max(max(table).bit_length(), 1)
    if bits * len(table) < 32:
        packed = sum(value << (bits * at) for at, value in enumerate(table))
        return jnp.bitwise_and(jnp.right_shift(jnp.int32(packed), index * bits), (1 << bits) - 1)
    out = jnp.int32(table[0])
    for at, value in enumerate(table[1:], 1):
        out = jnp.where(index == at, jnp.int32(value), out)
    return out


def forward_kernel(messages, rows, x_hbm, dy_hbm, w_hbm, factors_ref, *refs):
    outs = refs[: len(messages)]
    x_ref, dy_ref, w_ref, a_ref, b_ref, h_ref, total_ref, sems = refs[len(messages) :]
    width = x_hbm.shape[1]
    half = width // 2

    def fetch(at, source, target, index):
        copy = pltpu.make_async_copy(source.at[index], target.at[index], sems.at[at])
        copy.start()
        return copy

    copies = []
    for columns in (pl.ds(0, half), pl.ds(half, half)):
        copies.append(fetch(len(copies), x_hbm, x_ref, (slice(None), columns)))
        copies.append(fetch(len(copies), w_hbm, w_ref, columns))
        copies.append(fetch(len(copies), w_hbm, w_ref, pl.ds(columns.start + width, half)))
    for columns in (pl.ds(0, half), pl.ds(half, half)):
        copies.append(fetch(len(copies), dy_hbm, dy_ref, (slice(None), columns)))
        copies.append(fetch(len(copies), w_hbm, w_ref, pl.ds(columns.start + 2 * width, half)))

    def product(left, start, which):
        weight = w_ref[which * width + start : which * width + start + half]
        return jnp.dot(left[:, start : start + half], weight, preferred_element_type=jnp.float32)

    for copy in copies[:3]:
        copy.wait()
    a_ref[...] = product(x_ref, 0, 0)
    b_ref[...] = product(x_ref, 0, 1)
    for copy in copies[3:6]:
        copy.wait()
    a_ref[...] += product(x_ref, half, 0)
    b_ref[...] += product(x_ref, half, 1)
    for copy in copies[6:8]:
        copy.wait()
    h_ref[...] = product(dy_ref, 0, 2)
    for copy in copies[8:]:
        copy.wait()
    h_ref[...] += product(dy_ref, half, 2)
    for part in chunks(x_ref.shape[0]):
        d_gate, d_up, hidden = activation(a_ref[part, :], b_ref[part, :], h_ref[part, :])
        factors_ref[0, part, :] = d_gate
        factors_ref[1, part, :] = d_up
        factors_ref[2, part, :] = hidden
    per = width // rows
    for places, out_ref in zip(messages, outs):
        scales = jnp.zeros((PAD, out_ref.shape[1]), jnp.float32)
        for step, place in enumerate(places):
            at = place()
            kind = lax.div(at, per)
            column = pl.ds(pl.multiple_of(lax.rem(at, per) * rows, rows), rows)
            left = jnp.where(kind == 2, dy_ref[:, column], x_ref[:, column])
            total_ref[...] = lax.dot_general(
                left, factors_ref[kind], (((0,), (0,)), ((), ())), preferred_element_type=jnp.float32
            )
            top = fold(total_ref[:CHUNK, :])
            for part in chunks(rows)[1:]:
                top = jnp.maximum(top, fold(total_ref[part, :]))
            scale = write_codes(total_ref, top, out_ref, step * rows)
            row = lax.broadcasted_iota(jnp.int32, scales.shape, 0)
            scales = jnp.where(row == step, scale, scales)
        out_ref[len(places) * rows :, :] = scales.astype(jnp.bfloat16)


def forward(x, dy, stacked, messages, rows):
    tokens, width = x.shape
    hidden = stacked.shape[1]

    def place_of(table, block):
        steps = stacked.shape[0] // len(table) // rows
        return lambda: lookup(table, lax.axis_index("dp")) * steps + block

    places = [[place_of(*block) for block in blocks] for blocks in messages]
    return pl.pallas_call(
        lambda *refs: forward_kernel(places, rows, *refs),
        in_specs=[pl.BlockSpec(memory_space=pltpu.HBM)] * 3,
        out_shape=[jax.ShapeDtypeStruct((3, tokens, hidden), jnp.bfloat16)]
        + [jax.ShapeDtypeStruct((len(blocks) * rows + PAD, hidden), jnp.bfloat16) for blocks in messages],
        scratch_shapes=[
            pltpu.VMEM(x.shape, x.dtype),
            pltpu.VMEM(dy.shape, dy.dtype),
            pltpu.VMEM(stacked.shape, stacked.dtype),
            *[pltpu.VMEM((tokens, hidden), jnp.float32)] * 3,
            pltpu.VMEM((rows, hidden), jnp.float32),
            pltpu.SemaphoreType.DMA((10,)),
        ],
        compiler_params=pltpu.CompilerParams(vmem_limit_bytes=60 << 20),
        cost_estimate=CHEAP,
        name="forward",
    )(x, dy, stacked)


def pick(values, step):
    if all(value == values[0] + at for at, value in enumerate(values)):
        return step + values[0] if len(values) > 1 else jnp.int32(values[0])
    out = jnp.int32(values[0])
    for at, value in enumerate(values[1:], 1):
        out = jnp.where(step == at, value, out)
    return out


def piece_kernel(place, per, got, extra, last, *refs):
    step = pl.program_id(0)
    x_ref, dy_ref, d_ref = refs[:3]
    outs = refs[3 + 2 * len(got) + extra :]
    rows = x_ref.shape[1]
    left = jnp.where(lax.div(place(step), per) == 2, dy_ref[...], x_ref[...])
    total_ref = outs[-1]
    total_ref[...] = lax.dot_general(left, d_ref[0], (((0,), (0,)), ((), ())), preferred_element_type=jnp.float32)
    factors = []
    for at, blocks in enumerate(got):
        scales = refs[4 + 2 * at][...].astype(jnp.float32)
        row = lax.broadcasted_iota(jnp.int32, scales.shape, 0)
        here = pick([PAD if block is None else block for block in blocks], step)
        factors.append(jnp.sum(jnp.where(row == here, scales, 0.0), axis=0, keepdims=True) * (1.0 / TOP))
    top = jnp.zeros((8, total_ref.shape[1]), jnp.float32)
    for part in chunks(rows):
        total = total_ref[part, :]
        for at, factor in enumerate(factors):
            total = total + decode(refs[3 + 2 * at][part, :], factor)
        if last:
            outs[0][part, :] = total
        else:
            if factors:
                total_ref[part, :] = total
            top = jnp.maximum(top, fold(total))
    if not last:
        out_ref, scales_ref = outs[:2]
        scale = write_codes(total_ref, top, out_ref, pl.multiple_of(step * rows, rows))
        row = lax.broadcasted_iota(jnp.int32, scales_ref.shape, 0)
        scales_ref[...] = jnp.where(row == step, scale, jnp.where(step == 0, 0.0, scales_ref[...]))
        out_ref[pl.ds(out_ref.shape[0] - PAD, PAD), :] = scales_ref[...].astype(jnp.bfloat16)


def piece(x, dy, factors, rows, blocks, got=(), after=None, last=False, cost=PIECE):
    tokens, width = x.shape
    hidden = factors.shape[2]
    per = width // rows
    shard = 3 * width // len(blocks[0][0])
    steps = shard // rows
    tables = [table for table, _ in blocks]
    within = [block for _, block in blocks]

    def place(i):
        r = lax.axis_index("dp")
        owner = lookup(tables[0], r)
        for at, table in enumerate(tables[1:], 1):
            if table != tables[at - 1]:
                owner = jnp.where(i >= at, lookup(table, r), owner)
        return owner * steps + pick(within, i)

    def column(i):
        return (0, lax.rem(place(i), per))

    in_specs = [
        pl.BlockSpec((tokens, rows), column),
        pl.BlockSpec((tokens, rows), column),
        pl.BlockSpec((1, tokens, hidden), lambda i: (lax.div(place(i), per), 0, 0)),
    ]
    operands = [x, dy, factors]
    for message, parts in got:
        present = [part for part in parts if part is not None]
        nearest = [present[0] if part is None else part for part in parts]
        scales = (message.shape[0] - PAD) // PAD
        in_specs += [
            pl.BlockSpec((rows, hidden), lambda i, nearest=nearest: (pick(nearest, i), 0)),
            pl.BlockSpec((PAD, hidden), lambda i, scales=scales: (scales, 0)),
        ]
        operands += [message, message]
    extra = 0
    if after is not None:
        extra = 1
        operands.append(after)
        in_specs.append(pl.BlockSpec(memory_space=pl.ANY))
    if last:
        out_specs = pl.BlockSpec((rows, hidden), lambda i: (i, 0))
        out_shape = jax.ShapeDtypeStruct((len(blocks) * rows, hidden), jnp.float32)
        scratch = [pltpu.VMEM((rows, hidden), jnp.float32)]
    else:
        out_specs = pl.BlockSpec((len(blocks) * rows + PAD, hidden), lambda i: (0, 0))
        out_shape = jax.ShapeDtypeStruct((len(blocks) * rows + PAD, hidden), jnp.bfloat16)
        scratch = [pltpu.VMEM((PAD, hidden), jnp.float32), pltpu.VMEM((rows, hidden), jnp.float32)]
    return pl.pallas_call(
        lambda *refs: piece_kernel(place, per, [parts for _, parts in got], extra, last, *refs),
        grid=(len(blocks),),
        in_specs=in_specs,
        out_specs=out_specs,
        out_shape=out_shape,
        scratch_shapes=scratch,
        compiler_params=pltpu.CompilerParams(vmem_limit_bytes=LITTLE),
        cost_estimate=cost,
        name="piece",
    )(*operands)


def finish_kernel(rows, sum_ref, *refs):
    out_ref, squares_ref = refs[-2:]
    height, hidden = out_ref.shape
    codes = refs[:-2]
    scales = [code[height:, :].astype(jnp.float32) * (1.0 / TOP) for code in codes]
    top = jnp.zeros((8, hidden), jnp.float32)
    for part in chunks(height):
        block = part.start // rows
        total = sum_ref[part, :]
        for code, factor in zip(codes, scales):
            total = total + decode(code[part, :], factor[block : block + 1])
        out_ref[part, :] = total
        top = top + jnp.sum((total * total).reshape(-1, 8, hidden), axis=0)
    row = jnp.sum(sum(top[:, at : at + 128] for at in range(0, hidden, 128)), axis=0, keepdims=True)
    squares_ref[...] = jnp.broadcast_to(row, squares_ref.shape)


def finish(partial, messages, rows, count):
    whole = pl.BlockSpec(partial.shape, lambda i: (0, 0))
    return pl.pallas_call(
        lambda *refs: finish_kernel(rows, *refs),
        grid=(1,),
        in_specs=[whole] + [pl.BlockSpec(message.shape, lambda i: (0, 0)) for message in messages],
        out_specs=[whole, pl.BlockSpec((count, 128), lambda i: (0, 0))],
        out_shape=[
            jax.ShapeDtypeStruct(partial.shape, jnp.float32),
            jax.ShapeDtypeStruct((count, 128), jnp.float32),
        ],
        compiler_params=pltpu.CompilerParams(vmem_limit_bytes=LITTLE),
        cost_estimate=PIECE,
        name="finish",
    )(partial, *messages)


def join_kernel(rows, sum_ref, code_ref, out_ref, total_ref):
    height, hidden = sum_ref.shape
    scales = code_ref[height:, :].astype(jnp.float32) * (1.0 / TOP)
    row = lax.broadcasted_iota(jnp.int32, scales.shape, 0)
    new_scales = jnp.zeros_like(scales)
    for block in range(height // rows):
        top = jnp.zeros((8, hidden), jnp.float32)
        for part in chunks(rows):
            here = slice(block * rows + part.start, block * rows + part.stop)
            total = sum_ref[here, :] + decode(code_ref[here, :], scales[block : block + 1])
            total_ref[part, :] = total
            top = jnp.maximum(top, fold(total))
        scale = write_codes(total_ref, top, out_ref, block * rows)
        new_scales = jnp.where(row == block, scale, new_scales)
    out_ref[height:, :] = new_scales.astype(jnp.bfloat16)


def join(partial, message, rows):
    whole = pl.BlockSpec(message.shape, lambda i: (0, 0))
    return pl.pallas_call(
        lambda *refs: join_kernel(rows, *refs),
        grid=(1,),
        in_specs=[pl.BlockSpec(partial.shape, lambda i: (0, 0)), whole],
        out_specs=whole,
        out_shape=jax.ShapeDtypeStruct(message.shape, message.dtype),
        scratch_shapes=[pltpu.VMEM((rows, partial.shape[1]), jnp.float32)],
        compiler_params=pltpu.CompilerParams(vmem_limit_bytes=LITTLE),
        cost_estimate=PIECE,
        name="join",
    )(partial, message)


def update_kernel(max_norm, states, total_ref, g_ref, p_ref, m1_ref, m2_ref, *outs):
    clip = clip_of(jnp.sum(total_ref[...], keepdims=True), max_norm)
    for part in chunks(g_ref.shape[0]):
        param, first, second = adam(clip, g_ref[part, :], p_ref[part, :], m1_ref[part, :], m2_ref[part, :])
        values = (param, first, second) if states else (param.astype(jnp.bfloat16),)
        for out, value in zip(outs, values):
            out[part, :] = value


def update(total, shard, param, first, second, max_norm, rows, states):
    block = pl.BlockSpec((rows, shard.shape[1]), lambda i: (i, 0))
    dtypes = [jnp.float32] * 3 if states else [jnp.bfloat16]
    return pl.pallas_call(
        lambda *refs: update_kernel(max_norm, states, *refs),
        grid=(shard.shape[0] // rows,),
        in_specs=[pl.BlockSpec(total.shape, lambda i: (0, 0))] + [block] * 4,
        out_specs=[block] * len(dtypes),
        out_shape=[jax.ShapeDtypeStruct(shard.shape, dtype) for dtype in dtypes],
        compiler_params=pltpu.CompilerParams(vmem_limit_bytes=LITTLE),
        cost_estimate=CHEAP,
        name="states" if states else "update",
    )(total, shard, param, first, second)


def behind_of(value, other, cost=CHEAP):
    return pl.pallas_call(
        lambda *refs: None,
        grid=(1,),
        in_specs=[pl.BlockSpec(memory_space=pl.ANY), pl.BlockSpec((PAD, 128), lambda i: (0, 0))],
        out_specs=pl.BlockSpec(memory_space=pl.ANY),
        out_shape=jax.ShapeDtypeStruct(value.shape, value.dtype),
        input_output_aliases={0: 0},
        compiler_params=pltpu.CompilerParams(vmem_limit_bytes=LITTLE),
        cost_estimate=cost,
        name="behind",
    )(value, other)


def both_of(own, other, after, cut):
    columns = own.shape[1]

    def kernel(own_ref, other_ref, after_ref, both_ref):
        both_ref[...] = jnp.where(pl.program_id(0) == 0, own_ref[...], other_ref[...])

    return pl.pallas_call(
        kernel,
        grid=(2,),
        in_specs=[
            pl.BlockSpec((cut, columns), lambda i: (0, 0)),
            pl.BlockSpec((cut, columns), lambda i: (0, 0)),
            pl.BlockSpec((PAD, 128), lambda i: (0, 0)),
        ],
        out_specs=pl.BlockSpec((cut, columns), lambda i: (i, 0)),
        out_shape=jax.ShapeDtypeStruct((2 * cut, columns), own.dtype),
        compiler_params=pltpu.CompilerParams(vmem_limit_bytes=LITTLE),
        cost_estimate=PIECE,
        name="both",
    )(own, other, after)


def fill_kernel(moves, count, *refs):
    out, sems = refs[-2:]
    r = lax.axis_index("dp")
    copies = []
    for at, (source, low, size, table, shard, first) in enumerate(moves):
        to = pl.multiple_of(lookup(table, r) * shard + first, PAD)
        copies.append(pltpu.make_async_copy(refs[source].at[low : low + size], out.at[pl.ds(to, size)], sems.at[at]))
        copies[-1].start()
    for copy in copies:
        copy.wait()


def fill(buffer, values, moves, height):
    columns = values[0].shape[1]
    return pl.pallas_call(
        lambda *refs: fill_kernel(moves, len(values), *refs),
        in_specs=[pl.BlockSpec(memory_space=pltpu.VMEM)] * len(values)
        + [pl.BlockSpec(memory_space=pltpu.HBM)] * (buffer is not None),
        out_specs=pl.BlockSpec(memory_space=pltpu.HBM),
        out_shape=jax.ShapeDtypeStruct((height, columns), values[0].dtype),
        input_output_aliases={} if buffer is None else {len(values): 0},
        scratch_shapes=[pltpu.SemaphoreType.DMA((len(moves),))],
        compiler_params=pltpu.CompilerParams(vmem_limit_bytes=LITTLE),
        cost_estimate=CHEAP,
        name="fill",
    )(*values, *([] if buffer is None else [buffer]))


def paired(weights, inputs, out_grads, master, moment1, moment2):
    n = lax.axis_size("dp")
    pairs = n // 2
    ring = list(range(0, pairs, 2)) + list(range(pairs - 1 - pairs % 2, 0, -2))
    place = {pair: at for at, pair in enumerate(ring)}

    def at_offset(r, offset, flip):
        return 2 * ring[(place[r // 2] + offset) % pairs] + ((r % 2) ^ flip)

    def table(offset, flip):
        return [at_offset(r, offset, flip) for r in range(n)]

    def send(value, offset, flip=0):
        return lax.ppermute(value, "dp", [(r, at_offset(r, offset, flip)) for r in range(n)])

    stacked = weights[0]
    x, dy = inputs[0], out_grads[0]
    width = x.shape[1]
    shard_rows = stacked.shape[0] // n
    rows = math.gcd(shard_rows, width, 256)

    steps = shard_rows // rows

    every, most, rest, end = list(range(steps)), list(range(steps - 1)), list(range(1, steps)), steps - 1

    def at(*blocks):
        return [(table(offset, flip), block) for offset, flip, block in blocks]

    def made(blocks, got=(), **more):
        return piece(x, dy, factors, rows, blocks, got, **more)

    factors, message = forward(x, dy, stacked, [at(*[(2, 1, b) for b in every])], rows)
    cross_far = send(message, 0, 1)
    message = made(at((-1, 0, end), (-1, 1, end)))
    ahead = send(message, -1)
    message = made(at(*[(-1, 1, b) for b in most]), after=message)
    cross_back = send(message, 0, 1)
    own_far = made(at(*[(2, 0, b) for b in every]), after=message, last=True)
    message = made(at(*[(1, 1, b) for b in every]), after=own_far)
    cross_next = send(message, 0, 1)
    own_back = made(at(*[(-1, 0, b) for b in most]), after=message, last=True)
    by_ring = send(join(own_far, cross_far, rows), 1)
    message = join(own_back, cross_back, rows)
    from_ahead = send(message, -1)
    message = made(at(*[(0, 1, b) for b in every]), [(ahead, [None] * end + [1])], after=message)
    cross_own = send(message, 0, 1)
    from_behind = send(join(made(at(*[(1, 0, b) for b in every]), [(by_ring, every)], last=True), cross_next, rows), 1)
    partial = made(at(*[(0, 0, b) for b in every]), [(from_ahead, most + [None]), (ahead, [None] * end + [0])], last=True)
    shard, squares = finish(partial, [cross_own, from_behind], rows, n * lax.axis_size("section"))

    total = lax.all_to_all(squares, ("dp", "section"), 0, 0, tiled=True)
    max_norm = math.sqrt(lax.axis_size("section") * stacked.size)
    states = (shard, master[0], moment1[0], moment2[0], max_norm)
    (own,) = update(total, *states, shard_rows, False)

    cut = shard_rows * 5 // 8 // PAD * PAD
    other = send(own, 0, 1)
    behind = behind_of(send(own, 1), other)
    tail = send(own[cut:], -1)
    behind_cross = send(behind, 0, 1)
    far = send(behind, 1)
    tail = behind_of(tail, behind, cost_of(3.4))
    tail_cross = send(tail, 0, 1)
    both = send(both_of(own, other, behind_cross, cut), -1)
    far = behind_of(behind_of(far, behind_cross), tail_cross)
    far_cross = send(far, 0, 1)
    new_param, new_first, new_second = update(total, *states, rows, True)

    def move(value, offset, flip, low=0, first=0, size=shard_rows):
        return (value, low, size, table(offset, flip), shard_rows, first)

    gathered = fill(
        None,
        [own, other, behind, tail, behind_cross, tail_cross, far],
        [
            move(0, 0, 0),
            move(1, 0, 1),
            move(2, -1, 0),
            move(3, 1, 0, 0, cut, shard_rows - cut),
            move(4, -1, 1),
            move(5, 1, 1, 0, cut, shard_rows - cut),
            move(6, -2, 0),
        ],
        stacked.shape[0],
    )
    gathered = fill(
        gathered,
        [both, far_cross],
        [move(0, 1, 0, 0, 0, cut), move(0, 1, 1, cut, 0, cut), move(1, -2, 1)],
        stacked.shape[0],
    )
    return new_param[None], new_first[None], new_second[None], gathered[None]


def local(weights, *rest):
    n = lax.axis_size("dp")
    height = weights.shape[1]
    shard, width = height // n, height // 3
    fits = n == 8 and height % n == 0 and math.gcd(shard, width, 256) % 128 == 0 and shard // math.gcd(shard, width, 256) > 2
    return (paired if fits else plain)(weights, *rest)


def solution(mesh):
    whole = P("section", None, None)
    split = P("section", "dp", None)
    return jax.shard_map(
        local,
        mesh=mesh,
        in_specs=(whole, split, split, split, split, split),
        out_specs=(split, split, split, whole),
        check_vma=False,
    )
```
